32 devices in a mesh: grp: 2 (over y), seq: 4 (over z), dp: 2 (over x), head: 2 (over core).
Axes of the slice: x: 2, y: 2, z: 4, core: 2. Of those that a mesh axis runs over, the one named last changes fastest.
Arguments:
- tokens: bfloat16 [4, 512, 4096], P(('grp', 'dp'), 'seq', 'head'), parts along dimension 0, may hold values from -6 to 6
- ssd_input: bfloat16 [4, 512, 4096], P(('grp', 'dp'), 'seq', 'head'), parts along dimension 0, may hold values from -6 to 6
- grad_out: bfloat16 [4, 512, 4096], P(('grp', 'dp'), 'seq', 'head'), parts along dimension 0, may hold values from -6 to 6
- w_bc: bfloat16 [4096, 256], P(('head', 'dp')), may hold values from -0.0029296875 to 0.0029296875
- w_dt: bfloat16 [4096, 64], P(('head', 'dp')), may hold values from -0.09375 to 0.09375
- decay_rate: float32 [64], P('head'), may hold values from 0 to 1, as said below
- dt_bias: float32 [64], P('head'), may hold values from -2 to 0.5
Outputs:
- grad_input: bfloat16 [4, 512, 4096], P(('grp', 'dp'), 'seq', 'head'), parts along dimension 0
- grad_tokens: bfloat16 [4, 512, 4096], P(('grp', 'dp'), 'seq', 'head'), parts along dimension 0
- grad_w_bc: float32 [8192, 256], P(('grp', 'head', 'dp')), parts along dimension 0
- grad_w_dt: float32 [8192, 64], P(('grp', 'head', 'dp')), parts along dimension 0
The draws below stay inside these ranges and needn't reach their ends.
There are 2 independent parts, one for each index of `grp`. The reference program is written for one: setup_inputs(seed, part) draws one part's arguments, and reference() takes and returns one part's arrays. A program takes and returns all parts, laid end to end along the dimension named above; an argument that names none is the same for every part. Nothing has to cross between parts.
Inputs may be any that keep to these rules, and one draw needn't show every extreme that they name: `decay_rate`: each head's decay rate is positive.
All inputs are finite; a program needn't handle non-finite values.
Results may differ from the reference program's by a relative error of at most 0.0049.
Values may be sent and summed in bfloat16 or wider, within the bound.
No kernel may reach another device: no remote copies, remote signals or barrier semaphores. Data moves between devices by JAX's collectives and lax.ppermute only.
A program may use at most 64 MiB of HBM per device.

```python
import jax
import jax.numpy as jnp
from jax import lax

D = 4096
N = 128
P_SIZE = 64
HEADS = 64
TOK_DEV = 128
SEQS = 2
LEN = 512


def draw_decay_rate(key, part):
    key = jax.random.fold_in(key, 11)
    key_slow, key_fast, key_pick = jax.random.split(key, 3)
    slow = jnp.exp(jax.random.uniform(key_slow, (HEADS,), jnp.float32, jnp.log(0.5), jnp.log(3.0))) / LEN
    fast = jnp.exp(jax.random.uniform(key_fast, (HEADS,), jnp.float32, jnp.log(0.05), jnp.log(0.1)))
    share = 0.5
    picked = jax.random.uniform(key_pick, (HEADS,), jnp.float32) < share
    return jnp.where(picked, fast, slow).astype(jnp.float32)


def levels(stream_key, extent, cuts, smallest, top_value):
    def one(dim, parts):
        steps = jax.random.uniform(jax.random.fold_in(jax.random.fold_in(stream_key, 6), dim), (parts,), jnp.float32, smallest / len(cuts), top_value / len(cuts))
        return jnp.repeat(jnp.exp(steps), extent[dim] // parts).reshape((-1,) + (1,) * (len(extent) - dim - 1))

    loudness = one(*cuts[0])
    for cut in cuts[1:]:
        loudness = loudness * one(*cut)
    return loudness


def bell_draw(rng, shape, width, most, cuts=(), kind=jnp.bfloat16):
    values = jax.random.normal(rng, shape, jnp.float32) * width
    if len(cuts) > 0:
        values = levels(rng, shape, cuts, -0.22, 0.18) * values
    return jnp.clip(values, min=-most, max=most).astype(kind)


def setup_inputs(seed: int = 0, part: int = 0) -> dict:
    key_of = jax.random.split(jax.random.key(seed), 8)
    part_keys = jax.random.split(jax.random.fold_in(key_of[7], part), 8)
    return {
        "tokens": bell_draw(part_keys[0], (SEQS, LEN, D), 1.0, 6.0, ((0, 2), (1, 4), (2, 2))),
        "ssd_input": bell_draw(part_keys[1], (SEQS, LEN, HEADS * P_SIZE), 1.0, 6.0, ((0, 2), (1, 4), (2, 2))),
        "grad_out": bell_draw(part_keys[2], (SEQS, LEN, HEADS * P_SIZE), 1.0, 6.0, ((0, 2), (1, 4), (2, 2))),
        "w_bc": bell_draw(key_of[3], (D, 2 * N), (8 * D * N) ** -0.5, 0.0029296875, ((0, 4),)),
        "w_dt": bell_draw(key_of[4], (D, HEADS), D ** -0.5, 0.09375, ((0, 4),)),
        "decay_rate": draw_decay_rate(jax.random.fold_in(key_of[7], 71), part),
        "dt_bias": jnp.clip(-2.0 + 2.5 * jax.random.uniform(key_of[6], (HEADS,), jnp.float32) ** levels(key_of[6], (HEADS,), ((0, 2),), -0.2, 0.2), -2.0, 0.5),
    }


def unpack_block(values, bc_block, raw_block, decay_rate, dt_bias):
    row_count = values.shape[0]
    head_count = decay_rate.shape[0]
    state_size = bc_block.shape[1] // 2
    step_size = jax.nn.softplus(raw_block + dt_bias[None, :])
    cumulative = jnp.cumsum(-step_size * decay_rate[None, :], axis=0)
    per_head = values.reshape(row_count, head_count, -1)
    return (per_head, bc_block[:, :state_size], bc_block[:, state_size:], step_size, cumulative)

def block_state(values, bc_block, raw_block, decay_rate, dt_bias):
    per_head, input_vec, readout, step_size, cumulative = unpack_block(values, bc_block, raw_block, decay_rate, dt_bias)
    weights = jnp.exp(cumulative[-1][None, :] - cumulative) * step_size
    state = jnp.einsum('sh,shp,sn->hpn', weights, per_head, input_vec, precision=lax.Precision.HIGHEST)
    return (state, jnp.exp(cumulative[-1]))

def block_output(values, bc_block, raw_block, decay_rate, dt_bias, incoming):
    per_head, input_vec, readout, step_size, cumulative = unpack_block(values, bc_block, raw_block, decay_rate, dt_bias)
    row_count = values.shape[0]
    scores = jnp.dot(readout, input_vec.T, precision=lax.Precision.HIGHEST)
    position = jnp.arange(row_count)
    causal = position[:, None] >= position[None, :]
    leading = cumulative.T
    gap_matrix = leading[:, :, None] - leading[:, None, :]
    kernel = jnp.exp(jnp.where(causal[None], gap_matrix, -jnp.inf)) * scores[None] * step_size.T[:, None, :]
    within = jnp.einsum('hts,shp->thp', kernel, per_head, precision=lax.Precision.HIGHEST)
    carried = jnp.einsum('tn,hpn->thp', readout, incoming, precision=lax.Precision.HIGHEST)
    carried = carried * jnp.exp(cumulative)[:, :, None]
    return (within + carried).reshape(row_count, -1)

def ssd_sequence(values, bc_cols, raw_cols, decay_rate, dt_bias):
    block_count = values.shape[0] // TOK_DEV
    head_count = decay_rate.shape[0]
    head_size = values.shape[1] // head_count
    state_size = bc_cols.shape[1] // 2
    blocks = (values.reshape(block_count, TOK_DEV, -1), bc_cols.reshape(block_count, TOK_DEV, -1), raw_cols.reshape(block_count, TOK_DEV, -1))

    def advance(carried_state, block):
        value_block, bc_block, raw_block = block
        state, decay = block_state(value_block, bc_block, raw_block, decay_rate, dt_bias)
        output = block_output(value_block, bc_block, raw_block, decay_rate, dt_bias, carried_state)
        return (decay[:, None, None] * carried_state + state, output)
    start = jnp.zeros((head_count, head_size, state_size), jnp.float32)
    _, outputs = lax.scan(advance, start, blocks)
    return outputs.reshape(values.shape[0], -1)

def reference(tokens, ssd_input, grad_out, w_bc, w_dt, decay_rate, dt_bias):

    def one_sequence(members):
        features, values, cotangent = members
        bc_cols = jnp.dot(features, w_bc, preferred_element_type=jnp.float32)
        raw_cols = jnp.dot(features, w_dt, preferred_element_type=jnp.float32)

        def forward(value_arg, bc_arg, raw_arg):
            return ssd_sequence(value_arg, bc_arg, raw_arg, decay_rate, dt_bias)
        _, pullback = jax.vjp(forward, values.astype(jnp.float32), bc_cols, raw_cols)
        grad_values, grad_bc, grad_raw = pullback(cotangent.astype(jnp.float32))
        low_bc = grad_bc.astype(jnp.bfloat16)
        low_raw = grad_raw.astype(jnp.bfloat16)
        grad_features = (jnp.dot(low_bc, w_bc.T, preferred_element_type=jnp.float32) + jnp.dot(low_raw, w_dt.T, preferred_element_type=jnp.float32)).astype(jnp.bfloat16)
        weight_bc = jnp.dot(features.T, low_bc, preferred_element_type=jnp.float32)
        weight_dt = jnp.dot(features.T, low_raw, preferred_element_type=jnp.float32)
        return (grad_values.astype(jnp.bfloat16), grad_features, weight_bc, weight_dt)
    grad_input, grad_tokens, weight_bc, weight_dt = lax.map(one_sequence, (tokens, ssd_input, grad_out))
    scale = 1.0 / (SEQS * LEN)
    return (grad_input, grad_tokens, lax.optimization_barrier(jnp.sum(weight_bc, axis=0)) * scale, lax.optimization_barrier(jnp.sum(weight_dt, axis=0)) * scale)
```

```python
import jax
import jax.numpy as jnp
from jax import lax
from jax.sharding import PartitionSpec as P

CHUNKS = 4
BF = jnp.bfloat16
F32 = jnp.float32


def cyclic(a, axis, by):
    count = lax.axis_size(axis)
    return lax.ppermute(a, axis, [(i, (i + by) % count) for i in range(count)])


def along(a, axis, by):
    count = lax.axis_size(axis)
    return lax.ppermute(a, axis, [(i, i + by) for i in range(count) if 0 <= i + by < count])


def mm(a, b, ca, cb):
    return lax.dot_general(a, b, (((ca,), (cb,)), ((), ())), preferred_element_type=F32)


def relay(block, axis):
    count = lax.axis_size(axis)
    slots = []
    for way in (1, -1):
        held = block
        for _ in range(count - 1):
            held = along(held, axis, way)
            slots.append(held)
    return slots


def chain(own, decay, axis, way):
    count = lax.axis_size(axis)
    sent, total = own.astype(BF), None
    for hop in range(1, count):
        source = hop - 1 if way > 0 else count - hop
        got = lax.ppermute(sent, axis, [(source, source + way)])
        total = got if total is None else total + got
        if hop < count - 1:
            sent = (decay * got.astype(F32) + own).astype(BF)
    return total


def body(tokens, ssd_input, grad_out, w_bc, w_dt, decay_rate, dt_bias):
    feats, xb, gb = tokens[0], ssd_input[0], grad_out[0]
    rows, width = feats.shape
    heads = decay_rate.shape[0]
    size = width // heads
    n_dp, n_seq, n_head = (lax.axis_size(a) for a in ("dp", "seq", "head"))
    d, c = lax.axis_index("dp"), lax.axis_index("head")
    part = width // n_dp
    state_n = w_bc.shape[1] // 2

    def piece(r):
        return lax.dynamic_slice_in_dim(feats, ((d + r) % n_dp) * part, part, 1)

    items = [piece(0)] + [cyclic(piece(r), "dp", r) for r in range(1, n_dp)]
    block = jnp.concatenate(items, axis=0)

    def project(a):
        return jnp.concatenate([mm(a, w_bc, 1, 0), mm(a, w_dt, 1, 0)], axis=1)

    total = project(items[0])
    for r in range(1, n_dp):
        total = total + cyclic(project(items[r]), "dp", -r)
    proj = total
    for r in range(1, n_head):
        proj = proj + cyclic(total, "head", r)
    b = proj[:, :state_n].astype(BF)
    cc = proj[:, state_n : 2 * state_n].astype(BF)
    raw = lax.dynamic_slice_in_dim(proj[:, 2 * state_n :], c * heads, heads, 1)
    pre = raw + dt_bias[None]
    dt = jax.nn.softplus(pre)
    cum = jnp.cumsum(-dt * decay_rate[None], axis=0)
    last = cum[-1]
    grow = jnp.exp(cum)
    tail = jnp.exp(last[None] - cum)
    w = tail * dt
    decay = jnp.exp(last)

    def spread(a):
        return jnp.repeat(a, size, axis=1)

    wx = (spread(w) * xb.astype(F32)).astype(BF)
    eg = (spread(grow) * gb.astype(F32)).astype(BF)
    state = mm(wx, b, 0, 0)
    back = mm(eg, cc, 0, 0)
    step = width // CHUNKS
    dec = jnp.repeat(decay, size)[:, None]
    ins, outs = [], []
    for k in range(CHUNKS):
        s = slice(k * step, (k + 1) * step)
        ins.append(chain(state[s], dec[s], "seq", 1))
        outs.append(chain(back[s], dec[s], "seq", -1))
    incoming = jnp.concatenate(ins, axis=0)
    outgoing = jnp.concatenate(outs, axis=0)

    pos = jnp.arange(rows)
    causal = pos[:, None] >= pos[None, :]
    scores = mm(cc, b, 1, 1)
    lead = cum.T
    decays = jnp.exp(jnp.where(causal[None], lead[:, :, None] - lead[:, None, :], -jnp.inf)) * dt.T[:, None, :]
    kern = (decays * scores[None]).astype(BF)
    xh = xb.reshape(rows, heads, size)
    gh = gb.reshape(rows, heads, size)
    y = jnp.einsum("hts,shp->thp", kern, xh, preferred_element_type=F32)
    gx = jnp.einsum("hts,thp->shp", kern, gh, preferred_element_type=F32)
    m = jnp.einsum("thp,shp->hts", gh, xh, preferred_element_type=F32)
    ds = jnp.sum(decays * m, axis=0).astype(BF)
    xf, gf = xh.astype(F32), gh.astype(F32)
    rowsum = jnp.sum(y * gf, axis=2)
    colsum = jnp.sum(gx * xf, axis=2)

    u = mm(cc, incoming, 1, 1).reshape(rows, heads, size)
    v = mm(b, outgoing, 1, 1).reshape(rows, heads, size)
    dgrow = jnp.sum(u * gf, axis=2)
    dw = jnp.sum(v * xf, axis=2)
    gx = gx + w[:, :, None] * v
    db = mm(ds, cc, 0, 0) + mm(wx, outgoing, 1, 0)
    dc = mm(ds, b, 1, 0) + mm(eg, incoming, 1, 0)
    ddecay = jnp.sum((incoming.astype(F32) * outgoing.astype(F32)).reshape(heads, -1), axis=1)
    wdw = w * dw
    dcum = rowsum - colsum + grow * dgrow - wdw
    dlast = jnp.sum(wdw, axis=0) + decay * ddecay
    rev = jnp.cumsum(dcum[::-1], axis=0)[::-1] + dlast[None]
    ddt = colsum / dt + tail * dw - decay_rate[None] * rev
    graw = ddt * jax.nn.sigmoid(pre)

    local = jnp.concatenate([db, dc], axis=1)
    bc_back = local
    for r in range(1, n_head):
        bc_back = bc_back + cyclic(local, "head", r)
    raws = lax.all_gather(graw.astype(BF), "head", axis=1, tiled=True)
    low = jnp.concatenate([bc_back.astype(BF), raws], axis=1)

    panel = jnp.concatenate([w_bc, w_dt], axis=1)
    grads = jnp.zeros((rows, width), BF)
    for r in range(n_dp):
        other = panel if r == 0 else cyclic(panel, "dp", r)
        term = mm(low, other, 1, 1).astype(BF)
        grads = lax.dynamic_update_slice_in_dim(grads, term, ((d - r) % n_dp) * part, 1)

    lows = jnp.concatenate([low] + [cyclic(low, "dp", r) for r in range(1, n_dp)], axis=0)
    half = lows.shape[0] // n_head
    mine = lax.dynamic_slice_in_dim(lows, c * half, half, 0)
    toks = [block] + relay(block, "seq")
    got = relay(mine, "seq")
    total = mm(block, lows, 0, 0)
    for t, q in zip(toks[1:], got):
        q = lax.all_gather(q, "head", axis=0, tiled=True)
        total = total + mm(t, q, 0, 0)
    total = total * (1.0 / (rows * n_seq * n_dp))
    return (
        gx.reshape(rows, width).astype(BF)[None],
        grads[None],
        total[:, : 2 * state_n],
        total[:, 2 * state_n :],
    )


def solution(mesh):
    in_specs = (
        P(("grp", "dp"), "seq", "head"),
        P(("grp", "dp"), "seq", "head"),
        P(("grp", "dp"), "seq", "head"),
        P(("head", "dp"), None),
        P(("head", "dp"), None),
        P("head"),
        P("head"),
    )
    out_specs = (
        P(("grp", "dp"), "seq", "head"),
        P(("grp", "dp"), "seq", "head"),
        P(("grp", "head", "dp"), None),
        P(("grp", "head", "dp"), None),
    )
    return jax.shard_map(body, mesh=mesh, in_specs=in_specs, out_specs=out_specs, check_vma=False)
```

```python
import functools

import jax
import jax.numpy as jnp
from jax import lax
from jax.experimental import pallas as pl
from jax.experimental.pallas import tpu as pltpu
from jax.sharding import PartitionSpec as P

CHUNKS = 4
PARTS = 4
BF = jnp.bfloat16
F32 = jnp.float32
TOP = lax.Precision.HIGHEST
LIMIT = 56 * 1024 * 1024


def cyclic(a, axis, by):
    count = lax.axis_size(axis)
    return lax.ppermute(a, axis, [(i, (i + by) % count) for i in range(count)])


def mm(a, b, ca, cb, precision=None):
    return lax.dot_general(
        a, b, (((ca,), (cb,)), ((), ())), preferred_element_type=F32, precision=precision
    )


def halves(a):
    high = a.astype(BF)
    return high, (a - high.astype(F32)).astype(BF)


def head_lanes(heads, width, size, first=0):
    row = lax.broadcasted_iota(jnp.int32, (heads, width), 0)
    col = lax.broadcasted_iota(jnp.int32, (heads, width), 1) + first
    low = row * size
    return jnp.where((col >= low) & (col < low + size), 1.0, 0.0).astype(F32)


def spread(a, pick):
    high, low = halves(a)
    both = jnp.concatenate([pick, pick], axis=0)
    return mm(jnp.concatenate([high, low], axis=0), both, 0, 0)


def call(kernel, out_shape, flops, *args, scratch=()):
    size = sum(a.size * a.dtype.itemsize for a in args)
    return pl.pallas_call(
        kernel,
        out_shape=out_shape,
        in_specs=[pl.BlockSpec(memory_space=pltpu.VMEM)] * len(args),
        out_specs=jax.tree.map(lambda _: pl.BlockSpec(memory_space=pltpu.VMEM), out_shape),
        scratch_shapes=list(scratch),
        compiler_params=pltpu.CompilerParams(vmem_limit_bytes=LIMIT),
        cost_estimate=pl.CostEstimate(flops=flops, bytes_accessed=size, transcendentals=0),
    )(*args)


def struct(shape, dtype):
    return jax.ShapeDtypeStruct(shape, dtype)


def project_kernel(a_ref, bc_ref, dt_ref, out_ref):
    a = a_ref[...]
    state_n = bc_ref.shape[1] // 2
    rows = a.shape[0]
    bc = mm(a, bc_ref[...], 1, 0)
    out_ref[0:rows, :] = bc[:, :state_n]
    out_ref[rows : 2 * rows, :] = bc[:, state_n:]
    out_ref[2 * rows :, :] = mm(a, dt_ref[...], 1, 0).T


def project(a, w_bc, w_dt):
    rows = a.shape[0]
    total = 2 * rows + w_dt.shape[1]
    return call(
        project_kernel,
        struct((total, w_bc.shape[1] // 2), F32),
        2 * a.size * (w_bc.shape[1] + w_dt.shape[1]),
        a,
        w_bc,
        w_dt,
    )


def state_kernel(count, size, *refs):
    proj = refs[:count]
    x_ref, g_ref, rate_ref, bias_ref, own_ref, decay_ref, bc_ref, hp_ref = refs[count:]
    heads = rate_ref.shape[0]
    rows = x_ref.shape[0]
    chunks, step = own_ref.shape[1], own_ref.shape[3]
    first = pl.multiple_of(2 * rows + lax.axis_index("head") * heads, 8)
    bc = proj[0][0 : 2 * rows, :]
    pre = proj[0][pl.ds(first, heads), :] + bias_ref[...]
    for ref in proj[1:]:
        bc = bc + ref[0 : 2 * rows, :]
        pre = pre + ref[pl.ds(first, heads), :]
    bc_ref[...] = bc
    dt = jnp.maximum(pre, 0.0) + jnp.log1p(jnp.exp(-jnp.abs(pre)))
    row = lax.broadcasted_iota(jnp.int32, (rows, rows), 0)
    col = lax.broadcasted_iota(jnp.int32, (rows, rows), 1)
    cum = mm(-dt * rate_ref[...], jnp.where(row <= col, 1.0, 0.0), 1, 0, TOP)
    last = cum[:, rows - 1 : rows]
    grow = jnp.exp(cum)
    w = jnp.exp(last - cum) * dt
    decay = jnp.exp(last)
    for k, part in enumerate((pre, dt, cum, grow, w)):
        hp_ref[k * heads : (k + 1) * heads, :] = part
    way = lax.rem(lax.axis_index("seq"), 2)
    kinds = ((w, x_ref, bc[:rows], way), (grow, g_ref, bc[rows:], 1 - way))
    for scale, ref, vec, place in kinds:
        high, low = halves(vec.T)
        wide = jnp.concatenate([high, low], axis=1)
        for k in range(chunks):
            pick = head_lanes(heads, step, size, k * step)
            if place is way:
                decay_ref[k] = jnp.sum(pick * decay, axis=0, keepdims=True)
            value = spread(scale, pick.astype(BF)) * ref[:, k * step : (k + 1) * step].astype(F32)
            top, rest = halves(value)
            own_ref[place, k] = mm(wide, jnp.concatenate([top, top], axis=0), 1, 0) + mm(
                high, rest, 1, 0
            )


def inner_kernel(first, pairs, size, bc_ref, hp_ref, x_ref, g_ref, gx_ref, ds_ref, sums_ref, gy_ref, xg_ref):
    rows = x_ref.shape[0]
    heads = hp_ref.shape[0] // 5
    lanes = 2 * size
    width = pairs * lanes
    b, c = bc_ref[0:rows, :], bc_ref[rows : 2 * rows, :]
    scores = mm(c, b, 1, 1, TOP)
    row = lax.broadcasted_iota(jnp.int32, (rows, rows), 0)
    col = lax.broadcasted_iota(jnp.int32, (rows, rows), 1)
    causal = row >= col
    dt = hp_ref[heads : 2 * heads, :]
    cum = hp_ref[2 * heads : 3 * heads, :]
    cum_t = cum.T
    lane = lax.broadcasted_iota(jnp.int32, (rows, lanes), 1)
    sides = [jnp.where(lane < size, 1.0, 0.0).astype(BF), jnp.where(lane < size, 0.0, 1.0).astype(BF)]
    ds = jnp.zeros((rows, rows), F32)
    for j in range(pairs):
        place = slice(j * lanes, (j + 1) * lanes)
        here = slice((first + j) * lanes, (first + j + 1) * lanes)
        x, g = x_ref[:, here], g_ref[:, here]
        xs = jnp.concatenate([x * s for s in sides], axis=0)
        gs = jnp.concatenate([g * s for s in sides], axis=0)
        m = mm(gs, x, 1, 1)
        kern = []
        for i in range(2):
            h = 2 * (first + j) + i
            gap = cum_t[:, h : h + 1] - cum[h : h + 1, :]
            fall = jnp.exp(jnp.where(causal, gap, -jnp.inf)) * dt[h : h + 1, :]
            kern.append((fall * scores).astype(BF))
            ds = ds + fall * m[i * rows : (i + 1) * rows]
        y = mm(jnp.concatenate(kern, axis=1), xs, 1, 0)
        gx = mm(jnp.concatenate(kern, axis=0), gs, 0, 0)
        gx_ref[:, place] = gx
        after = slice(width + j * lanes, width + (j + 1) * lanes)
        gy_ref[:, place], gy_ref[:, after] = halves(g.astype(F32) * y)
        xg_ref[:, place], xg_ref[:, after] = halves(x.astype(F32) * gx)
    ds_ref[...] = ds
    pick = head_lanes(2 * pairs, width, size).astype(BF)
    pick = jnp.concatenate([pick, pick], axis=1)
    sums_ref[0] = mm(pick, gy_ref[...], 1, 1)
    sums_ref[1] = mm(pick, xg_ref[...], 1, 1)


def outer_kernel(size, parts, *refs):
    in_ref, out_ref, x_ref, g_ref, bc_ref, hp_ref, decay_ref, rate_ref = refs[:8]
    gxs, dss, sums = (refs[8 + k * parts : 8 + (k + 1) * parts] for k in range(3))
    grad_ref, back_ref, wv_ref, eu_ref, io_ref = refs[8 + 3 * parts :]
    rows, width = x_ref.shape
    heads = rate_ref.shape[0]
    chunks, step = decay_ref.shape[0], decay_ref.shape[2]
    piece = width // parts
    b, c = bc_ref[0:rows, :], bc_ref[rows : 2 * rows, :]
    pre, dt, cum, grow, w = (hp_ref[k * heads : (k + 1) * heads, :] for k in range(5))
    ds = dss[0][...]
    for ref in dss[1:]:
        ds = ds + ref[...]
    db = mm(c, ds, 0, 0, TOP)
    dc = mm(b, ds, 0, 1, TOP)
    b_wide = jnp.concatenate(halves(b), axis=1)
    c_wide = jnp.concatenate(halves(c), axis=1)
    for k in range(chunks):
        place = slice(k * step, (k + 1) * step)
        after = slice(width + k * step, width + (k + 1) * step)
        pick = head_lanes(heads, step, size, k * step).astype(BF)
        incoming, outgoing = in_ref[k], out_ref[k]
        u = mm(c_wide, jnp.concatenate([incoming, incoming], axis=0), 1, 0)
        v = mm(b_wide, jnp.concatenate([outgoing, outgoing], axis=0), 1, 0)
        scale = spread(w, pick)
        wx = scale * x_ref[:, place].astype(F32)
        eg = spread(grow, pick) * g_ref[:, place].astype(F32)
        for q in range(step // piece) if step >= piece else (0,):
            if step >= piece:
                at = k * step + q * piece
                inner = slice(q * piece, (q + 1) * piece)
                term = gxs[at // piece][...]
            else:
                at, inner = k * step, slice(0, step)
                term = gxs[at // piece][:, at % piece : at % piece + step]
            total = term + scale[:, inner] * v[:, inner]
            grad_ref[:, at : at + total.shape[1]] = total.astype(BF)
        wv_ref[:, place], wv_ref[:, after] = halves(wx * v)
        eu_ref[:, place], eu_ref[:, after] = halves(eg * u)
        db = db + mm(
            jnp.concatenate([outgoing, outgoing], axis=1), jnp.concatenate(halves(wx), axis=1), 1, 1
        )
        dc = dc + mm(
            jnp.concatenate([incoming, incoming], axis=1), jnp.concatenate(halves(eg), axis=1), 1, 1
        )
        io_ref[:, place] = jnp.sum(incoming.astype(F32) * outgoing.astype(F32), axis=0, keepdims=True)
    pick = head_lanes(heads, width, size)
    ddecay = jnp.sum(pick * io_ref[...], axis=1, keepdims=True)
    pick = pick.astype(BF)
    pick = jnp.concatenate([pick, pick], axis=1)
    wdw = mm(pick, wv_ref[...], 1, 1)
    egu = mm(pick, eu_ref[...], 1, 1)
    rowsum = jnp.concatenate([s[0] for s in sums], axis=0)
    colsum = jnp.concatenate([s[1] for s in sums], axis=0)
    dcum = rowsum - colsum + egu - wdw
    row = lax.broadcasted_iota(jnp.int32, (rows, rows), 0)
    col = lax.broadcasted_iota(jnp.int32, (rows, rows), 1)
    rev = mm(dcum, jnp.where(row >= col, 1.0, 0.0), 1, 0, TOP)
    decay = grow[:, rows - 1 : rows]
    rev = rev + jnp.sum(wdw, axis=1, keepdims=True) + decay * ddecay
    gate = 1.0 / (1.0 + jnp.exp(-pre))
    small = 1e-30
    ratio = jnp.where(dt > small, gate / jnp.maximum(dt, small), 1.0)
    back_ref[0:rows, :] = db
    back_ref[rows : 2 * rows, :] = dc
    back_ref[2 * rows :, :] = (colsum + wdw) * ratio - rate_ref[...] * rev * gate


def low_kernel(count, heads, *refs):
    out_ref = refs[count]
    top = refs[0].shape[0] - heads
    me = lax.axis_index("head")
    total = refs[0][0:top, :]
    for ref in refs[1:count]:
        total = total + ref[0:top, :]
    out_ref[0:top, :] = total.astype(BF)
    for r in range(count):
        at = pl.multiple_of(top + lax.rem(me - r + count, count) * heads, 16)
        out_ref[pl.ds(at, heads), :] = refs[r][top:, :].astype(BF)


def token_kernel(count, low_ref, *refs):
    out_ref = refs[2 * count]
    me = lax.axis_index("dp")
    low = low_ref[...]
    cols = refs[0].shape[1]
    part = refs[0].shape[0]
    for r in range(count):
        at = pl.multiple_of(lax.rem(me - r + count, count) * part, 128)
        term = mm(low[:cols], refs[2 * r][...], 0, 1) + mm(low[cols:], refs[2 * r + 1][...], 0, 1)
        out_ref[:, pl.ds(at, part)] = term.astype(BF)


def weight_kernel(scale, count, low_ref, *refs):
    toks, bc_ref, dt_ref = refs[:count], refs[count], refs[count + 1]
    seqs, rows, part = toks[0].shape
    cols = bc_ref.shape[1]
    total = jnp.zeros((low_ref.shape[2], part), F32)
    me = lax.axis_index("seq")
    for r in range(count):
        for s in range(seqs):
            at = lax.rem(me - s + seqs, seqs)
            total = total + mm(low_ref[r, s], toks[r][at], 1, 0)
    total = total * scale
    bc_ref[...] = total[:cols].T
    dt_ref[...] = total[cols:].T


def chains(own, decay):
    count = lax.axis_size("seq")
    place = lax.axis_index("seq")
    chunks = own.shape[1]
    even = lax.rem(place, 2) == 0
    links = [
        [(i, i + 1) for i in range(0, count - 1, 2)],
        [(i, i + 1) for i in range(1, count - 1, 2)],
    ]
    pairs = []
    for group in links:
        to = {i: i for i in range(count)}
        for i, j in group:
            to[i], to[j] = j, i
        pairs.append(sorted(to.items()))
    shape = (chunks + 1,) + own.shape[2:]
    stores = [jnp.zeros(shape, BF), jnp.zeros(shape, BF)]
    got = [None, None]
    ends = (place == 0) | (place == count - 1)
    for slot in range(1, count + chunks - 1):
        fresh = [None, None]
        for kind in (0, 1):
            used = any(
                0 <= slot - hop < chunks
                for i, j in links[kind]
                for hop in (j, count - j)
            )
            if not used:
                continue
            goes_up = even if kind == 0 else ~even
            chunk = jnp.clip(jnp.where(goes_up, slot - place - 1, slot - count + place), 0, chunks - 1)
            value = lax.dynamic_index_in_dim(own[kind], chunk, 0, False)
            before = got[1 - kind]
            if before is not None:
                kept = before.astype(F32) * lax.dynamic_index_in_dim(decay, chunk, 0, False)
                value = value + (jnp.where(ends, 0.0, kept) if kind == 0 else kept)
            fresh[kind] = lax.ppermute(value.astype(BF), "seq", pairs[kind])
        got = fresh
        for kind in (0, 1):
            if got[kind] is None:
                continue
            below = ~even if kind == 0 else even
            chunk = jnp.where(below, slot - place, slot - count + place + 1)
            chunk = jnp.where((chunk >= 0) & (chunk < chunks), chunk, chunks)
            stores[kind] = lax.dynamic_update_index_in_dim(stores[kind], got[kind], chunk, 0)
    first, second = stores
    incoming = jnp.where(even, second, first)
    outgoing = jnp.where(even, first, second)
    incoming = jnp.where(place == 0, jnp.zeros_like(incoming), incoming)
    outgoing = jnp.where(place == count - 1, jnp.zeros_like(outgoing), outgoing)
    return incoming, outgoing


def body(tokens, ssd_input, grad_out, w_bc, w_dt, decay_rate, dt_bias):
    feats, x, g = tokens[0], ssd_input[0], grad_out[0]
    rows, width = feats.shape
    heads = decay_rate.shape[0]
    size = width // heads
    n_dp, n_seq, n_head = (lax.axis_size(a) for a in ("dp", "seq", "head"))
    d = lax.axis_index("dp")
    part = width // n_dp
    state_n = w_bc.shape[1] // 2
    rate, bias = decay_rate[:, None], dt_bias[:, None]

    def piece(r):
        return lax.dynamic_slice_in_dim(feats, ((d + r) % n_dp) * part, part, 1)

    items = [piece(0)] + [cyclic(piece(r), "dp", r) for r in range(1, n_dp)]
    toks = [lax.all_gather(a, "seq") for a in items]

    total = project(items[0], w_bc, w_dt)
    for r in range(1, n_dp):
        total = total + cyclic(project(items[r], w_bc, w_dt), "dp", -r)
    proj = [total] + [cyclic(total, "head", r) for r in range(1, n_head)]
    step = width // CHUNKS
    own, decay, bc, hp = call(
        functools.partial(state_kernel, n_head, size),
        (
            struct((2, CHUNKS, state_n, step), F32),
            struct((CHUNKS, 1, step), F32),
            struct((2 * rows, state_n), F32),
            struct((5 * heads, rows), F32),
        ),
        12 * rows * width * state_n,
        *proj,
        x,
        g,
        rate,
        bias,
    )
    incoming, outgoing = chains(own, decay)
    pairs = width // (2 * size) // PARTS
    span = width // PARTS
    inner = [
        call(
            functools.partial(inner_kernel, q * pairs, pairs, size),
            (
                struct((rows, span), F32),
                struct((rows, rows), F32),
                struct((2, 2 * pairs, rows), F32),
            ),
            8 * rows * rows * span,
            bc,
            hp,
            x,
            g,
            scratch=(pltpu.VMEM((rows, 2 * span), BF), pltpu.VMEM((rows, 2 * span), BF)),
        )
        for q in range(PARTS)
    ]
    grad_x, back = call(
        functools.partial(outer_kernel, size, PARTS),
        (struct((rows, width), BF), struct((2 * rows + heads, rows), F32)),
        16 * rows * width * state_n,
        incoming,
        outgoing,
        x,
        g,
        bc,
        hp,
        decay,
        rate,
        *[a[0] for a in inner],
        *[a[1] for a in inner],
        *[a[2] for a in inner],
        scratch=(
            pltpu.VMEM((rows, 2 * width), BF),
            pltpu.VMEM((rows, 2 * width), BF),
            pltpu.VMEM((1, width), F32),
        ),
    )
    backs = [back] + [cyclic(back, "head", r) for r in range(1, n_head)]
    low = call(
        functools.partial(low_kernel, n_head, heads),
        struct((2 * rows + n_head * heads, rows), BF),
        0,
        *backs,
    )
    weights = [(w_bc, w_dt)] + [
        (cyclic(w_bc, "dp", r), cyclic(w_dt, "dp", r)) for r in range(1, n_dp)
    ]
    grads = call(
        functools.partial(token_kernel, n_dp),
        struct((rows, width), BF),
        2 * rows * width * low.shape[0],
        low,
        *[a for pair in weights for a in pair],
    )
    share = low.shape[0] // n_head
    c = lax.axis_index("head")
    mine = lax.dynamic_slice_in_dim(low, c * share, share, 0)
    rest = []
    for r in range(n_dp):
        for s in range(n_seq):
            if r == 0 and s == 0:
                rest.append(mine)
                continue
            pairs_to = [
                (j * n_dp + i, (j + s) % n_seq * n_dp + (i + r) % n_dp)
                for i in range(n_dp)
                for j in range(n_seq)
            ]
            rest.append(lax.ppermute(mine, ("seq", "dp"), pairs_to))
    lows = jnp.stack(rest).reshape(n_dp, n_seq, share, rows)
    lows = lax.all_gather(lows, "head", axis=2, tiled=True)
    grad_bc, grad_dt = call(
        functools.partial(weight_kernel, 1.0 / (rows * n_seq * n_dp), n_dp),
        (struct((part, 2 * state_n), F32), struct((part, n_head * heads), F32)),
        2 * n_dp * n_seq * rows * part * low.shape[0],
        lows,
        *toks,
    )
    return grad_x[None], grads[None], grad_bc, grad_dt


def solution(mesh):
    in_specs = (
        P(("grp", "dp"), "seq", "head"),
        P(("grp", "dp"), "seq", "head"),
        P(("grp", "dp"), "seq", "head"),
        P(("head", "dp"), None),
        P(("head", "dp"), None),
        P("head"),
        P("head"),
    )
    out_specs = (
        P(("grp", "dp"), "seq", "head"),
        P(("grp", "dp"), "seq", "head"),
        P(("grp", "head", "dp"), None),
        P(("grp", "head", "dp"), None),
    )
    return jax.shard_map(body, mesh=mesh, in_specs=in_specs, out_specs=out_specs, check_vma=False)
```

```python
import functools

import jax
import jax.numpy as jnp
from jax import lax
from jax.experimental import pallas as pl
from jax.experimental.pallas import tpu as pltpu
from jax.sharding import PartitionSpec as P

CHUNKS = 4
PARTS = 4
EARLY = 2
GROUPS = 8
BF = jnp.bfloat16
F32 = jnp.float32
TOP = lax.Precision.HIGHEST
LIMIT = 56 * 1024 * 1024


def cyclic(a, axis, by):
    count = lax.axis_size(axis)
    return lax.ppermute(a, axis, [(i, (i + by) % count) for i in range(count)])


def mm(a, b, ca, cb, precision=None):
    return lax.dot_general(
        a, b, (((ca,), (cb,)), ((), ())), preferred_element_type=F32, precision=precision
    )


def halves(a):
    high = a.astype(BF)
    return high, (a - high.astype(F32)).astype(BF)


def head_lanes(heads, width, size, first=0):
    row = lax.broadcasted_iota(jnp.int32, (heads, width), 0)
    col = lax.broadcasted_iota(jnp.int32, (heads, width), 1) + first
    low = row * size
    return jnp.where((col >= low) & (col < low + size), 1.0, 0.0).astype(F32)


def spread(a, pick):
    high, low = halves(a)
    both = jnp.concatenate([pick, pick], axis=0)
    return mm(jnp.concatenate([high, low], axis=0), both, 0, 0)


VMEM = pl.BlockSpec(memory_space=pltpu.VMEM)
ANY = pl.BlockSpec(memory_space=pl.ANY)


def call(kernel, out_shape, flops, *args, scratch=(), specs=None, out_specs=None):
    size = sum(a.size * a.dtype.itemsize for a in args)
    return pl.pallas_call(
        kernel,
        out_shape=out_shape,
        grid=(1,),
        in_specs=specs or [VMEM] * len(args),
        out_specs=out_specs or jax.tree.map(lambda _: VMEM, out_shape),
        scratch_shapes=list(scratch),
        compiler_params=pltpu.CompilerParams(vmem_limit_bytes=LIMIT),
        cost_estimate=pl.CostEstimate(flops=flops, bytes_accessed=size, transcendentals=0),
    )(*args)


def struct(shape, dtype):
    return jax.ShapeDtypeStruct(shape, dtype)


def after(a, *others):
    return lax.optimization_barrier((a, others))[0]


def matchings(count):
    groups = [[(i, i + 1) for i in range(kind, count - 1, 2)] for kind in (0, 1)]
    pairs = []
    for group in groups:
        to = {i: i for i in range(count)}
        for i, j in group:
            to[i], to[j] = j, i
        pairs.append(sorted(to.items()))
    return groups, pairs


def split_kernel(count, a_ref, *refs):
    outs, sems = refs[:count], refs[count]
    me = lax.axis_index("dp")
    part = outs[0].shape[1]
    copies = []
    for r in range(count):
        at = pl.multiple_of(lax.rem(me + r, count) * part, 128)
        copies.append(pltpu.make_async_copy(a_ref.at[:, pl.ds(at, part)], outs[r], sems.at[r]))
    for copy in copies:
        copy.start()
    for copy in copies:
        copy.wait()


def project_kernel(a_ref, bc_ref, dt_ref, out_ref):
    a = a_ref[...]
    state_n = bc_ref.shape[1] // 2
    rows = a.shape[0]
    bc = mm(a, bc_ref[...], 1, 0)
    out_ref[0:rows, :] = bc[:, :state_n]
    out_ref[rows : 2 * rows, :] = bc[:, state_n:]
    out_ref[2 * rows :, :] = mm(dt_ref[...], a, 1, 1)


def project(a, w_bc, w_dt):
    rows = a.shape[0]
    total = 2 * rows + w_dt.shape[0]
    return call(
        project_kernel,
        struct((total, w_bc.shape[1] // 2), F32),
        2 * a.size * total,
        a,
        w_bc,
        w_dt,
    )


def state_kernel(count, size, *refs):
    proj = refs[:count]
    x_ref, g_ref, rate_ref, bias_ref, own_ref, decay_ref, bc_ref, hp_ref = refs[count:]
    heads = rate_ref.shape[1]
    rows = x_ref.shape[0]
    rate, bias = rate_ref[...].T, bias_ref[...].T
    chunks, step = own_ref.shape[1], own_ref.shape[3]
    first = pl.multiple_of(2 * rows + lax.axis_index("head") * heads, 8)
    bc = proj[0][0 : 2 * rows, :]
    pre = proj[0][pl.ds(first, heads), :] + bias
    for ref in proj[1:]:
        bc = bc + ref[0 : 2 * rows, :]
        pre = pre + ref[pl.ds(first, heads), :]
    bc_ref[...] = bc
    dt = jnp.maximum(pre, 0.0) + jnp.log1p(jnp.exp(-jnp.abs(pre)))
    row = lax.broadcasted_iota(jnp.int32, (rows, rows), 0)
    col = lax.broadcasted_iota(jnp.int32, (rows, rows), 1)
    cum = mm(-dt * rate, jnp.where(row <= col, 1.0, 0.0), 1, 0, TOP)
    last = cum[:, rows - 1 : rows]
    grow = jnp.exp(cum)
    w = jnp.exp(last - cum) * dt
    decay = jnp.exp(last)
    for k, part in enumerate((pre, dt, cum, grow, w)):
        hp_ref[k * heads : (k + 1) * heads, :] = part
    way = lax.rem(lax.axis_index("seq"), 2)
    kinds = ((w, x_ref, bc[:rows], way), (grow, g_ref, bc[rows:], 1 - way))
    for scale, ref, vec, place in kinds:
        high, low = halves(vec.T)
        wide = jnp.concatenate([high, low], axis=1)
        for k in range(chunks):
            pick = head_lanes(heads, step, size, k * step)
            if place is way:
                decay_ref[k] = jnp.sum(pick * decay, axis=0, keepdims=True)
            value = spread(scale, pick.astype(BF)) * ref[:, k * step : (k + 1) * step].astype(F32)
            top, rest = halves(value)
            own_ref[place, k] = mm(wide, jnp.concatenate([top, top], axis=0), 1, 0) + mm(
                high, rest, 1, 0
            )


def inner_kernel(first, pairs, size, bc_ref, hp_ref, x_ref, g_ref, *refs):
    gx_ref, ds_ref, sums_ref = refs[-5:-2]
    gy_ref, xg_ref = refs[-2:]
    rows = x_ref.shape[0]
    heads = hp_ref.shape[0] // 5
    lanes = 2 * size
    width = pairs * lanes
    if len(refs) == 6 and first > 0:
        scores = refs[0][...]
    else:
        scores = mm(bc_ref[rows : 2 * rows, :], bc_ref[0:rows, :], 1, 1, TOP)
        refs[0][...] = scores
    row = lax.broadcasted_iota(jnp.int32, (rows, rows), 0)
    col = lax.broadcasted_iota(jnp.int32, (rows, rows), 1)
    causal = row >= col
    dt = hp_ref[heads : 2 * heads, :]
    cum = hp_ref[2 * heads : 3 * heads, :]
    cum_t = cum.T
    lane = lax.broadcasted_iota(jnp.int32, (rows, lanes), 1)
    sides = [jnp.where(lane < size, 1.0, 0.0).astype(BF), jnp.where(lane < size, 0.0, 1.0).astype(BF)]
    ds = jnp.zeros((rows, rows), F32)
    for j in range(pairs):
        place = slice(j * lanes, (j + 1) * lanes)
        x, g = x_ref[:, place], g_ref[:, place]
        xs = jnp.concatenate([x * s for s in sides], axis=0)
        gs = jnp.concatenate([g * s for s in sides], axis=0)
        m = mm(gs, x, 1, 1)
        kern = []
        for i in range(2):
            h = 2 * (first + j) + i
            gap = cum_t[:, h : h + 1] - cum[h : h + 1, :]
            fall = jnp.exp(jnp.where(causal, gap, -jnp.inf)) * dt[h : h + 1, :]
            kern.append((fall * scores).astype(BF))
            ds = ds + fall * m[i * rows : (i + 1) * rows]
        y = mm(jnp.concatenate(kern, axis=1), xs, 1, 0)
        gx = mm(jnp.concatenate(kern, axis=0), gs, 0, 0)
        gx_ref[:, place] = gx
        late = slice(width + j * lanes, width + (j + 1) * lanes)
        gy_ref[:, place], gy_ref[:, late] = halves(g.astype(F32) * y)
        xg_ref[:, place], xg_ref[:, late] = halves(x.astype(F32) * gx)
    ds_ref[...] = ds
    pick = head_lanes(2 * pairs, width, size).astype(BF)
    pick = jnp.concatenate([pick, pick], axis=1)
    sums_ref[0] = mm(pick, gy_ref[...], 1, 1)
    sums_ref[1] = mm(pick, xg_ref[...], 1, 1)


def outer_kernel(size, parts, *refs):
    store_ref, x_ref, g_ref, bc_ref, hp_ref, decay_ref, rate_ref = refs[:7]
    gxs, dss, sums = (refs[7 + k * parts : 7 + (k + 1) * parts] for k in range(3))
    grad_ref, keep_ref, give_ref, wv_ref, eu_ref, io_ref = refs[7 + 3 * parts :]
    odd = lax.rem(lax.axis_index("seq"), 2)
    rate = rate_ref[...].T
    rows, width = x_ref.shape
    heads = rate_ref.shape[1]
    chunks, step = decay_ref.shape[0], decay_ref.shape[2]
    piece = width // parts
    b, c = bc_ref[0:rows, :], bc_ref[rows : 2 * rows, :]
    pre, dt, cum, grow, w = (hp_ref[k * heads : (k + 1) * heads, :] for k in range(5))
    ds = dss[0][...]
    for ref in dss[1:]:
        ds = ds + ref[...]
    db = mm(c, ds, 0, 0, TOP)
    dc = mm(b, ds, 0, 1, TOP)
    b_wide = jnp.concatenate(halves(b), axis=1)
    c_wide = jnp.concatenate(halves(c), axis=1)
    for k in range(chunks):
        place = slice(k * step, (k + 1) * step)
        late = slice(width + k * step, width + (k + 1) * step)
        pick = head_lanes(heads, step, size, k * step).astype(BF)
        incoming, outgoing = store_ref[1 - odd, k], store_ref[odd, k]
        u = mm(c_wide, jnp.concatenate([incoming, incoming], axis=0), 1, 0)
        v = mm(b_wide, jnp.concatenate([outgoing, outgoing], axis=0), 1, 0)
        scale = spread(w, pick)
        wx = scale * x_ref[:, place].astype(F32)
        eg = spread(grow, pick) * g_ref[:, place].astype(F32)
        for q in range(step // piece) if step >= piece else (0,):
            if step >= piece:
                at = k * step + q * piece
                inner = slice(q * piece, (q + 1) * piece)
                term = gxs[at // piece][...]
            else:
                at, inner = k * step, slice(0, step)
                term = gxs[at // piece][:, at % piece : at % piece + step]
            total = term + scale[:, inner] * v[:, inner]
            grad_ref[:, at : at + total.shape[1]] = total.astype(BF)
        wv_ref[:, place], wv_ref[:, late] = halves(wx * v)
        eu_ref[:, place], eu_ref[:, late] = halves(eg * u)
        db = db + mm(
            jnp.concatenate([outgoing, outgoing], axis=1), jnp.concatenate(halves(wx), axis=1), 1, 1
        )
        dc = dc + mm(
            jnp.concatenate([incoming, incoming], axis=1), jnp.concatenate(halves(eg), axis=1), 1, 1
        )
        io_ref[:, place] = jnp.sum(incoming.astype(F32) * outgoing.astype(F32), axis=0, keepdims=True)
    pick = head_lanes(heads, width, size)
    ddecay = jnp.sum(pick * io_ref[...], axis=1, keepdims=True)
    pick = pick.astype(BF)
    pick = jnp.concatenate([pick, pick], axis=1)
    wdw = mm(pick, wv_ref[...], 1, 1)
    egu = mm(pick, eu_ref[...], 1, 1)
    rowsum = jnp.concatenate([s[0] for s in sums], axis=0)
    colsum = jnp.concatenate([s[1] for s in sums], axis=0)
    dcum = rowsum - colsum + egu - wdw
    row = lax.broadcasted_iota(jnp.int32, (rows, rows), 0)
    col = lax.broadcasted_iota(jnp.int32, (rows, rows), 1)
    rev = mm(dcum, jnp.where(row >= col, 1.0, 0.0), 1, 0, TOP)
    decay = grow[:, rows - 1 : rows]
    rev = rev + jnp.sum(wdw, axis=1, keepdims=True) + decay * ddecay
    gate = 1.0 / (1.0 + jnp.exp(-pre))
    small = 1e-30
    ratio = jnp.where(dt > small, gate / jnp.maximum(dt, small), 1.0)
    core = lax.axis_index("head")
    keep_ref[0:rows, :] = jnp.where(core == 0, db, dc)
    keep_ref[rows:, :] = (colsum + wdw) * ratio - rate * rev * gate
    give_ref[...] = jnp.where(core == 0, dc, db)


def token_kernel(count, mine_ref, other_ref, *refs):
    out_ref = refs[2 * count]
    me, core = lax.axis_index("dp"), lax.axis_index("head")
    part, cols = refs[0].shape
    half = cols // 2
    heads = refs[1].shape[0] // 2
    for r in range(count):
        at = pl.multiple_of(lax.rem(me - r + count, count) * part, 128)
        total = None
        for k, ref in enumerate((mine_ref, other_ref)):
            at_col = pl.multiple_of(lax.rem(core + k, 2) * half, 128)
            at_row = pl.multiple_of(lax.rem(core + k, 2) * heads, 16)
            term = mm(ref[0:half, :], refs[2 * r][:, pl.ds(at_col, half)], 0, 1)
            term = term + mm(ref[half : mine_ref.shape[0], :], refs[2 * r + 1][pl.ds(at_row, heads), :], 0, 0)
            total = term if total is None else total + term
        out_ref[:, pl.ds(at, part)] = total.astype(BF)


def weight_kernel(scale, n_dp, n_seq, slots, *refs):
    count = 2 * len(slots) if n_dp > 1 else len(slots)
    toks, lows = refs[:count], refs[count:-6]
    bc_ref, dt_ref, tok_ref, low_ref, tok_sem, low_sem = refs[-6:]
    rows = toks[0].shape[0]
    share = lows[0].shape[0]
    per = lows[n_dp * n_seq].shape[0] // share
    core, place = lax.axis_index("head"), lax.axis_index("seq")
    even = lax.rem(place, 2) == 0
    copies = []
    for r in range(n_dp):
        for k, (kind, hop) in enumerate(slots):
            above = even if kind == 0 else ~even
            block = jnp.where(above, place + hop, place - hop)
            fits = (block >= 0) & (block < n_seq)
            if hop > 0 and kind == 1:
                fits = fits & jnp.where(above, place < n_seq - 1, place > 0)
            at = pl.multiple_of(jnp.clip(block, 0, n_seq - 1) * rows, 128)
            source = toks[k] if r == 0 else toks[len(slots) + k].at[pl.ds((r - 1) * rows, rows)]
            copy = pltpu.make_async_copy(source, tok_ref.at[r, pl.ds(at, rows)], tok_sem.at[r, k])
            copies.append((fits, copy))
    for r in range(n_dp):
        for s in range(n_seq):
            block = lax.rem(place - s + n_seq, n_seq)
            at = pl.multiple_of(block * rows, 128)
            for k in range(2):
                index = r * n_seq + s
                row = pl.multiple_of(lax.rem(core + k, 2) * share, 16)
                source = lows[index]
                if k == 1:
                    source = lows[n_dp * n_seq + index // per].at[pl.ds(index % per * share, share)]
                copy = pltpu.make_async_copy(
                    source, low_ref.at[r, pl.ds(row, share), pl.ds(at, rows)], low_sem.at[index, k]
                )
                copies.append((None, copy))
    for fits, copy in copies:
        if fits is None:
            copy.start()
        else:
            pl.when(fits)(copy.start)
    for fits, copy in copies:
        if fits is None:
            copy.wait()
        else:
            pl.when(fits)(copy.wait)
    total = mm(low_ref[0], tok_ref[0], 1, 0)
    for r in range(1, n_dp):
        total = total + mm(low_ref[r], tok_ref[r], 1, 0)
    total = total * scale
    half = bc_ref.shape[1] // 2
    heads = dt_ref.shape[0] // 2
    for k in range(2):
        bc_ref[:, k * half : (k + 1) * half] = total[k * share : k * share + half].T
        dt_ref[k * heads : (k + 1) * heads, :] = total[k * share + half : (k + 1) * share]


def relay(block, hops, held=None):
    count = lax.axis_size("seq")
    groups, pairs = matchings(count)
    held = held or [block, block]
    found, slots = [], []
    for hop in hops:
        fresh = [None, None]
        for kind in (0, 1):
            if any(i - hop + 1 >= 0 or j + hop - 1 < count for i, j in groups[kind]):
                fresh[kind] = lax.ppermute(held[1 - kind], "seq", pairs[kind])
                found.append(fresh[kind])
                slots.append((kind, hop))
        held = [h if f is None else f for f, h in zip(fresh, held)]
    return found, slots, held


def chains(own, decay, inner):
    count = lax.axis_size("seq")
    place = lax.axis_index("seq")
    chunks = own.shape[1]
    even = lax.rem(place, 2) == 0
    groups, pairs = matchings(count)
    store = jnp.zeros((2, chunks + 1) + own.shape[2:], BF)
    got = [None, None]
    done, todo = [], list(inner)
    ends = (place == 0) | (place == count - 1)
    for slot in range(1, count + chunks - 1):
        fresh, sent = [None, None], []
        for kind in (0, 1):
            used = any(
                0 <= slot - hop < chunks for i, j in groups[kind] for hop in (j, count - j)
            )
            if not used:
                continue
            goes_up = even if kind == 0 else ~even
            chunk = jnp.where(goes_up, slot - place - 1, slot - count + place)
            chunk = jnp.clip(chunk, 0, chunks - 1)
            zero = jnp.zeros_like(chunk)
            value = lax.dynamic_slice(
                own, (zero + kind, chunk, zero, zero), (1, 1) + own.shape[2:]
            )[0, 0]
            before = got[1 - kind]
            if before is not None:
                kept = before.astype(F32) * lax.dynamic_index_in_dim(decay, chunk, 0, False)
                value = value + (jnp.where(ends, 0.0, kept) if kind == 0 else kept)
            sent.append(value.astype(BF))
            fresh[kind] = lax.ppermute(sent[-1], "seq", pairs[kind])
        if todo:
            done.append(todo.pop(0)(*sent))
        ready = [a for a in fresh if a is not None] + ([done[-1][0]] if done else [])
        got = list(fresh)
        if len(ready) > 1:
            kept = lax.optimization_barrier(tuple(ready))
            live = [k for k in (0, 1) if fresh[k] is not None]
            for k, a in zip(live, kept):
                got[k] = a
        for kind in (0, 1):
            if got[kind] is None:
                continue
            below = ~even if kind == 0 else even
            chunk = jnp.where(below, slot - place, slot - count + place + 1)
            fits = (chunk >= 0) & (chunk < chunks)
            if kind == 1:
                fits = fits & ~ends
            chunk = jnp.where(fits, chunk, chunks)
            zero = jnp.zeros_like(chunk)
            store = lax.dynamic_update_slice(
                store, got[kind][None, None], (zero + kind, chunk, zero, zero)
            )
    done += [make() for make in todo]
    return store, done


def body(tokens, ssd_input, grad_out, w_bc, w_dt, decay_rate, dt_bias):
    feats, x, g = tokens[0], ssd_input[0], grad_out[0]
    rows, width = feats.shape
    heads = decay_rate.shape[0]
    size = width // heads
    n_dp, n_seq = lax.axis_size("dp"), lax.axis_size("seq")
    part = width // n_dp
    state_n = w_bc.shape[1] // 2
    w_dt = w_dt.T
    rate, bias = decay_rate[None], dt_bias[None]

    pieces = call(
        functools.partial(split_kernel, n_dp),
        [struct((rows, part), BF)] * n_dp,
        0,
        feats,
        scratch=[pltpu.SemaphoreType.DMA((n_dp,))],
        specs=[ANY],
        out_specs=[ANY] * n_dp,
    )
    items = [pieces[0]] + [cyclic(pieces[r], "dp", r) for r in range(1, n_dp)]
    first = project(items[0], w_bc, w_dt)
    partials = [first] + [
        cyclic(project(items[r], w_bc, w_dt), "dp", -r) for r in range(1, n_dp)
    ]
    proj = partials + [cyclic(a, "head", 1) for a in partials]
    cut = min(1 + EARLY, n_seq)
    early, slots, held = relay(items[0], range(1, cut))
    x = after(x, *early)
    step = width // CHUNKS
    own, decay, bc, hp = call(
        functools.partial(state_kernel, 2 * n_dp, size),
        (
            struct((2, CHUNKS, state_n, step), F32),
            struct((CHUNKS, 1, step), F32),
            struct((2 * rows, state_n), F32),
            struct((5 * heads, rows), F32),
        ),
        12 * rows * width * state_n,
        *proj,
        x,
        g,
        rate,
        bias,
    )
    pairs = width // (2 * size) // PARTS
    span = width // PARTS
    shared = []

    def inner(q, *others):
        held = after(bc, *others) if others else bc
        square = struct((rows, rows), F32)
        block = pl.BlockSpec((rows, span), lambda _: (0, q))
        out = call(
            functools.partial(inner_kernel, q * pairs, pairs, size),
            ([square] if q == 0 else [])
            + [struct((rows, span), F32), square, struct((2, 2 * pairs, rows), F32)],
            8 * rows * rows * span,
            held,
            hp,
            x,
            g,
            *shared,
            scratch=(pltpu.VMEM((rows, 2 * span), BF), pltpu.VMEM((rows, 2 * span), BF)),
            specs=[VMEM, VMEM, block, block] + [VMEM] * len(shared),
        )
        if q == 0:
            shared.append(out[0])
            out = out[1:]
        return out

    store, inners = chains(own, decay, [functools.partial(inner, q) for q in range(PARTS)])
    grad_x, keep, give = call(
        functools.partial(outer_kernel, size, PARTS),
        (
            struct((rows, width), BF),
            struct((rows + heads, rows), F32),
            struct((rows, rows), F32),
        ),
        16 * rows * width * state_n,
        store,
        x,
        g,
        bc,
        hp,
        decay,
        rate,
        *[a[0] for a in inners],
        *[a[1] for a in inners],
        *[a[2] for a in inners],
        scratch=(
            pltpu.VMEM((rows, 2 * width), BF),
            pltpu.VMEM((rows, 2 * width), BF),
            pltpu.VMEM((1, width), F32),
        ),
    )
    taken = cyclic(give, "head", 1)
    mine = jnp.concatenate([keep[:rows] + taken, keep[rows:]], axis=0).astype(BF)
    w_bc_later, w_dt_later = after((w_bc, w_dt), hp)
    weights = [w_bc, w_dt]
    for r in range(1, n_dp):
        weights += [cyclic(w_bc_later, "dp", r), cyclic(w_dt_later, "dp", r)]
    lows = []
    for r in range(n_dp):
        for s in range(n_seq):
            pairs_to = [
                (j * n_dp + i, (j + s) % n_seq * n_dp + (i + r) % n_dp)
                for i in range(n_dp)
                for j in range(n_seq)
            ]
            got = mine if r == s == 0 else lax.ppermute(mine, ("seq", "dp"), pairs_to)
            lows.append(got)
    per = -(-len(lows) // GROUPS)
    groups = [lows[k : k + per] for k in range(0, len(lows), per)]
    swapped = [cyclic(a[0] if per == 1 else jnp.concatenate(a, axis=0), "head", 1) for a in groups]
    grads = call(
        functools.partial(token_kernel, n_dp),
        struct((rows, width), BF),
        2 * rows * width * (2 * state_n + 2 * heads),
        lows[0],
        swapped[0],
        *weights,
    )
    held = after(tuple(held), store)
    found, rest, _ = relay(items[0], range(cut, n_seq), list(held))
    slots = [(0, 0)] + slots + rest
    toks = [items[0]] + early + found
    if n_dp > 1:
        others = items[1] if n_dp == 2 else jnp.concatenate(items[1:], axis=0)
        found, _, _ = relay(after(others, store), range(1, n_seq))
        toks += [others] + found
    cols = 2 * (rows + heads)
    grad_bc, grad_dt = call(
        functools.partial(weight_kernel, 1.0 / (rows * n_seq * n_dp), n_dp, n_seq, slots),
        (struct((part, 2 * state_n), F32), struct((2 * heads, part), F32)),
        2 * n_dp * n_seq * rows * part * cols,
        *toks,
        *lows,
        *swapped,
        specs=[ANY] * (len(toks) + len(lows) + len(swapped)),
        scratch=(
            pltpu.VMEM((n_dp, n_seq * rows, part), BF),
            pltpu.VMEM((n_dp, cols, n_seq * rows), BF),
            pltpu.SemaphoreType.DMA((n_dp, len(slots))),
            pltpu.SemaphoreType.DMA((len(lows), 2)),
        ),
    )
    return grad_x[None], grads[None], grad_bc, grad_dt.T


def solution(mesh):
    in_specs = (
        P(("grp", "dp"), "seq", "head"),
        P(("grp", "dp"), "seq", "head"),
        P(("grp", "dp"), "seq", "head"),
        P(("head", "dp"), None),
        P(("head", "dp"), None),
        P("head"),
        P("head"),
    )
    out_specs = (
        P(("grp", "dp"), "seq", "head"),
        P(("grp", "dp"), "seq", "head"),
        P(("grp", "head", "dp"), None),
        P(("grp", "head", "dp"), None),
    )
    return jax.shard_map(body, mesh=mesh, in_specs=in_specs, out_specs=out_specs, check_vma=False)
```

```python
import functools

import jax
import jax.numpy as jnp
from jax import lax
from jax.experimental import pallas as pl
from jax.experimental.pallas import tpu as pltpu
from jax.sharding import PartitionSpec as P

CHUNKS = 2
PARTS = 4
EARLY = (3, 0)
EAGER = 2
BF = jnp.bfloat16
F32 = jnp.float32
TOP = lax.Precision.HIGHEST
LIMIT = 56 * 1024 * 1024


def cyclic(a, axis, by):
    count = lax.axis_size(axis)
    return lax.ppermute(a, axis, [(i, (i + by) % count) for i in range(count)])


def mm(a, b, ca, cb, precision=None):
    return lax.dot_general(
        a, b, (((ca,), (cb,)), ((), ())), preferred_element_type=F32, precision=precision
    )


def halves(a):
    high = a.astype(BF)
    return high, (a - high.astype(F32)).astype(BF)


def head_lanes(heads, width, size, first=0):
    row = lax.broadcasted_iota(jnp.int32, (heads, width), 0)
    col = lax.broadcasted_iota(jnp.int32, (heads, width), 1) + first
    low = row * size
    return jnp.where((col >= low) & (col < low + size), 1.0, 0.0).astype(F32)


def spread(a, pick):
    high, low = halves(a)
    both = jnp.concatenate([pick, pick], axis=0)
    return mm(jnp.concatenate([high, low], axis=0), both, 0, 0)


VMEM = pl.BlockSpec(memory_space=pltpu.VMEM)
ANY = pl.BlockSpec(memory_space=pl.ANY)


def call(kernel, out_shape, flops, *args, scratch=(), specs=None, out_specs=None):
    size = sum(a.size * a.dtype.itemsize for a in args)
    return pl.pallas_call(
        kernel,
        out_shape=out_shape,
        grid=(1,),
        in_specs=specs or [VMEM] * len(args),
        out_specs=out_specs or jax.tree.map(lambda _: VMEM, out_shape),
        scratch_shapes=list(scratch),
        compiler_params=pltpu.CompilerParams(vmem_limit_bytes=LIMIT),
        cost_estimate=pl.CostEstimate(flops=flops, bytes_accessed=size, transcendentals=0),
    )(*args)


def struct(shape, dtype):
    return jax.ShapeDtypeStruct(shape, dtype)


def after(a, *others):
    return lax.optimization_barrier((a, others))[0]


def matchings(count):
    groups = [[(i, i + 1) for i in range(kind, count - 1, 2)] for kind in (0, 1)]
    pairs = []
    for group in groups:
        to = {i: i for i in range(count)}
        for i, j in group:
            to[i], to[j] = j, i
        pairs.append(sorted(to.items()))
    return groups, pairs


def split_kernel(a_ref, *outs):
    count = len(outs)
    me = lax.axis_index("dp")
    part = outs[0].shape[1]
    for r in range(count):
        at = pl.multiple_of(lax.rem(me + r, count) * part, 128)
        outs[r][...] = a_ref[:, pl.ds(at, part)]


def project_kernel(a_ref, bc_ref, dt_ref, out_ref):
    a = a_ref[...]
    state_n = bc_ref.shape[1] // 2
    rows = a.shape[0]
    bc = mm(a, bc_ref[...], 1, 0)
    out_ref[0:rows, :] = bc[:, :state_n]
    out_ref[rows : 2 * rows, :] = bc[:, state_n:]
    out_ref[2 * rows :, :] = mm(dt_ref[...], a, 1, 1)


def project(a, w_bc, w_dt):
    rows = a.shape[0]
    total = 2 * rows + w_dt.shape[0]
    return call(
        project_kernel,
        struct((total, w_bc.shape[1] // 2), F32),
        2 * a.size * total,
        a,
        w_bc,
        w_dt,
    )


def state_kernel(count, size, *refs):
    proj = refs[:count]
    x_ref, g_ref, rate_ref, bias_ref, own_ref, decay_ref, bc_ref, hp_ref = refs[count : count + 8]
    firsts = refs[count + 8 :]
    heads = rate_ref.shape[1]
    rows = x_ref.shape[0]
    rate, bias = rate_ref[...].T, bias_ref[...].T
    chunks, step = own_ref.shape[1], own_ref.shape[3]
    first = pl.multiple_of(2 * rows + lax.axis_index("head") * heads, 8)
    bc = proj[0][0 : 2 * rows, :]
    pre = proj[0][pl.ds(first, heads), :] + bias
    for ref in proj[1:]:
        bc = bc + ref[0 : 2 * rows, :]
        pre = pre + ref[pl.ds(first, heads), :]
    bc_ref[...] = bc
    dt = jnp.maximum(pre, 0.0) + jnp.log1p(jnp.exp(-jnp.abs(pre)))
    row = lax.broadcasted_iota(jnp.int32, (rows, rows), 0)
    col = lax.broadcasted_iota(jnp.int32, (rows, rows), 1)
    cum = mm(-dt * rate, jnp.where(row <= col, 1.0, 0.0), 1, 0, TOP)
    last = cum[:, rows - 1 : rows]
    grow = jnp.exp(cum)
    w = jnp.exp(last - cum) * dt
    decay = jnp.exp(last)
    for k, part in enumerate((pre, dt, cum, grow, w)):
        hp_ref[k * heads : (k + 1) * heads, :] = part
    lowest = lax.axis_index("seq") == 0
    sides = []
    for vec in (bc[:rows], bc[rows:]):
        high, low = halves(vec.T)
        sides.append((jnp.concatenate([high, low], axis=1), high))
    for k in range(chunks):
        pick = head_lanes(heads, step, size, k * step)
        decay_ref[k] = jnp.sum(pick * decay, axis=0, keepdims=True)
        pick = pick.astype(BF)
        both = []
        for kind, (scale, ref) in enumerate(((w, x_ref), (grow, g_ref))):
            wide, high = sides[kind]
            value = spread(scale, pick) * ref[:, k * step : (k + 1) * step].astype(F32)
            top, rest = halves(value)
            value = mm(wide, jnp.concatenate([top, top], axis=0), 1, 0) + mm(high, rest, 1, 0)
            own_ref[kind, k] = value
            both.append(value)
        firsts[k][...] = jnp.where(lowest, both[0], both[1]).astype(BF)


def inner_kernel(first, pairs, size, bc_ref, hp_ref, x_ref, g_ref, *refs):
    gx_ref, ds_ref, sums_ref = refs[-5:-2]
    gy_ref, xg_ref = refs[-2:]
    rows = x_ref.shape[0]
    heads = hp_ref.shape[0] // 5
    lanes = 2 * size
    width = pairs * lanes
    if len(refs) == 6 and first > 0:
        scores = refs[0][...]
    else:
        scores = mm(bc_ref[rows : 2 * rows, :], bc_ref[0:rows, :], 1, 1, TOP)
        refs[0][...] = scores
    row = lax.broadcasted_iota(jnp.int32, (rows, rows), 0)
    col = lax.broadcasted_iota(jnp.int32, (rows, rows), 1)
    causal = row >= col
    dt = hp_ref[heads : 2 * heads, :]
    cum = hp_ref[2 * heads : 3 * heads, :]
    cum_t = cum.T
    lane = lax.broadcasted_iota(jnp.int32, (rows, lanes), 1)
    sides = [jnp.where(lane < size, 1.0, 0.0).astype(BF), jnp.where(lane < size, 0.0, 1.0).astype(BF)]
    ds = jnp.zeros((rows, rows), F32)
    for j in range(pairs):
        place = slice(j * lanes, (j + 1) * lanes)
        x, g = x_ref[:, place], g_ref[:, place]
        xs = jnp.concatenate([x * s for s in sides], axis=0)
        gs = jnp.concatenate([g * s for s in sides], axis=0)
        m = mm(gs, x, 1, 1)
        kern = []
        for i in range(2):
            h = 2 * (first + j) + i
            gap = cum_t[:, h : h + 1] - cum[h : h + 1, :]
            fall = jnp.exp(jnp.where(causal, gap, -jnp.inf)) * dt[h : h + 1, :]
            kern.append((fall * scores).astype(BF))
            ds = ds + fall * m[i * rows : (i + 1) * rows]
        y = mm(jnp.concatenate(kern, axis=1), xs, 1, 0)
        gx = mm(jnp.concatenate(kern, axis=0), gs, 0, 0)
        gx_ref[:, place] = gx
        late = slice(width + j * lanes, width + (j + 1) * lanes)
        gy_ref[:, place], gy_ref[:, late] = halves(g.astype(F32) * y)
        xg_ref[:, place], xg_ref[:, late] = halves(x.astype(F32) * gx)
    ds_ref[...] = ds
    pick = head_lanes(2 * pairs, width, size).astype(BF)
    pick = jnp.concatenate([pick, pick], axis=1)
    sums_ref[0] = mm(pick, gy_ref[...], 1, 1)
    sums_ref[1] = mm(pick, xg_ref[...], 1, 1)


def outer_kernel(size, parts, *refs):
    store_ref, x_ref, g_ref, bc_ref, hp_ref, decay_ref, rate_ref = refs[:7]
    gxs, dss, sums = (refs[7 + k * parts : 7 + (k + 1) * parts] for k in range(3))
    grad_ref, keep_ref, give_ref, wv_ref, eu_ref, io_ref = refs[7 + 3 * parts :]
    rate = rate_ref[...].T
    rows, width = x_ref.shape
    heads = rate_ref.shape[1]
    chunks, step = decay_ref.shape[0], decay_ref.shape[2]
    piece = width // parts
    b, c = bc_ref[0:rows, :], bc_ref[rows : 2 * rows, :]
    pre, dt, cum, grow, w = (hp_ref[k * heads : (k + 1) * heads, :] for k in range(5))
    ds = dss[0][...]
    for ref in dss[1:]:
        ds = ds + ref[...]
    db = mm(c, ds, 0, 0, TOP)
    dc = mm(b, ds, 0, 1, TOP)
    b_wide = jnp.concatenate(halves(b), axis=1)
    c_wide = jnp.concatenate(halves(c), axis=1)
    for k in range(chunks):
        place = slice(k * step, (k + 1) * step)
        late = slice(width + k * step, width + (k + 1) * step)
        pick = head_lanes(heads, step, size, k * step).astype(BF)
        incoming, outgoing = store_ref[0, k], store_ref[1, k]
        u = mm(c_wide, jnp.concatenate([incoming, incoming], axis=0), 1, 0)
        v = mm(b_wide, jnp.concatenate([outgoing, outgoing], axis=0), 1, 0)
        scale = spread(w, pick)
        wx = scale * x_ref[:, place].astype(F32)
        eg = spread(grow, pick) * g_ref[:, place].astype(F32)
        for q in range(step // piece) if step >= piece else (0,):
            if step >= piece:
                at = k * step + q * piece
                inner = slice(q * piece, (q + 1) * piece)
                term = gxs[at // piece][...]
            else:
                at, inner = k * step, slice(0, step)
                term = gxs[at // piece][:, at % piece : at % piece + step]
            total = term + scale[:, inner] * v[:, inner]
            grad_ref[:, at : at + total.shape[1]] = total.astype(BF)
        wv_ref[:, place], wv_ref[:, late] = halves(wx * v)
        eu_ref[:, place], eu_ref[:, late] = halves(eg * u)
        db = db + mm(
            jnp.concatenate([outgoing, outgoing], axis=1), jnp.concatenate(halves(wx), axis=1), 1, 1
        )
        dc = dc + mm(
            jnp.concatenate([incoming, incoming], axis=1), jnp.concatenate(halves(eg), axis=1), 1, 1
        )
        io_ref[:, place] = jnp.sum(incoming.astype(F32) * outgoing.astype(F32), axis=0, keepdims=True)
    pick = head_lanes(heads, width, size)
    ddecay = jnp.sum(pick * io_ref[...], axis=1, keepdims=True)
    pick = pick.astype(BF)
    pick = jnp.concatenate([pick, pick], axis=1)
    wdw = mm(pick, wv_ref[...], 1, 1)
    egu = mm(pick, eu_ref[...], 1, 1)
    rowsum = jnp.concatenate([s[0] for s in sums], axis=0)
    colsum = jnp.concatenate([s[1] for s in sums], axis=0)
    dcum = rowsum - colsum + egu - wdw
    row = lax.broadcasted_iota(jnp.int32, (rows, rows), 0)
    col = lax.broadcasted_iota(jnp.int32, (rows, rows), 1)
    rev = mm(dcum, jnp.where(row >= col, 1.0, 0.0), 1, 0, TOP)
    decay = grow[:, rows - 1 : rows]
    rev = rev + jnp.sum(wdw, axis=1, keepdims=True) + decay * ddecay
    gate = 1.0 / (1.0 + jnp.exp(-pre))
    small = 1e-30
    ratio = jnp.where(dt > small, gate / jnp.maximum(dt, small), 1.0)
    core = lax.axis_index("head")
    keep_ref[0:rows, :] = jnp.where(core == 0, db, dc)
    keep_ref[rows:, :] = (colsum + wdw) * ratio - rate * rev * gate
    give_ref[...] = jnp.where(core == 0, dc, db)


def token_kernel(count, mine_ref, other_ref, *refs):
    out_ref = refs[2 * count]
    me, core = lax.axis_index("dp"), lax.axis_index("head")
    part, cols = refs[0].shape
    half = cols // 2
    heads = refs[1].shape[0] // 2
    for r in range(count):
        at = pl.multiple_of(lax.rem(me - r + count, count) * part, 128)
        total = None
        for k, ref in enumerate((mine_ref, other_ref)):
            at_col = pl.multiple_of(lax.rem(core + k, 2) * half, 128)
            at_row = pl.multiple_of(lax.rem(core + k, 2) * heads, 16)
            term = mm(ref[0:half, :], refs[2 * r][:, pl.ds(at_col, half)], 0, 1)
            term = term + mm(ref[half:, :], refs[2 * r + 1][pl.ds(at_row, heads), :], 0, 0)
            total = term if total is None else total + term
        out_ref[:, pl.ds(at, part)] = total.astype(BF)


def weight_kernel(scale, n_dp, n_seq, slots, *refs):
    count = 2 * len(slots) if n_dp > 1 else len(slots)
    toks, lows = refs[:count], refs[count:-6]
    bc_ref, dt_ref, tok_ref, low_ref, tok_sem, low_sem = refs[-6:]
    rows = toks[0].shape[0]
    share = lows[0].shape[1]
    core, place, me = lax.axis_index("head"), lax.axis_index("seq"), lax.axis_index("dp")
    even = lax.rem(place, 2) == 0
    copies = []
    for r in range(n_dp):
        for k, (kind, hop) in enumerate(slots):
            above = even if kind == 0 else ~even
            block = jnp.where(above, place + hop, place - hop)
            fits = (block >= 0) & (block < n_seq)
            if hop > 0 and kind == 1:
                fits = fits & jnp.where(above, place < n_seq - 1, place > 0)
            at = pl.multiple_of(jnp.clip(block, 0, n_seq - 1) * rows, 128)
            source = toks[k] if r == 0 else toks[len(slots) + k].at[pl.ds((r - 1) * rows, rows)]
            copy = pltpu.make_async_copy(source, tok_ref.at[r, pl.ds(at, rows)], tok_sem.at[r, k])
            copies.append((fits, copy))
    for r in range(n_dp):
        for s in range(n_seq):
            index = s * n_dp + lax.rem(me - r + n_dp, n_dp)
            for k in range(2):
                row = pl.multiple_of(lax.rem(core + k, 2) * share, 16)
                copy = pltpu.make_async_copy(
                    lows[k].at[index],
                    low_ref.at[r, pl.ds(row, share), pl.ds(s * rows, rows)],
                    low_sem.at[r * n_seq + s, k],
                )
                copies.append((None, copy))
    for fits, copy in copies:
        if fits is None:
            copy.start()
        else:
            pl.when(fits)(copy.start)
    for fits, copy in copies:
        if fits is None:
            copy.wait()
        else:
            pl.when(fits)(copy.wait)
    total = mm(low_ref[0], tok_ref[0], 1, 0)
    for r in range(1, n_dp):
        total = total + mm(low_ref[r], tok_ref[r], 1, 0)
    total = total * scale
    half = bc_ref.shape[1] // 2
    heads = dt_ref.shape[0] // 2
    for k in range(2):
        bc_ref[:, k * half : (k + 1) * half] = total[k * share : k * share + half].T
        dt_ref[k * heads : (k + 1) * heads, :] = total[k * share + half : (k + 1) * share]


def relay(block, hops, held=None):
    count = lax.axis_size("seq")
    groups, pairs = matchings(count)
    held = held or [block, block]
    found, slots = [], []
    for hop in hops:
        fresh = [None, None]
        for kind in (0, 1):
            if any(i - hop + 1 >= 0 or j + hop - 1 < count for i, j in groups[kind]):
                fresh[kind] = lax.ppermute(held[1 - kind], "seq", pairs[kind])
                found.append(fresh[kind])
                slots.append((kind, hop))
        held = [h if f is None else f for f, h in zip(fresh, held)]
    return found, slots, held


def chains(first, own, decay, inner, early):
    count = lax.axis_size("seq")
    place = lax.axis_index("seq")
    chunks = len(first)
    store = jnp.zeros((2, chunks + 1) + own.shape[2:], BF)
    got = list(first)
    done = [make() for make in inner[:EAGER]]
    for hop in range(1, count):
        to = {i: i for i in range(count)}
        for i in (hop - 1, count - hop - 1):
            to[i], to[i + 1] = i + 1, i
        for k in range(chunks):
            sent = got[k]
            if hop > 1:
                value = jnp.where(place == hop - 1, own[0, k], own[1, k])
                sent = (value + decay[k] * sent.astype(F32)).astype(BF)
            if hop == 2 and k == 0:
                sent = after(sent, *early)
                done += [make(sent) for make in inner[EAGER:]]
            got[k] = lax.ppermute(sent, "seq", sorted(to.items()))
            kind = jnp.where(place == hop, 0, 1)
            fits = (place == hop) | (place == count - hop - 1)
            at = jnp.where(fits, k, chunks)
            zero = jnp.zeros_like(at)
            store = lax.dynamic_update_slice(store, got[k][None, None], (kind, at, zero, zero))
    return store, done


def body(tokens, ssd_input, grad_out, w_bc, w_dt, decay_rate, dt_bias):
    feats, x, g = tokens[0], ssd_input[0], grad_out[0]
    rows, width = feats.shape
    heads = decay_rate.shape[0]
    size = width // heads
    n_dp, n_seq = lax.axis_size("dp"), lax.axis_size("seq")
    part = width // n_dp
    state_n = w_bc.shape[1] // 2
    w_dt = w_dt.T
    rate, bias = decay_rate[None], dt_bias[None]

    pieces = call(split_kernel, [struct((rows, part), BF)] * n_dp, 0, feats)
    items = [pieces[0]] + [cyclic(pieces[r], "dp", r) for r in range(1, n_dp)]
    groups = items[:1]
    if n_dp > 1:
        groups.append(items[1] if n_dp == 2 else jnp.concatenate(items[1:], axis=0))
    cuts = [min(1 + hop, n_seq) for hop in EARLY[: len(groups)]]
    moved = [relay(a, range(1, cut)) for a, cut in zip(groups, cuts)]
    early = [a for m in moved[1:] for a in m[0]] + moved[0][0][4:]
    near = moved[0][0]
    partials = [project(items[0], w_bc, w_dt)] + [
        cyclic(project(items[r], w_bc, w_dt), "dp", -r) for r in range(1, n_dp)
    ]
    partials[1:] = [after(a, *near[:2]) for a in partials[1:]]
    proj = partials + [cyclic(a, "head", 1) for a in partials]
    x = after(x, *near[2:4])
    step = width // CHUNKS
    own, decay, bc, hp, *first = call(
        functools.partial(state_kernel, 2 * n_dp, size),
        (
            struct((2, CHUNKS, state_n, step), F32),
            struct((CHUNKS, 1, step), F32),
            struct((2 * rows, state_n), F32),
            struct((5 * heads, rows), F32),
        )
        + (struct((state_n, step), BF),) * CHUNKS,
        12 * rows * width * state_n,
        *proj,
        x,
        g,
        rate,
        bias,
    )
    pairs = width // (2 * size) // PARTS
    span = width // PARTS
    shared = []

    def inner(q, *others):
        held = after(bc, *others) if others else bc
        square = struct((rows, rows), F32)
        block = pl.BlockSpec((rows, span), lambda _: (0, q))
        out = call(
            functools.partial(inner_kernel, q * pairs, pairs, size),
            ([square] if q == 0 else [])
            + [struct((rows, span), F32), square, struct((2, 2 * pairs, rows), F32)],
            8 * rows * rows * span,
            held,
            hp,
            x,
            g,
            *shared,
            scratch=(pltpu.VMEM((rows, 2 * span), BF), pltpu.VMEM((rows, 2 * span), BF)),
            specs=[VMEM, VMEM, block, block] + [VMEM] * len(shared),
        )
        if q == 0:
            shared.append(out[0])
            out = out[1:]
        return out

    store, inners = chains(first, own, decay, [functools.partial(inner, q) for q in range(PARTS)], early)
    grad_x, keep, give = call(
        functools.partial(outer_kernel, size, PARTS),
        (
            struct((rows, width), BF),
            struct((rows + heads, rows), F32),
            struct((rows, rows), F32),
        ),
        16 * rows * width * state_n,
        store,
        x,
        g,
        bc,
        hp,
        decay,
        rate,
        *[a[0] for a in inners],
        *[a[1] for a in inners],
        *[a[2] for a in inners],
        scratch=(
            pltpu.VMEM((rows, 2 * width), BF),
            pltpu.VMEM((rows, 2 * width), BF),
            pltpu.VMEM((1, width), F32),
        ),
    )
    taken = cyclic(give, "head", 1)
    mine = jnp.concatenate([keep[:rows] + taken, keep[rows:]], axis=0).astype(BF)
    w_bc_later, w_dt_later = after((w_bc, w_dt), hp)
    weights = [w_bc, w_dt]
    for r in range(1, n_dp):
        weights += [cyclic(w_bc_later, "dp", r), cyclic(w_dt_later, "dp", r)]
    count = n_dp * n_seq
    lows = lax.all_to_all(
        jnp.broadcast_to(mine[None], (count,) + mine.shape), ("seq", "dp"), 0, 0, tiled=True
    )
    swapped = cyclic(lows, "head", 1)
    other = cyclic(mine, "head", 1)
    grads = call(
        functools.partial(token_kernel, n_dp),
        struct((rows, width), BF),
        2 * rows * width * (2 * state_n + 2 * heads),
        mine,
        other,
        *weights,
    )
    toks = []
    for a, cut, (found, near, held) in zip(groups, cuts, moved):
        rest, far, _ = relay(a, range(cut, n_seq), list(after(tuple(held), store)))
        slots = [(0, 0)] + near + far
        toks += [a] + found + rest
    cols = 2 * (rows + heads)
    grad_bc, grad_dt = call(
        functools.partial(weight_kernel, 1.0 / (rows * n_seq * n_dp), n_dp, n_seq, slots),
        (struct((part, 2 * state_n), F32), struct((2 * heads, part), F32)),
        2 * n_dp * n_seq * rows * part * cols,
        *toks,
        lows,
        swapped,
        specs=[ANY] * (len(toks) + 2),
        scratch=(
            pltpu.VMEM((n_dp, n_seq * rows, part), BF),
            pltpu.VMEM((n_dp, cols, n_seq * rows), BF),
            pltpu.SemaphoreType.DMA((n_dp, len(slots))),
            pltpu.SemaphoreType.DMA((count, 2)),
        ),
    )
    return grad_x[None], grads[None], grad_bc, grad_dt.T


def solution(mesh):
    in_specs = (
        P(("grp", "dp"), "seq", "head"),
        P(("grp", "dp"), "seq", "head"),
        P(("grp", "dp"), "seq", "head"),
        P(("head", "dp"), None),
        P(("head", "dp"), None),
        P("head"),
        P("head"),
    )
    out_specs = (
        P(("grp", "dp"), "seq", "head"),
        P(("grp", "dp"), "seq", "head"),
        P(("grp", "head", "dp"), None),
        P(("grp", "head", "dp"), None),
    )
    return jax.shard_map(body, mesh=mesh, in_specs=in_specs, out_specs=out_specs, check_vma=False)
```

```python
import functools

import jax
import jax.numpy as jnp
from jax import lax
from jax.experimental import pallas as pl
from jax.experimental.pallas import tpu as pltpu
from jax.sharding import PartitionSpec as P

CHUNKS = 2
PARTS = 4
EARLY = (3, 1)
EAGER = 2
BF = jnp.bfloat16
F32 = jnp.float32
TOP = lax.Precision.HIGHEST
PER_US = 1.15e9
LIMIT = 56 * 1024 * 1024


def cyclic(a, axis, by):
    count = lax.axis_size(axis)
    return lax.ppermute(a, axis, [(i, (i + by) % count) for i in range(count)])


def mm(a, b, ca, cb, precision=None):
    return lax.dot_general(
        a, b, (((ca,), (cb,)), ((), ())), preferred_element_type=F32, precision=precision
    )


def halves(a):
    high = a.astype(BF)
    return high, (a - high.astype(F32)).astype(BF)


def head_lanes(heads, width, size, first=0):
    row = lax.broadcasted_iota(jnp.int32, (heads, width), 0)
    col = lax.broadcasted_iota(jnp.int32, (heads, width), 1) + first
    low = row * size
    return jnp.where((col >= low) & (col < low + size), 1.0, 0.0).astype(F32)


def spread(a, pick):
    high, low = halves(a)
    both = jnp.concatenate([pick, pick], axis=0)
    return mm(jnp.concatenate([high, low], axis=0), both, 0, 0)


VMEM = pl.BlockSpec(memory_space=pltpu.VMEM)
ANY = pl.BlockSpec(memory_space=pl.ANY)


def call(kernel, out_shape, span_us, *args, scratch=(), specs=None, out_specs=None):
    size = sum(a.size * a.dtype.itemsize for a in args)
    return pl.pallas_call(
        kernel,
        out_shape=out_shape,
        grid=(1,),
        in_specs=specs or [VMEM] * len(args),
        out_specs=out_specs or jax.tree.map(lambda _: VMEM, out_shape),
        scratch_shapes=list(scratch),
        compiler_params=pltpu.CompilerParams(vmem_limit_bytes=LIMIT),
        cost_estimate=pl.CostEstimate(
            flops=int(span_us * PER_US), bytes_accessed=size, transcendentals=0
        ),
    )(*args)


def struct(shape, dtype):
    return jax.ShapeDtypeStruct(shape, dtype)


def after(a, *others):
    return lax.optimization_barrier((a, others))[0]


def matchings(count):
    groups = [[(i, i + 1) for i in range(kind, count - 1, 2)] for kind in (0, 1)]
    pairs = []
    for group in groups:
        to = {i: i for i in range(count)}
        for i, j in group:
            to[i], to[j] = j, i
        pairs.append(sorted(to.items()))
    return groups, pairs


def split_kernel(a_ref, *outs):
    count = len(outs)
    me = lax.axis_index("dp")
    part = outs[0].shape[1]
    for r in range(count):
        at = pl.multiple_of(lax.rem(me + r, count) * part, 128)
        outs[r][...] = a_ref[:, pl.ds(at, part)]


def project_kernel(a_ref, bc_ref, dt_ref, out_ref):
    a = a_ref[...]
    state_n = bc_ref.shape[1] // 2
    rows = a.shape[0]
    bc = mm(a, bc_ref[...], 1, 0)
    out_ref[0:rows, :] = bc[:, :state_n]
    out_ref[rows : 2 * rows, :] = bc[:, state_n:]
    out_ref[2 * rows :, :] = mm(dt_ref[...], a, 1, 1)


def project(a, w_bc, w_dt):
    rows = a.shape[0]
    total = 2 * rows + w_dt.shape[0]
    return call(
        project_kernel,
        struct((total, w_bc.shape[1] // 2), F32),
        2.1,
        a,
        w_bc,
        w_dt,
    )


def state_kernel(count, size, *refs):
    proj = refs[:count]
    x_ref, g_ref, rate_ref, bias_ref, own_ref, decay_ref, bc_ref, hp_ref = refs[count : count + 8]
    firsts = refs[count + 8 :]
    heads = rate_ref.shape[1]
    rows = x_ref.shape[0]
    rate, bias = rate_ref[...].T, bias_ref[...].T
    chunks, step = own_ref.shape[1], own_ref.shape[3]
    first = pl.multiple_of(2 * rows + lax.axis_index("head") * heads, 8)
    bc = proj[0][0 : 2 * rows, :]
    pre = proj[0][pl.ds(first, heads), :] + bias
    for ref in proj[1:]:
        bc = bc + ref[0 : 2 * rows, :]
        pre = pre + ref[pl.ds(first, heads), :]
    bc_ref[...] = bc
    dt = jnp.maximum(pre, 0.0) + jnp.log1p(jnp.exp(-jnp.abs(pre)))
    row = lax.broadcasted_iota(jnp.int32, (rows, rows), 0)
    col = lax.broadcasted_iota(jnp.int32, (rows, rows), 1)
    cum = mm(-dt * rate, jnp.where(row <= col, 1.0, 0.0), 1, 0, TOP)
    last = cum[:, rows - 1 : rows]
    grow = jnp.exp(cum)
    w = jnp.exp(last - cum) * dt
    decay = jnp.exp(last)
    for k, part in enumerate((pre, dt, cum, grow, w)):
        hp_ref[k * heads : (k + 1) * heads, :] = part
    lowest = lax.axis_index("seq") == 0
    sides = []
    for vec in (bc[:rows], bc[rows:]):
        high, low = halves(vec.T)
        sides.append((jnp.concatenate([high, low], axis=1), high))
    for k in range(chunks):
        pick = head_lanes(heads, step, size, k * step)
        decay_ref[k] = jnp.sum(pick * decay, axis=0, keepdims=True)
        pick = pick.astype(BF)
        both = []
        for kind, (scale, ref) in enumerate(((w, x_ref), (grow, g_ref))):
            wide, high = sides[kind]
            value = spread(scale, pick) * ref[:, k * step : (k + 1) * step].astype(F32)
            top, rest = halves(value)
            value = mm(wide, jnp.concatenate([top, top], axis=0), 1, 0) + mm(high, rest, 1, 0)
            own_ref[kind, k] = value
            both.append(value)
        firsts[k][...] = jnp.where(lowest, both[0], both[1]).astype(BF)


def inner_kernel(first, pairs, size, bc_ref, hp_ref, x_ref, g_ref, *refs):
    gx_ref, ds_ref, sums_ref = refs[-5:-2]
    gy_ref, xg_ref = refs[-2:]
    rows = x_ref.shape[0]
    heads = hp_ref.shape[0] // 5
    lanes = 2 * size
    width = pairs * lanes
    if len(refs) == 6 and first > 0:
        scores = refs[0][...]
    else:
        scores = mm(bc_ref[rows : 2 * rows, :], bc_ref[0:rows, :], 1, 1, TOP)
        refs[0][...] = scores
    row = lax.broadcasted_iota(jnp.int32, (rows, rows), 0)
    col = lax.broadcasted_iota(jnp.int32, (rows, rows), 1)
    causal = row >= col
    dt = hp_ref[heads : 2 * heads, :]
    cum = hp_ref[2 * heads : 3 * heads, :]
    cum_t = cum.T
    lane = lax.broadcasted_iota(jnp.int32, (rows, lanes), 1)
    sides = [jnp.where(lane < size, 1.0, 0.0).astype(BF), jnp.where(lane < size, 0.0, 1.0).astype(BF)]
    ds = jnp.zeros((rows, rows), F32)
    for j in range(pairs):
        place = slice(j * lanes, (j + 1) * lanes)
        x, g = x_ref[:, place], g_ref[:, place]
        xs = jnp.concatenate([x * s for s in sides], axis=0)
        gs = jnp.concatenate([g * s for s in sides], axis=0)
        m = mm(gs, x, 1, 1)
        kern = []
        for i in range(2):
            h = 2 * (first + j) + i
            gap = cum_t[:, h : h + 1] - cum[h : h + 1, :]
            fall = jnp.exp(jnp.where(causal, gap, -jnp.inf)) * dt[h : h + 1, :]
            kern.append((fall * scores).astype(BF))
            ds = ds + fall * m[i * rows : (i + 1) * rows]
        y = mm(jnp.concatenate(kern, axis=1), xs, 1, 0)
        gx = mm(jnp.concatenate(kern, axis=0), gs, 0, 0)
        gx_ref[:, place] = gx
        late = slice(width + j * lanes, width + (j + 1) * lanes)
        gy_ref[:, place], gy_ref[:, late] = halves(g.astype(F32) * y)
        xg_ref[:, place], xg_ref[:, late] = halves(x.astype(F32) * gx)
    ds_ref[...] = ds
    pick = head_lanes(2 * pairs, width, size).astype(BF)
    pick = jnp.concatenate([pick, pick], axis=1)
    sums_ref[0] = mm(pick, gy_ref[...], 1, 1)
    sums_ref[1] = mm(pick, xg_ref[...], 1, 1)


def outer_kernel(size, parts, *refs):
    store_ref, x_ref, g_ref, bc_ref, hp_ref, decay_ref, rate_ref = refs[:7]
    gxs, dss, sums = (refs[7 + k * parts : 7 + (k + 1) * parts] for k in range(3))
    grad_ref, keep_ref, give_ref, wv_ref, eu_ref, io_ref = refs[7 + 3 * parts :]
    rate = rate_ref[...].T
    rows, width = x_ref.shape
    heads = rate_ref.shape[1]
    chunks, step = decay_ref.shape[0], decay_ref.shape[2]
    piece = width // parts
    b, c = bc_ref[0:rows, :], bc_ref[rows : 2 * rows, :]
    pre, dt, cum, grow, w = (hp_ref[k * heads : (k + 1) * heads, :] for k in range(5))
    ds = dss[0][...]
    for ref in dss[1:]:
        ds = ds + ref[...]
    db = mm(c, ds, 0, 0, TOP)
    dc = mm(b, ds, 0, 1, TOP)
    b_wide = jnp.concatenate(halves(b), axis=1)
    c_wide = jnp.concatenate(halves(c), axis=1)
    for k in range(chunks):
        place = slice(k * step, (k + 1) * step)
        late = slice(width + k * step, width + (k + 1) * step)
        pick = head_lanes(heads, step, size, k * step).astype(BF)
        incoming, outgoing = store_ref[0, k], store_ref[1, k]
        u = mm(c_wide, jnp.concatenate([incoming, incoming], axis=0), 1, 0)
        v = mm(b_wide, jnp.concatenate([outgoing, outgoing], axis=0), 1, 0)
        scale = spread(w, pick)
        wx = scale * x_ref[:, place].astype(F32)
        eg = spread(grow, pick) * g_ref[:, place].astype(F32)
        for q in range(step // piece) if step >= piece else (0,):
            if step >= piece:
                at = k * step + q * piece
                inner = slice(q * piece, (q + 1) * piece)
                term = gxs[at // piece][...]
            else:
                at, inner = k * step, slice(0, step)
                term = gxs[at // piece][:, at % piece : at % piece + step]
            total = term + scale[:, inner] * v[:, inner]
            grad_ref[:, at : at + total.shape[1]] = total.astype(BF)
        wv_ref[:, place], wv_ref[:, late] = halves(wx * v)
        eu_ref[:, place], eu_ref[:, late] = halves(eg * u)
        db = db + mm(
            jnp.concatenate([outgoing, outgoing], axis=1), jnp.concatenate(halves(wx), axis=1), 1, 1
        )
        dc = dc + mm(
            jnp.concatenate([incoming, incoming], axis=1), jnp.concatenate(halves(eg), axis=1), 1, 1
        )
        io_ref[:, place] = jnp.sum(incoming.astype(F32) * outgoing.astype(F32), axis=0, keepdims=True)
    pick = head_lanes(heads, width, size)
    ddecay = jnp.sum(pick * io_ref[...], axis=1, keepdims=True)
    pick = pick.astype(BF)
    pick = jnp.concatenate([pick, pick], axis=1)
    wdw = mm(pick, wv_ref[...], 1, 1)
    egu = mm(pick, eu_ref[...], 1, 1)
    rowsum = jnp.concatenate([s[0] for s in sums], axis=0)
    colsum = jnp.concatenate([s[1] for s in sums], axis=0)
    dcum = rowsum - colsum + egu - wdw
    row = lax.broadcasted_iota(jnp.int32, (rows, rows), 0)
    col = lax.broadcasted_iota(jnp.int32, (rows, rows), 1)
    rev = mm(dcum, jnp.where(row >= col, 1.0, 0.0), 1, 0, TOP)
    decay = grow[:, rows - 1 : rows]
    rev = rev + jnp.sum(wdw, axis=1, keepdims=True) + decay * ddecay
    gate = 1.0 / (1.0 + jnp.exp(-pre))
    small = 1e-30
    ratio = jnp.where(dt > small, gate / jnp.maximum(dt, small), 1.0)
    core = lax.axis_index("head")
    keep_ref[0:rows, :] = jnp.where(core == 0, db, dc)
    keep_ref[rows:, :] = (colsum + wdw) * ratio - rate * rev * gate
    give_ref[...] = jnp.where(core == 0, dc, db)


def low_kernel(keep_ref, taken_ref, out_ref):
    rows = taken_ref.shape[0]
    low = keep_ref[0:rows, :] + taken_ref[...]
    low = jnp.concatenate([low, keep_ref[rows:, :]], axis=0).astype(BF)
    for k in range(out_ref.shape[0]):
        out_ref[k] = low


def token_kernel(count, mine_ref, other_ref, *refs):
    out_ref = refs[2 * count]
    me, core = lax.axis_index("dp"), lax.axis_index("head")
    part, cols = refs[0].shape
    half = cols // 2
    heads = refs[1].shape[0] // 2
    for r in range(count):
        at = pl.multiple_of(lax.rem(me - r + count, count) * part, 128)
        total = None
        for k, ref in enumerate((mine_ref, other_ref)):
            at_col = pl.multiple_of(lax.rem(core + k, 2) * half, 128)
            at_row = pl.multiple_of(lax.rem(core + k, 2) * heads, 16)
            term = mm(ref[0:half, :], refs[2 * r][:, pl.ds(at_col, half)], 0, 1)
            term = term + mm(ref[half:, :], refs[2 * r + 1][pl.ds(at_row, heads), :], 0, 0)
            total = term if total is None else total + term
        out_ref[:, pl.ds(at, part)] = total.astype(BF)


def weight_kernel(scale, n_dp, n_seq, slots, *refs):
    count = 2 * len(slots) if n_dp > 1 else len(slots)
    toks, lows = refs[:count], refs[count:-6]
    bc_ref, dt_ref, tok_ref, low_ref, tok_sem, low_sem = refs[-6:]
    rows = toks[0].shape[0]
    share = lows[0].shape[1]
    core, place, me = lax.axis_index("head"), lax.axis_index("seq"), lax.axis_index("dp")
    even = lax.rem(place, 2) == 0
    copies = []
    for r in range(n_dp):
        for k, (kind, hop) in enumerate(slots):
            above = even if kind == 0 else ~even
            block = jnp.where(above, place + hop, place - hop)
            fits = (block >= 0) & (block < n_seq)
            if hop > 0 and kind == 1:
                fits = fits & jnp.where(above, place < n_seq - 1, place > 0)
            at = pl.multiple_of(jnp.clip(block, 0, n_seq - 1) * rows, 128)
            source = toks[k] if r == 0 else toks[len(slots) + k].at[pl.ds((r - 1) * rows, rows)]
            copy = pltpu.make_async_copy(source, tok_ref.at[r, pl.ds(at, rows)], tok_sem.at[r, k])
            copies.append((fits, copy))
    for r in range(n_dp):
        for s in range(n_seq):
            index = s * n_dp + lax.rem(me - r + n_dp, n_dp)
            for k in range(2):
                row = pl.multiple_of(lax.rem(core + k, 2) * share, 16)
                copy = pltpu.make_async_copy(
                    lows[k].at[index],
                    low_ref.at[r, pl.ds(row, share), pl.ds(s * rows, rows)],
                    low_sem.at[r * n_seq + s, k],
                )
                copies.append((None, copy))
    for fits, copy in copies:
        if fits is None:
            copy.start()
        else:
            pl.when(fits)(copy.start)
    for fits, copy in copies:
        if fits is None:
            copy.wait()
        else:
            pl.when(fits)(copy.wait)
    total = mm(low_ref[0], tok_ref[0], 1, 0)
    for r in range(1, n_dp):
        total = total + mm(low_ref[r], tok_ref[r], 1, 0)
    total = total * scale
    half = bc_ref.shape[1] // 2
    heads = dt_ref.shape[0] // 2
    for k in range(2):
        bc_ref[:, k * half : (k + 1) * half] = total[k * share : k * share + half].T
        dt_ref[k * heads : (k + 1) * heads, :] = total[k * share + half : (k + 1) * share]


def relay(block, hops, held=None):
    count = lax.axis_size("seq")
    groups, pairs = matchings(count)
    held = held or [block, block]
    found, slots = [], []
    for hop in hops:
        fresh = [None, None]
        for kind in (0, 1):
            if any(i - hop + 1 >= 0 or j + hop - 1 < count for i, j in groups[kind]):
                fresh[kind] = lax.ppermute(held[1 - kind], "seq", pairs[kind])
                found.append(fresh[kind])
                slots.append((kind, hop))
        held = [h if f is None else f for f, h in zip(fresh, held)]
    return found, slots, held


def chains(first, own, decay, inner, weights):
    count = lax.axis_size("seq")
    place = lax.axis_index("seq")
    chunks = len(first)
    store = jnp.zeros((2, chunks + 1) + own.shape[2:], BF)
    got = list(first)
    done, todo, extra = [], list(inner), []
    last = count + chunks - 2
    for slot in range(1, last + 1):
        steps = [(hop, slot - hop) for hop in range(1, count) if 0 <= slot - hop < chunks]
        sent = []
        for hop, k in steps:
            value = got[k]
            if hop > 1:
                value = jnp.where(place == hop - 1, own[0, k], own[1, k])
                value = (value + decay[k] * got[k].astype(F32)).astype(BF)
            sent.append(value)
        for (hop, k), value in zip(steps, sent):
            to = {i: i for i in range(count)}
            for i in (hop - 1, count - hop - 1):
                to[i], to[i + 1] = i + 1, i
            got[k] = lax.ppermute(value, "seq", sorted(to.items()))
        for _ in range(-(-len(todo) // (last + 1 - slot))):
            done.append(todo.pop(0)(*sent))
        if slot == 1:
            extra = weights(*sent)
        if slot < last:
            held = [got[k] for _, k in steps] + [d[0] for d in done[-1:]]
            if slot == last - 1:
                held += extra
            if slot == 1 and chunks > 1:
                held.append(got[1])
            kept = lax.optimization_barrier(tuple(held))
            for (_, k), a in zip(steps, kept):
                got[k] = a
            if slot == 1 and chunks > 1:
                got[1] = kept[-1]
        for hop, k in steps:
            kind = jnp.where(place == hop, 0, 1)
            fits = (place == hop) | (place == count - hop - 1)
            at = jnp.where(fits, k, chunks)
            zero = jnp.zeros_like(at)
            store = lax.dynamic_update_slice(store, got[k][None, None], (kind, at, zero, zero))
    done += [make() for make in todo]
    return store, done


def body(tokens, ssd_input, grad_out, w_bc, w_dt, decay_rate, dt_bias):
    feats, x, g = tokens[0], ssd_input[0], grad_out[0]
    rows, width = feats.shape
    heads = decay_rate.shape[0]
    size = width // heads
    n_dp, n_seq = lax.axis_size("dp"), lax.axis_size("seq")
    part = width // n_dp
    state_n = w_bc.shape[1] // 2
    w_dt = w_dt.T
    rate, bias = decay_rate[None], dt_bias[None]

    pieces = call(split_kernel, [struct((rows, part), BF)] * n_dp, 1.9, feats)
    items = [pieces[0]] + [cyclic(pieces[r], "dp", r) for r in range(1, n_dp)]
    groups = items[:1]
    if n_dp > 1:
        groups.append(items[1] if n_dp == 2 else jnp.concatenate(items[1:], axis=0))
    cuts = [min(1 + hop, n_seq) for hop in EARLY[: len(groups)]]
    moved = [relay(a, range(1, cut)) for a, cut in zip(groups, cuts)]
    early = [a for m in moved[1:] for a in m[0]] + moved[0][0][4:]
    near = moved[0][0]
    partials = [project(items[0], w_bc, w_dt)] + [
        cyclic(project(items[r], w_bc, w_dt), "dp", -r) for r in range(1, n_dp)
    ]
    partials[1:] = [after(a, *near[:2]) for a in partials[1:]]
    proj = partials + [cyclic(a, "head", 1) for a in partials]
    x = after(x, *near[2:4])
    step = width // CHUNKS
    own, decay, bc, hp, *first = call(
        functools.partial(state_kernel, 2 * n_dp, size),
        (
            struct((2, CHUNKS, state_n, step), F32),
            struct((CHUNKS, 1, step), F32),
            struct((2 * rows, state_n), F32),
            struct((5 * heads, rows), F32),
        )
        + (struct((state_n, step), BF),) * CHUNKS,
        4.9,
        *proj,
        x,
        g,
        rate,
        bias,
    )
    pairs = width // (2 * size) // PARTS
    span = width // PARTS
    shared = []

    def inner(q, *others):
        held = after(bc, *others) if others else bc
        square = struct((rows, rows), F32)
        block = pl.BlockSpec((rows, span), lambda _: (0, q))
        out = call(
            functools.partial(inner_kernel, q * pairs, pairs, size),
            ([square] if q == 0 else [])
            + [struct((rows, span), F32), square, struct((2, 2 * pairs, rows), F32)],
                2.6,
            held,
            hp,
            x,
            g,
            *shared,
            scratch=(pltpu.VMEM((rows, 2 * span), BF), pltpu.VMEM((rows, 2 * span), BF)),
            specs=[VMEM, VMEM, block, block] + [VMEM] * len(shared),
        )
        if q == 0:
            shared.append(out[0])
            out = out[1:]
        return out

    weights = [w_bc, w_dt]

    def fetch(*others):
        for r in range(1, n_dp):
            weights.extend(cyclic(after(a, *others), "dp", r) for a in (w_bc, w_dt))
        return weights[2:]

    first[0] = after(first[0], *early)
    store, inners = chains(first, own, decay, [functools.partial(inner, q) for q in range(PARTS)], fetch)
    grad_x, keep, give = call(
        functools.partial(outer_kernel, size, PARTS),
        (
            struct((rows, width), BF),
            struct((rows + heads, rows), F32),
            struct((rows, rows), F32),
        ),
        5.4,
        store,
        x,
        g,
        bc,
        hp,
        decay,
        rate,
        *[a[0] for a in inners],
        *[a[1] for a in inners],
        *[a[2] for a in inners],
        scratch=(
            pltpu.VMEM((rows, 2 * width), BF),
            pltpu.VMEM((rows, 2 * width), BF),
            pltpu.VMEM((1, width), F32),
        ),
    )
    taken = cyclic(give, "head", 1)
    count = n_dp * n_seq
    copies = call(low_kernel, struct((count, rows + heads, rows), BF), 1.2, keep, taken)
    mine = copies[0]
    lows = lax.all_to_all(copies, ("seq", "dp"), 0, 0, tiled=True)
    swapped = cyclic(lows, "head", 1)
    other = cyclic(mine, "head", 1)
    grads = call(
        functools.partial(token_kernel, n_dp),
        struct((rows, width), BF),
        2.9,
        mine,
        other,
        *weights,
    )
    toks = []
    for a, cut, (found, near, held) in zip(groups, cuts, moved):
        rest, far, _ = relay(a, range(cut, n_seq), list(after(tuple(held), store)))
        slots = [(0, 0)] + near + far
        toks += [a] + found + rest
    cols = 2 * (rows + heads)
    grad_bc, grad_dt = call(
        functools.partial(weight_kernel, 1.0 / (rows * n_seq * n_dp), n_dp, n_seq, slots),
        (struct((part, 2 * state_n), F32), struct((2 * heads, part), F32)),
        4.0,
        *toks,
        lows,
        swapped,
        specs=[ANY] * (len(toks) + 2),
        scratch=(
            pltpu.VMEM((n_dp, n_seq * rows, part), BF),
            pltpu.VMEM((n_dp, cols, n_seq * rows), BF),
            pltpu.SemaphoreType.DMA((n_dp, len(slots))),
            pltpu.SemaphoreType.DMA((count, 2)),
        ),
    )
    return grad_x[None], grads[None], grad_bc, grad_dt.T


def solution(mesh):
    in_specs = (
        P(("grp", "dp"), "seq", "head"),
        P(("grp", "dp"), "seq", "head"),
        P(("grp", "dp"), "seq", "head"),
        P(("head", "dp"), None),
        P(("head", "dp"), None),
        P("head"),
        P("head"),
    )
    out_specs = (
        P(("grp", "dp"), "seq", "head"),
        P(("grp", "dp"), "seq", "head"),
        P(("grp", "head", "dp"), None),
        P(("grp", "head", "dp"), None),
    )
    return jax.shard_map(body, mesh=mesh, in_specs=in_specs, out_specs=out_specs, check_vma=False)
```

```python
import functools

import jax
import jax.numpy as jnp
from jax import lax
from jax.experimental import pallas as pl
from jax.experimental.pallas import tpu as pltpu
from jax.sharding import PartitionSpec as P

CHUNKS = 2
PARTS = 4
BF = jnp.bfloat16
F32 = jnp.float32
TOP = lax.Precision.HIGHEST
PER_US = 1.15e9
LIMIT = 56 * 1024 * 1024


def cyclic(a, axis, by):
    count = lax.axis_size(axis)
    return lax.ppermute(a, axis, [(i, (i + by) % count) for i in range(count)])


def mm(a, b, ca, cb, precision=None):
    return lax.dot_general(
        a, b, (((ca,), (cb,)), ((), ())), preferred_element_type=F32, precision=precision
    )


def halves(a):
    high = a.astype(BF)
    return high, (a - high.astype(F32)).astype(BF)


def head_lanes(heads, width, size, first=0):
    row = lax.broadcasted_iota(jnp.int32, (heads, width), 0)
    col = lax.broadcasted_iota(jnp.int32, (heads, width), 1) + first
    low = row * size
    return jnp.where((col >= low) & (col < low + size), 1.0, 0.0).astype(F32)


def spread(a, pick):
    high, low = halves(a)
    both = jnp.concatenate([pick, pick], axis=0)
    return mm(jnp.concatenate([high, low], axis=0), both, 0, 0)


VMEM = pl.BlockSpec(memory_space=pltpu.VMEM)
ANY = pl.BlockSpec(memory_space=pl.ANY)


def call(kernel, out_shape, span_us, *args, scratch=(), specs=None, out_specs=None):
    size = sum(a.size * a.dtype.itemsize for a in args)
    return pl.pallas_call(
        kernel,
        out_shape=out_shape,
        grid=(1,),
        in_specs=specs or [VMEM] * len(args),
        out_specs=out_specs or jax.tree.map(lambda _: VMEM, out_shape),
        scratch_shapes=list(scratch),
        compiler_params=pltpu.CompilerParams(vmem_limit_bytes=LIMIT),
        cost_estimate=pl.CostEstimate(
            flops=int(span_us * PER_US), bytes_accessed=size, transcendentals=0
        ),
    )(*args)


def struct(shape, dtype):
    return jax.ShapeDtypeStruct(shape, dtype)


def after(a, *others):
    return lax.optimization_barrier((a, others))[0]


def matchings(count):
    groups = [[(i, i + 1) for i in range(kind, count - 1, 2)] for kind in (0, 1)]
    pairs = []
    for group in groups:
        to = {i: i for i in range(count)}
        for i, j in group:
            to[i], to[j] = j, i
        pairs.append(sorted(to.items()))
    return groups, pairs


def split_kernel(a_ref, *outs):
    count = len(outs)
    me = lax.axis_index("dp")
    part = outs[0].shape[1]
    for r in range(count):
        at = pl.multiple_of(lax.rem(me + r, count) * part, 128)
        outs[r][...] = a_ref[:, pl.ds(at, part)]


def project_kernel(a_ref, bc_ref, dt_ref, out_ref):
    a = a_ref[...]
    state_n = bc_ref.shape[1] // 2
    rows = a.shape[0]
    bc = mm(a, bc_ref[...], 1, 0)
    out_ref[0:rows, :] = bc[:, :state_n]
    out_ref[rows : 2 * rows, :] = bc[:, state_n:]
    out_ref[2 * rows :, :] = mm(dt_ref[...], a, 1, 1)


def project(a, w_bc, w_dt):
    rows = a.shape[0]
    total = 2 * rows + w_dt.shape[0]
    return call(
        project_kernel,
        struct((total, w_bc.shape[1] // 2), F32),
        2.1,
        a,
        w_bc,
        w_dt,
    )


def state_kernel(count, size, *refs):
    proj = refs[:count]
    x_ref, g_ref, rate_ref, bias_ref, own_ref, decay_ref, bc_ref, hp_ref = refs[count : count + 8]
    firsts = refs[count + 8 :]
    heads = rate_ref.shape[1]
    rows = x_ref.shape[0]
    rate, bias = rate_ref[...].T, bias_ref[...].T
    chunks, step = own_ref.shape[1], own_ref.shape[3]
    first = pl.multiple_of(2 * rows + lax.axis_index("head") * heads, 8)
    bc = proj[0][0 : 2 * rows, :]
    pre = proj[0][pl.ds(first, heads), :] + bias
    for ref in proj[1:]:
        bc = bc + ref[0 : 2 * rows, :]
        pre = pre + ref[pl.ds(first, heads), :]
    bc_ref[...] = bc
    dt = jnp.maximum(pre, 0.0) + jnp.log1p(jnp.exp(-jnp.abs(pre)))
    row = lax.broadcasted_iota(jnp.int32, (rows, rows), 0)
    col = lax.broadcasted_iota(jnp.int32, (rows, rows), 1)
    cum = mm(-dt * rate, jnp.where(row <= col, 1.0, 0.0), 1, 0, TOP)
    last = cum[:, rows - 1 : rows]
    grow = jnp.exp(cum)
    w = jnp.exp(last - cum) * dt
    decay = jnp.exp(last)
    for k, part in enumerate((pre, dt, cum, grow, w)):
        hp_ref[k * heads : (k + 1) * heads, :] = part
    lowest = lax.axis_index("seq") == 0
    sides = []
    for vec in (bc[:rows], bc[rows:]):
        high, low = halves(vec.T)
        sides.append((jnp.concatenate([high, low], axis=1), high))
    for k in range(chunks):
        pick = head_lanes(heads, step, size, k * step)
        decay_ref[k] = jnp.sum(pick * decay, axis=0, keepdims=True)
        pick = pick.astype(BF)
        both = []
        for kind, (scale, ref) in enumerate(((w, x_ref), (grow, g_ref))):
            wide, high = sides[kind]
            value = spread(scale, pick) * ref[:, k * step : (k + 1) * step].astype(F32)
            top, rest = halves(value)
            value = mm(wide, jnp.concatenate([top, top], axis=0), 1, 0) + mm(high, rest, 1, 0)
            own_ref[kind, k] = value
            both.append(value)
        firsts[k][...] = jnp.where(lowest, both[0], both[1]).astype(BF)


def inner_kernel(first, pairs, size, bc_ref, hp_ref, x_ref, g_ref, *refs):
    gx_ref, ds_ref, sums_ref = refs[-5:-2]
    gy_ref, xg_ref = refs[-2:]
    rows = x_ref.shape[0]
    heads = hp_ref.shape[0] // 5
    lanes = 2 * size
    width = pairs * lanes
    if len(refs) == 6 and first > 0:
        scores = refs[0][...]
    else:
        scores = mm(bc_ref[rows : 2 * rows, :], bc_ref[0:rows, :], 1, 1, TOP)
        refs[0][...] = scores
    row = lax.broadcasted_iota(jnp.int32, (rows, rows), 0)
    col = lax.broadcasted_iota(jnp.int32, (rows, rows), 1)
    causal = row >= col
    dt = hp_ref[heads : 2 * heads, :]
    cum = hp_ref[2 * heads : 3 * heads, :]
    cum_t = cum.T
    lane = lax.broadcasted_iota(jnp.int32, (rows, lanes), 1)
    sides = [jnp.where(lane < size, 1.0, 0.0).astype(BF), jnp.where(lane < size, 0.0, 1.0).astype(BF)]
    ds = jnp.zeros((rows, rows), F32)
    for j in range(pairs):
        place = slice(j * lanes, (j + 1) * lanes)
        x, g = x_ref[:, place], g_ref[:, place]
        xs = jnp.concatenate([x * s for s in sides], axis=0)
        gs = jnp.concatenate([g * s for s in sides], axis=0)
        m = mm(gs, x, 1, 1)
        kern = []
        for i in range(2):
            h = 2 * (first + j) + i
            gap = cum_t[:, h : h + 1] - cum[h : h + 1, :]
            fall = jnp.exp(jnp.where(causal, gap, -jnp.inf)) * dt[h : h + 1, :]
            kern.append((fall * scores).astype(BF))
            ds = ds + fall * m[i * rows : (i + 1) * rows]
        y = mm(jnp.concatenate(kern, axis=1), xs, 1, 0)
        gx = mm(jnp.concatenate(kern, axis=0), gs, 0, 0)
        gx_ref[:, place] = gx
        late = slice(width + j * lanes, width + (j + 1) * lanes)
        gy_ref[:, place], gy_ref[:, late] = halves(g.astype(F32) * y)
        xg_ref[:, place], xg_ref[:, late] = halves(x.astype(F32) * gx)
    ds_ref[...] = ds
    pick = head_lanes(2 * pairs, width, size).astype(BF)
    pick = jnp.concatenate([pick, pick], axis=1)
    sums_ref[0] = mm(pick, gy_ref[...], 1, 1)
    sums_ref[1] = mm(pick, xg_ref[...], 1, 1)


def outer_kernel(size, parts, *refs):
    store_ref, x_ref, g_ref, bc_ref, hp_ref, decay_ref, rate_ref = refs[:7]
    gxs, dss, sums = (refs[7 + k * parts : 7 + (k + 1) * parts] for k in range(3))
    grad_ref, keep_ref, give_ref, wv_ref, eu_ref, io_ref = refs[7 + 3 * parts :]
    rate = rate_ref[...].T
    rows, width = x_ref.shape
    heads = rate_ref.shape[1]
    chunks, step = decay_ref.shape[0], decay_ref.shape[2]
    piece = width // parts
    b, c = bc_ref[0:rows, :], bc_ref[rows : 2 * rows, :]
    pre, dt, cum, grow, w = (hp_ref[k * heads : (k + 1) * heads, :] for k in range(5))
    ds = dss[0][...]
    for ref in dss[1:]:
        ds = ds + ref[...]
    db = mm(c, ds, 0, 0, TOP)
    dc = mm(b, ds, 0, 1, TOP)
    b_wide = jnp.concatenate(halves(b), axis=1)
    c_wide = jnp.concatenate(halves(c), axis=1)
    for k in range(chunks):
        place = slice(k * step, (k + 1) * step)
        late = slice(width + k * step, width + (k + 1) * step)
        pick = head_lanes(heads, step, size, k * step).astype(BF)
        incoming, outgoing = store_ref[0, k], store_ref[1, k]
        u = mm(c_wide, jnp.concatenate([incoming, incoming], axis=0), 1, 0)
        v = mm(b_wide, jnp.concatenate([outgoing, outgoing], axis=0), 1, 0)
        scale = spread(w, pick)
        wx = scale * x_ref[:, place].astype(F32)
        eg = spread(grow, pick) * g_ref[:, place].astype(F32)
        for q in range(step // piece) if step >= piece else (0,):
            if step >= piece:
                at = k * step + q * piece
                inner = slice(q * piece, (q + 1) * piece)
                term = gxs[at // piece][...]
            else:
                at, inner = k * step, slice(0, step)
                term = gxs[at // piece][:, at % piece : at % piece + step]
            total = term + scale[:, inner] * v[:, inner]
            grad_ref[:, at : at + total.shape[1]] = total.astype(BF)
        wv_ref[:, place], wv_ref[:, late] = halves(wx * v)
        eu_ref[:, place], eu_ref[:, late] = halves(eg * u)
        db = db + mm(
            jnp.concatenate([outgoing, outgoing], axis=1), jnp.concatenate(halves(wx), axis=1), 1, 1
        )
        dc = dc + mm(
            jnp.concatenate([incoming, incoming], axis=1), jnp.concatenate(halves(eg), axis=1), 1, 1
        )
        io_ref[:, place] = jnp.sum(incoming.astype(F32) * outgoing.astype(F32), axis=0, keepdims=True)
    pick = head_lanes(heads, width, size)
    ddecay = jnp.sum(pick * io_ref[...], axis=1, keepdims=True)
    pick = pick.astype(BF)
    pick = jnp.concatenate([pick, pick], axis=1)
    wdw = mm(pick, wv_ref[...], 1, 1)
    egu = mm(pick, eu_ref[...], 1, 1)
    rowsum = jnp.concatenate([s[0] for s in sums], axis=0)
    colsum = jnp.concatenate([s[1] for s in sums], axis=0)
    dcum = rowsum - colsum + egu - wdw
    row = lax.broadcasted_iota(jnp.int32, (rows, rows), 0)
    col = lax.broadcasted_iota(jnp.int32, (rows, rows), 1)
    rev = mm(dcum, jnp.where(row >= col, 1.0, 0.0), 1, 0, TOP)
    decay = grow[:, rows - 1 : rows]
    rev = rev + jnp.sum(wdw, axis=1, keepdims=True) + decay * ddecay
    gate = 1.0 / (1.0 + jnp.exp(-pre))
    small = 1e-30
    ratio = jnp.where(dt > small, gate / jnp.maximum(dt, small), 1.0)
    core = lax.axis_index("head")
    keep_ref[0:rows, :] = jnp.where(core == 0, db, dc)
    keep_ref[rows:, :] = (colsum + wdw) * ratio - rate * rev * gate
    give_ref[...] = jnp.where(core == 0, dc, db)


def low_kernel(keep_ref, taken_ref, out_ref):
    rows = taken_ref.shape[0]
    low = keep_ref[0:rows, :] + taken_ref[...]
    low = jnp.concatenate([low, keep_ref[rows:, :]], axis=0).astype(BF)
    for k in range(out_ref.shape[0]):
        out_ref[k] = low


def token_kernel(count, mine_ref, other_ref, *refs):
    out_ref = refs[2 * count]
    me, core = lax.axis_index("dp"), lax.axis_index("head")
    part, cols = refs[0].shape
    half = cols // 2
    heads = refs[1].shape[0] // 2
    for r in range(count):
        at = pl.multiple_of(lax.rem(me - r + count, count) * part, 128)
        total = None
        for k, ref in enumerate((mine_ref, other_ref)):
            at_col = pl.multiple_of(lax.rem(core + k, 2) * half, 128)
            at_row = pl.multiple_of(lax.rem(core + k, 2) * heads, 16)
            term = mm(ref[0:half, :], refs[2 * r][:, pl.ds(at_col, half)], 0, 1)
            term = term + mm(ref[half:, :], refs[2 * r + 1][pl.ds(at_row, heads), :], 0, 0)
            total = term if total is None else total + term
        out_ref[:, pl.ds(at, part)] = total.astype(BF)


def weight_kernel(scale, n_dp, n_seq, slots, *refs):
    count = 2 * len(slots) if n_dp > 1 else len(slots)
    toks, lows = refs[:count], refs[count:-6]
    bc_ref, dt_ref, tok_ref, low_ref, tok_sem, low_sem = refs[-6:]
    rows = toks[0].shape[0]
    share = lows[0].shape[1]
    core, place, me = lax.axis_index("head"), lax.axis_index("seq"), lax.axis_index("dp")
    even = lax.rem(place, 2) == 0
    copies = []
    for r in range(n_dp):
        for k, (kind, hop) in enumerate(slots):
            above = even if kind == 0 else ~even
            block = jnp.where(above, place + hop, place - hop)
            fits = (block >= 0) & (block < n_seq)
            if hop > 0 and kind == 1:
                fits = fits & jnp.where(above, place < n_seq - 1, place > 0)
            at = pl.multiple_of(jnp.clip(block, 0, n_seq - 1) * rows, 128)
            source = toks[k] if r == 0 else toks[len(slots) + k].at[pl.ds((r - 1) * rows, rows)]
            copy = pltpu.make_async_copy(source, tok_ref.at[r, pl.ds(at, rows)], tok_sem.at[r, k])
            copies.append((fits, copy))
    for r in range(n_dp):
        for s in range(n_seq):
            index = s * n_dp + lax.rem(me - r + n_dp, n_dp)
            for k in range(2):
                row = pl.multiple_of(lax.rem(core + k, 2) * share, 16)
                copy = pltpu.make_async_copy(
                    lows[k].at[index],
                    low_ref.at[r, pl.ds(row, share), pl.ds(s * rows, rows)],
                    low_sem.at[r * n_seq + s, k],
                )
                copies.append((None, copy))
    for fits, copy in copies:
        if fits is None:
            copy.start()
        else:
            pl.when(fits)(copy.start)
    for fits, copy in copies:
        if fits is None:
            copy.wait()
        else:
            pl.when(fits)(copy.wait)
    total = mm(low_ref[0], tok_ref[0], 1, 0)
    for r in range(1, n_dp):
        total = total + mm(low_ref[r], tok_ref[r], 1, 0)
    total = total * scale
    half = bc_ref.shape[1] // 2
    heads = dt_ref.shape[0] // 2
    for k in range(2):
        bc_ref[:, k * half : (k + 1) * half] = total[k * share : k * share + half].T
        dt_ref[k * heads : (k + 1) * heads, :] = total[k * share + half : (k + 1) * share]


def relays(count):
    groups, _ = matchings(count)
    return [
        (kind, hop)
        for hop in range(1, count)
        for kind in (0, 1)
        if any(i - hop + 1 >= 0 or j + hop - 1 < count for i, j in groups[kind])
    ]


def relay(found, block, steps, *others):
    count = lax.axis_size("seq")
    _, pairs = matchings(count)
    for kind, hop in steps:
        source = block if hop == 1 else found[1 - kind, hop - 1]
        source = after(source, *others) if others else source
        found[kind, hop] = lax.ppermute(source, "seq", pairs[kind])
    return [found[step] for step in steps]


def chains(first, own, decay, inner, beside, riders):
    count = lax.axis_size("seq")
    place = lax.axis_index("seq")
    chunks = len(first)
    store = jnp.zeros((2, chunks + 1) + own.shape[2:], BF)
    got = list(first)
    done, todo, extra = [], list(inner), []
    last = count + chunks - 2
    for slot in range(1, last + 1):
        steps = [(hop, slot - hop) for hop in range(1, count) if 0 <= slot - hop < chunks]
        sent = []
        for hop, k in steps:
            value = got[k]
            if hop == 1 and k < len(riders):
                value = jnp.where((place == 0) | (place == count - 1), value, riders[k])
            if hop > 1:
                value = jnp.where(place == hop - 1, own[0, k], own[1, k])
                value = (value + decay[k] * got[k].astype(F32)).astype(BF)
            sent.append(value)
        for (hop, k), value in zip(steps, sent):
            to = {i: i for i in range(count)}
            for i in (hop - 1, count - hop - 1):
                to[i], to[i + 1] = i + 1, i
            got[k] = lax.ppermute(value, "seq", sorted(to.items()))
            if hop == 1 and k < len(riders):
                riders[k] = got[k]
        for _ in range(-(-len(todo) // (last + 1 - slot))):
            done.append(todo.pop(0)(*sent))
        if slot == 1:
            extra, soon = beside(*sent)
        if slot < last:
            held = [got[k] for _, k in steps] + [d[0] for d in done[-1:]]
            if slot == last - 1:
                held += extra
            if slot == 2:
                held += soon
            if slot == 1 and chunks > 1:
                held.append(got[1])
            kept = lax.optimization_barrier(tuple(held))
            for (_, k), a in zip(steps, kept):
                got[k] = a
            if slot == 1 and chunks > 1:
                got[1] = kept[-1]
        for hop, k in steps:
            kind = jnp.where(place == hop, 0, 1)
            fits = (place == hop) | (place == count - hop - 1)
            at = jnp.where(fits, k, chunks)
            zero = jnp.zeros_like(at)
            store = lax.dynamic_update_slice(store, got[k][None, None], (kind, at, zero, zero))
    done += [make() for make in todo]
    return store, done


def body(tokens, ssd_input, grad_out, w_bc, w_dt, decay_rate, dt_bias):
    feats, x, g = tokens[0], ssd_input[0], grad_out[0]
    rows, width = feats.shape
    heads = decay_rate.shape[0]
    size = width // heads
    n_dp, n_seq = lax.axis_size("dp"), lax.axis_size("seq")
    part = width // n_dp
    state_n = w_bc.shape[1] // 2
    w_dt = w_dt.T
    rate, bias = decay_rate[None], dt_bias[None]

    pieces = call(split_kernel, [struct((rows, part), BF)] * n_dp, 1.9, feats)
    items = [pieces[0]] + [cyclic(pieces[r], "dp", r) for r in range(1, n_dp)]
    groups = items[:1]
    if n_dp > 1:
        groups.append(items[1] if n_dp == 2 else jnp.concatenate(items[1:], axis=0))
    found = [{} for _ in groups]
    slots = relays(n_seq)
    step = width // CHUNKS
    ride = n_seq == 4 and all(a.shape == (state_n, step) for a in groups)
    second = [(kind, hop) for kind, hop in slots if hop == 2 and not (ride and kind == 0)]
    near = relay(found[0], groups[0], slots[:2])
    partials = [project(items[0], w_bc, w_dt)] + [
        cyclic(project(items[r], w_bc, w_dt), "dp", -r) for r in range(1, n_dp)
    ]
    partials[1:] = [after(a, *near) for a in partials[1:]]
    proj = partials + [cyclic(a, "head", 1) for a in partials]
    x = after(x, *relay(found[0], groups[0], second))
    early = []
    if n_dp > 1:
        early = relay(found[1], groups[1], slots[:2], *proj[n_dp - 1 : n_dp])
    own, decay, bc, hp, *first = call(
        functools.partial(state_kernel, 2 * n_dp, size),
        (
            struct((2, CHUNKS, state_n, step), F32),
            struct((CHUNKS, 1, step), F32),
            struct((2 * rows, state_n), F32),
            struct((5 * heads, rows), F32),
        )
        + (struct((state_n, step), BF),) * CHUNKS,
        4.9,
        *proj,
        x,
        g,
        rate,
        bias,
    )
    pairs = width // (2 * size) // PARTS
    span = width // PARTS
    shared = []

    def inner(q, *others):
        held = after(bc, *others) if others else bc
        square = struct((rows, rows), F32)
        block = pl.BlockSpec((rows, span), lambda _: (0, q))
        out = call(
            functools.partial(inner_kernel, q * pairs, pairs, size),
            ([square] if q == 0 else [])
            + [struct((rows, span), F32), square, struct((2, 2 * pairs, rows), F32)],
                2.6,
            held,
            hp,
            x,
            g,
            *shared,
            scratch=(pltpu.VMEM((rows, 2 * span), BF), pltpu.VMEM((rows, 2 * span), BF)),
            specs=[VMEM, VMEM, block, block] + [VMEM] * len(shared),
        )
        if q == 0:
            shared.append(out[0])
            out = out[1:]
        return out

    weights = [w_bc, w_dt]

    def beside(*others):
        for r in range(1, n_dp):
            weights.extend(cyclic(after(a, *others), "dp", r) for a in (w_bc, w_dt))
        return weights[2:], relay(found[1], groups[1], second, *others) if n_dp > 1 else []

    first[0] = after(first[0], *early)
    riders = [f[1, 1] for f in found] if ride else []
    calls = [functools.partial(inner, q) for q in range(PARTS)]
    store, inners = chains(first, own, decay, calls, beside, riders)
    for f, a in zip(found, riders):
        f[0, 2] = a
    done = relay(found[0], groups[0], [step for step in slots if step not in found[0]], store)
    grad_x, keep, give = call(
        functools.partial(outer_kernel, size, PARTS),
        (
            struct((rows, width), BF),
            struct((rows + heads, rows), F32),
            struct((rows, rows), F32),
        ),
        5.4,
        store,
        x,
        g,
        bc,
        hp,
        decay,
        rate,
        *[a[0] for a in inners],
        *[a[1] for a in inners],
        *[a[2] for a in inners],
        scratch=(
            pltpu.VMEM((rows, 2 * width), BF),
            pltpu.VMEM((rows, 2 * width), BF),
            pltpu.VMEM((1, width), F32),
        ),
    )
    taken = after(cyclic(give, "head", 1), *done)
    count = n_dp * n_seq
    copies = call(low_kernel, struct((count, rows + heads, rows), BF), 1.2, keep, taken)
    mine = copies[0]
    lows = lax.all_to_all(copies, ("seq", "dp"), 0, 0, tiled=True)
    swapped = cyclic(lows, "head", 1)
    other = cyclic(mine, "head", 1)
    grads = call(
        functools.partial(token_kernel, n_dp),
        struct((rows, width), BF),
        2.9,
        mine,
        other,
        *weights,
    )
    toks = []
    for f, a in zip(found, groups):
        relay(f, a, [step for step in slots if step not in f], store)
        toks += [a] + [f[step] for step in slots]
    slots = [(0, 0)] + slots
    cols = 2 * (rows + heads)
    grad_bc, grad_dt = call(
        functools.partial(weight_kernel, 1.0 / (rows * n_seq * n_dp), n_dp, n_seq, slots),
        (struct((part, 2 * state_n), F32), struct((2 * heads, part), F32)),
        4.0,
        *toks,
        lows,
        swapped,
        specs=[ANY] * (len(toks) + 2),
        scratch=(
            pltpu.VMEM((n_dp, n_seq * rows, part), BF),
            pltpu.VMEM((n_dp, cols, n_seq * rows), BF),
            pltpu.SemaphoreType.DMA((n_dp, len(slots))),
            pltpu.SemaphoreType.DMA((count, 2)),
        ),
    )
    return grad_x[None], grads[None], grad_bc, grad_dt.T


def solution(mesh):
    in_specs = (
        P(("grp", "dp"), "seq", "head"),
        P(("grp", "dp"), "seq", "head"),
        P(("grp", "dp"), "seq", "head"),
        P(("head", "dp"), None),
        P(("head", "dp"), None),
        P("head"),
        P("head"),
    )
    out_specs = (
        P(("grp", "dp"), "seq", "head"),
        P(("grp", "dp"), "seq", "head"),
        P(("grp", "head", "dp"), None),
        P(("grp", "head", "dp"), None),
    )
    return jax.shard_map(body, mesh=mesh, in_specs=in_specs, out_specs=out_specs, check_vma=False)
```

```python
import functools

import jax
import jax.numpy as jnp
from jax import lax
from jax.experimental import pallas as pl
from jax.experimental.pallas import tpu as pltpu
from jax.sharding import PartitionSpec as P

CHUNKS = 2
PARTS = 4
BF = jnp.bfloat16
F32 = jnp.float32
TOP = lax.Precision.HIGHEST
PER_US = 1.15e9
LIMIT = 56 * 1024 * 1024


def cyclic(a, axis, by):
    count = lax.axis_size(axis)
    return lax.ppermute(a, axis, [(i, (i + by) % count) for i in range(count)])


def mm(a, b, ca, cb, precision=None):
    return lax.dot_general(
        a, b, (((ca,), (cb,)), ((), ())), preferred_element_type=F32, precision=precision
    )


def halves(a):
    high = a.astype(BF)
    return high, (a - high.astype(F32)).astype(BF)


def head_lanes(heads, width, size, first=0):
    row = lax.broadcasted_iota(jnp.int32, (heads, width), 0)
    col = lax.broadcasted_iota(jnp.int32, (heads, width), 1) + first
    low = row * size
    return jnp.where((col >= low) & (col < low + size), 1.0, 0.0).astype(F32)


def spread(a, pick):
    high, low = halves(a)
    both = jnp.concatenate([pick, pick], axis=0)
    return mm(jnp.concatenate([high, low], axis=0), both, 0, 0)


VMEM = pl.BlockSpec(memory_space=pltpu.VMEM)
ANY = pl.BlockSpec(memory_space=pl.ANY)


def call(kernel, out_shape, span_us, *args, scratch=(), specs=None, out_specs=None):
    size = sum(a.size * a.dtype.itemsize for a in args)
    return pl.pallas_call(
        kernel,
        out_shape=out_shape,
        grid=(1,),
        in_specs=specs or [VMEM] * len(args),
        out_specs=out_specs or jax.tree.map(lambda _: VMEM, out_shape),
        scratch_shapes=list(scratch),
        compiler_params=pltpu.CompilerParams(vmem_limit_bytes=LIMIT),
        cost_estimate=pl.CostEstimate(
            flops=int(span_us * PER_US), bytes_accessed=size, transcendentals=0
        ),
    )(*args)


def struct(shape, dtype):
    return jax.ShapeDtypeStruct(shape, dtype)


def after(a, *others):
    return lax.optimization_barrier((a, others))[0]


def matchings(count):
    groups = [[(i, i + 1) for i in range(kind, count - 1, 2)] for kind in (0, 1)]
    pairs = []
    for group in groups:
        to = {i: i for i in range(count)}
        for i, j in group:
            to[i], to[j] = j, i
        pairs.append(sorted(to.items()))
    return groups, pairs


def split_kernel(a_ref, *outs):
    count = len(outs)
    me = lax.axis_index("dp")
    part = outs[0].shape[1]
    for r in range(count):
        at = pl.multiple_of(lax.rem(me + r, count) * part, 128)
        outs[r][...] = a_ref[:, pl.ds(at, part)]


def project_kernel(a_ref, bc_ref, dt_ref, out_ref):
    a = a_ref[...]
    state_n = bc_ref.shape[1] // 2
    rows = a.shape[0]
    bc = mm(a, bc_ref[...], 1, 0)
    out_ref[0:rows, :] = bc[:, :state_n]
    out_ref[rows : 2 * rows, :] = bc[:, state_n:]
    out_ref[2 * rows :, :] = mm(dt_ref[...], a, 1, 1)


def project(a, w_bc, w_dt):
    rows = a.shape[0]
    total = 2 * rows + w_dt.shape[0]
    return call(
        project_kernel,
        struct((total, w_bc.shape[1] // 2), F32),
        2.1,
        a,
        w_bc,
        w_dt,
    )


def state_kernel(count, size, ride, *refs):
    proj = refs[:count]
    x_ref, g_ref, rate_ref, bias_ref = refs[count : count + 4]
    riders = refs[count + 4 : count + 4 + ride]
    own_ref, bc_ref, hp_ref = refs[count + 4 + ride : count + 7 + ride]
    outs = refs[count + 7 + ride :]
    firsts, decays = outs[: len(outs) // 2], outs[len(outs) // 2 :]
    heads = rate_ref.shape[1]
    rows = x_ref.shape[0]
    rate, bias = rate_ref[...].T, bias_ref[...].T
    chunks, step = own_ref.shape[1], own_ref.shape[3]
    first = pl.multiple_of(2 * rows + lax.axis_index("head") * heads, 8)
    bc = proj[0][0 : 2 * rows, :]
    pre = proj[0][pl.ds(first, heads), :] + bias
    for ref in proj[1:]:
        bc = bc + ref[0 : 2 * rows, :]
        pre = pre + ref[pl.ds(first, heads), :]
    bc_ref[...] = bc
    dt = jnp.maximum(pre, 0.0) + jnp.log1p(jnp.exp(-jnp.abs(pre)))
    row = lax.broadcasted_iota(jnp.int32, (rows, rows), 0)
    col = lax.broadcasted_iota(jnp.int32, (rows, rows), 1)
    cum = mm(-dt * rate, jnp.where(row <= col, 1.0, 0.0), 1, 0, TOP)
    last = cum[:, rows - 1 : rows]
    grow = jnp.exp(cum)
    w = jnp.exp(last - cum) * dt
    decay = jnp.exp(last)
    for k, part in enumerate((pre, dt, cum, grow, w)):
        hp_ref[k * heads : (k + 1) * heads, :] = part
    place = lax.axis_index("seq")
    lowest = place == 0
    sides = []
    for vec in (bc[:rows], bc[rows:]):
        high, low = halves(vec.T)
        sides.append((jnp.concatenate([high, low], axis=1), high))
    for k in range(chunks):
        pick = head_lanes(heads, step, size, k * step)
        decays[k][...] = jnp.sum(pick * decay, axis=0, keepdims=True)
        pick = pick.astype(BF)
        both = []
        for kind, (scale, ref) in enumerate(((w, x_ref), (grow, g_ref))):
            wide, high = sides[kind]
            value = spread(scale, pick) * ref[:, k * step : (k + 1) * step].astype(F32)
            top, rest = halves(value)
            value = mm(wide, jnp.concatenate([top, top], axis=0), 1, 0) + mm(high, rest, 1, 0)
            own_ref[kind, k] = value
            both.append(value)
        firsts[k][...] = jnp.where(lowest, both[0], both[1]).astype(BF)
        if k < ride:
            rider = riders[k]

            @pl.when((place > 0) & (place < lax.axis_size("seq") - 1))
            def _():
                firsts[k][...] = rider[...]


def inner_kernel(first, pairs, size, bc_ref, hp_ref, x_ref, g_ref, *refs):
    gx_ref, ds_ref, sums_ref = refs[-5:-2]
    gy_ref, xg_ref = refs[-2:]
    rows = x_ref.shape[0]
    heads = hp_ref.shape[0] // 5
    lanes = 2 * size
    width = pairs * lanes
    if len(refs) == 6 and first > 0:
        scores = refs[0][...]
    else:
        scores = mm(bc_ref[rows : 2 * rows, :], bc_ref[0:rows, :], 1, 1, TOP)
        refs[0][...] = scores
    row = lax.broadcasted_iota(jnp.int32, (rows, rows), 0)
    col = lax.broadcasted_iota(jnp.int32, (rows, rows), 1)
    causal = row >= col
    dt = hp_ref[heads : 2 * heads, :]
    cum = hp_ref[2 * heads : 3 * heads, :]
    cum_t = cum.T
    lane = lax.broadcasted_iota(jnp.int32, (rows, lanes), 1)
    sides = [jnp.where(lane < size, 1.0, 0.0).astype(BF), jnp.where(lane < size, 0.0, 1.0).astype(BF)]
    ds = jnp.zeros((rows, rows), F32)
    for j in range(pairs):
        place = slice(j * lanes, (j + 1) * lanes)
        x, g = x_ref[:, place], g_ref[:, place]
        xs = jnp.concatenate([x * s for s in sides], axis=0)
        gs = jnp.concatenate([g * s for s in sides], axis=0)
        m = mm(gs, x, 1, 1)
        kern = []
        for i in range(2):
            h = 2 * (first + j) + i
            gap = cum_t[:, h : h + 1] - cum[h : h + 1, :]
            fall = jnp.exp(jnp.where(causal, gap, -jnp.inf)) * dt[h : h + 1, :]
            kern.append((fall * scores).astype(BF))
            ds = ds + fall * m[i * rows : (i + 1) * rows]
        y = mm(jnp.concatenate(kern, axis=1), xs, 1, 0)
        gx = mm(jnp.concatenate(kern, axis=0), gs, 0, 0)
        gx_ref[:, place] = gx
        late = slice(width + j * lanes, width + (j + 1) * lanes)
        gy_ref[:, place], gy_ref[:, late] = halves(g.astype(F32) * y)
        xg_ref[:, place], xg_ref[:, late] = halves(x.astype(F32) * gx)
    ds_ref[...] = ds
    pick = head_lanes(2 * pairs, width, size).astype(BF)
    pick = jnp.concatenate([pick, pick], axis=1)
    sums_ref[0] = mm(pick, gy_ref[...], 1, 1)
    sums_ref[1] = mm(pick, xg_ref[...], 1, 1)


def outer_kernel(size, parts, *refs):
    store_ref, x_ref, g_ref, bc_ref, hp_ref, rate_ref = refs[:6]
    gxs, dss, sums = (refs[6 + k * parts : 6 + (k + 1) * parts] for k in range(3))
    grad_ref, keep_ref, give_ref, wv_ref, eu_ref, io_ref = refs[6 + 3 * parts :]
    rate = rate_ref[...].T
    rows, width = x_ref.shape
    heads = rate_ref.shape[1]
    chunks, step = store_ref.shape[1] - 1, store_ref.shape[3]
    piece = width // parts
    b, c = bc_ref[0:rows, :], bc_ref[rows : 2 * rows, :]
    pre, dt, cum, grow, w = (hp_ref[k * heads : (k + 1) * heads, :] for k in range(5))
    ds = dss[0][...]
    for ref in dss[1:]:
        ds = ds + ref[...]
    db = mm(c, ds, 0, 0, TOP)
    dc = mm(b, ds, 0, 1, TOP)
    b_wide = jnp.concatenate(halves(b), axis=1)
    c_wide = jnp.concatenate(halves(c), axis=1)
    for k in range(chunks):
        place = slice(k * step, (k + 1) * step)
        late = slice(width + k * step, width + (k + 1) * step)
        pick = head_lanes(heads, step, size, k * step).astype(BF)
        incoming, outgoing = store_ref[0, k], store_ref[1, k]
        u = mm(c_wide, jnp.concatenate([incoming, incoming], axis=0), 1, 0)
        v = mm(b_wide, jnp.concatenate([outgoing, outgoing], axis=0), 1, 0)
        scale = spread(w, pick)
        wx = scale * x_ref[:, place].astype(F32)
        eg = spread(grow, pick) * g_ref[:, place].astype(F32)
        for q in range(step // piece) if step >= piece else (0,):
            if step >= piece:
                at = k * step + q * piece
                inner = slice(q * piece, (q + 1) * piece)
                term = gxs[at // piece][...]
            else:
                at, inner = k * step, slice(0, step)
                term = gxs[at // piece][:, at % piece : at % piece + step]
            total = term + scale[:, inner] * v[:, inner]
            grad_ref[:, at : at + total.shape[1]] = total.astype(BF)
        wv_ref[:, place], wv_ref[:, late] = halves(wx * v)
        eu_ref[:, place], eu_ref[:, late] = halves(eg * u)
        db = db + mm(
            jnp.concatenate([outgoing, outgoing], axis=1), jnp.concatenate(halves(wx), axis=1), 1, 1
        )
        dc = dc + mm(
            jnp.concatenate([incoming, incoming], axis=1), jnp.concatenate(halves(eg), axis=1), 1, 1
        )
        io_ref[:, place] = jnp.sum(incoming.astype(F32) * outgoing.astype(F32), axis=0, keepdims=True)
    pick = head_lanes(heads, width, size)
    ddecay = jnp.sum(pick * io_ref[...], axis=1, keepdims=True)
    pick = pick.astype(BF)
    pick = jnp.concatenate([pick, pick], axis=1)
    wdw = mm(pick, wv_ref[...], 1, 1)
    egu = mm(pick, eu_ref[...], 1, 1)
    rowsum = jnp.concatenate([s[0] for s in sums], axis=0)
    colsum = jnp.concatenate([s[1] for s in sums], axis=0)
    dcum = rowsum - colsum + egu - wdw
    row = lax.broadcasted_iota(jnp.int32, (rows, rows), 0)
    col = lax.broadcasted_iota(jnp.int32, (rows, rows), 1)
    rev = mm(dcum, jnp.where(row >= col, 1.0, 0.0), 1, 0, TOP)
    decay = grow[:, rows - 1 : rows]
    rev = rev + jnp.sum(wdw, axis=1, keepdims=True) + decay * ddecay
    gate = 1.0 / (1.0 + jnp.exp(-pre))
    small = 1e-30
    ratio = jnp.where(dt > small, gate / jnp.maximum(dt, small), 1.0)
    core = lax.axis_index("head")
    keep_ref[0:rows, :] = jnp.where(core == 0, db, dc)
    keep_ref[rows:, :] = (colsum + wdw) * ratio - rate * rev * gate
    give_ref[...] = jnp.where(core == 0, dc, db)


def low_kernel(keep_ref, taken_ref, out_ref):
    rows = taken_ref.shape[0]
    low = keep_ref[0:rows, :] + taken_ref[...]
    low = jnp.concatenate([low, keep_ref[rows:, :]], axis=0).astype(BF)
    for k in range(out_ref.shape[0]):
        out_ref[k] = low


def token_kernel(count, mine_ref, other_ref, *refs):
    out_ref = refs[2 * count]
    me, core = lax.axis_index("dp"), lax.axis_index("head")
    part, cols = refs[0].shape
    half = cols // 2
    heads = refs[1].shape[0] // 2
    for r in range(count):
        at = pl.multiple_of(lax.rem(me - r + count, count) * part, 128)
        total = None
        for k, ref in enumerate((mine_ref, other_ref)):
            at_col = pl.multiple_of(lax.rem(core + k, 2) * half, 128)
            at_row = pl.multiple_of(lax.rem(core + k, 2) * heads, 16)
            term = mm(ref[0:half, :], refs[2 * r][:, pl.ds(at_col, half)], 0, 1)
            term = term + mm(ref[half:, :], refs[2 * r + 1][pl.ds(at_row, heads), :], 0, 0)
            total = term if total is None else total + term
        out_ref[:, pl.ds(at, part)] = total.astype(BF)


def weight_kernel(scale, n_dp, n_seq, slots, *refs):
    count = 2 * len(slots) if n_dp > 1 else len(slots)
    toks, lows = refs[:count], refs[count:-6]
    bc_ref, dt_ref, tok_ref, low_ref, tok_sem, low_sem = refs[-6:]
    rows = toks[0].shape[0]
    share = lows[0].shape[1]
    core, place, me = lax.axis_index("head"), lax.axis_index("seq"), lax.axis_index("dp")
    even = lax.rem(place, 2) == 0
    copies = []
    for r in range(n_dp):
        for k, (kind, hop) in enumerate(slots):
            above = even if kind == 0 else ~even
            block = jnp.where(above, place + hop, place - hop)
            fits = (block >= 0) & (block < n_seq)
            if hop > 0 and kind == 1:
                fits = fits & jnp.where(above, place < n_seq - 1, place > 0)
            at = pl.multiple_of(jnp.clip(block, 0, n_seq - 1) * rows, 128)
            source = toks[k] if r == 0 else toks[len(slots) + k].at[pl.ds((r - 1) * rows, rows)]
            copy = pltpu.make_async_copy(source, tok_ref.at[r, pl.ds(at, rows)], tok_sem.at[r, k])
            copies.append((fits, copy))
    for r in range(n_dp):
        for s in range(n_seq):
            index = s * n_dp + lax.rem(me - r + n_dp, n_dp)
            for k in range(2):
                row = pl.multiple_of(lax.rem(core + k, 2) * share, 16)
                copy = pltpu.make_async_copy(
                    lows[k].at[index],
                    low_ref.at[r, pl.ds(row, share), pl.ds(s * rows, rows)],
                    low_sem.at[r * n_seq + s, k],
                )
                copies.append((None, copy))
    for fits, copy in copies:
        if fits is None:
            copy.start()
        else:
            pl.when(fits)(copy.start)
    for fits, copy in copies:
        if fits is None:
            copy.wait()
        else:
            pl.when(fits)(copy.wait)
    total = mm(low_ref[0], tok_ref[0], 1, 0)
    for r in range(1, n_dp):
        total = total + mm(low_ref[r], tok_ref[r], 1, 0)
    total = total * scale
    half = bc_ref.shape[1] // 2
    heads = dt_ref.shape[0] // 2
    for k in range(2):
        bc_ref[:, k * half : (k + 1) * half] = total[k * share : k * share + half].T
        dt_ref[k * heads : (k + 1) * heads, :] = total[k * share + half : (k + 1) * share]


def relays(count):
    groups, _ = matchings(count)
    return [
        (kind, hop)
        for hop in range(1, count)
        for kind in (0, 1)
        if any(i - hop + 1 >= 0 or j + hop - 1 < count for i, j in groups[kind])
    ]


def relay(found, block, steps, *others):
    count = lax.axis_size("seq")
    _, pairs = matchings(count)
    for kind, hop in steps:
        source = block if hop == 1 else found[1 - kind, hop - 1]
        source = after(source, *others) if others else source
        found[kind, hop] = lax.ppermute(source, "seq", pairs[kind])
    return [found[step] for step in steps]


def chains(first, own, decay, inner, beside, riders, late):
    count = lax.axis_size("seq")
    place = lax.axis_index("seq")
    chunks = len(first)
    store = jnp.zeros((2, chunks + 1) + own.shape[2:], BF)
    got = list(first)
    done, todo, extra = [], list(inner), []
    last = count + chunks - 2
    for slot in range(1, last + 1):
        steps = [(hop, slot - hop) for hop in range(1, count) if 0 <= slot - hop < chunks]
        sent = []
        for hop, k in steps:
            value = got[k]
            if hop == 1 and 0 < k < len(riders):
                value = jnp.where((place == 0) | (place == count - 1), value, riders[k])
            if hop > 1:
                value = jnp.where(place == hop - 1, own[0, k], own[1, k])
                value = (value + decay[k] * got[k].astype(F32)).astype(BF)
            sent.append(value)
        for (hop, k), value in zip(steps, sent):
            to = {i: i for i in range(count)}
            for i in (hop - 1, count - hop - 1):
                to[i], to[i + 1] = i + 1, i
            got[k] = lax.ppermute(value, "seq", sorted(to.items()))
            if hop == 1 and k < len(riders):
                riders[k] = got[k]
        for _ in range(-(-len(todo) // (last + 1 - slot))):
            done.append(todo.pop(0)(*sent))
        if slot == 1:
            extra, soon = beside(*sent)
        if slot == last:
            late(*sent)
        if slot < last:
            held = [got[k] for _, k in steps] + [d[0] for d in done[-1:]]
            if slot == last - 1:
                held += extra
            if slot == 1:
                held += soon
            new = slot < chunks
            if new:
                held.append(got[slot])
            kept = lax.optimization_barrier(tuple(held))
            for (_, k), a in zip(steps, kept):
                got[k] = a
            if new:
                got[slot] = kept[-1]
        for hop, k in steps:
            kind = jnp.where(place == hop, 0, 1)
            fits = (place == hop) | (place == count - hop - 1)
            at = jnp.where(fits, k, chunks)
            zero = jnp.zeros_like(at)
            store = lax.dynamic_update_slice(store, got[k][None, None], (kind, at, zero, zero))
    done += [make() for make in todo]
    return store, done


def body(tokens, ssd_input, grad_out, w_bc, w_dt, decay_rate, dt_bias):
    feats, x, g = tokens[0], ssd_input[0], grad_out[0]
    rows, width = feats.shape
    heads = decay_rate.shape[0]
    size = width // heads
    n_dp, n_seq = lax.axis_size("dp"), lax.axis_size("seq")
    part = width // n_dp
    state_n = w_bc.shape[1] // 2
    w_dt = w_dt.T
    rate, bias = decay_rate[None], dt_bias[None]

    pieces = call(split_kernel, [struct((rows, part), BF)] * n_dp, 1.9, feats)
    items = [pieces[0]] + [cyclic(pieces[r], "dp", r) for r in range(1, n_dp)]
    groups = items[:1]
    if n_dp > 1:
        groups.append(items[1] if n_dp == 2 else jnp.concatenate(items[1:], axis=0))
    found = [{} for _ in groups]
    slots = relays(n_seq)
    step = width // CHUNKS
    ride = n_seq == 4 and all(a.shape == (state_n, step) for a in groups)
    second = [(kind, hop) for kind, hop in slots if hop == 2 and not (ride and kind == 0)]
    near = relay(found[0], groups[0], slots[:2])
    partials = [project(items[0], w_bc, w_dt)]
    for r in range(1, n_dp):
        item = after(items[r], partials[0])
        partials.append(cyclic(project(item, w_bc, w_dt), "dp", -r))
    partials[1:] = [after(a, *near) for a in partials[1:]]
    proj = partials + [cyclic(a, "head", 1) for a in partials]
    x = after(x, *relay(found[0], groups[0], second))
    early = []
    if n_dp > 1:
        early = relay(found[1], groups[1], slots[: 1 if ride else 2])
        x = after(x, *early)
    own, bc, hp, *outs = call(
        functools.partial(state_kernel, 2 * n_dp, size, int(ride)),
        (
            struct((2, CHUNKS, state_n, step), F32),
            struct((2 * rows, state_n), F32),
            struct((5 * heads, rows), F32),
        )
        + (struct((state_n, step), BF),) * CHUNKS
        + (struct((1, step), F32),) * CHUNKS,
        1.0,
        *proj,
        x,
        g,
        rate,
        bias,
        *([found[0][1, 1]] if ride else []),
    )
    first, decay = outs[:CHUNKS], outs[CHUNKS:]
    pairs = width // (2 * size) // PARTS
    span = width // PARTS
    shared = []

    def inner(q, *others):
        held = after(bc, *others) if others else bc
        square = struct((rows, rows), F32)
        block = pl.BlockSpec((rows, span), lambda _: (0, q))
        out = call(
            functools.partial(inner_kernel, q * pairs, pairs, size),
            ([square] if q == 0 else [])
            + [struct((rows, span), F32), square, struct((2, 2 * pairs, rows), F32)],
                2.6,
            held,
            hp,
            x,
            g,
            *shared,
            scratch=(pltpu.VMEM((rows, 2 * span), BF), pltpu.VMEM((rows, 2 * span), BF)),
            specs=[VMEM, VMEM, block, block] + [VMEM] * len(shared),
        )
        if q == 0:
            shared.append(out[0])
            out = out[1:]
        return out

    weights = [w_bc, w_dt]

    def beside(*others):
        for r in range(1, n_dp):
            weights.extend(cyclic(after(a, *others), "dp", r) for a in (w_bc, w_dt))
        if not ride or n_dp == 1:
            return weights[2:], []
        riders.extend(relay(found[1], groups[1], [(1, 1)], *others))
        return weights[2:], riders[1:]

    def late(*others):
        if n_dp > 1:
            relay(found[1], groups[1], second, *others)

    riders = [found[0][1, 1]] if ride else []
    calls = [functools.partial(inner, q) for q in range(PARTS)]
    store, inners = chains(first, own, decay, calls, beside, riders, late)
    for f, a in zip(found, riders):
        f[0, 2] = a
    done = []
    for f, a in zip(found, groups):
        done += relay(f, a, [step for step in slots if step not in f], store)
    grad_x, keep, give = call(
        functools.partial(outer_kernel, size, PARTS),
        (
            struct((rows, width), BF),
            struct((rows + heads, rows), F32),
            struct((rows, rows), F32),
        ),
        5.4,
        store,
        x,
        g,
        bc,
        hp,
        rate,
        *[a[0] for a in inners],
        *[a[1] for a in inners],
        *[a[2] for a in inners],
        scratch=(
            pltpu.VMEM((rows, 2 * width), BF),
            pltpu.VMEM((rows, 2 * width), BF),
            pltpu.VMEM((1, width), F32),
        ),
    )
    taken = after(cyclic(give, "head", 1), *done)
    count = n_dp * n_seq
    copies = call(low_kernel, struct((count, rows + heads, rows), BF), 1.2, keep, taken)
    mine = copies[0]
    lows = lax.all_to_all(copies, ("seq", "dp"), 0, 0, tiled=True)
    swapped = cyclic(lows, "head", 1)
    other = cyclic(mine, "head", 1)
    grads = call(
        functools.partial(token_kernel, n_dp),
        struct((rows, width), BF),
        2.9,
        mine,
        other,
        *weights,
    )
    toks = []
    for f, a in zip(found, groups):
        toks += [a] + [f[step] for step in slots]
    slots = [(0, 0)] + slots
    cols = 2 * (rows + heads)
    grad_bc, grad_dt = call(
        functools.partial(weight_kernel, 1.0 / (rows * n_seq * n_dp), n_dp, n_seq, slots),
        (struct((part, 2 * state_n), F32), struct((2 * heads, part), F32)),
        4.0,
        *toks,
        lows,
        swapped,
        specs=[ANY] * (len(toks) + 2),
        scratch=(
            pltpu.VMEM((n_dp, n_seq * rows, part), BF),
            pltpu.VMEM((n_dp, cols, n_seq * rows), BF),
            pltpu.SemaphoreType.DMA((n_dp, len(slots))),
            pltpu.SemaphoreType.DMA((count, 2)),
        ),
    )
    return grad_x[None], grads[None], grad_bc, grad_dt.T


def solution(mesh):
    in_specs = (
        P(("grp", "dp"), "seq", "head"),
        P(("grp", "dp"), "seq", "head"),
        P(("grp", "dp"), "seq", "head"),
        P(("head", "dp"), None),
        P(("head", "dp"), None),
        P("head"),
        P("head"),
    )
    out_specs = (
        P(("grp", "dp"), "seq", "head"),
        P(("grp", "dp"), "seq", "head"),
        P(("grp", "head", "dp"), None),
        P(("grp", "head", "dp"), None),
    )
    return jax.shard_map(body, mesh=mesh, in_specs=in_specs, out_specs=out_specs, check_vma=False)
```

```python
import functools

import jax
import jax.numpy as jnp
from jax import lax
from jax.experimental import pallas as pl
from jax.experimental.pallas import tpu as pltpu
from jax.sharding import PartitionSpec as P

CHUNKS = 2
PARTS = 4
BF = jnp.bfloat16
F32 = jnp.float32
TOP = lax.Precision.HIGHEST
PER_US = 1.15e9
LIMIT = 16 * 1024 * 1024


def cyclic(a, axis, by):
    count = lax.axis_size(axis)
    return lax.ppermute(a, axis, [(i, (i + by) % count) for i in range(count)])


def mm(a, b, ca, cb, precision=None):
    return lax.dot_general(
        a, b, (((ca,), (cb,)), ((), ())), preferred_element_type=F32, precision=precision
    )


def halves(a):
    high = a.astype(BF)
    return high, (a - high.astype(F32)).astype(BF)


def head_lanes(heads, width, size, first=0):
    row = lax.broadcasted_iota(jnp.int32, (heads, width), 0)
    col = lax.broadcasted_iota(jnp.int32, (heads, width), 1) + first
    low = row * size
    return jnp.where((col >= low) & (col < low + size), 1.0, 0.0).astype(F32)


def spread(a, pick):
    high, low = halves(a)
    both = jnp.concatenate([pick, pick], axis=0)
    return mm(jnp.concatenate([high, low], axis=0), both, 0, 0)


VMEM = pl.BlockSpec(memory_space=pltpu.VMEM)
ANY = pl.BlockSpec(memory_space=pl.ANY)


def call(kernel, out_shape, span_us, *args, scratch=(), specs=None, limit=LIMIT):
    size = sum(a.size * a.dtype.itemsize for a in args)
    return pl.pallas_call(
        kernel,
        out_shape=out_shape,
        grid=(1,),
        in_specs=specs or [VMEM] * len(args),
        out_specs=jax.tree.map(lambda _: VMEM, out_shape),
        scratch_shapes=list(scratch),
        compiler_params=pltpu.CompilerParams(vmem_limit_bytes=limit),
        cost_estimate=pl.CostEstimate(
            flops=int(span_us * PER_US), bytes_accessed=size, transcendentals=0
        ),
    )(*args)


def struct(shape, dtype):
    return jax.ShapeDtypeStruct(shape, dtype)


def after(a, *others):
    return lax.optimization_barrier((a, others))[0]


def matchings(count):
    groups = [[(i, i + 1) for i in range(kind, count - 1, 2)] for kind in (0, 1)]
    pairs = []
    for group in groups:
        to = {i: i for i in range(count)}
        for i, j in group:
            to[i], to[j] = j, i
        pairs.append(sorted(to.items()))
    return groups, pairs


def split_kernel(a_ref, *outs):
    count = len(outs)
    me = lax.axis_index("dp")
    part = outs[0].shape[1]
    for r in range(count):
        at = pl.multiple_of(lax.rem(me + r, count) * part, 128)
        outs[r][...] = a_ref[:, pl.ds(at, part)]


def project_kernel(a_ref, bc_ref, dt_ref, out_ref):
    a = a_ref[...]
    state_n = bc_ref.shape[1] // 2
    rows = a.shape[0]
    bc = mm(a, bc_ref[...], 1, 0)
    out_ref[0:rows, :] = bc[:, :state_n]
    out_ref[rows : 2 * rows, :] = bc[:, state_n:]
    out_ref[2 * rows :, :] = mm(dt_ref[...], a, 1, 1)


def project(a, w_bc, w_dt):
    rows = a.shape[0]
    total = 2 * rows + w_dt.shape[0]
    return call(
        project_kernel,
        struct((total, w_bc.shape[1] // 2), F32),
        2.1,
        a,
        w_bc,
        w_dt,
    )


def state_kernel(count, size, ride, *refs):
    proj = refs[:count]
    x_ref, g_ref, rate_ref, bias_ref = refs[count : count + 4]
    riders = refs[count + 4 : count + 4 + ride]
    own_ref, bc_ref, hp_ref = refs[count + 4 + ride : count + 7 + ride]
    outs = refs[count + 7 + ride :]
    firsts, decays = outs[: len(outs) // 2], outs[len(outs) // 2 :]
    heads = rate_ref.shape[1]
    rows = x_ref.shape[0]
    rate, bias = rate_ref[...].T, bias_ref[...].T
    chunks, step = own_ref.shape[1], own_ref.shape[3]
    first = pl.multiple_of(2 * rows + lax.axis_index("head") * heads, 8)
    bc = proj[0][0 : 2 * rows, :]
    pre = proj[0][pl.ds(first, heads), :] + bias
    for ref in proj[1:]:
        bc = bc + ref[0 : 2 * rows, :]
        pre = pre + ref[pl.ds(first, heads), :]
    bc_ref[...] = bc
    dt = jnp.maximum(pre, 0.0) + jnp.log1p(jnp.exp(-jnp.abs(pre)))
    row = lax.broadcasted_iota(jnp.int32, (rows, rows), 0)
    col = lax.broadcasted_iota(jnp.int32, (rows, rows), 1)
    cum = mm(-dt * rate, jnp.where(row <= col, 1.0, 0.0), 1, 0, TOP)
    last = cum[:, rows - 1 : rows]
    grow = jnp.exp(cum)
    w = jnp.exp(last - cum) * dt
    decay = jnp.exp(last)
    for k, part in enumerate((pre, dt, cum, grow, w)):
        hp_ref[k * heads : (k + 1) * heads, :] = part
    place = lax.axis_index("seq")
    lowest = place == 0
    sides = []
    for vec in (bc[:rows], bc[rows:]):
        high, low = halves(vec.T)
        sides.append((jnp.concatenate([high, low], axis=1), high))
    for k in range(chunks):
        pick = head_lanes(heads, step, size, k * step)
        decays[k][...] = jnp.sum(pick * decay, axis=0, keepdims=True)
        pick = pick.astype(BF)
        both = []
        for kind, (scale, ref) in enumerate(((w, x_ref), (grow, g_ref))):
            wide, high = sides[kind]
            value = spread(scale, pick) * ref[:, k * step : (k + 1) * step].astype(F32)
            top, rest = halves(value)
            value = mm(wide, jnp.concatenate([top, top], axis=0), 1, 0) + mm(high, rest, 1, 0)
            own_ref[kind, k] = value
            both.append(value)
        firsts[k][...] = jnp.where(lowest, both[0], both[1]).astype(BF)
        if k < ride:
            rider = riders[k]

            @pl.when((place > 0) & (place < lax.axis_size("seq") - 1))
            def _():
                firsts[k][...] = rider[...]


def inner_kernel(first, pairs, size, bc_ref, hp_ref, x_ref, g_ref, *refs):
    gx_ref, ds_ref, sums_ref = refs[-5:-2]
    gy_ref, xg_ref = refs[-2:]
    rows = x_ref.shape[0]
    heads = hp_ref.shape[0] // 5
    lanes = 2 * size
    width = pairs * lanes
    if len(refs) == 6 and first > 0:
        scores = refs[0][...]
    else:
        scores = mm(bc_ref[rows : 2 * rows, :], bc_ref[0:rows, :], 1, 1, TOP)
        refs[0][...] = scores
    row = lax.broadcasted_iota(jnp.int32, (rows, rows), 0)
    col = lax.broadcasted_iota(jnp.int32, (rows, rows), 1)
    causal = row >= col
    dt = hp_ref[heads : 2 * heads, :]
    cum = hp_ref[2 * heads : 3 * heads, :]
    cum_t = cum.T
    lane = lax.broadcasted_iota(jnp.int32, (rows, lanes), 1)
    sides = [jnp.where(lane < size, 1.0, 0.0).astype(BF), jnp.where(lane < size, 0.0, 1.0).astype(BF)]
    ds = jnp.zeros((rows, rows), F32)
    for j in range(pairs):
        place = slice(j * lanes, (j + 1) * lanes)
        x, g = x_ref[:, place], g_ref[:, place]
        xs = jnp.concatenate([x * s for s in sides], axis=0)
        gs = jnp.concatenate([g * s for s in sides], axis=0)
        m = mm(gs, x, 1, 1)
        kern = []
        for i in range(2):
            h = 2 * (first + j) + i
            gap = cum_t[:, h : h + 1] - cum[h : h + 1, :]
            fall = jnp.exp(jnp.where(causal, gap, -jnp.inf)) * dt[h : h + 1, :]
            kern.append((fall * scores).astype(BF))
            ds = ds + fall * m[i * rows : (i + 1) * rows]
        y = mm(jnp.concatenate(kern, axis=1), xs, 1, 0)
        gx = mm(jnp.concatenate(kern, axis=0), gs, 0, 0)
        gx_ref[:, place] = gx
        late = slice(width + j * lanes, width + (j + 1) * lanes)
        gy_ref[:, place], gy_ref[:, late] = halves(g.astype(F32) * y)
        xg_ref[:, place], xg_ref[:, late] = halves(x.astype(F32) * gx)
    ds_ref[...] = ds
    pick = head_lanes(2 * pairs, width, size).astype(BF)
    pick = jnp.concatenate([pick, pick], axis=1)
    sums_ref[0] = mm(pick, gy_ref[...], 1, 1)
    sums_ref[1] = mm(pick, xg_ref[...], 1, 1)


def outer_kernel(size, parts, *refs):
    store_ref, x_ref, g_ref, bc_ref, hp_ref, rate_ref = refs[:6]
    gxs, dss, sums = (refs[6 + k * parts : 6 + (k + 1) * parts] for k in range(3))
    grad_ref, keep_ref, give_ref, wv_ref, eu_ref, io_ref = refs[6 + 3 * parts :]
    rate = rate_ref[...].T
    rows, width = x_ref.shape
    heads = rate_ref.shape[1]
    chunks, step = store_ref.shape[1] - 1, store_ref.shape[3]
    piece = width // parts
    b, c = bc_ref[0:rows, :], bc_ref[rows : 2 * rows, :]
    pre, dt, cum, grow, w = (hp_ref[k * heads : (k + 1) * heads, :] for k in range(5))
    ds = dss[0][...]
    for ref in dss[1:]:
        ds = ds + ref[...]
    db = mm(c, ds, 0, 0, TOP)
    dc = mm(b, ds, 0, 1, TOP)
    b_wide = jnp.concatenate(halves(b), axis=1)
    c_wide = jnp.concatenate(halves(c), axis=1)
    for k in range(chunks):
        place = slice(k * step, (k + 1) * step)
        late = slice(width + k * step, width + (k + 1) * step)
        pick = head_lanes(heads, step, size, k * step).astype(BF)
        incoming, outgoing = store_ref[0, k], store_ref[1, k]
        u = mm(c_wide, jnp.concatenate([incoming, incoming], axis=0), 1, 0)
        v = mm(b_wide, jnp.concatenate([outgoing, outgoing], axis=0), 1, 0)
        scale = spread(w, pick)
        wx = scale * x_ref[:, place].astype(F32)
        eg = spread(grow, pick) * g_ref[:, place].astype(F32)
        for q in range(step // piece) if step >= piece else (0,):
            if step >= piece:
                at = k * step + q * piece
                inner = slice(q * piece, (q + 1) * piece)
                term = gxs[at // piece][...]
            else:
                at, inner = k * step, slice(0, step)
                term = gxs[at // piece][:, at % piece : at % piece + step]
            total = term + scale[:, inner] * v[:, inner]
            grad_ref[:, at : at + total.shape[1]] = total.astype(BF)
        wv_ref[:, place], wv_ref[:, late] = halves(wx * v)
        eu_ref[:, place], eu_ref[:, late] = halves(eg * u)
        db = db + mm(
            jnp.concatenate([outgoing, outgoing], axis=1), jnp.concatenate(halves(wx), axis=1), 1, 1
        )
        dc = dc + mm(
            jnp.concatenate([incoming, incoming], axis=1), jnp.concatenate(halves(eg), axis=1), 1, 1
        )
        io_ref[:, place] = jnp.sum(incoming.astype(F32) * outgoing.astype(F32), axis=0, keepdims=True)
    pick = head_lanes(heads, width, size)
    ddecay = jnp.sum(pick * io_ref[...], axis=1, keepdims=True)
    pick = pick.astype(BF)
    pick = jnp.concatenate([pick, pick], axis=1)
    wdw = mm(pick, wv_ref[...], 1, 1)
    egu = mm(pick, eu_ref[...], 1, 1)
    rowsum = jnp.concatenate([s[0] for s in sums], axis=0)
    colsum = jnp.concatenate([s[1] for s in sums], axis=0)
    dcum = rowsum - colsum + egu - wdw
    row = lax.broadcasted_iota(jnp.int32, (rows, rows), 0)
    col = lax.broadcasted_iota(jnp.int32, (rows, rows), 1)
    rev = mm(dcum, jnp.where(row >= col, 1.0, 0.0), 1, 0, TOP)
    decay = grow[:, rows - 1 : rows]
    rev = rev + jnp.sum(wdw, axis=1, keepdims=True) + decay * ddecay
    gate = 1.0 / (1.0 + jnp.exp(-pre))
    small = 1e-30
    ratio = jnp.where(dt > small, gate / jnp.maximum(dt, small), 1.0)
    core = lax.axis_index("head")
    keep_ref[0:rows, :] = jnp.where(core == 0, db, dc)
    keep_ref[rows:, :] = (colsum + wdw) * ratio - rate * rev * gate
    give_ref[...] = jnp.where(core == 0, dc, db)


def low_kernel(keep_ref, taken_ref, out_ref):
    rows = taken_ref.shape[0]
    low = keep_ref[0:rows, :] + taken_ref[...]
    low = jnp.concatenate([low, keep_ref[rows:, :]], axis=0).astype(BF)
    for k in range(out_ref.shape[0]):
        out_ref[k] = low


def token_kernel(count, mine_ref, other_ref, *refs):
    out_ref = refs[2 * count]
    me, core = lax.axis_index("dp"), lax.axis_index("head")
    part, cols = refs[0].shape
    half = cols // 2
    heads = refs[1].shape[0] // 2
    for r in range(count):
        at = pl.multiple_of(lax.rem(me - r + count, count) * part, 128)
        total = None
        for k, ref in enumerate((mine_ref, other_ref)):
            at_col = pl.multiple_of(lax.rem(core + k, 2) * half, 128)
            at_row = pl.multiple_of(lax.rem(core + k, 2) * heads, 16)
            term = mm(ref[0:half, :], refs[2 * r][:, pl.ds(at_col, half)], 0, 1)
            term = term + mm(ref[half:, :], refs[2 * r + 1][pl.ds(at_row, heads), :], 0, 0)
            total = term if total is None else total + term
        out_ref[:, pl.ds(at, part)] = total.astype(BF)


def weight_kernel(scale, n_dp, n_seq, slots, *refs):
    count = 2 * len(slots) if n_dp > 1 else len(slots)
    toks, lows = refs[:count], refs[count:-6]
    bc_ref, dt_ref, tok_ref, low_ref, tok_sem, low_sem = refs[-6:]
    rows = toks[0].shape[0]
    share = lows[0].shape[1]
    core, place, me = lax.axis_index("head"), lax.axis_index("seq"), lax.axis_index("dp")
    even = lax.rem(place, 2) == 0
    copies = []
    for r in range(n_dp):
        for k, (kind, hop) in enumerate(slots):
            above = even if kind == 0 else ~even
            block = jnp.where(above, place + hop, place - hop)
            fits = (block >= 0) & (block < n_seq)
            if hop > 0 and kind == 1:
                fits = fits & jnp.where(above, place < n_seq - 1, place > 0)
            at = pl.multiple_of(jnp.clip(block, 0, n_seq - 1) * rows, 128)
            source = toks[k] if r == 0 else toks[len(slots) + k].at[pl.ds((r - 1) * rows, rows)]
            copy = pltpu.make_async_copy(source, tok_ref.at[r, pl.ds(at, rows)], tok_sem.at[r, k])
            copies.append((fits, copy))
    for r in range(n_dp):
        for s in range(n_seq):
            index = s * n_dp + lax.rem(me - r + n_dp, n_dp)
            for k in range(2):
                row = pl.multiple_of(lax.rem(core + k, 2) * share, 16)
                copy = pltpu.make_async_copy(
                    lows[k].at[index],
                    low_ref.at[r, pl.ds(row, share), pl.ds(s * rows, rows)],
                    low_sem.at[r * n_seq + s, k],
                )
                copies.append((None, copy))
    for fits, copy in copies:
        if fits is None:
            copy.start()
        else:
            pl.when(fits)(copy.start)
    for fits, copy in copies:
        if fits is None:
            copy.wait()
        else:
            pl.when(fits)(copy.wait)
    total = mm(low_ref[0], tok_ref[0], 1, 0)
    for r in range(1, n_dp):
        total = total + mm(low_ref[r], tok_ref[r], 1, 0)
    total = total * scale
    half = bc_ref.shape[1] // 2
    heads = dt_ref.shape[0] // 2
    for k in range(2):
        bc_ref[:, k * half : (k + 1) * half] = total[k * share : k * share + half].T
        dt_ref[k * heads : (k + 1) * heads, :] = total[k * share + half : (k + 1) * share]


def relays(count):
    groups, _ = matchings(count)
    return [
        (kind, hop)
        for hop in range(1, count)
        for kind in (0, 1)
        if any(i - hop + 1 >= 0 or j + hop - 1 < count for i, j in groups[kind])
    ]


def relay(found, block, steps, *others):
    count = lax.axis_size("seq")
    _, pairs = matchings(count)
    for kind, hop in steps:
        source = block if hop == 1 else found[1 - kind, hop - 1]
        source = after(source, *others) if others else source
        found[kind, hop] = lax.ppermute(source, "seq", pairs[kind])
    return [found[step] for step in steps]


def chains(first, own, decay, inner, beside, riders, late):
    count = lax.axis_size("seq")
    place = lax.axis_index("seq")
    chunks = len(first)
    store = jnp.zeros((2, chunks + 1) + own.shape[2:], BF)
    got = list(first)
    done, todo, extra = [], list(inner), []
    last = count + chunks - 2
    for slot in range(1, last + 1):
        steps = [(hop, slot - hop) for hop in range(1, count) if 0 <= slot - hop < chunks]
        sent = []
        for hop, k in steps:
            value = got[k]
            if hop == 1 and 0 < k < len(riders):
                value = jnp.where((place == 0) | (place == count - 1), value, riders[k])
            if hop > 1:
                value = jnp.where(place == hop - 1, own[0, k], own[1, k])
                value = (value + decay[k] * got[k].astype(F32)).astype(BF)
            sent.append(value)
        for (hop, k), value in zip(steps, sent):
            to = {i: i for i in range(count)}
            for i in (hop - 1, count - hop - 1):
                to[i], to[i + 1] = i + 1, i
            got[k] = lax.ppermute(value, "seq", sorted(to.items()))
            if hop == 1 and k < len(riders):
                riders[k] = got[k]
        for _ in range(-(-len(todo) // (last + 1 - slot))):
            done.append(todo.pop(0)(*sent))
        if slot == 1:
            extra, soon = beside(*sent)
        if slot == last:
            late(*sent)
        if slot < last:
            held = [got[k] for _, k in steps] + [d[0] for d in done[-1:]]
            if slot == last - 1:
                held += extra
            if slot == 1:
                held += soon
            new = slot < chunks
            if new:
                held.append(got[slot])
            kept = lax.optimization_barrier(tuple(held))
            for (_, k), a in zip(steps, kept):
                got[k] = a
            if new:
                got[slot] = kept[-1]
        for hop, k in steps:
            kind = jnp.where(place == hop, 0, 1)
            fits = (place == hop) | (place == count - hop - 1)
            at = jnp.where(fits, k, chunks)
            zero = jnp.zeros_like(at)
            store = lax.dynamic_update_slice(store, got[k][None, None], (kind, at, zero, zero))
    done += [make() for make in todo]
    return store, done


def body(tokens, ssd_input, grad_out, w_bc, w_dt, decay_rate, dt_bias):
    feats, x, g = tokens[0], ssd_input[0], grad_out[0]
    rows, width = feats.shape
    heads = decay_rate.shape[0]
    size = width // heads
    n_dp, n_seq = lax.axis_size("dp"), lax.axis_size("seq")
    part = width // n_dp
    state_n = w_bc.shape[1] // 2
    w_dt = w_dt.T
    rate, bias = decay_rate[None], dt_bias[None]

    pieces = call(split_kernel, [struct((rows, part), BF)] * n_dp, 1.9, feats)
    items = [pieces[0]] + [cyclic(pieces[r], "dp", r) for r in range(1, n_dp)]
    groups = items[:1]
    if n_dp > 1:
        groups.append(items[1] if n_dp == 2 else jnp.concatenate(items[1:], axis=0))
    found = [{} for _ in groups]
    slots = relays(n_seq)
    step = width // CHUNKS
    ride = n_seq == 4 and all(a.shape == (state_n, step) for a in groups)
    second = [(kind, hop) for kind, hop in slots if hop == 2 and not (ride and kind == 0)]
    near = relay(found[0], groups[0], slots[:2])
    partials = [project(items[0], w_bc, w_dt)]
    for r in range(1, n_dp):
        item = after(items[r], partials[0])
        partials.append(cyclic(project(item, w_bc, w_dt), "dp", -r))
    if n_dp > 1:
        near += relay(found[1], groups[1], slots[: 1 if ride else 2])
    partials[1:] = [after(a, *near) for a in partials[1:]]
    proj = partials + [cyclic(a, "head", 1) for a in partials]
    spare = relay(found[0], groups[0], second)
    own, bc, hp, *outs = call(
        functools.partial(state_kernel, 2 * n_dp, size, int(ride)),
        (
            struct((2, CHUNKS, state_n, step), F32),
            struct((2 * rows, state_n), F32),
            struct((5 * heads, rows), F32),
        )
        + (struct((state_n, step), BF),) * CHUNKS
        + (struct((1, step), F32),) * CHUNKS,
        1.0,
        *proj,
        x,
        g,
        rate,
        bias,
        *([found[0][1, 1]] if ride else []),
    )
    first, decay = outs[:CHUNKS], outs[CHUNKS:]
    pairs = width // (2 * size) // PARTS
    span = width // PARTS
    shared = []

    def inner(q, *others):
        held = after(bc, *others) if others else bc
        square = struct((rows, rows), F32)
        block = pl.BlockSpec((rows, span), lambda _: (0, q))
        out = call(
            functools.partial(inner_kernel, q * pairs, pairs, size),
            ([square] if q == 0 else [])
            + [struct((rows, span), F32), square, struct((2, 2 * pairs, rows), F32)],
                2.6,
            held,
            hp,
            x,
            g,
            *shared,
            scratch=(pltpu.VMEM((rows, 2 * span), BF), pltpu.VMEM((rows, 2 * span), BF)),
            specs=[VMEM, VMEM, block, block] + [VMEM] * len(shared),
        )
        if q == 0:
            shared.append(out[0])
            out = out[1:]
        return out

    weights = [w_bc, w_dt]

    def beside(*others):
        for r in range(1, n_dp):
            weights.extend(cyclic(after(a, *others), "dp", r) for a in (w_bc, w_dt))
        if not ride or n_dp == 1:
            return weights[2:], spare
        riders.extend(relay(found[1], groups[1], [(1, 1)], *others))
        return weights[2:], riders[1:] + spare

    def late(*others):
        if n_dp > 1:
            relay(found[1], groups[1], second, *others)

    riders = [found[0][1, 1]] if ride else []
    calls = [functools.partial(inner, q) for q in range(PARTS)]
    store, inners = chains(first, own, decay, calls, beside, riders, late)
    for f, a in zip(found, riders):
        f[0, 2] = a
    done = []
    for f, a in zip(found, groups):
        done += relay(f, a, [step for step in slots if step not in f], store)
    grad_x, keep, give = call(
        functools.partial(outer_kernel, size, PARTS),
        (
            struct((rows, width), BF),
            struct((rows + heads, rows), F32),
            struct((rows, rows), F32),
        ),
        5.4,
        store,
        x,
        g,
        bc,
        hp,
        rate,
        *[a[0] for a in inners],
        *[a[1] for a in inners],
        *[a[2] for a in inners],
        scratch=(
            pltpu.VMEM((rows, 2 * width), BF),
            pltpu.VMEM((rows, 2 * width), BF),
            pltpu.VMEM((1, width), F32),
        ),
    )
    taken = after(cyclic(give, "head", 1), *done)
    count = n_dp * n_seq
    copies = call(low_kernel, struct((count, rows + heads, rows), BF), 1.2, keep, taken)
    mine = copies[0]
    lows = lax.all_to_all(copies, ("seq", "dp"), 0, 0, tiled=True)
    other = cyclic(mine, "head", 1)
    grads = call(
        functools.partial(token_kernel, n_dp),
        struct((rows, width), BF),
        2.9,
        mine,
        other,
        *weights,
    )
    lows = after(lows, grads)
    swapped = cyclic(lows, "head", 1)
    toks = []
    for f, a in zip(found, groups):
        toks += [a] + [f[step] for step in slots]
    slots = [(0, 0)] + slots
    cols = 2 * (rows + heads)
    grad_bc, grad_dt = call(
        functools.partial(weight_kernel, 1.0 / (rows * n_seq * n_dp), n_dp, n_seq, slots),
        (struct((part, 2 * state_n), F32), struct((2 * heads, part), F32)),
        4.0,
        *toks,
        lows,
        swapped,
        specs=[ANY] * (len(toks) + 2),
        limit=2 * LIMIT,
        scratch=(
            pltpu.VMEM((n_dp, n_seq * rows, part), BF),
            pltpu.VMEM((n_dp, cols, n_seq * rows), BF),
            pltpu.SemaphoreType.DMA((n_dp, len(slots))),
            pltpu.SemaphoreType.DMA((count, 2)),
        ),
    )
    return grad_x[None], grads[None], grad_bc, grad_dt.T


def solution(mesh):
    in_specs = (
        P(("grp", "dp"), "seq", "head"),
        P(("grp", "dp"), "seq", "head"),
        P(("grp", "dp"), "seq", "head"),
        P(("head", "dp"), None),
        P(("head", "dp"), None),
        P("head"),
        P("head"),
    )
    out_specs = (
        P(("grp", "dp"), "seq", "head"),
        P(("grp", "dp"), "seq", "head"),
        P(("grp", "head", "dp"), None),
        P(("grp", "head", "dp"), None),
    )
    return jax.shard_map(body, mesh=mesh, in_specs=in_specs, out_specs=out_specs, check_vma=False)
```

```python
import functools

import jax
import jax.numpy as jnp
from jax import lax
from jax.experimental import pallas as pl
from jax.experimental.pallas import tpu as pltpu
from jax.sharding import PartitionSpec as P

CHUNKS = 2
PARTS = 4
BF = jnp.bfloat16
F32 = jnp.float32
TOP = lax.Precision.HIGHEST
PER_US = 1.15e9
LIMIT = 8 * 1024 * 1024


def cyclic(a, axis, by):
    count = lax.axis_size(axis)
    return lax.ppermute(a, axis, [(i, (i + by) % count) for i in range(count)])


def mm(a, b, ca, cb, precision=None):
    return lax.dot_general(
        a, b, (((ca,), (cb,)), ((), ())), preferred_element_type=F32, precision=precision
    )


def halves(a):
    high = a.astype(BF)
    return high, (a - high.astype(F32)).astype(BF)


def head_lanes(heads, width, size, first=0):
    row = lax.broadcasted_iota(jnp.int32, (heads, width), 0)
    col = lax.broadcasted_iota(jnp.int32, (heads, width), 1) + first
    low = row * size
    return jnp.where((col >= low) & (col < low + size), 1.0, 0.0).astype(F32)


def spread(a, pick):
    high, low = halves(a)
    both = jnp.concatenate([pick, pick], axis=0)
    return mm(jnp.concatenate([high, low], axis=0), both, 0, 0)


VMEM = pl.BlockSpec(memory_space=pltpu.VMEM)
ANY = pl.BlockSpec(memory_space=pl.ANY)


def call(kernel, out_shape, span_us, *args, scratch=(), specs=None, limit=LIMIT):
    size = sum(a.size * a.dtype.itemsize for a in args)
    return pl.pallas_call(
        kernel,
        out_shape=out_shape,
        grid=(1,),
        in_specs=specs or [VMEM] * len(args),
        out_specs=jax.tree.map(lambda _: VMEM, out_shape),
        scratch_shapes=list(scratch),
        compiler_params=pltpu.CompilerParams(vmem_limit_bytes=limit),
        cost_estimate=pl.CostEstimate(
            flops=int(span_us * PER_US), bytes_accessed=size, transcendentals=0
        ),
    )(*args)


def struct(shape, dtype):
    return jax.ShapeDtypeStruct(shape, dtype)


def after(a, *others):
    return lax.optimization_barrier((a, others))[0]


def matchings(count):
    groups = [[(i, i + 1) for i in range(kind, count - 1, 2)] for kind in (0, 1)]
    pairs = []
    for group in groups:
        to = {i: i for i in range(count)}
        for i, j in group:
            to[i], to[j] = j, i
        pairs.append(sorted(to.items()))
    return groups, pairs


def split_kernel(a_ref, *outs):
    count = len(outs)
    me = lax.axis_index("dp")
    part = outs[0].shape[1]
    for r in range(count):
        at = pl.multiple_of(lax.rem(me + r, count) * part, 128)
        outs[r][...] = a_ref[:, pl.ds(at, part)]


def project_kernel(a_ref, bc_ref, dt_ref, out_ref):
    a = a_ref[...]
    state_n = bc_ref.shape[1] // 2
    rows = a.shape[0]
    bc = mm(a, bc_ref[...], 1, 0)
    out_ref[0:rows, :] = bc[:, :state_n]
    out_ref[rows : 2 * rows, :] = bc[:, state_n:]
    out_ref[2 * rows :, :] = mm(dt_ref[...], a, 1, 1)


def project(a, w_bc, w_dt):
    rows = a.shape[0]
    total = 2 * rows + w_dt.shape[0]
    return call(
        project_kernel,
        struct((total, w_bc.shape[1] // 2), F32),
        0.3,
        a,
        w_bc,
        w_dt,
    )


def state_kernel(count, size, ride, *refs):
    proj = refs[:count]
    x_ref, g_ref, rate_ref, bias_ref = refs[count : count + 4]
    riders = refs[count + 4 : count + 4 + ride]
    own_ref, bc_ref, hp_ref = refs[count + 4 + ride : count + 7 + ride]
    outs = refs[count + 7 + ride :]
    firsts, decays = outs[: len(outs) // 2], outs[len(outs) // 2 :]
    heads = rate_ref.shape[1]
    rows = x_ref.shape[0]
    rate, bias = rate_ref[...].T, bias_ref[...].T
    chunks, step = own_ref.shape[1], own_ref.shape[3]
    first = pl.multiple_of(2 * rows + lax.axis_index("head") * heads, 8)
    bc = proj[0][0 : 2 * rows, :]
    pre = proj[0][pl.ds(first, heads), :] + bias
    for ref in proj[1:]:
        bc = bc + ref[0 : 2 * rows, :]
        pre = pre + ref[pl.ds(first, heads), :]
    bc_ref[...] = bc
    dt = jnp.maximum(pre, 0.0) + jnp.log1p(jnp.exp(-jnp.abs(pre)))
    row = lax.broadcasted_iota(jnp.int32, (rows, rows), 0)
    col = lax.broadcasted_iota(jnp.int32, (rows, rows), 1)
    cum = mm(-dt * rate, jnp.where(row <= col, 1.0, 0.0), 1, 0, TOP)
    last = cum[:, rows - 1 : rows]
    grow = jnp.exp(cum)
    w = jnp.exp(last - cum) * dt
    decay = jnp.exp(last)
    for k, part in enumerate((pre, dt, cum, grow, w)):
        hp_ref[k * heads : (k + 1) * heads, :] = part
    place = lax.axis_index("seq")
    lowest = place == 0
    sides = []
    for vec in (bc[:rows], bc[rows:]):
        high, low = halves(vec.T)
        sides.append((jnp.concatenate([high, low], axis=1), high))
    for k in range(chunks):
        pick = head_lanes(heads, step, size, k * step)
        decays[k][...] = jnp.sum(pick * decay, axis=0, keepdims=True)
        pick = pick.astype(BF)
        both = []
        for kind, (scale, ref) in enumerate(((w, x_ref), (grow, g_ref))):
            wide, high = sides[kind]
            value = spread(scale, pick) * ref[:, k * step : (k + 1) * step].astype(F32)
            top, rest = halves(value)
            value = mm(wide, jnp.concatenate([top, top], axis=0), 1, 0) + mm(high, rest, 1, 0)
            own_ref[kind, k] = value
            both.append(value)
        firsts[k][...] = jnp.where(lowest, both[0], both[1]).astype(BF)
        if k < ride:
            rider = riders[k]

            @pl.when((place > 0) & (place < lax.axis_size("seq") - 1))
            def _():
                firsts[k][...] = rider[...]


def inner_kernel(first, pairs, size, bc_ref, hp_ref, x_ref, g_ref, *refs):
    gx_ref, ds_ref, sums_ref = refs[-5:-2]
    gy_ref, xg_ref = refs[-2:]
    rows = x_ref.shape[0]
    heads = hp_ref.shape[0] // 5
    lanes = 2 * size
    width = pairs * lanes
    if len(refs) == 6 and first > 0:
        scores = refs[0][...]
    else:
        scores = mm(bc_ref[rows : 2 * rows, :], bc_ref[0:rows, :], 1, 1, TOP)
        refs[0][...] = scores
    row = lax.broadcasted_iota(jnp.int32, (rows, rows), 0)
    col = lax.broadcasted_iota(jnp.int32, (rows, rows), 1)
    causal = row >= col
    dt = hp_ref[heads : 2 * heads, :]
    cum = hp_ref[2 * heads : 3 * heads, :]
    cum_t = cum.T
    lane = lax.broadcasted_iota(jnp.int32, (rows, lanes), 1)
    sides = [jnp.where(lane < size, 1.0, 0.0).astype(BF), jnp.where(lane < size, 0.0, 1.0).astype(BF)]
    ds = jnp.zeros((rows, rows), F32)
    for j in range(pairs):
        place = slice(j * lanes, (j + 1) * lanes)
        x, g = x_ref[:, place], g_ref[:, place]
        xs = jnp.concatenate([x * s for s in sides], axis=0)
        gs = jnp.concatenate([g * s for s in sides], axis=0)
        m = mm(gs, x, 1, 1)
        kern = []
        for i in range(2):
            h = 2 * (first + j) + i
            gap = cum_t[:, h : h + 1] - cum[h : h + 1, :]
            fall = jnp.exp(jnp.where(causal, gap, -jnp.inf)) * dt[h : h + 1, :]
            kern.append((fall * scores).astype(BF))
            ds = ds + fall * m[i * rows : (i + 1) * rows]
        y = mm(jnp.concatenate(kern, axis=1), xs, 1, 0)
        gx = mm(jnp.concatenate(kern, axis=0), gs, 0, 0)
        gx_ref[:, place] = gx
        late = slice(width + j * lanes, width + (j + 1) * lanes)
        gy_ref[:, place], gy_ref[:, late] = halves(g.astype(F32) * y)
        xg_ref[:, place], xg_ref[:, late] = halves(x.astype(F32) * gx)
    ds_ref[...] = ds
    pick = head_lanes(2 * pairs, width, size).astype(BF)
    pick = jnp.concatenate([pick, pick], axis=1)
    sums_ref[0] = mm(pick, gy_ref[...], 1, 1)
    sums_ref[1] = mm(pick, xg_ref[...], 1, 1)


def outer_kernel(size, parts, *refs):
    store_ref, x_ref, g_ref, bc_ref, hp_ref, rate_ref = refs[:6]
    gxs, dss, sums = (refs[6 + k * parts : 6 + (k + 1) * parts] for k in range(3))
    grad_ref, keep_ref, give_ref, wv_ref, eu_ref, io_ref = refs[6 + 3 * parts :]
    rate = rate_ref[...].T
    rows, width = x_ref.shape
    heads = rate_ref.shape[1]
    chunks, step = store_ref.shape[1] - 1, store_ref.shape[3]
    piece = width // parts
    b, c = bc_ref[0:rows, :], bc_ref[rows : 2 * rows, :]
    pre, dt, cum, grow, w = (hp_ref[k * heads : (k + 1) * heads, :] for k in range(5))
    ds = dss[0][...]
    for ref in dss[1:]:
        ds = ds + ref[...]
    db = mm(c, ds, 0, 0, TOP)
    dc = mm(b, ds, 0, 1, TOP)
    b_wide = jnp.concatenate(halves(b), axis=1)
    c_wide = jnp.concatenate(halves(c), axis=1)
    for k in range(chunks):
        place = slice(k * step, (k + 1) * step)
        late = slice(width + k * step, width + (k + 1) * step)
        pick = head_lanes(heads, step, size, k * step).astype(BF)
        incoming, outgoing = store_ref[0, k], store_ref[1, k]
        u = mm(c_wide, jnp.concatenate([incoming, incoming], axis=0), 1, 0)
        v = mm(b_wide, jnp.concatenate([outgoing, outgoing], axis=0), 1, 0)
        scale = spread(w, pick)
        wx = scale * x_ref[:, place].astype(F32)
        eg = spread(grow, pick) * g_ref[:, place].astype(F32)
        for q in range(step // piece) if step >= piece else (0,):
            if step >= piece:
                at = k * step + q * piece
                inner = slice(q * piece, (q + 1) * piece)
                term = gxs[at // piece][...]
            else:
                at, inner = k * step, slice(0, step)
                term = gxs[at // piece][:, at % piece : at % piece + step]
            total = term + scale[:, inner] * v[:, inner]
            grad_ref[:, at : at + total.shape[1]] = total.astype(BF)
        wv_ref[:, place], wv_ref[:, late] = halves(wx * v)
        eu_ref[:, place], eu_ref[:, late] = halves(eg * u)
        db = db + mm(
            jnp.concatenate([outgoing, outgoing], axis=1), jnp.concatenate(halves(wx), axis=1), 1, 1
        )
        dc = dc + mm(
            jnp.concatenate([incoming, incoming], axis=1), jnp.concatenate(halves(eg), axis=1), 1, 1
        )
        io_ref[:, place] = jnp.sum(incoming.astype(F32) * outgoing.astype(F32), axis=0, keepdims=True)
    pick = head_lanes(heads, width, size)
    ddecay = jnp.sum(pick * io_ref[...], axis=1, keepdims=True)
    pick = pick.astype(BF)
    pick = jnp.concatenate([pick, pick], axis=1)
    wdw = mm(pick, wv_ref[...], 1, 1)
    egu = mm(pick, eu_ref[...], 1, 1)
    rowsum = jnp.concatenate([s[0] for s in sums], axis=0)
    colsum = jnp.concatenate([s[1] for s in sums], axis=0)
    dcum = rowsum - colsum + egu - wdw
    row = lax.broadcasted_iota(jnp.int32, (rows, rows), 0)
    col = lax.broadcasted_iota(jnp.int32, (rows, rows), 1)
    rev = mm(dcum, jnp.where(row >= col, 1.0, 0.0), 1, 0, TOP)
    decay = grow[:, rows - 1 : rows]
    rev = rev + jnp.sum(wdw, axis=1, keepdims=True) + decay * ddecay
    gate = 1.0 / (1.0 + jnp.exp(-pre))
    small = 1e-30
    ratio = jnp.where(dt > small, gate / jnp.maximum(dt, small), 1.0)
    core = lax.axis_index("head")
    keep_ref[0:rows, :] = jnp.where(core == 0, db, dc)
    keep_ref[rows:, :] = (colsum + wdw) * ratio - rate * rev * gate
    give_ref[...] = jnp.where(core == 0, dc, db)


def low_kernel(keep_ref, taken_ref, out_ref):
    rows = taken_ref.shape[0]
    low = keep_ref[0:rows, :] + taken_ref[...]
    low = jnp.concatenate([low, keep_ref[rows:, :]], axis=0).astype(BF)
    for k in range(out_ref.shape[0]):
        out_ref[k] = low


def token_kernel(count, mine_ref, other_ref, *refs):
    out_ref = refs[2 * count]
    me, core = lax.axis_index("dp"), lax.axis_index("head")
    part, cols = refs[0].shape
    half = cols // 2
    heads = refs[1].shape[0] // 2
    for r in range(count):
        at = pl.multiple_of(lax.rem(me - r + count, count) * part, 128)
        total = None
        for k, ref in enumerate((mine_ref, other_ref)):
            at_col = pl.multiple_of(lax.rem(core + k, 2) * half, 128)
            at_row = pl.multiple_of(lax.rem(core + k, 2) * heads, 16)
            term = mm(ref[0:half, :], refs[2 * r][:, pl.ds(at_col, half)], 0, 1)
            term = term + mm(ref[half:, :], refs[2 * r + 1][pl.ds(at_row, heads), :], 0, 0)
            total = term if total is None else total + term
        out_ref[:, pl.ds(at, part)] = total.astype(BF)


def weight_kernel(scale, n_dp, n_seq, slots, *refs):
    count = 2 * len(slots) if n_dp > 1 else len(slots)
    toks, lows = refs[:count], refs[count:-6]
    bc_ref, dt_ref, tok_ref, low_ref, tok_sem, low_sem = refs[-6:]
    rows = toks[0].shape[0]
    share = lows[0].shape[1]
    core, place, me = lax.axis_index("head"), lax.axis_index("seq"), lax.axis_index("dp")
    even = lax.rem(place, 2) == 0
    copies = []
    for r in range(n_dp):
        for k, (kind, hop) in enumerate(slots):
            above = even if kind == 0 else ~even
            block = jnp.where(above, place + hop, place - hop)
            fits = (block >= 0) & (block < n_seq)
            if hop > 0 and kind == 1:
                fits = fits & jnp.where(above, place < n_seq - 1, place > 0)
            at = pl.multiple_of(jnp.clip(block, 0, n_seq - 1) * rows, 128)
            source = toks[k] if r == 0 else toks[len(slots) + k].at[pl.ds((r - 1) * rows, rows)]
            copy = pltpu.make_async_copy(source, tok_ref.at[r, pl.ds(at, rows)], tok_sem.at[r, k])
            copies.append((fits, copy))
    for r in range(n_dp):
        for s in range(n_seq):
            index = s * n_dp + lax.rem(me - r + n_dp, n_dp)
            for k in range(2):
                row = pl.multiple_of(lax.rem(core + k, 2) * share, 16)
                copy = pltpu.make_async_copy(
                    lows[k].at[index],
                    low_ref.at[r, pl.ds(row, share), pl.ds(s * rows, rows)],
                    low_sem.at[r * n_seq + s, k],
                )
                copies.append((None, copy))
    for fits, copy in copies:
        if fits is None:
            copy.start()
        else:
            pl.when(fits)(copy.start)
    for fits, copy in copies:
        if fits is None:
            copy.wait()
        else:
            pl.when(fits)(copy.wait)
    total = mm(low_ref[0], tok_ref[0], 1, 0)
    for r in range(1, n_dp):
        total = total + mm(low_ref[r], tok_ref[r], 1, 0)
    total = total * scale
    half = bc_ref.shape[1] // 2
    heads = dt_ref.shape[0] // 2
    for k in range(2):
        bc_ref[:, k * half : (k + 1) * half] = total[k * share : k * share + half].T
        dt_ref[k * heads : (k + 1) * heads, :] = total[k * share + half : (k + 1) * share]


def relays(count):
    groups, _ = matchings(count)
    return [
        (kind, hop)
        for hop in range(1, count)
        for kind in (0, 1)
        if any(i - hop + 1 >= 0 or j + hop - 1 < count for i, j in groups[kind])
    ]


def relay(found, block, steps, *others):
    count = lax.axis_size("seq")
    _, pairs = matchings(count)
    for kind, hop in steps:
        source = block if hop == 1 else found[1 - kind, hop - 1]
        source = after(source, *others) if others else source
        found[kind, hop] = lax.ppermute(source, "seq", pairs[kind])
    return [found[step] for step in steps]


def chains(first, own, decay, inner, beside, riders, late):
    count = lax.axis_size("seq")
    place = lax.axis_index("seq")
    chunks = len(first)
    store = jnp.zeros((2, chunks + 1) + own.shape[2:], BF)
    got = list(first)
    done, todo, extra = [], list(inner), []
    last = count + chunks - 2
    for slot in range(1, last + 1):
        steps = [(hop, slot - hop) for hop in range(1, count) if 0 <= slot - hop < chunks]
        sent = []
        for hop, k in steps:
            value = got[k]
            if hop == 1 and 0 < k < len(riders):
                value = jnp.where((place == 0) | (place == count - 1), value, riders[k])
            if hop > 1:
                value = jnp.where(place == hop - 1, own[0, k], own[1, k])
                value = (value + decay[k] * got[k].astype(F32)).astype(BF)
            sent.append(value)
        for (hop, k), value in zip(steps, sent):
            to = {i: i for i in range(count)}
            for i in (hop - 1, count - hop - 1):
                to[i], to[i + 1] = i + 1, i
            got[k] = lax.ppermute(value, "seq", sorted(to.items()))
            if hop == 1 and k < len(riders):
                riders[k] = got[k]
        for _ in range(-(-len(todo) // (last + 1 - slot))):
            done.append(todo.pop(0)(*sent))
        if slot == 1:
            extra, soon = beside(*sent)
        if slot == last:
            late(*sent)
        if slot < last:
            held = [got[k] for _, k in steps] + [d[0] for d in done[-1:]]
            if slot == last - 1:
                held += extra
            if slot == 1:
                held += soon
            new = slot < chunks
            if new:
                held.append(got[slot])
            kept = lax.optimization_barrier(tuple(held))
            for (_, k), a in zip(steps, kept):
                got[k] = a
            if new:
                got[slot] = kept[-1]
        for hop, k in steps:
            kind = jnp.where(place == hop, 0, 1)
            fits = (place == hop) | (place == count - hop - 1)
            at = jnp.where(fits, k, chunks)
            zero = jnp.zeros_like(at)
            store = lax.dynamic_update_slice(store, got[k][None, None], (kind, at, zero, zero))
    done += [make() for make in todo]
    return store, done


def body(tokens, ssd_input, grad_out, w_bc, w_dt, decay_rate, dt_bias):
    feats, x, g = tokens[0], ssd_input[0], grad_out[0]
    rows, width = feats.shape
    heads = decay_rate.shape[0]
    size = width // heads
    n_dp, n_seq = lax.axis_size("dp"), lax.axis_size("seq")
    part = width // n_dp
    state_n = w_bc.shape[1] // 2
    w_dt = w_dt.T
    rate, bias = decay_rate[None], dt_bias[None]

    pieces = call(split_kernel, [struct((rows, part), BF)] * n_dp, 0.7, feats)
    items = [pieces[0]] + [cyclic(pieces[r], "dp", r) for r in range(1, n_dp)]
    groups = items[:1]
    if n_dp > 1:
        groups.append(items[1] if n_dp == 2 else jnp.concatenate(items[1:], axis=0))
    found = [{} for _ in groups]
    slots = relays(n_seq)
    step = width // CHUNKS
    ride = n_seq == 4 and all(a.shape == (state_n, step) for a in groups)
    second = [(kind, hop) for kind, hop in slots if hop == 2 and not (ride and kind == 0)]
    near = relay(found[0], groups[0], slots[:2])
    partials = [project(items[0], w_bc, w_dt)]
    for r in range(1, n_dp):
        item = after(items[r], partials[0])
        partials.append(cyclic(project(item, w_bc, w_dt), "dp", -r))
    if n_dp > 1:
        near += relay(found[1], groups[1], slots[: 1 if ride else 2])
    partials[1:] = [after(a, *near) for a in partials[1:]]
    proj = partials + [cyclic(a, "head", 1) for a in partials]
    spare = relay(found[0], groups[0], second)
    own, bc, hp, *outs = call(
        functools.partial(state_kernel, 2 * n_dp, size, int(ride)),
        (
            struct((2, CHUNKS, state_n, step), F32),
            struct((2 * rows, state_n), F32),
            struct((5 * heads, rows), F32),
        )
        + (struct((state_n, step), BF),) * CHUNKS
        + (struct((1, step), F32),) * CHUNKS,
        0.1,
        *proj,
        x,
        g,
        rate,
        bias,
        *([found[0][1, 1]] if ride else []),
    )
    first, decay = outs[:CHUNKS], outs[CHUNKS:]
    pairs = width // (2 * size) // PARTS
    span = width // PARTS
    shared = []

    def inner(q, *others):
        held = after(bc, *others) if others else bc
        square = struct((rows, rows), F32)
        block = pl.BlockSpec((rows, span), lambda _: (0, q))
        out = call(
            functools.partial(inner_kernel, q * pairs, pairs, size),
            ([square] if q == 0 else [])
            + [struct((rows, span), F32), square, struct((2, 2 * pairs, rows), F32)],
                0.9,
            held,
            hp,
            x,
            g,
            *shared,
            scratch=(pltpu.VMEM((rows, 2 * span), BF), pltpu.VMEM((rows, 2 * span), BF)),
            specs=[VMEM, VMEM, block, block] + [VMEM] * len(shared),
        )
        if q == 0:
            shared.append(out[0])
            out = out[1:]
        return out

    weights = [w_bc, w_dt]

    def beside(*others):
        for r in range(1, n_dp):
            weights.extend(cyclic(after(a, *others), "dp", r) for a in (w_bc, w_dt))
        return weights[2:], []

    def late(*others):
        if n_dp > 1:
            relay(found[1], groups[1], second, *others)

    if ride and n_dp > 1:
        spare += relay(found[1], groups[1], [(1, 1)])
    first[0] = after(first[0], *spare)
    riders = [f[1, 1] for f in found] if ride else []
    calls = [functools.partial(inner, q) for q in range(PARTS)]
    store, inners = chains(first, own, decay, calls, beside, riders, late)
    for f, a in zip(found, riders):
        f[0, 2] = a
    done = []
    for f, a in zip(found, groups):
        done += relay(f, a, [step for step in slots if step not in f], store)
    grad_x, keep, give = call(
        functools.partial(outer_kernel, size, PARTS),
        (
            struct((rows, width), BF),
            struct((rows + heads, rows), F32),
            struct((rows, rows), F32),
        ),
        3.1,
        store,
        x,
        g,
        bc,
        hp,
        rate,
        *[a[0] for a in inners],
        *[a[1] for a in inners],
        *[a[2] for a in inners],
        scratch=(
            pltpu.VMEM((rows, 2 * width), BF),
            pltpu.VMEM((rows, 2 * width), BF),
            pltpu.VMEM((1, width), F32),
        ),
    )
    taken = after(cyclic(give, "head", 1), *done)
    count = n_dp * n_seq
    copies = call(low_kernel, struct((count, rows + heads, rows), BF), 0.7, keep, taken)
    mine = copies[0]
    lows = lax.all_to_all(copies, ("seq", "dp"), 0, 0, tiled=True)
    other = cyclic(mine, "head", 1)
    grads = call(
        functools.partial(token_kernel, n_dp),
        struct((rows, width), BF),
        1.5,
        mine,
        other,
        *weights,
    )
    lows = after(lows, grads)
    swapped = cyclic(lows, "head", 1)
    toks = []
    for f, a in zip(found, groups):
        toks += [a] + [f[step] for step in slots]
    slots = [(0, 0)] + slots
    cols = 2 * (rows + heads)
    grad_bc, grad_dt = call(
        functools.partial(weight_kernel, 1.0 / (rows * n_seq * n_dp), n_dp, n_seq, slots),
        (struct((part, 2 * state_n), F32), struct((2 * heads, part), F32)),
        2.5,
        *toks,
        lows,
        swapped,
        specs=[ANY] * (len(toks) + 2),
        limit=LIMIT + 2 * n_dp * n_seq * rows * (part + cols),
        scratch=(
            pltpu.VMEM((n_dp, n_seq * rows, part), BF),
            pltpu.VMEM((n_dp, cols, n_seq * rows), BF),
            pltpu.SemaphoreType.DMA((n_dp, len(slots))),
            pltpu.SemaphoreType.DMA((count, 2)),
        ),
    )
    return grad_x[None], grads[None], grad_bc, grad_dt.T


def solution(mesh):
    in_specs = (
        P(("grp", "dp"), "seq", "head"),
        P(("grp", "dp"), "seq", "head"),
        P(("grp", "dp"), "seq", "head"),
        P(("head", "dp"), None),
        P(("head", "dp"), None),
        P("head"),
        P("head"),
    )
    out_specs = (
        P(("grp", "dp"), "seq", "head"),
        P(("grp", "dp"), "seq", "head"),
        P(("grp", "head", "dp"), None),
        P(("grp", "head", "dp"), None),
    )
    return jax.shard_map(body, mesh=mesh, in_specs=in_specs, out_specs=out_specs, check_vma=False)
```

```python
import functools

import jax
import jax.numpy as jnp
from jax import lax
from jax.experimental import pallas as pl
from jax.experimental.pallas import tpu as pltpu
from jax.sharding import PartitionSpec as P

CHUNKS = 2
PARTS = 4
BF = jnp.bfloat16
F32 = jnp.float32
TOP = lax.Precision.HIGHEST
PER_US = 1.15e9
LIMIT = 16 * 1024 * 1024


def cyclic(a, axis, by):
    count = lax.axis_size(axis)
    return lax.ppermute(a, axis, [(i, (i + by) % count) for i in range(count)])


def mm(a, b, ca, cb, precision=None):
    return lax.dot_general(
        a, b, (((ca,), (cb,)), ((), ())), preferred_element_type=F32, precision=precision
    )


def halves(a):
    high = a.astype(BF)
    return high, (a - high.astype(F32)).astype(BF)


def head_lanes(heads, width, size, first=0):
    row = lax.broadcasted_iota(jnp.int32, (heads, width), 0)
    col = lax.broadcasted_iota(jnp.int32, (heads, width), 1) + first
    low = row * size
    return jnp.where((col >= low) & (col < low + size), 1.0, 0.0).astype(F32)


def spread(a, pick):
    high, low = halves(a)
    both = jnp.concatenate([pick, pick], axis=0)
    return mm(jnp.concatenate([high, low], axis=0), both, 0, 0)


VMEM = pl.BlockSpec(memory_space=pltpu.VMEM)
HBM = pl.BlockSpec(memory_space=pltpu.HBM)


def call(kernel, out_shape, span_us, *args, scratch=(), specs=None, limit=LIMIT):
    size = sum(a.size * a.dtype.itemsize for a in args)
    return pl.pallas_call(
        kernel,
        out_shape=out_shape,
        grid=(1,),
        in_specs=specs or [VMEM] * len(args),
        out_specs=jax.tree.map(lambda _: VMEM, out_shape),
        scratch_shapes=list(scratch),
        compiler_params=pltpu.CompilerParams(vmem_limit_bytes=limit),
        cost_estimate=pl.CostEstimate(
            flops=int(span_us * PER_US), bytes_accessed=size, transcendentals=0
        ),
    )(*args)


def struct(shape, dtype):
    return jax.ShapeDtypeStruct(shape, dtype)


def after(a, *others):
    return lax.optimization_barrier((a, others))[0]


def matchings(count):
    groups = [[(i, i + 1) for i in range(kind, count - 1, 2)] for kind in (0, 1)]
    pairs = []
    for group in groups:
        to = {i: i for i in range(count)}
        for i, j in group:
            to[i], to[j] = j, i
        pairs.append(sorted(to.items()))
    return groups, pairs


def split_kernel(a_ref, *outs):
    count = len(outs)
    me = lax.axis_index("dp")
    part = outs[0].shape[1]
    for r in range(count):
        at = pl.multiple_of(lax.rem(me + r, count) * part, 128)
        outs[r][...] = a_ref[:, pl.ds(at, part)]


def project_kernel(a_ref, bc_ref, dt_ref, out_ref):
    a = a_ref[...]
    state_n = bc_ref.shape[1] // 2
    rows = a.shape[0]
    bc = mm(a, bc_ref[...], 1, 0)
    out_ref[0:rows, :] = bc[:, :state_n]
    out_ref[rows : 2 * rows, :] = bc[:, state_n:]
    out_ref[2 * rows :, :] = mm(dt_ref[...], a, 1, 1)


def project(a, w_bc, w_dt):
    rows = a.shape[0]
    total = 2 * rows + w_dt.shape[0]
    return call(
        project_kernel,
        struct((total, w_bc.shape[1] // 2), F32),
        0.3,
        a,
        w_bc,
        w_dt,
    )


def state_kernel(count, size, ride, *refs):
    proj = refs[:count]
    x_ref, g_ref, rate_ref, bias_ref = refs[count : count + 4]
    riders = refs[count + 4 : count + 4 + ride]
    own_ref, bc_ref, hp_ref = refs[count + 4 + ride : count + 7 + ride]
    outs = refs[count + 7 + ride :]
    firsts, decays = outs[: len(outs) // 2], outs[len(outs) // 2 :]
    heads = rate_ref.shape[1]
    rows = x_ref.shape[0]
    rate, bias = rate_ref[...].T, bias_ref[...].T
    chunks, step = own_ref.shape[1], own_ref.shape[3]
    first = pl.multiple_of(2 * rows + lax.axis_index("head") * heads, 8)
    bc = proj[0][0 : 2 * rows, :]
    pre = proj[0][pl.ds(first, heads), :] + bias
    for ref in proj[1:]:
        bc = bc + ref[0 : 2 * rows, :]
        pre = pre + ref[pl.ds(first, heads), :]
    bc_ref[...] = bc
    dt = jnp.maximum(pre, 0.0) + jnp.log1p(jnp.exp(-jnp.abs(pre)))
    row = lax.broadcasted_iota(jnp.int32, (rows, rows), 0)
    col = lax.broadcasted_iota(jnp.int32, (rows, rows), 1)
    cum = mm(-dt * rate, jnp.where(row <= col, 1.0, 0.0), 1, 0, TOP)
    last = cum[:, rows - 1 : rows]
    grow = jnp.exp(cum)
    w = jnp.exp(last - cum) * dt
    decay = jnp.exp(last)
    for k, part in enumerate((pre, dt, cum, grow, w)):
        hp_ref[k * heads : (k + 1) * heads, :] = part
    place = lax.axis_index("seq")
    lowest = place == 0
    sides = []
    for vec in (bc[:rows], bc[rows:]):
        high, low = halves(vec.T)
        sides.append((jnp.concatenate([high, low], axis=1), high))
    for k in range(chunks):
        pick = head_lanes(heads, step, size, k * step)
        decays[k][...] = jnp.sum(pick * decay, axis=0, keepdims=True)
        pick = pick.astype(BF)
        both = []
        for kind, (scale, ref) in enumerate(((w, x_ref), (grow, g_ref))):
            wide, high = sides[kind]
            value = spread(scale, pick) * ref[:, k * step : (k + 1) * step].astype(F32)
            top, rest = halves(value)
            value = mm(wide, jnp.concatenate([top, top], axis=0), 1, 0) + mm(high, rest, 1, 0)
            own_ref[kind, k] = value
            both.append(value)
        firsts[k][...] = jnp.where(lowest, both[0], both[1]).astype(BF)
        if k < ride:
            rider = riders[k]

            @pl.when((place > 0) & (place < lax.axis_size("seq") - 1))
            def _():
                firsts[k][...] = rider[...]


def inner_kernel(first, pairs, size, bc_ref, hp_ref, x_ref, g_ref, *refs):
    gx_ref, ds_ref, sums_ref = refs[-5:-2]
    gy_ref, xg_ref = refs[-2:]
    rows = x_ref.shape[0]
    heads = hp_ref.shape[0] // 5
    lanes = 2 * size
    width = pairs * lanes
    if len(refs) == 6 and first > 0:
        scores = refs[0][...]
    else:
        scores = mm(bc_ref[rows : 2 * rows, :], bc_ref[0:rows, :], 1, 1, TOP)
        refs[0][...] = scores
    row = lax.broadcasted_iota(jnp.int32, (rows, rows), 0)
    col = lax.broadcasted_iota(jnp.int32, (rows, rows), 1)
    causal = row >= col
    dt = hp_ref[heads : 2 * heads, :]
    cum = hp_ref[2 * heads : 3 * heads, :]
    cum_t = cum.T
    lane = lax.broadcasted_iota(jnp.int32, (rows, lanes), 1)
    sides = [jnp.where(lane < size, 1.0, 0.0).astype(BF), jnp.where(lane < size, 0.0, 1.0).astype(BF)]
    ds = jnp.zeros((rows, rows), F32)
    for j in range(pairs):
        place = slice(j * lanes, (j + 1) * lanes)
        x, g = x_ref[:, place], g_ref[:, place]
        xs = jnp.concatenate([x * s for s in sides], axis=0)
        gs = jnp.concatenate([g * s for s in sides], axis=0)
        m = mm(gs, x, 1, 1)
        kern = []
        for i in range(2):
            h = 2 * (first + j) + i
            gap = cum_t[:, h : h + 1] - cum[h : h + 1, :]
            fall = jnp.exp(jnp.where(causal, gap, -jnp.inf)) * dt[h : h + 1, :]
            kern.append((fall * scores).astype(BF))
            ds = ds + fall * m[i * rows : (i + 1) * rows]
        y = mm(jnp.concatenate(kern, axis=1), xs, 1, 0)
        gx = mm(jnp.concatenate(kern, axis=0), gs, 0, 0)
        gx_ref[:, place] = gx
        late = slice(width + j * lanes, width + (j + 1) * lanes)
        gy_ref[:, place], gy_ref[:, late] = halves(g.astype(F32) * y)
        xg_ref[:, place], xg_ref[:, late] = halves(x.astype(F32) * gx)
    ds_ref[...] = ds
    pick = head_lanes(2 * pairs, width, size).astype(BF)
    pick = jnp.concatenate([pick, pick], axis=1)
    sums_ref[0] = mm(pick, gy_ref[...], 1, 1)
    sums_ref[1] = mm(pick, xg_ref[...], 1, 1)


def outer_kernel(size, parts, *refs):
    store_ref, x_ref, g_ref, bc_ref, hp_ref, rate_ref = refs[:6]
    gxs, dss, sums = (refs[6 + k * parts : 6 + (k + 1) * parts] for k in range(3))
    grad_ref, keep_ref, give_ref, wv_ref, eu_ref, io_ref = refs[6 + 3 * parts :]
    rate = rate_ref[...].T
    rows, width = x_ref.shape
    heads = rate_ref.shape[1]
    chunks, step = store_ref.shape[1] - 1, store_ref.shape[3]
    piece = width // parts
    b, c = bc_ref[0:rows, :], bc_ref[rows : 2 * rows, :]
    pre, dt, cum, grow, w = (hp_ref[k * heads : (k + 1) * heads, :] for k in range(5))
    ds = dss[0][...]
    for ref in dss[1:]:
        ds = ds + ref[...]
    db = mm(c, ds, 0, 0, TOP)
    dc = mm(b, ds, 0, 1, TOP)
    b_wide = jnp.concatenate(halves(b), axis=1)
    c_wide = jnp.concatenate(halves(c), axis=1)
    for k in range(chunks):
        place = slice(k * step, (k + 1) * step)
        late = slice(width + k * step, width + (k + 1) * step)
        pick = head_lanes(heads, step, size, k * step).astype(BF)
        incoming, outgoing = store_ref[0, k], store_ref[1, k]
        u = mm(c_wide, jnp.concatenate([incoming, incoming], axis=0), 1, 0)
        v = mm(b_wide, jnp.concatenate([outgoing, outgoing], axis=0), 1, 0)
        scale = spread(w, pick)
        wx = scale * x_ref[:, place].astype(F32)
        eg = spread(grow, pick) * g_ref[:, place].astype(F32)
        for q in range(step // piece) if step >= piece else (0,):
            if step >= piece:
                at = k * step + q * piece
                inner = slice(q * piece, (q + 1) * piece)
                term = gxs[at // piece][...]
            else:
                at, inner = k * step, slice(0, step)
                term = gxs[at // piece][:, at % piece : at % piece + step]
            total = term + scale[:, inner] * v[:, inner]
            grad_ref[:, at : at + total.shape[1]] = total.astype(BF)
        wv_ref[:, place], wv_ref[:, late] = halves(wx * v)
        eu_ref[:, place], eu_ref[:, late] = halves(eg * u)
        db = db + mm(
            jnp.concatenate([outgoing, outgoing], axis=1), jnp.concatenate(halves(wx), axis=1), 1, 1
        )
        dc = dc + mm(
            jnp.concatenate([incoming, incoming], axis=1), jnp.concatenate(halves(eg), axis=1), 1, 1
        )
        io_ref[:, place] = jnp.sum(incoming.astype(F32) * outgoing.astype(F32), axis=0, keepdims=True)
    pick = head_lanes(heads, width, size)
    ddecay = jnp.sum(pick * io_ref[...], axis=1, keepdims=True)
    pick = pick.astype(BF)
    pick = jnp.concatenate([pick, pick], axis=1)
    wdw = mm(pick, wv_ref[...], 1, 1)
    egu = mm(pick, eu_ref[...], 1, 1)
    rowsum = jnp.concatenate([s[0] for s in sums], axis=0)
    colsum = jnp.concatenate([s[1] for s in sums], axis=0)
    dcum = rowsum - colsum + egu - wdw
    row = lax.broadcasted_iota(jnp.int32, (rows, rows), 0)
    col = lax.broadcasted_iota(jnp.int32, (rows, rows), 1)
    rev = mm(dcum, jnp.where(row >= col, 1.0, 0.0), 1, 0, TOP)
    decay = grow[:, rows - 1 : rows]
    rev = rev + jnp.sum(wdw, axis=1, keepdims=True) + decay * ddecay
    gate = 1.0 / (1.0 + jnp.exp(-pre))
    small = 1e-30
    ratio = jnp.where(dt > small, gate / jnp.maximum(dt, small), 1.0)
    core = lax.axis_index("head")
    keep_ref[0:rows, :] = jnp.where(core == 0, db, dc)
    keep_ref[rows:, :] = (colsum + wdw) * ratio - rate * rev * gate
    give_ref[...] = jnp.where(core == 0, dc, db)


def low_kernel(keep_ref, taken_ref, out_ref):
    rows = taken_ref.shape[0]
    low = keep_ref[0:rows, :] + taken_ref[...]
    low = jnp.concatenate([low, keep_ref[rows:, :]], axis=0).astype(BF)
    for k in range(out_ref.shape[0]):
        out_ref[k] = low


def token_kernel(count, mine_ref, other_ref, *refs):
    out_ref = refs[2 * count]
    me, core = lax.axis_index("dp"), lax.axis_index("head")
    part, cols = refs[0].shape
    half = cols // 2
    heads = refs[1].shape[0] // 2
    for r in range(count):
        at = pl.multiple_of(lax.rem(me - r + count, count) * part, 128)
        total = None
        for k, ref in enumerate((mine_ref, other_ref)):
            at_col = pl.multiple_of(lax.rem(core + k, 2) * half, 128)
            at_row = pl.multiple_of(lax.rem(core + k, 2) * heads, 16)
            term = mm(ref[0:half, :], refs[2 * r][:, pl.ds(at_col, half)], 0, 1)
            term = term + mm(ref[half:, :], refs[2 * r + 1][pl.ds(at_row, heads), :], 0, 0)
            total = term if total is None else total + term
        out_ref[:, pl.ds(at, part)] = total.astype(BF)


def weight_kernel(scale, n_dp, n_seq, slots, *refs):
    count = 2 * len(slots) if n_dp > 1 else len(slots)
    toks, lows = refs[:count], refs[count:-6]
    bc_ref, dt_ref, tok_ref, low_ref, tok_sem, low_sem = refs[-6:]
    rows = toks[0].shape[0]
    share = lows[0].shape[1]
    core, place, me = lax.axis_index("head"), lax.axis_index("seq"), lax.axis_index("dp")
    even = lax.rem(place, 2) == 0
    copies = []
    for r in range(n_dp):
        for k, (kind, hop) in enumerate(slots):
            above = even if kind == 0 else ~even
            block = jnp.where(above, place + hop, place - hop)
            fits = (block >= 0) & (block < n_seq)
            if hop > 0 and kind == 1:
                fits = fits & jnp.where(above, place < n_seq - 1, place > 0)
            at = pl.multiple_of(jnp.clip(block, 0, n_seq - 1) * rows, 128)
            source = toks[k] if r == 0 else toks[len(slots) + k].at[pl.ds((r - 1) * rows, rows)]
            copy = pltpu.make_async_copy(source, tok_ref.at[r, pl.ds(at, rows)], tok_sem.at[r, k])
            copies.append((fits, copy))
    for r in range(n_dp):
        for s in range(n_seq):
            index = s * n_dp + lax.rem(me - r + n_dp, n_dp)
            for k in range(2):
                row = pl.multiple_of(lax.rem(core + k, 2) * share, 16)
                copy = pltpu.make_async_copy(
                    lows[k].at[index],
                    low_ref.at[r, pl.ds(row, share), pl.ds(s * rows, rows)],
                    low_sem.at[r * n_seq + s, k],
                )
                copies.append((None, copy))
    for fits, copy in copies:
        if fits is None:
            copy.start()
        else:
            pl.when(fits)(copy.start)
    for fits, copy in copies:
        if fits is None:
            copy.wait()
        else:
            pl.when(fits)(copy.wait)
    total = mm(low_ref[0], tok_ref[0], 1, 0)
    for r in range(1, n_dp):
        total = total + mm(low_ref[r], tok_ref[r], 1, 0)
    total = total * scale
    half = bc_ref.shape[1] // 2
    heads = dt_ref.shape[0] // 2
    for k in range(2):
        bc_ref[:, k * half : (k + 1) * half] = total[k * share : k * share + half].T
        dt_ref[k * heads : (k + 1) * heads, :] = total[k * share + half : (k + 1) * share]


def relays(count):
    groups, _ = matchings(count)
    return [
        (kind, hop)
        for hop in range(1, count)
        for kind in (0, 1)
        if any(i - hop + 1 >= 0 or j + hop - 1 < count for i, j in groups[kind])
    ]


def relay(found, block, steps, *others):
    count = lax.axis_size("seq")
    _, pairs = matchings(count)
    for kind, hop in steps:
        source = block if hop == 1 else found[1 - kind, hop - 1]
        source = after(source, *others) if others else source
        found[kind, hop] = lax.ppermute(source, "seq", pairs[kind])
    return [found[step] for step in steps]


def chains(first, own, decay, inner, beside, riders, late):
    count = lax.axis_size("seq")
    place = lax.axis_index("seq")
    chunks = len(first)
    store = jnp.zeros((2, chunks + 1) + own.shape[2:], BF)
    got = list(first)
    done, todo, extra = [], list(inner), []
    last = count + chunks - 2
    for slot in range(1, last + 1):
        steps = [(hop, slot - hop) for hop in range(1, count) if 0 <= slot - hop < chunks]
        sent = []
        for hop, k in steps:
            value = got[k]
            if hop == 1 and 0 < k < len(riders):
                value = jnp.where((place == 0) | (place == count - 1), value, riders[k])
            if hop > 1:
                value = jnp.where(place == hop - 1, own[0, k], own[1, k])
                value = (value + decay[k] * got[k].astype(F32)).astype(BF)
            sent.append(value)
        for (hop, k), value in zip(steps, sent):
            to = {i: i for i in range(count)}
            for i in (hop - 1, count - hop - 1):
                to[i], to[i + 1] = i + 1, i
            got[k] = lax.ppermute(value, "seq", sorted(to.items()))
            if hop == 1 and k < len(riders):
                riders[k] = got[k]
        for _ in range(-(-len(todo) // (last + 1 - slot))):
            done.append(todo.pop(0)(*sent))
        if slot == 1:
            extra, soon = beside(*sent)
        if slot == last:
            late(*sent)
        if slot < last:
            held = [got[k] for _, k in steps] + [d[0] for d in done[-1:]]
            if slot == last - 1:
                held += extra
            if slot == 1:
                held += soon
            new = slot < chunks
            if new:
                held.append(got[slot])
            kept = lax.optimization_barrier(tuple(held))
            for (_, k), a in zip(steps, kept):
                got[k] = a
            if new:
                got[slot] = kept[-1]
        for hop, k in steps:
            kind = jnp.where(place == hop, 0, 1)
            fits = (place == hop) | (place == count - hop - 1)
            at = jnp.where(fits, k, chunks)
            zero = jnp.zeros_like(at)
            store = lax.dynamic_update_slice(store, got[k][None, None], (kind, at, zero, zero))
    done += [make() for make in todo]
    return store, done


def body(tokens, ssd_input, grad_out, w_bc, w_dt, decay_rate, dt_bias):
    feats, x, g = tokens[0], ssd_input[0], grad_out[0]
    rows, width = feats.shape
    heads = decay_rate.shape[0]
    size = width // heads
    n_dp, n_seq = lax.axis_size("dp"), lax.axis_size("seq")
    part = width // n_dp
    state_n = w_bc.shape[1] // 2
    w_dt = w_dt.T
    rate, bias = decay_rate[None], dt_bias[None]

    pieces = call(split_kernel, [struct((rows, part), BF)] * n_dp, 0.7, feats)
    items = [pieces[0]] + [cyclic(pieces[r], "dp", r) for r in range(1, n_dp)]
    groups = items[:1]
    if n_dp > 1:
        groups.append(items[1] if n_dp == 2 else jnp.concatenate(items[1:], axis=0))
    found = [{} for _ in groups]
    slots = relays(n_seq)
    step = width // CHUNKS
    ride = n_seq == 4 and all(a.shape == (state_n, step) for a in groups)
    second = [(kind, hop) for kind, hop in slots if hop == 2 and not (ride and kind == 0)]
    near = relay(found[0], groups[0], slots[:2])
    partials = [project(items[0], w_bc, w_dt)]
    for r in range(1, n_dp):
        item = after(items[r], partials[0])
        partials.append(cyclic(project(item, w_bc, w_dt), "dp", -r))
    if n_dp > 1:
        near += relay(found[1], groups[1], slots[: 1 if ride else 2])
    partials[1:] = [after(a, *near) for a in partials[1:]]
    proj = partials + [cyclic(a, "head", 1) for a in partials]
    spare = relay(found[0], groups[0], second)
    own, bc, hp, *outs = call(
        functools.partial(state_kernel, 2 * n_dp, size, int(ride)),
        (
            struct((2, CHUNKS, state_n, step), F32),
            struct((2 * rows, state_n), F32),
            struct((5 * heads, rows), F32),
        )
        + (struct((state_n, step), BF),) * CHUNKS
        + (struct((1, step), F32),) * CHUNKS,
        0.1,
        *proj,
        x,
        g,
        rate,
        bias,
        *([found[0][1, 1]] if ride else []),
    )
    first, decay = outs[:CHUNKS], outs[CHUNKS:]
    pairs = width // (2 * size) // PARTS
    span = width // PARTS
    shared = []

    def inner(q, *others):
        held = after(bc, *others) if others else bc
        square = struct((rows, rows), F32)
        block = pl.BlockSpec((rows, span), lambda _: (0, q))
        out = call(
            functools.partial(inner_kernel, q * pairs, pairs, size),
            ([square] if q == 0 else [])
            + [struct((rows, span), F32), square, struct((2, 2 * pairs, rows), F32)],
                0.9,
            held,
            hp,
            x,
            g,
            *shared,
            scratch=(pltpu.VMEM((rows, 2 * span), BF), pltpu.VMEM((rows, 2 * span), BF)),
            specs=[VMEM, VMEM, block, block] + [VMEM] * len(shared),
        )
        if q == 0:
            shared.append(out[0])
            out = out[1:]
        return out

    weights = [w_bc, w_dt]

    def beside(*others):
        for r in range(1, n_dp):
            weights.extend(cyclic(after(a, *others), "dp", r) for a in (w_bc, w_dt))
        return weights[2:], []

    def late(*others):
        if n_dp > 1:
            relay(found[1], groups[1], second, *others)

    if ride and n_dp > 1:
        spare += relay(found[1], groups[1], [(1, 1)])
    first[0] = after(first[0], *spare)
    riders = [f[1, 1] for f in found] if ride else []
    calls = [functools.partial(inner, q) for q in range(PARTS)]
    store, inners = chains(first, own, decay, calls, beside, riders, late)
    for f, a in zip(found, riders):
        f[0, 2] = a
    done = [relay(f, a, [t for t in slots if t not in f], store) for f, a in zip(found, groups)]
    grad_x, keep, give = call(
        functools.partial(outer_kernel, size, PARTS),
        (
            struct((rows, width), BF),
            struct((rows + heads, rows), F32),
            struct((rows, rows), F32),
        ),
        3.1,
        store,
        x,
        g,
        bc,
        hp,
        rate,
        *[a[0] for a in inners],
        *[a[1] for a in inners],
        *[a[2] for a in inners],
        scratch=(
            pltpu.VMEM((rows, 2 * width), BF),
            pltpu.VMEM((rows, 2 * width), BF),
            pltpu.VMEM((1, width), F32),
        ),
    )
    taken = after(cyclic(give, "head", 1), *done[0])
    count = n_dp * n_seq
    copies = call(low_kernel, struct((count, rows + heads, rows), BF), 0.7, keep, taken)
    mine = copies[0]
    lows = lax.all_to_all(copies, ("seq", "dp"), 0, 0, tiled=True)
    other = cyclic(mine, "head", 1)
    grads = call(
        functools.partial(token_kernel, n_dp),
        struct((rows, width), BF),
        1.5,
        after(mine, *done[-1]),
        other,
        *weights,
    )
    lows = after(lows, grads)
    swapped = cyclic(lows, "head", 1)
    toks = []
    for f, a in zip(found, groups):
        toks += [a] + [f[step] for step in slots]
    slots = [(0, 0)] + slots
    cols = 2 * (rows + heads)
    grad_bc, grad_dt = call(
        functools.partial(weight_kernel, 1.0 / (rows * n_seq * n_dp), n_dp, n_seq, slots),
        (struct((part, 2 * state_n), F32), struct((2 * heads, part), F32)),
        2.5,
        *toks,
        lows,
        swapped,
        specs=[HBM] * len(toks) + [VMEM] * 2,
        limit=LIMIT + 2 * n_dp * n_seq * rows * (part + cols),
        scratch=(
            pltpu.VMEM((n_dp, n_seq * rows, part), BF),
            pltpu.VMEM((n_dp, cols, n_seq * rows), BF),
            pltpu.SemaphoreType.DMA((n_dp, len(slots))),
            pltpu.SemaphoreType.DMA((count, 2)),
        ),
    )
    return grad_x[None], grads[None], grad_bc, grad_dt.T


def solution(mesh):
    in_specs = (
        P(("grp", "dp"), "seq", "head"),
        P(("grp", "dp"), "seq", "head"),
        P(("grp", "dp"), "seq", "head"),
        P(("head", "dp"), None),
        P(("head", "dp"), None),
        P("head"),
        P("head"),
    )
    out_specs = (
        P(("grp", "dp"), "seq", "head"),
        P(("grp", "dp"), "seq", "head"),
        P(("grp", "head", "dp"), None),
        P(("grp", "head", "dp"), None),
    )
    return jax.shard_map(body, mesh=mesh, in_specs=in_specs, out_specs=out_specs, check_vma=False)
```

```python
import functools

import jax
import jax.numpy as jnp
from jax import lax
from jax.experimental import pallas as pl
from jax.experimental.pallas import tpu as pltpu
from jax.sharding import PartitionSpec as P

CHUNKS = 2
PARTS = 4
BF = jnp.bfloat16
F32 = jnp.float32
TOP = lax.Precision.HIGHEST
PER_US = 1.15e9
LIMIT = 16 * 1024 * 1024


def cyclic(a, axis, by):
    count = lax.axis_size(axis)
    return lax.ppermute(a, axis, [(i, (i + by) % count) for i in range(count)])


def mm(a, b, ca, cb, precision=None):
    return lax.dot_general(
        a, b, (((ca,), (cb,)), ((), ())), preferred_element_type=F32, precision=precision
    )


def halves(a):
    high = a.astype(BF)
    return high, (a - high.astype(F32)).astype(BF)


def head_lanes(heads, width, size, first=0):
    row = lax.broadcasted_iota(jnp.int32, (heads, width), 0)
    col = lax.broadcasted_iota(jnp.int32, (heads, width), 1) + first
    low = row * size
    return jnp.where((col >= low) & (col < low + size), 1.0, 0.0).astype(F32)


def spread(a, pick):
    high, low = halves(a)
    both = jnp.concatenate([pick, pick], axis=0)
    return mm(jnp.concatenate([high, low], axis=0), both, 0, 0)


VMEM = pl.BlockSpec(memory_space=pltpu.VMEM)
HBM = pl.BlockSpec(memory_space=pltpu.HBM)


def call(kernel, out_shape, span_us, *args, scratch=(), specs=None, limit=LIMIT):
    size = sum(a.size * a.dtype.itemsize for a in args)
    return pl.pallas_call(
        kernel,
        out_shape=out_shape,
        grid=(1,),
        in_specs=specs or [VMEM] * len(args),
        out_specs=jax.tree.map(lambda _: VMEM, out_shape),
        scratch_shapes=list(scratch),
        compiler_params=pltpu.CompilerParams(vmem_limit_bytes=limit),
        cost_estimate=pl.CostEstimate(
            flops=int(span_us * PER_US), bytes_accessed=size, transcendentals=0
        ),
    )(*args)


def struct(shape, dtype):
    return jax.ShapeDtypeStruct(shape, dtype)


def after(a, *others):
    return lax.optimization_barrier((a, others))[0]


def matchings(count):
    groups = [[(i, i + 1) for i in range(kind, count - 1, 2)] for kind in (0, 1)]
    pairs = []
    for group in groups:
        to = {i: i for i in range(count)}
        for i, j in group:
            to[i], to[j] = j, i
        pairs.append(sorted(to.items()))
    return groups, pairs


def split_kernel(a_ref, *outs):
    count = len(outs)
    me = lax.axis_index("dp")
    part = outs[0].shape[1]
    for r in range(count):
        at = pl.multiple_of(lax.rem(me + r, count) * part, 128)
        outs[r][...] = a_ref[:, pl.ds(at, part)]


def project_kernel(a_ref, bc_ref, dt_ref, out_ref):
    a = a_ref[...]
    state_n = bc_ref.shape[1] // 2
    rows = a.shape[0]
    bc = mm(a, bc_ref[...], 1, 0)
    out_ref[0:rows, :] = bc[:, :state_n]
    out_ref[rows : 2 * rows, :] = bc[:, state_n:]
    out_ref[2 * rows :, :] = mm(dt_ref[...], a, 1, 1)


def project(a, w_bc, w_dt):
    rows = a.shape[0]
    total = 2 * rows + w_dt.shape[0]
    return call(
        project_kernel,
        struct((total, w_bc.shape[1] // 2), F32),
        2.1,
        a,
        w_bc,
        w_dt,
    )


def state_kernel(count, size, ride, *refs):
    proj = refs[:count]
    x_ref, g_ref, rate_ref, bias_ref = refs[count : count + 4]
    riders = refs[count + 4 : count + 4 + ride]
    own_ref, bc_ref, hp_ref = refs[count + 4 + ride : count + 7 + ride]
    outs = refs[count + 7 + ride :]
    firsts, decays = outs[: len(outs) // 2], outs[len(outs) // 2 :]
    heads = rate_ref.shape[1]
    rows = x_ref.shape[0]
    rate, bias = rate_ref[...].T, bias_ref[...].T
    chunks, step = own_ref.shape[1], own_ref.shape[3]
    first = pl.multiple_of(2 * rows + lax.axis_index("head") * heads, 8)
    bc = proj[0][0 : 2 * rows, :]
    pre = proj[0][pl.ds(first, heads), :] + bias
    for ref in proj[1:]:
        bc = bc + ref[0 : 2 * rows, :]
        pre = pre + ref[pl.ds(first, heads), :]
    bc_ref[...] = bc
    dt = jnp.maximum(pre, 0.0) + jnp.log1p(jnp.exp(-jnp.abs(pre)))
    row = lax.broadcasted_iota(jnp.int32, (rows, rows), 0)
    col = lax.broadcasted_iota(jnp.int32, (rows, rows), 1)
    cum = mm(-dt * rate, jnp.where(row <= col, 1.0, 0.0), 1, 0, TOP)
    last = cum[:, rows - 1 : rows]
    grow = jnp.exp(cum)
    w = jnp.exp(last - cum) * dt
    decay = jnp.exp(last)
    for k, part in enumerate((pre, dt, cum, grow, w)):
        hp_ref[k * heads : (k + 1) * heads, :] = part
    place = lax.axis_index("seq")
    lowest = place == 0
    sides = []
    for vec in (bc[:rows], bc[rows:]):
        high, low = halves(vec.T)
        sides.append((jnp.concatenate([high, low], axis=1), high))
    for k in range(chunks):
        pick = head_lanes(heads, step, size, k * step)
        decays[k][...] = jnp.sum(pick * decay, axis=0, keepdims=True)
        pick = pick.astype(BF)
        both = []
        for kind, (scale, ref) in enumerate(((w, x_ref), (grow, g_ref))):
            wide, high = sides[kind]
            value = spread(scale, pick) * ref[:, k * step : (k + 1) * step].astype(F32)
            top, rest = halves(value)
            value = mm(wide, jnp.concatenate([top, top], axis=0), 1, 0) + mm(high, rest, 1, 0)
            own_ref[kind, k] = value
            both.append(value)
        firsts[k][...] = jnp.where(lowest, both[0], both[1]).astype(BF)
        if k < ride:
            rider = riders[k]

            @pl.when((place > 0) & (place < lax.axis_size("seq") - 1))
            def _():
                firsts[k][...] = rider[...]


def inner_kernel(first, pairs, size, bc_ref, hp_ref, x_ref, g_ref, *refs):
    gx_ref, ds_ref, sums_ref = refs[-5:-2]
    gy_ref, xg_ref = refs[-2:]
    rows = x_ref.shape[0]
    heads = hp_ref.shape[0] // 5
    lanes = 2 * size
    width = pairs * lanes
    if len(refs) == 6 and first > 0:
        scores = refs[0][...]
    else:
        scores = mm(bc_ref[rows : 2 * rows, :], bc_ref[0:rows, :], 1, 1, TOP)
        refs[0][...] = scores
    row = lax.broadcasted_iota(jnp.int32, (rows, rows), 0)
    col = lax.broadcasted_iota(jnp.int32, (rows, rows), 1)
    causal = row >= col
    dt = hp_ref[heads : 2 * heads, :]
    cum = hp_ref[2 * heads : 3 * heads, :]
    cum_t = cum.T
    lane = lax.broadcasted_iota(jnp.int32, (rows, lanes), 1)
    sides = [jnp.where(lane < size, 1.0, 0.0).astype(BF), jnp.where(lane < size, 0.0, 1.0).astype(BF)]
    ds = jnp.zeros((rows, rows), F32)
    for j in range(pairs):
        place = slice(j * lanes, (j + 1) * lanes)
        x, g = x_ref[:, place], g_ref[:, place]
        xs = jnp.concatenate([x * s for s in sides], axis=0)
        gs = jnp.concatenate([g * s for s in sides], axis=0)
        m = mm(gs, x, 1, 1)
        kern = []
        for i in range(2):
            h = 2 * (first + j) + i
            gap = cum_t[:, h : h + 1] - cum[h : h + 1, :]
            fall = jnp.exp(jnp.where(causal, gap, -jnp.inf)) * dt[h : h + 1, :]
            kern.append((fall * scores).astype(BF))
            ds = ds + fall * m[i * rows : (i + 1) * rows]
        y = mm(jnp.concatenate(kern, axis=1), xs, 1, 0)
        gx = mm(jnp.concatenate(kern, axis=0), gs, 0, 0)
        gx_ref[:, place] = gx
        late = slice(width + j * lanes, width + (j + 1) * lanes)
        gy_ref[:, place], gy_ref[:, late] = halves(g.astype(F32) * y)
        xg_ref[:, place], xg_ref[:, late] = halves(x.astype(F32) * gx)
    ds_ref[...] = ds
    pick = head_lanes(2 * pairs, width, size).astype(BF)
    pick = jnp.concatenate([pick, pick], axis=1)
    sums_ref[0] = mm(pick, gy_ref[...], 1, 1)
    sums_ref[1] = mm(pick, xg_ref[...], 1, 1)


def outer_kernel(size, parts, *refs):
    store_ref, x_ref, g_ref, bc_ref, hp_ref, rate_ref = refs[:6]
    gxs, dss, sums = (refs[6 + k * parts : 6 + (k + 1) * parts] for k in range(3))
    grad_ref, keep_ref, give_ref, wv_ref, eu_ref, io_ref = refs[6 + 3 * parts :]
    rate = rate_ref[...].T
    rows, width = x_ref.shape
    heads = rate_ref.shape[1]
    chunks, step = store_ref.shape[1] - 1, store_ref.shape[3]
    piece = width // parts
    b, c = bc_ref[0:rows, :], bc_ref[rows : 2 * rows, :]
    pre, dt, cum, grow, w = (hp_ref[k * heads : (k + 1) * heads, :] for k in range(5))
    ds = dss[0][...]
    for ref in dss[1:]:
        ds = ds + ref[...]
    db = mm(c, ds, 0, 0, TOP)
    dc = mm(b, ds, 0, 1, TOP)
    b_wide = jnp.concatenate(halves(b), axis=1)
    c_wide = jnp.concatenate(halves(c), axis=1)
    for k in range(chunks):
        place = slice(k * step, (k + 1) * step)
        late = slice(width + k * step, width + (k + 1) * step)
        pick = head_lanes(heads, step, size, k * step).astype(BF)
        incoming, outgoing = store_ref[0, k], store_ref[1, k]
        u = mm(c_wide, jnp.concatenate([incoming, incoming], axis=0), 1, 0)
        v = mm(b_wide, jnp.concatenate([outgoing, outgoing], axis=0), 1, 0)
        scale = spread(w, pick)
        wx = scale * x_ref[:, place].astype(F32)
        eg = spread(grow, pick) * g_ref[:, place].astype(F32)
        for q in range(step // piece) if step >= piece else (0,):
            if step >= piece:
                at = k * step + q * piece
                inner = slice(q * piece, (q + 1) * piece)
                term = gxs[at // piece][...]
            else:
                at, inner = k * step, slice(0, step)
                term = gxs[at // piece][:, at % piece : at % piece + step]
            total = term + scale[:, inner] * v[:, inner]
            grad_ref[:, at : at + total.shape[1]] = total.astype(BF)
        wv_ref[:, place], wv_ref[:, late] = halves(wx * v)
        eu_ref[:, place], eu_ref[:, late] = halves(eg * u)
        db = db + mm(
            jnp.concatenate([outgoing, outgoing], axis=1), jnp.concatenate(halves(wx), axis=1), 1, 1
        )
        dc = dc + mm(
            jnp.concatenate([incoming, incoming], axis=1), jnp.concatenate(halves(eg), axis=1), 1, 1
        )
        io_ref[:, place] = jnp.sum(incoming.astype(F32) * outgoing.astype(F32), axis=0, keepdims=True)
    pick = head_lanes(heads, width, size)
    ddecay = jnp.sum(pick * io_ref[...], axis=1, keepdims=True)
    pick = pick.astype(BF)
    pick = jnp.concatenate([pick, pick], axis=1)
    wdw = mm(pick, wv_ref[...], 1, 1)
    egu = mm(pick, eu_ref[...], 1, 1)
    rowsum = jnp.concatenate([s[0] for s in sums], axis=0)
    colsum = jnp.concatenate([s[1] for s in sums], axis=0)
    dcum = rowsum - colsum + egu - wdw
    row = lax.broadcasted_iota(jnp.int32, (rows, rows), 0)
    col = lax.broadcasted_iota(jnp.int32, (rows, rows), 1)
    rev = mm(dcum, jnp.where(row >= col, 1.0, 0.0), 1, 0, TOP)
    decay = grow[:, rows - 1 : rows]
    rev = rev + jnp.sum(wdw, axis=1, keepdims=True) + decay * ddecay
    gate = 1.0 / (1.0 + jnp.exp(-pre))
    small = 1e-30
    ratio = jnp.where(dt > small, gate / jnp.maximum(dt, small), 1.0)
    core = lax.axis_index("head")
    keep_ref[0:rows, :] = jnp.where(core == 0, db, dc)
    keep_ref[rows:, :] = (colsum + wdw) * ratio - rate * rev * gate
    give_ref[...] = jnp.where(core == 0, dc, db)


def low_kernel(keep_ref, taken_ref, out_ref):
    rows = taken_ref.shape[0]
    low = keep_ref[0:rows, :] + taken_ref[...]
    low = jnp.concatenate([low, keep_ref[rows:, :]], axis=0).astype(BF)
    for k in range(out_ref.shape[0]):
        out_ref[k] = low


def token_kernel(count, mine_ref, other_ref, *refs):
    out_ref = refs[2 * count]
    me, core = lax.axis_index("dp"), lax.axis_index("head")
    part, cols = refs[0].shape
    half = cols // 2
    heads = refs[1].shape[0] // 2
    for r in range(count):
        at = pl.multiple_of(lax.rem(me - r + count, count) * part, 128)
        total = None
        for k, ref in enumerate((mine_ref, other_ref)):
            at_col = pl.multiple_of(lax.rem(core + k, 2) * half, 128)
            at_row = pl.multiple_of(lax.rem(core + k, 2) * heads, 16)
            term = mm(ref[0:half, :], refs[2 * r][:, pl.ds(at_col, half)], 0, 1)
            term = term + mm(ref[half:, :], refs[2 * r + 1][pl.ds(at_row, heads), :], 0, 0)
            total = term if total is None else total + term
        out_ref[:, pl.ds(at, part)] = total.astype(BF)


def weight_kernel(scale, n_dp, n_seq, slots, *refs):
    count = 2 * len(slots) if n_dp > 1 else len(slots)
    toks, lows = refs[:count], refs[count:-6]
    bc_ref, dt_ref, tok_ref, low_ref, tok_sem, low_sem = refs[-6:]
    rows = toks[0].shape[0]
    share = lows[0].shape[1]
    core, place, me = lax.axis_index("head"), lax.axis_index("seq"), lax.axis_index("dp")
    even = lax.rem(place, 2) == 0
    copies = []
    for r in range(n_dp):
        for k, (kind, hop) in enumerate(slots):
            above = even if kind == 0 else ~even
            block = jnp.where(above, place + hop, place - hop)
            fits = (block >= 0) & (block < n_seq)
            if hop > 0 and kind == 1:
                fits = fits & jnp.where(above, place < n_seq - 1, place > 0)
            at = pl.multiple_of(jnp.clip(block, 0, n_seq - 1) * rows, 128)
            source = toks[k] if r == 0 else toks[len(slots) + k].at[pl.ds((r - 1) * rows, rows)]
            copy = pltpu.make_async_copy(source, tok_ref.at[r, pl.ds(at, rows)], tok_sem.at[r, k])
            copies.append((fits, copy))
    for r in range(n_dp):
        for s in range(n_seq):
            index = s * n_dp + lax.rem(me - r + n_dp, n_dp)
            for k in range(2):
                row = pl.multiple_of(lax.rem(core + k, 2) * share, 16)
                copy = pltpu.make_async_copy(
                    lows[k].at[index],
                    low_ref.at[r, pl.ds(row, share), pl.ds(s * rows, rows)],
                    low_sem.at[r * n_seq + s, k],
                )
                copies.append((None, copy))
    for fits, copy in copies:
        if fits is None:
            copy.start()
        else:
            pl.when(fits)(copy.start)
    for fits, copy in copies:
        if fits is None:
            copy.wait()
        else:
            pl.when(fits)(copy.wait)
    total = mm(low_ref[0], tok_ref[0], 1, 0)
    for r in range(1, n_dp):
        total = total + mm(low_ref[r], tok_ref[r], 1, 0)
    total = total * scale
    half = bc_ref.shape[1] // 2
    heads = dt_ref.shape[0] // 2
    for k in range(2):
        bc_ref[:, k * half : (k + 1) * half] = total[k * share : k * share + half].T
        dt_ref[k * heads : (k + 1) * heads, :] = total[k * share + half : (k + 1) * share]


def relays(count):
    groups, _ = matchings(count)
    return [
        (kind, hop)
        for hop in range(1, count)
        for kind in (0, 1)
        if any(i - hop + 1 >= 0 or j + hop - 1 < count for i, j in groups[kind])
    ]


def relay(found, block, steps, *others):
    count = lax.axis_size("seq")
    _, pairs = matchings(count)
    for kind, hop in steps:
        source = block if hop == 1 else found[1 - kind, hop - 1]
        source = after(source, *others) if others else source
        found[kind, hop] = lax.ppermute(source, "seq", pairs[kind])
    return [found[step] for step in steps]


def chains(first, own, decay, inner, beside, riders, late):
    count = lax.axis_size("seq")
    place = lax.axis_index("seq")
    chunks = len(first)
    store = jnp.zeros((2, chunks + 1) + own.shape[2:], BF)
    got = list(first)
    done, todo, extra = [], list(inner), []
    last = count + chunks - 2
    for slot in range(1, last + 1):
        steps = [(hop, slot - hop) for hop in range(1, count) if 0 <= slot - hop < chunks]
        sent = []
        for hop, k in steps:
            value = got[k]
            if hop == 1 and 0 < k < len(riders):
                value = jnp.where((place == 0) | (place == count - 1), value, riders[k])
            if hop > 1:
                value = jnp.where(place == hop - 1, own[0, k], own[1, k])
                value = (value + decay[k] * got[k].astype(F32)).astype(BF)
            sent.append(value)
        for (hop, k), value in zip(steps, sent):
            to = {i: i for i in range(count)}
            for i in (hop - 1, count - hop - 1):
                to[i], to[i + 1] = i + 1, i
            got[k] = lax.ppermute(value, "seq", sorted(to.items()))
            if hop == 1 and k < len(riders):
                riders[k] = got[k]
        for _ in range(-(-len(todo) // (last + 1 - slot))):
            done.append(todo.pop(0)(*sent))
        if slot == 1:
            extra, soon = beside(*sent)
        if slot == last:
            late(*sent)
        if slot < last:
            held = [got[k] for _, k in steps] + [d[0] for d in done[-1:]]
            if slot == last - 1:
                held += extra
            if slot == 1:
                held += soon
            new = slot < chunks
            if new:
                held.append(got[slot])
            kept = lax.optimization_barrier(tuple(held))
            for (_, k), a in zip(steps, kept):
                got[k] = a
            if new:
                got[slot] = kept[-1]
        for hop, k in steps:
            kind = jnp.where(place == hop, 0, 1)
            fits = (place == hop) | (place == count - hop - 1)
            at = jnp.where(fits, k, chunks)
            zero = jnp.zeros_like(at)
            store = lax.dynamic_update_slice(store, got[k][None, None], (kind, at, zero, zero))
    done += [make() for make in todo]
    return store, done


def body(tokens, ssd_input, grad_out, w_bc, w_dt, decay_rate, dt_bias):
    feats, x, g = tokens[0], ssd_input[0], grad_out[0]
    rows, width = feats.shape
    heads = decay_rate.shape[0]
    size = width // heads
    n_dp, n_seq = lax.axis_size("dp"), lax.axis_size("seq")
    part = width // n_dp
    state_n = w_bc.shape[1] // 2
    w_dt = w_dt.T
    rate, bias = decay_rate[None], dt_bias[None]

    pieces = call(split_kernel, [struct((rows, part), BF)] * n_dp, 1.9, feats)
    items = [pieces[0]] + [cyclic(pieces[r], "dp", r) for r in range(1, n_dp)]
    groups = items[:1]
    if n_dp > 1:
        groups.append(items[1] if n_dp == 2 else jnp.concatenate(items[1:], axis=0))
    found = [{} for _ in groups]
    slots = relays(n_seq)
    step = width // CHUNKS
    ride = n_seq == 4 and all(a.shape == (state_n, step) for a in groups)
    second = [(kind, hop) for kind, hop in slots if hop == 2 and not (ride and kind == 0)]
    near = relay(found[0], groups[0], slots[:2])
    partials = [project(items[0], w_bc, w_dt)]
    for r in range(1, n_dp):
        item = after(items[r], partials[0])
        partials.append(cyclic(project(item, w_bc, w_dt), "dp", -r))
    if n_dp > 1:
        near += relay(found[1], groups[1], slots[: 1 if ride else 2])
    partials[1:] = [after(a, *near) for a in partials[1:]]
    proj = partials + [cyclic(a, "head", 1) for a in partials]
    spare = relay(found[0], groups[0], second)
    own, bc, hp, *outs = call(
        functools.partial(state_kernel, 2 * n_dp, size, int(ride)),
        (
            struct((2, CHUNKS, state_n, step), F32),
            struct((2 * rows, state_n), F32),
            struct((5 * heads, rows), F32),
        )
        + (struct((state_n, step), BF),) * CHUNKS
        + (struct((1, step), F32),) * CHUNKS,
        1.0,
        *proj,
        x,
        g,
        rate,
        bias,
        *([found[0][1, 1]] if ride else []),
    )
    first, decay = outs[:CHUNKS], outs[CHUNKS:]
    pairs = width // (2 * size) // PARTS
    span = width // PARTS
    shared = []

    def inner(q, *others):
        held = after(bc, *others) if others else bc
        square = struct((rows, rows), F32)
        block = pl.BlockSpec((rows, span), lambda _: (0, q))
        out = call(
            functools.partial(inner_kernel, q * pairs, pairs, size),
            ([square] if q == 0 else [])
            + [struct((rows, span), F32), square, struct((2, 2 * pairs, rows), F32)],
                2.6,
            held,
            hp,
            x,
            g,
            *shared,
            scratch=(pltpu.VMEM((rows, 2 * span), BF), pltpu.VMEM((rows, 2 * span), BF)),
            specs=[VMEM, VMEM, block, block] + [VMEM] * len(shared),
        )
        if q == 0:
            shared.append(out[0])
            out = out[1:]
        return out

    weights = [w_bc, w_dt]

    def beside(*others):
        for r in range(1, n_dp):
            weights.extend(cyclic(after(a, *others), "dp", r) for a in (w_bc, w_dt))
        return weights[2:], []

    def late(*others):
        if n_dp > 1:
            relay(found[1], groups[1], second, *others)

    if ride and n_dp > 1:
        spare += relay(found[1], groups[1], [(1, 1)])
    first[0] = after(first[0], *spare)
    riders = [f[1, 1] for f in found] if ride else []
    calls = [functools.partial(inner, q) for q in range(PARTS)]
    store, inners = chains(first, own, decay, calls, beside, riders, late)
    for f, a in zip(found, riders):
        f[0, 2] = a
    done = [relay(f, a, [t for t in slots if t not in f], store) for f, a in zip(found, groups)]
    grad_x, keep, give = call(
        functools.partial(outer_kernel, size, PARTS),
        (
            struct((rows, width), BF),
            struct((rows + heads, rows), F32),
            struct((rows, rows), F32),
        ),
        5.4,
        store,
        x,
        g,
        bc,
        hp,
        rate,
        *[a[0] for a in inners],
        *[a[1] for a in inners],
        *[a[2] for a in inners],
        scratch=(
            pltpu.VMEM((rows, 2 * width), BF),
            pltpu.VMEM((rows, 2 * width), BF),
            pltpu.VMEM((1, width), F32),
        ),
    )
    taken = after(cyclic(give, "head", 1), *[a for d in done for a in d])
    count = n_dp * n_seq
    copies = call(low_kernel, struct((count, rows + heads, rows), BF), 1.2, keep, taken)
    mine = copies[0]
    lows = lax.all_to_all(copies, ("seq", "dp"), 0, 0, tiled=True)
    other = cyclic(mine, "head", 1)
    grads = call(
        functools.partial(token_kernel, n_dp),
        struct((rows, width), BF),
        2.9,
        mine,
        other,
        *weights,
    )
    lows = after(lows, grads)
    swapped = cyclic(lows, "head", 1)
    toks = []
    for f, a in zip(found, groups):
        toks += [a] + [f[step] for step in slots]
    slots = [(0, 0)] + slots
    cols = 2 * (rows + heads)
    grad_bc, grad_dt = call(
        functools.partial(weight_kernel, 1.0 / (rows * n_seq * n_dp), n_dp, n_seq, slots),
        (struct((part, 2 * state_n), F32), struct((2 * heads, part), F32)),
        4.0,
        *toks,
        lows,
        swapped,
        specs=[HBM] * (len(toks) + 2),
        limit=56 * 1024 * 1024,
        scratch=(
            pltpu.VMEM((n_dp, n_seq * rows, part), BF),
            pltpu.VMEM((n_dp, cols, n_seq * rows), BF),
            pltpu.SemaphoreType.DMA((n_dp, len(slots))),
            pltpu.SemaphoreType.DMA((count, 2)),
        ),
    )
    return grad_x[None], grads[None], grad_bc, grad_dt.T


def solution(mesh):
    in_specs = (
        P(("grp", "dp"), "seq", "head"),
        P(("grp", "dp"), "seq", "head"),
        P(("grp", "dp"), "seq", "head"),
        P(("head", "dp"), None),
        P(("head", "dp"), None),
        P("head"),
        P("head"),
    )
    out_specs = (
        P(("grp", "dp"), "seq", "head"),
        P(("grp", "dp"), "seq", "head"),
        P(("grp", "head", "dp"), None),
        P(("grp", "head", "dp"), None),
    )
    return jax.shard_map(body, mesh=mesh, in_specs=in_specs, out_specs=out_specs, check_vma=False)
```

```python
import functools

import jax
import jax.numpy as jnp
from jax import lax
from jax.experimental import pallas as pl
from jax.experimental.pallas import tpu as pltpu
from jax.sharding import PartitionSpec as P

CHUNKS = 2
PARTS = 4
BF = jnp.bfloat16
F32 = jnp.float32
TOP = lax.Precision.HIGHEST
PER_US = 1.15e9
LIMIT = 16 * 1024 * 1024


def cyclic(a, axis, by):
    count = lax.axis_size(axis)
    return lax.ppermute(a, axis, [(i, (i + by) % count) for i in range(count)])


def mm(a, b, ca, cb, precision=None):
    return lax.dot_general(
        a, b, (((ca,), (cb,)), ((), ())), preferred_element_type=F32, precision=precision
    )


def halves(a):
    high = a.astype(BF)
    return high, (a - high.astype(F32)).astype(BF)


def head_lanes(heads, width, size, first=0):
    row = lax.broadcasted_iota(jnp.int32, (heads, width), 0)
    col = lax.broadcasted_iota(jnp.int32, (heads, width), 1) + first
    low = row * size
    return jnp.where((col >= low) & (col < low + size), 1.0, 0.0).astype(F32)


def spread(a, pick):
    high, low = halves(a)
    both = jnp.concatenate([pick, pick], axis=0)
    return mm(jnp.concatenate([high, low], axis=0), both, 0, 0)


VMEM = pl.BlockSpec(memory_space=pltpu.VMEM)
HBM = pl.BlockSpec(memory_space=pltpu.HBM)


def call(kernel, out_shape, span_us, *args, scratch=(), specs=None, out_specs=None, aliases={}, limit=LIMIT):
    size = sum(a.size * a.dtype.itemsize for a in args)
    return pl.pallas_call(
        kernel,
        out_shape=out_shape,
        grid=(1,),
        in_specs=specs or [VMEM] * len(args),
        out_specs=out_specs or jax.tree.map(lambda _: VMEM, out_shape),
        input_output_aliases=aliases,
        scratch_shapes=list(scratch),
        compiler_params=pltpu.CompilerParams(vmem_limit_bytes=limit),
        cost_estimate=pl.CostEstimate(
            flops=int(span_us * PER_US), bytes_accessed=size, transcendentals=0
        ),
    )(*args)


def struct(shape, dtype):
    return jax.ShapeDtypeStruct(shape, dtype)


def after(a, *others):
    return lax.optimization_barrier((a, others))[0]


def matchings(count):
    groups = [[(i, i + 1) for i in range(kind, count - 1, 2)] for kind in (0, 1)]
    pairs = []
    for group in groups:
        to = {i: i for i in range(count)}
        for i, j in group:
            to[i], to[j] = j, i
        pairs.append(sorted(to.items()))
    return groups, pairs


def split_kernel(a_ref, *outs):
    count = len(outs)
    me = lax.axis_index("dp")
    part = outs[0].shape[1]
    for r in range(count):
        at = pl.multiple_of(lax.rem(me + r, count) * part, 128)
        outs[r][...] = a_ref[:, pl.ds(at, part)]


def project_kernel(a_ref, bc_ref, dt_ref, out_ref):
    a = a_ref[...]
    state_n = bc_ref.shape[1] // 2
    rows = a.shape[0]
    bc = mm(a, bc_ref[...], 1, 0)
    out_ref[0:rows, :] = bc[:, :state_n]
    out_ref[rows : 2 * rows, :] = bc[:, state_n:]
    out_ref[2 * rows :, :] = mm(dt_ref[...], a, 1, 1)


def project(a, w_bc, w_dt):
    rows = a.shape[0]
    total = 2 * rows + w_dt.shape[0]
    return call(
        project_kernel,
        struct((total, w_bc.shape[1] // 2), F32),
        2.1,
        a,
        w_bc,
        w_dt,
    )


def state_kernel(count, size, ride, *refs):
    proj = refs[:count]
    x_ref, g_ref, rate_ref, bias_ref = refs[count : count + 4]
    riders = refs[count + 4 : count + 4 + ride]
    own_ref, bc_ref, hp_ref = refs[count + 4 + ride : count + 7 + ride]
    outs = refs[count + 7 + ride :]
    firsts, decays = outs[: len(outs) // 2], outs[len(outs) // 2 :]
    heads = rate_ref.shape[1]
    rows = x_ref.shape[0]
    rate, bias = rate_ref[...].T, bias_ref[...].T
    chunks, step = own_ref.shape[1], own_ref.shape[3]
    first = pl.multiple_of(2 * rows + lax.axis_index("head") * heads, 8)
    bc = proj[0][0 : 2 * rows, :]
    pre = proj[0][pl.ds(first, heads), :] + bias
    for ref in proj[1:]:
        bc = bc + ref[0 : 2 * rows, :]
        pre = pre + ref[pl.ds(first, heads), :]
    bc_ref[...] = bc
    dt = jnp.maximum(pre, 0.0) + jnp.log1p(jnp.exp(-jnp.abs(pre)))
    row = lax.broadcasted_iota(jnp.int32, (rows, rows), 0)
    col = lax.broadcasted_iota(jnp.int32, (rows, rows), 1)
    cum = mm(-dt * rate, jnp.where(row <= col, 1.0, 0.0), 1, 0, TOP)
    last = cum[:, rows - 1 : rows]
    grow = jnp.exp(cum)
    w = jnp.exp(last - cum) * dt
    decay = jnp.exp(last)
    for k, part in enumerate((pre, dt, cum, grow, w)):
        hp_ref[k * heads : (k + 1) * heads, :] = part
    place = lax.axis_index("seq")
    lowest = place == 0
    sides = []
    for vec in (bc[:rows], bc[rows:]):
        high, low = halves(vec.T)
        sides.append((jnp.concatenate([high, low], axis=1), high))
    for k in range(chunks):
        pick = head_lanes(heads, step, size, k * step)
        decays[k][...] = jnp.sum(pick * decay, axis=0, keepdims=True)
        pick = pick.astype(BF)
        both = []
        for kind, (scale, ref) in enumerate(((w, x_ref), (grow, g_ref))):
            wide, high = sides[kind]
            value = spread(scale, pick) * ref[:, k * step : (k + 1) * step].astype(F32)
            top, rest = halves(value)
            value = mm(wide, jnp.concatenate([top, top], axis=0), 1, 0) + mm(high, rest, 1, 0)
            own_ref[kind, k] = value
            both.append(value)
        firsts[k][...] = jnp.where(lowest, both[0], both[1]).astype(BF)
        if k < ride:
            rider = riders[k]

            @pl.when((place > 0) & (place < lax.axis_size("seq") - 1))
            def _():
                firsts[k][...] = rider[...]


def inner_kernel(first, pairs, size, bc_ref, hp_ref, x_ref, g_ref, *refs):
    gx_ref, ds_ref, sums_ref = refs[-5:-2]
    gy_ref, xg_ref = refs[-2:]
    rows = x_ref.shape[0]
    heads = hp_ref.shape[0] // 5
    lanes = 2 * size
    width = pairs * lanes
    if len(refs) == 6 and first > 0:
        scores = refs[0][...]
    else:
        scores = mm(bc_ref[rows : 2 * rows, :], bc_ref[0:rows, :], 1, 1, TOP)
        refs[0][...] = scores
    row = lax.broadcasted_iota(jnp.int32, (rows, rows), 0)
    col = lax.broadcasted_iota(jnp.int32, (rows, rows), 1)
    causal = row >= col
    dt = hp_ref[heads : 2 * heads, :]
    cum = hp_ref[2 * heads : 3 * heads, :]
    cum_t = cum.T
    lane = lax.broadcasted_iota(jnp.int32, (rows, lanes), 1)
    sides = [jnp.where(lane < size, 1.0, 0.0).astype(BF), jnp.where(lane < size, 0.0, 1.0).astype(BF)]
    ds = jnp.zeros((rows, rows), F32)
    for j in range(pairs):
        place = slice(j * lanes, (j + 1) * lanes)
        x, g = x_ref[:, place], g_ref[:, place]
        xs = jnp.concatenate([x * s for s in sides], axis=0)
        gs = jnp.concatenate([g * s for s in sides], axis=0)
        m = mm(gs, x, 1, 1)
        kern = []
        for i in range(2):
            h = 2 * (first + j) + i
            gap = cum_t[:, h : h + 1] - cum[h : h + 1, :]
            fall = jnp.exp(jnp.where(causal, gap, -jnp.inf)) * dt[h : h + 1, :]
            kern.append((fall * scores).astype(BF))
            ds = ds + fall * m[i * rows : (i + 1) * rows]
        y = mm(jnp.concatenate(kern, axis=1), xs, 1, 0)
        gx = mm(jnp.concatenate(kern, axis=0), gs, 0, 0)
        gx_ref[:, place] = gx
        late = slice(width + j * lanes, width + (j + 1) * lanes)
        gy_ref[:, place], gy_ref[:, late] = halves(g.astype(F32) * y)
        xg_ref[:, place], xg_ref[:, late] = halves(x.astype(F32) * gx)
    ds_ref[...] = ds
    pick = head_lanes(2 * pairs, width, size).astype(BF)
    pick = jnp.concatenate([pick, pick], axis=1)
    sums_ref[0] = mm(pick, gy_ref[...], 1, 1)
    sums_ref[1] = mm(pick, xg_ref[...], 1, 1)


def outer_kernel(k, chunks, size, parts, *refs):
    store_ref, x_ref, g_ref, bc_ref, hp_ref, rate_ref = refs[:6]
    gxs, dss, sums = (refs[6 + q * parts : 6 + (q + 1) * parts] for q in range(3))
    rest = refs[6 + 3 * parts :]
    wv_ref, eu_ref = rest[-2:]
    rows, step = x_ref.shape
    all_heads = rate_ref.shape[1]
    heads = all_heads // chunks
    mine = slice(k * heads, (k + 1) * heads)
    piece = step // parts
    b, c = bc_ref[0:rows, :], bc_ref[rows : 2 * rows, :]
    pre, dt, cum, grow, w = (
        hp_ref[q * all_heads + k * heads : q * all_heads + (k + 1) * heads, :] for q in range(5)
    )
    rate = rate_ref[...].T[mine]
    ds = dss[0][...]
    for ref in dss[1:]:
        ds = ds + ref[...]
    db = mm(c, ds, 0, 0, TOP)
    dc = mm(b, ds, 0, 1, TOP)
    b_wide = jnp.concatenate(halves(b), axis=1)
    c_wide = jnp.concatenate(halves(c), axis=1)
    pick = head_lanes(heads, step, size).astype(BF)
    incoming, outgoing = store_ref[0], store_ref[1]
    u = mm(c_wide, jnp.concatenate([incoming, incoming], axis=0), 1, 0)
    v = mm(b_wide, jnp.concatenate([outgoing, outgoing], axis=0), 1, 0)
    scale = spread(w, pick)
    wx = scale * x_ref[...].astype(F32)
    eg = spread(grow, pick) * g_ref[...].astype(F32)
    grad_ref = rest[-5] if k == chunks - 1 else rest[-4]
    for q in range(parts):
        place = slice(q * piece, (q + 1) * piece)
        grad_ref[:, place] = (gxs[q][...] + scale[:, place] * v[:, place]).astype(BF)
    wv_ref[:, :step], wv_ref[:, step:] = halves(wx * v)
    eu_ref[:, :step], eu_ref[:, step:] = halves(eg * u)
    db = db + mm(
        jnp.concatenate([outgoing, outgoing], axis=1), jnp.concatenate(halves(wx), axis=1), 1, 1
    )
    dc = dc + mm(
        jnp.concatenate([incoming, incoming], axis=1), jnp.concatenate(halves(eg), axis=1), 1, 1
    )
    both = jnp.sum(incoming.astype(F32) * outgoing.astype(F32), axis=0, keepdims=True)
    ddecay = jnp.sum(pick.astype(F32) * both, axis=1, keepdims=True)
    pick = jnp.concatenate([pick, pick], axis=1)
    wdw = mm(pick, wv_ref[...], 1, 1)
    egu = mm(pick, eu_ref[...], 1, 1)
    rowsum = jnp.concatenate([s[0] for s in sums], axis=0)
    colsum = jnp.concatenate([s[1] for s in sums], axis=0)
    dcum = rowsum - colsum + egu - wdw
    row = lax.broadcasted_iota(jnp.int32, (rows, rows), 0)
    col = lax.broadcasted_iota(jnp.int32, (rows, rows), 1)
    rev = mm(dcum, jnp.where(row >= col, 1.0, 0.0), 1, 0, TOP)
    decay = grow[:, rows - 1 : rows]
    rev = rev + jnp.sum(wdw, axis=1, keepdims=True) + decay * ddecay
    gate = 1.0 / (1.0 + jnp.exp(-pre))
    small = 1e-30
    ratio = jnp.where(dt > small, gate / jnp.maximum(dt, small), 1.0)
    graw = (colsum + wdw) * ratio - rate * rev * gate
    if k > 0:
        before_ref = rest[1]
        db = db + before_ref[0:rows, :]
        dc = dc + before_ref[rows : 2 * rows, :]
        graw = jnp.concatenate([before_ref[2 * rows :, :], graw], axis=0)
    if k == chunks - 1:
        keep_ref, give_ref = rest[-4], rest[-3]
        core = lax.axis_index("head")
        keep_ref[0:rows, :] = jnp.where(core == 0, db, dc)
        keep_ref[rows:, :] = graw
        give_ref[...] = jnp.where(core == 0, dc, db)
    else:
        back_ref = rest[-3]
        back_ref[0:rows, :] = db
        back_ref[rows : 2 * rows, :] = dc
        back_ref[2 * rows :, :] = graw


def low_kernel(keep_ref, taken_ref, out_ref):
    rows = taken_ref.shape[0]
    low = keep_ref[0:rows, :] + taken_ref[...]
    low = jnp.concatenate([low, keep_ref[rows:, :]], axis=0).astype(BF)
    for k in range(out_ref.shape[0]):
        out_ref[k] = low


def token_kernel(count, mine_ref, other_ref, *refs):
    out_ref = refs[2 * count]
    me, core = lax.axis_index("dp"), lax.axis_index("head")
    part, cols = refs[0].shape
    half = cols // 2
    heads = refs[1].shape[0] // 2
    for r in range(count):
        at = pl.multiple_of(lax.rem(me - r + count, count) * part, 128)
        total = None
        for k, ref in enumerate((mine_ref, other_ref)):
            at_col = pl.multiple_of(lax.rem(core + k, 2) * half, 128)
            at_row = pl.multiple_of(lax.rem(core + k, 2) * heads, 16)
            term = mm(ref[0:half, :], refs[2 * r][:, pl.ds(at_col, half)], 0, 1)
            term = term + mm(ref[half:, :], refs[2 * r + 1][pl.ds(at_row, heads), :], 0, 0)
            total = term if total is None else total + term
        out_ref[:, pl.ds(at, part)] = total.astype(BF)


def weight_kernel(scale, n_dp, n_seq, slots, *refs):
    count = 2 * len(slots) if n_dp > 1 else len(slots)
    toks, lows = refs[:count], refs[count:-6]
    bc_ref, dt_ref, tok_ref, low_ref, tok_sem, low_sem = refs[-6:]
    rows = toks[0].shape[0]
    share = lows[0].shape[1]
    core, place, me = lax.axis_index("head"), lax.axis_index("seq"), lax.axis_index("dp")
    even = lax.rem(place, 2) == 0
    copies = []
    for r in range(n_dp):
        for k, (kind, hop) in enumerate(slots):
            above = even if kind == 0 else ~even
            block = jnp.where(above, place + hop, place - hop)
            fits = (block >= 0) & (block < n_seq)
            if hop > 0 and kind == 1:
                fits = fits & jnp.where(above, place < n_seq - 1, place > 0)
            at = pl.multiple_of(jnp.clip(block, 0, n_seq - 1) * rows, 128)
            source = toks[k] if r == 0 else toks[len(slots) + k].at[pl.ds((r - 1) * rows, rows)]
            copy = pltpu.make_async_copy(source, tok_ref.at[r, pl.ds(at, rows)], tok_sem.at[r, k])
            copies.append((fits, copy))
    for r in range(n_dp):
        for s in range(n_seq):
            index = s * n_dp + lax.rem(me - r + n_dp, n_dp)
            for k in range(2):
                row = pl.multiple_of(lax.rem(core + k, 2) * share, 16)
                copy = pltpu.make_async_copy(
                    lows[k].at[index],
                    low_ref.at[r, pl.ds(row, share), pl.ds(s * rows, rows)],
                    low_sem.at[r * n_seq + s, k],
                )
                copies.append((None, copy))
    for fits, copy in copies:
        if fits is None:
            copy.start()
        else:
            pl.when(fits)(copy.start)
    for fits, copy in copies:
        if fits is None:
            copy.wait()
        else:
            pl.when(fits)(copy.wait)
    total = mm(low_ref[0], tok_ref[0], 1, 0)
    for r in range(1, n_dp):
        total = total + mm(low_ref[r], tok_ref[r], 1, 0)
    total = total * scale
    half = bc_ref.shape[1] // 2
    heads = dt_ref.shape[0] // 2
    for k in range(2):
        bc_ref[:, k * half : (k + 1) * half] = total[k * share : k * share + half].T
        dt_ref[k * heads : (k + 1) * heads, :] = total[k * share + half : (k + 1) * share]


def relays(count):
    groups, _ = matchings(count)
    return [
        (kind, hop)
        for hop in range(1, count)
        for kind in (0, 1)
        if any(i - hop + 1 >= 0 or j + hop - 1 < count for i, j in groups[kind])
    ]


def relay(found, block, steps, *others):
    count = lax.axis_size("seq")
    _, pairs = matchings(count)
    for kind, hop in steps:
        source = block if hop == 1 else found[1 - kind, hop - 1]
        source = after(source, *others) if others else source
        found[kind, hop] = lax.ppermute(source, "seq", pairs[kind])
    return [found[step] for step in steps]


def chains(first, own, decay, inner, beside, riders, late):
    count = lax.axis_size("seq")
    place = lax.axis_index("seq")
    chunks = len(first)
    stores = [jnp.zeros((3,) + own.shape[2:], BF) for _ in range(chunks)]
    got = list(first)
    done, todo, extra = [], list(inner), []
    last = count + chunks - 2
    for slot in range(1, last + 1):
        steps = [(hop, slot - hop) for hop in range(1, count) if 0 <= slot - hop < chunks]
        sent = []
        for hop, k in steps:
            value = got[k]
            if hop == 1 and 0 < k < len(riders):
                value = jnp.where((place == 0) | (place == count - 1), value, riders[k])
            if hop > 1:
                value = jnp.where(place == hop - 1, own[0, k], own[1, k])
                value = (value + decay[k] * got[k].astype(F32)).astype(BF)
            sent.append(value)
        for (hop, k), value in zip(steps, sent):
            to = {i: i for i in range(count)}
            for i in (hop - 1, count - hop - 1):
                to[i], to[i + 1] = i + 1, i
            got[k] = lax.ppermute(value, "seq", sorted(to.items()))
            if hop == 1 and k < len(riders):
                riders[k] = got[k]
        for _ in range(-(-len(todo) // (last + 1 - slot))):
            done.append(todo.pop(0)(*sent))
        if slot == 1:
            extra, soon = beside(*sent)
        if slot == last:
            late(*sent)
        if slot < last:
            held = [got[k] for _, k in steps] + [d[0] for d in done[-1:]]
            if slot == last - 1:
                held += extra
            if slot == 1:
                held += soon
            new = slot < chunks
            if new:
                held.append(got[slot])
            kept = lax.optimization_barrier(tuple(held))
            for (_, k), a in zip(steps, kept):
                got[k] = a
            if new:
                got[slot] = kept[-1]
        for hop, k in steps:
            kind = jnp.where(place == hop, 0, jnp.where(place == count - hop - 1, 1, 2))
            zero = jnp.zeros_like(kind)
            stores[k] = lax.dynamic_update_slice(stores[k], got[k][None], (kind, zero, zero))
    done += [make() for make in todo]
    return stores, done


def body(tokens, ssd_input, grad_out, w_bc, w_dt, decay_rate, dt_bias):
    feats, x, g = tokens[0], ssd_input[0], grad_out[0]
    rows, width = feats.shape
    heads = decay_rate.shape[0]
    size = width // heads
    n_dp, n_seq = lax.axis_size("dp"), lax.axis_size("seq")
    part = width // n_dp
    state_n = w_bc.shape[1] // 2
    w_dt = w_dt.T
    rate, bias = decay_rate[None], dt_bias[None]

    pieces = call(split_kernel, [struct((rows, part), BF)] * n_dp, 1.9, feats)
    items = [pieces[0]] + [cyclic(pieces[r], "dp", r) for r in range(1, n_dp)]
    groups = items[:1]
    if n_dp > 1:
        groups.append(items[1] if n_dp == 2 else jnp.concatenate(items[1:], axis=0))
    found = [{} for _ in groups]
    slots = relays(n_seq)
    step = width // CHUNKS
    ride = n_seq == 4 and all(a.shape == (state_n, step) for a in groups)
    second = [(kind, hop) for kind, hop in slots if hop == 2 and not (ride and kind == 0)]
    near = relay(found[0], groups[0], slots[:2])
    partials = [project(items[0], w_bc, w_dt)]
    for r in range(1, n_dp):
        item = after(items[r], partials[0])
        partials.append(cyclic(project(item, w_bc, w_dt), "dp", -r))
    if n_dp > 1:
        near += relay(found[1], groups[1], slots[: 1 if ride else 2])
    partials[1:] = [after(a, *near) for a in partials[1:]]
    proj = partials + [cyclic(a, "head", 1) for a in partials]
    spare = relay(found[0], groups[0], second)
    own, bc, hp, *outs = call(
        functools.partial(state_kernel, 2 * n_dp, size, int(ride)),
        (
            struct((2, CHUNKS, state_n, step), F32),
            struct((2 * rows, state_n), F32),
            struct((5 * heads, rows), F32),
        )
        + (struct((state_n, step), BF),) * CHUNKS
        + (struct((1, step), F32),) * CHUNKS,
        0.1,
        *proj,
        x,
        g,
        rate,
        bias,
        *([found[0][1, 1]] if ride else []),
    )
    first, decay = outs[:CHUNKS], outs[CHUNKS:]
    pairs = width // (2 * size) // PARTS
    span = width // PARTS
    shared = []

    def inner(q, *others):
        held = after(bc, *others) if others else bc
        square = struct((rows, rows), F32)
        block = pl.BlockSpec((rows, span), lambda _: (0, q))
        out = call(
            functools.partial(inner_kernel, q * pairs, pairs, size),
            ([square] if q == 0 else [])
            + [struct((rows, span), F32), square, struct((2, 2 * pairs, rows), F32)],
                2.6,
            held,
            hp,
            x,
            g,
            *shared,
            scratch=(pltpu.VMEM((rows, 2 * span), BF), pltpu.VMEM((rows, 2 * span), BF)),
            specs=[VMEM, VMEM, block, block] + [VMEM] * len(shared),
        )
        if q == 0:
            shared.append(out[0])
            out = out[1:]
        return out

    weights = [w_bc, w_dt]

    def beside(*others):
        for r in range(1, n_dp):
            weights.extend(cyclic(after(a, *others), "dp", r) for a in (w_bc, w_dt))
        if not ride or n_dp == 1:
            return weights[2:], []
        riders.extend(relay(found[1], groups[1], [(1, 1)], *others))
        return weights[2:], riders[1:]

    def late(*others):
        if n_dp > 1:
            relay(found[1], groups[1], second, *others)

    first[0] = after(first[0], *spare)
    riders = [found[0][1, 1]] if ride else []
    calls = [functools.partial(inner, q) for q in range(PARTS)]
    stores, inners = chains(first, own, decay, calls, beside, riders, late)
    for f, a in zip(found, riders):
        f[0, 2] = a
    done = [relay(f, a, [t for t in slots if t not in f], stores[-1]) for f, a in zip(found, groups)]
    each = PARTS // CHUNKS
    grad_x, back = None, []
    for k in range(CHUNKS):
        last = k == CHUNKS - 1
        block = pl.BlockSpec((rows, step), lambda _, k=k: (0, k))
        made = (k + 1) * (heads // CHUNKS)
        sums = (struct((rows + heads, rows), F32), struct((rows, rows), F32))
        inputs = [stores[k], x, g, bc, hp, rate]
        for q in range(3):
            inputs += [a[q] for a in inners[k * each : (k + 1) * each]]
        specs = [VMEM, block, block] + [VMEM] * (len(inputs) - 3)
        if k > 0:
            inputs += [grad_x] + back
            specs += [HBM, VMEM]
        grad_x, *back = call(
            functools.partial(outer_kernel, k, CHUNKS, size, each),
            (struct((rows, width), BF),)
            + (sums if last else (struct((2 * rows + made, rows), F32),)),
            5.4 / CHUNKS,
            *inputs,
            scratch=(pltpu.VMEM((rows, 2 * step), BF), pltpu.VMEM((rows, 2 * step), BF)),
            specs=specs,
            out_specs=(block,) + (VMEM,) * (2 if last else 1),
            aliases={len(inputs) - 2: 0} if k > 0 else {},
        )
    keep, give = back
    taken = after(cyclic(give, "head", 1), *[a for d in done for a in d])
    count = n_dp * n_seq
    copies = call(low_kernel, struct((count, rows + heads, rows), BF), 1.2, keep, taken)
    mine = copies[0]
    lows = lax.all_to_all(copies, ("seq", "dp"), 0, 0, tiled=True)
    other = cyclic(mine, "head", 1)
    grads = call(
        functools.partial(token_kernel, n_dp),
        struct((rows, width), BF),
        2.9,
        mine,
        other,
        *weights,
    )
    lows = after(lows, grads)
    swapped = cyclic(lows, "head", 1)
    toks = []
    for f, a in zip(found, groups):
        toks += [a] + [f[step] for step in slots]
    slots = [(0, 0)] + slots
    cols = 2 * (rows + heads)
    grad_bc, grad_dt = call(
        functools.partial(weight_kernel, 1.0 / (rows * n_seq * n_dp), n_dp, n_seq, slots),
        (struct((part, 2 * state_n), F32), struct((2 * heads, part), F32)),
        4.0,
        *toks,
        lows,
        swapped,
        specs=[HBM] * (len(toks) + 2),
        limit=56 * 1024 * 1024,
        scratch=(
            pltpu.VMEM((n_dp, n_seq * rows, part), BF),
            pltpu.VMEM((n_dp, cols, n_seq * rows), BF),
            pltpu.SemaphoreType.DMA((n_dp, len(slots))),
            pltpu.SemaphoreType.DMA((count, 2)),
        ),
    )
    return grad_x[None], grads[None], grad_bc, grad_dt.T


def solution(mesh):
    in_specs = (
        P(("grp", "dp"), "seq", "head"),
        P(("grp", "dp"), "seq", "head"),
        P(("grp", "dp"), "seq", "head"),
        P(("head", "dp"), None),
        P(("head", "dp"), None),
        P("head"),
        P("head"),
    )
    out_specs = (
        P(("grp", "dp"), "seq", "head"),
        P(("grp", "dp"), "seq", "head"),
        P(("grp", "head", "dp"), None),
        P(("grp", "head", "dp"), None),
    )
    return jax.shard_map(body, mesh=mesh, in_specs=in_specs, out_specs=out_specs, check_vma=False)
```

```python
import functools

import jax
import jax.numpy as jnp
from jax import lax
from jax.experimental import pallas as pl
from jax.experimental.pallas import tpu as pltpu
from jax.sharding import PartitionSpec as P

CHUNKS = 2
PARTS = 4
BF = jnp.bfloat16
F32 = jnp.float32
TOP = lax.Precision.HIGHEST
PER_US = 1.15e9
LIMIT = 16 * 1024 * 1024


def cyclic(a, axis, by):
    count = lax.axis_size(axis)
    return lax.ppermute(a, axis, [(i, (i + by) % count) for i in range(count)])


def mm(a, b, ca, cb, precision=None):
    return lax.dot_general(
        a, b, (((ca,), (cb,)), ((), ())), preferred_element_type=F32, precision=precision
    )


def halves(a):
    high = a.astype(BF)
    return high, (a - high.astype(F32)).astype(BF)


def head_lanes(heads, width, size, first=0):
    row = lax.broadcasted_iota(jnp.int32, (heads, width), 0)
    col = lax.broadcasted_iota(jnp.int32, (heads, width), 1) + first
    low = row * size
    return jnp.where((col >= low) & (col < low + size), 1.0, 0.0).astype(F32)


def spread(a, pick):
    high, low = halves(a)
    both = jnp.concatenate([pick, pick], axis=0)
    return mm(jnp.concatenate([high, low], axis=0), both, 0, 0)


VMEM = pl.BlockSpec(memory_space=pltpu.VMEM)
HBM = pl.BlockSpec(memory_space=pltpu.HBM)


def call(kernel, out_shape, span_us, *args, scratch=(), specs=None, out_specs=None, aliases={}, limit=LIMIT):
    size = sum(a.size * a.dtype.itemsize for a in args)
    return pl.pallas_call(
        kernel,
        out_shape=out_shape,
        grid=(1,),
        in_specs=specs or [VMEM] * len(args),
        out_specs=out_specs or jax.tree.map(lambda _: VMEM, out_shape),
        input_output_aliases=aliases,
        scratch_shapes=list(scratch),
        compiler_params=pltpu.CompilerParams(vmem_limit_bytes=limit),
        cost_estimate=pl.CostEstimate(
            flops=int(span_us * PER_US), bytes_accessed=size, transcendentals=0
        ),
    )(*args)


def struct(shape, dtype):
    return jax.ShapeDtypeStruct(shape, dtype)


def after(a, *others):
    return lax.optimization_barrier((a, others))[0]


def matchings(count):
    groups = [[(i, i + 1) for i in range(kind, count - 1, 2)] for kind in (0, 1)]
    pairs = []
    for group in groups:
        to = {i: i for i in range(count)}
        for i, j in group:
            to[i], to[j] = j, i
        pairs.append(sorted(to.items()))
    return groups, pairs


def split_kernel(a_ref, *outs):
    count = len(outs)
    me = lax.axis_index("dp")
    part = outs[0].shape[1]
    for r in range(count):
        at = pl.multiple_of(lax.rem(me + r, count) * part, 128)
        outs[r][...] = a_ref[:, pl.ds(at, part)]


def project_kernel(a_ref, bc_ref, dt_ref, out_ref):
    a = a_ref[...]
    state_n = bc_ref.shape[1] // 2
    rows = a.shape[0]
    bc = mm(a, bc_ref[...], 1, 0)
    out_ref[0:rows, :] = bc[:, :state_n]
    out_ref[rows : 2 * rows, :] = bc[:, state_n:]
    out_ref[2 * rows :, :] = mm(dt_ref[...], a, 1, 1)


def project(a, w_bc, w_dt):
    rows = a.shape[0]
    total = 2 * rows + w_dt.shape[0]
    return call(
        project_kernel,
        struct((total, w_bc.shape[1] // 2), F32),
        2.1,
        a,
        w_bc,
        w_dt,
    )


def state_kernel(count, size, ride, *refs):
    proj = refs[:count]
    x_ref, g_ref, rate_ref, bias_ref = refs[count : count + 4]
    riders = refs[count + 4 : count + 4 + ride]
    own_ref, bc_ref, hp_ref = refs[count + 4 + ride : count + 7 + ride]
    outs = refs[count + 7 + ride :]
    firsts, decays = outs[: len(outs) // 2], outs[len(outs) // 2 :]
    heads = rate_ref.shape[1]
    rows = x_ref.shape[0]
    rate, bias = rate_ref[...].T, bias_ref[...].T
    chunks, step = own_ref.shape[1], own_ref.shape[3]
    first = pl.multiple_of(2 * rows + lax.axis_index("head") * heads, 8)
    bc = proj[0][0 : 2 * rows, :]
    pre = proj[0][pl.ds(first, heads), :] + bias
    for ref in proj[1:]:
        bc = bc + ref[0 : 2 * rows, :]
        pre = pre + ref[pl.ds(first, heads), :]
    bc_ref[...] = bc
    dt = jnp.maximum(pre, 0.0) + jnp.log1p(jnp.exp(-jnp.abs(pre)))
    row = lax.broadcasted_iota(jnp.int32, (rows, rows), 0)
    col = lax.broadcasted_iota(jnp.int32, (rows, rows), 1)
    cum = mm(-dt * rate, jnp.where(row <= col, 1.0, 0.0), 1, 0, TOP)
    last = cum[:, rows - 1 : rows]
    grow = jnp.exp(cum)
    w = jnp.exp(last - cum) * dt
    decay = jnp.exp(last)
    for k, part in enumerate((pre, dt, cum, grow, w)):
        hp_ref[k * heads : (k + 1) * heads, :] = part
    place = lax.axis_index("seq")
    lowest = place == 0
    sides = []
    for vec in (bc[:rows], bc[rows:]):
        high, low = halves(vec.T)
        sides.append((jnp.concatenate([high, low], axis=1), high))
    for k in range(chunks):
        pick = head_lanes(heads, step, size, k * step)
        decays[k][...] = jnp.sum(pick * decay, axis=0, keepdims=True)
        pick = pick.astype(BF)
        both = []
        for kind, (scale, ref) in enumerate(((w, x_ref), (grow, g_ref))):
            wide, high = sides[kind]
            value = spread(scale, pick) * ref[:, k * step : (k + 1) * step].astype(F32)
            top, rest = halves(value)
            value = mm(wide, jnp.concatenate([top, top], axis=0), 1, 0) + mm(high, rest, 1, 0)
            own_ref[kind, k] = value
            both.append(value)
        firsts[k][...] = jnp.where(lowest, both[0], both[1]).astype(BF)
        if k < ride:
            rider = riders[k]

            @pl.when((place > 0) & (place < lax.axis_size("seq") - 1))
            def _():
                firsts[k][...] = rider[...]


def inner_kernel(first, pairs, size, bc_ref, hp_ref, x_ref, g_ref, *refs):
    gx_ref, ds_ref, sums_ref = refs[-5:-2]
    gy_ref, xg_ref = refs[-2:]
    rows = x_ref.shape[0]
    heads = hp_ref.shape[0] // 5
    lanes = 2 * size
    width = pairs * lanes
    if len(refs) == 6 and first > 0:
        scores = refs[0][...]
    else:
        scores = mm(bc_ref[rows : 2 * rows, :], bc_ref[0:rows, :], 1, 1, TOP)
        refs[0][...] = scores
    row = lax.broadcasted_iota(jnp.int32, (rows, rows), 0)
    col = lax.broadcasted_iota(jnp.int32, (rows, rows), 1)
    causal = row >= col
    dt = hp_ref[heads : 2 * heads, :]
    cum = hp_ref[2 * heads : 3 * heads, :]
    cum_t = cum.T
    lane = lax.broadcasted_iota(jnp.int32, (rows, lanes), 1)
    sides = [jnp.where(lane < size, 1.0, 0.0).astype(BF), jnp.where(lane < size, 0.0, 1.0).astype(BF)]
    ds = jnp.zeros((rows, rows), F32)
    for j in range(pairs):
        place = slice(j * lanes, (j + 1) * lanes)
        x, g = x_ref[:, place], g_ref[:, place]
        xs = jnp.concatenate([x * s for s in sides], axis=0)
        gs = jnp.concatenate([g * s for s in sides], axis=0)
        m = mm(gs, x, 1, 1)
        kern = []
        for i in range(2):
            h = 2 * (first + j) + i
            gap = cum_t[:, h : h + 1] - cum[h : h + 1, :]
            fall = jnp.exp(jnp.where(causal, gap, -jnp.inf)) * dt[h : h + 1, :]
            kern.append((fall * scores).astype(BF))
            ds = ds + fall * m[i * rows : (i + 1) * rows]
        y = mm(jnp.concatenate(kern, axis=1), xs, 1, 0)
        gx = mm(jnp.concatenate(kern, axis=0), gs, 0, 0)
        gx_ref[:, place] = gx
        late = slice(width + j * lanes, width + (j + 1) * lanes)
        gy_ref[:, place], gy_ref[:, late] = halves(g.astype(F32) * y)
        xg_ref[:, place], xg_ref[:, late] = halves(x.astype(F32) * gx)
    ds_ref[...] = ds
    pick = head_lanes(2 * pairs, width, size).astype(BF)
    pick = jnp.concatenate([pick, pick], axis=1)
    sums_ref[0] = mm(pick, gy_ref[...], 1, 1)
    sums_ref[1] = mm(pick, xg_ref[...], 1, 1)


def outer_kernel(k, chunks, size, parts, *refs):
    store_ref, x_ref, g_ref, bc_ref, hp_ref, rate_ref = refs[:6]
    gxs, dss, sums = (refs[6 + q * parts : 6 + (q + 1) * parts] for q in range(3))
    rest = refs[6 + 3 * parts :]
    wv_ref, eu_ref = rest[-2:]
    rows, step = x_ref.shape
    all_heads = rate_ref.shape[1]
    heads = all_heads // chunks
    mine = slice(k * heads, (k + 1) * heads)
    piece = step // parts
    b, c = bc_ref[0:rows, :], bc_ref[rows : 2 * rows, :]
    pre, dt, cum, grow, w = (
        hp_ref[q * all_heads + k * heads : q * all_heads + (k + 1) * heads, :] for q in range(5)
    )
    rate = rate_ref[...].T[mine]
    ds = dss[0][...]
    for ref in dss[1:]:
        ds = ds + ref[...]
    db = mm(c, ds, 0, 0, TOP)
    dc = mm(b, ds, 0, 1, TOP)
    b_wide = jnp.concatenate(halves(b), axis=1)
    c_wide = jnp.concatenate(halves(c), axis=1)
    pick = head_lanes(heads, step, size).astype(BF)
    incoming, outgoing = store_ref[0], store_ref[1]
    u = mm(c_wide, jnp.concatenate([incoming, incoming], axis=0), 1, 0)
    v = mm(b_wide, jnp.concatenate([outgoing, outgoing], axis=0), 1, 0)
    scale = spread(w, pick)
    wx = scale * x_ref[...].astype(F32)
    eg = spread(grow, pick) * g_ref[...].astype(F32)
    grad_ref = rest[-5] if k == chunks - 1 else rest[-4]
    for q in range(parts):
        place = slice(q * piece, (q + 1) * piece)
        grad_ref[:, place] = (gxs[q][...] + scale[:, place] * v[:, place]).astype(BF)
    wv_ref[:, :step], wv_ref[:, step:] = halves(wx * v)
    eu_ref[:, :step], eu_ref[:, step:] = halves(eg * u)
    db = db + mm(
        jnp.concatenate([outgoing, outgoing], axis=1), jnp.concatenate(halves(wx), axis=1), 1, 1
    )
    dc = dc + mm(
        jnp.concatenate([incoming, incoming], axis=1), jnp.concatenate(halves(eg), axis=1), 1, 1
    )
    both = jnp.sum(incoming.astype(F32) * outgoing.astype(F32), axis=0, keepdims=True)
    ddecay = jnp.sum(pick.astype(F32) * both, axis=1, keepdims=True)
    pick = jnp.concatenate([pick, pick], axis=1)
    wdw = mm(pick, wv_ref[...], 1, 1)
    egu = mm(pick, eu_ref[...], 1, 1)
    rowsum = jnp.concatenate([s[0] for s in sums], axis=0)
    colsum = jnp.concatenate([s[1] for s in sums], axis=0)
    dcum = rowsum - colsum + egu - wdw
    row = lax.broadcasted_iota(jnp.int32, (rows, rows), 0)
    col = lax.broadcasted_iota(jnp.int32, (rows, rows), 1)
    rev = mm(dcum, jnp.where(row >= col, 1.0, 0.0), 1, 0, TOP)
    decay = grow[:, rows - 1 : rows]
    rev = rev + jnp.sum(wdw, axis=1, keepdims=True) + decay * ddecay
    gate = 1.0 / (1.0 + jnp.exp(-pre))
    small = 1e-30
    ratio = jnp.where(dt > small, gate / jnp.maximum(dt, small), 1.0)
    graw = (colsum + wdw) * ratio - rate * rev * gate
    if k > 0:
        before_ref = rest[1]
        db = db + before_ref[0:rows, :]
        dc = dc + before_ref[rows : 2 * rows, :]
        graw = jnp.concatenate([before_ref[2 * rows :, :], graw], axis=0)
    if k == chunks - 1:
        keep_ref, give_ref = rest[-4], rest[-3]
        core = lax.axis_index("head")
        keep_ref[0:rows, :] = jnp.where(core == 0, db, dc)
        keep_ref[rows:, :] = graw
        give_ref[...] = jnp.where(core == 0, dc, db)
    else:
        back_ref = rest[-3]
        back_ref[0:rows, :] = db
        back_ref[rows : 2 * rows, :] = dc
        back_ref[2 * rows :, :] = graw


def low_kernel(keep_ref, taken_ref, out_ref):
    rows = taken_ref.shape[0]
    low = keep_ref[0:rows, :] + taken_ref[...]
    low = jnp.concatenate([low, keep_ref[rows:, :]], axis=0).astype(BF)
    for k in range(out_ref.shape[0]):
        out_ref[k] = low


def token_kernel(count, mine_ref, other_ref, *refs):
    out_ref = refs[2 * count]
    me, core = lax.axis_index("dp"), lax.axis_index("head")
    part, cols = refs[0].shape
    half = cols // 2
    heads = refs[1].shape[0] // 2
    for r in range(count):
        at = pl.multiple_of(lax.rem(me - r + count, count) * part, 128)
        total = None
        for k, ref in enumerate((mine_ref, other_ref)):
            at_col = pl.multiple_of(lax.rem(core + k, 2) * half, 128)
            at_row = pl.multiple_of(lax.rem(core + k, 2) * heads, 16)
            term = mm(ref[0:half, :], refs[2 * r][:, pl.ds(at_col, half)], 0, 1)
            term = term + mm(ref[half:, :], refs[2 * r + 1][pl.ds(at_row, heads), :], 0, 0)
            total = term if total is None else total + term
        out_ref[:, pl.ds(at, part)] = total.astype(BF)


def order_kernel(n_dp, n_seq, slots, *refs):
    out_ref, sem = refs[-2:]
    toks = refs[:-2]
    rows = toks[0].shape[0]
    place = lax.axis_index("seq")
    even = lax.rem(place, 2) == 0
    copies = []
    for r in range(n_dp):
        for k, (kind, hop) in enumerate(slots):
            above = even if kind == 0 else ~even
            block = jnp.where(above, place + hop, place - hop)
            fits = (block >= 0) & (block < n_seq)
            if hop > 0 and kind == 1:
                fits = fits & jnp.where(above, place < n_seq - 1, place > 0)
            at = pl.multiple_of(jnp.clip(block, 0, n_seq - 1) * rows, 128)
            source = toks[k] if r == 0 else toks[len(slots) + k].at[pl.ds((r - 1) * rows, rows)]
            copy = pltpu.make_async_copy(source, out_ref.at[r, pl.ds(at, rows)], sem.at[r, k])
            copies.append((fits, copy))
    for fits, copy in copies:
        pl.when(fits)(copy.start)
    for fits, copy in copies:
        pl.when(fits)(copy.wait)


def weight_kernel(scale, n_dp, n_seq, tok_ref, *refs):
    lows = refs[:2]
    bc_ref, dt_ref, low_ref, low_sem = refs[2:]
    rows = tok_ref.shape[1] // n_seq
    share = lows[0].shape[1]
    core, me = lax.axis_index("head"), lax.axis_index("dp")
    copies = []
    for r in range(n_dp):
        for s in range(n_seq):
            index = s * n_dp + lax.rem(me - r + n_dp, n_dp)
            for k in range(2):
                row = pl.multiple_of(lax.rem(core + k, 2) * share, 16)
                copies.append(
                    pltpu.make_async_copy(
                        lows[k].at[index],
                        low_ref.at[r, pl.ds(row, share), pl.ds(s * rows, rows)],
                        low_sem.at[r * n_seq + s, k],
                    )
                )
    for copy in copies:
        copy.start()
    for copy in copies:
        copy.wait()
    total = mm(low_ref[0], tok_ref[0], 1, 0)
    for r in range(1, n_dp):
        total = total + mm(low_ref[r], tok_ref[r], 1, 0)
    total = total * scale
    half = bc_ref.shape[1] // 2
    heads = dt_ref.shape[0] // 2
    for k in range(2):
        bc_ref[:, k * half : (k + 1) * half] = total[k * share : k * share + half].T
        dt_ref[k * heads : (k + 1) * heads, :] = total[k * share + half : (k + 1) * share]


def relays(count):
    groups, _ = matchings(count)
    return [
        (kind, hop)
        for hop in range(1, count)
        for kind in (0, 1)
        if any(i - hop + 1 >= 0 or j + hop - 1 < count for i, j in groups[kind])
    ]


def relay(found, block, steps, *others):
    count = lax.axis_size("seq")
    _, pairs = matchings(count)
    for kind, hop in steps:
        source = block if hop == 1 else found[1 - kind, hop - 1]
        source = after(source, *others) if others else source
        found[kind, hop] = lax.ppermute(source, "seq", pairs[kind])
    return [found[step] for step in steps]


def chains(first, own, decay, inner, beside, riders, late):
    count = lax.axis_size("seq")
    place = lax.axis_index("seq")
    chunks = len(first)
    stores = [jnp.zeros((3,) + own.shape[2:], BF) for _ in range(chunks)]
    got = list(first)
    done, todo, extra = [], list(inner), []
    last = count + chunks - 2
    for slot in range(1, last + 1):
        steps = [(hop, slot - hop) for hop in range(1, count) if 0 <= slot - hop < chunks]
        sent = []
        for hop, k in steps:
            value = got[k]
            if hop == 1 and 0 < k < len(riders):
                value = jnp.where((place == 0) | (place == count - 1), value, riders[k])
            if hop > 1:
                value = jnp.where(place == hop - 1, own[0, k], own[1, k])
                value = (value + decay[k] * got[k].astype(F32)).astype(BF)
            sent.append(value)
        for (hop, k), value in zip(steps, sent):
            to = {i: i for i in range(count)}
            for i in (hop - 1, count - hop - 1):
                to[i], to[i + 1] = i + 1, i
            got[k] = lax.ppermute(value, "seq", sorted(to.items()))
            if hop == 1 and k < len(riders):
                riders[k] = got[k]
        for _ in range(-(-len(todo) // (last + 1 - slot))):
            done.append(todo.pop(0)(*sent))
        if slot == 1:
            extra = beside(*sent)
        if slot == last:
            k = steps[-1][1]
            got[k] = after(got[k], *late(*sent))
        if slot < last:
            held = [got[k] for _, k in steps] + [d[0] for d in done[-1:]]
            if slot == last - 1:
                held += extra
            new = slot < chunks
            if new:
                held.append(got[slot])
            kept = lax.optimization_barrier(tuple(held))
            for (_, k), a in zip(steps, kept):
                got[k] = a
            if new:
                got[slot] = kept[-1]
        for hop, k in steps:
            kind = jnp.where(place == hop, 0, jnp.where(place == count - hop - 1, 1, 2))
            zero = jnp.zeros_like(kind)
            stores[k] = lax.dynamic_update_slice(stores[k], got[k][None], (kind, zero, zero))
    done += [make() for make in todo]
    return stores, done


def body(tokens, ssd_input, grad_out, w_bc, w_dt, decay_rate, dt_bias):
    feats, x, g = tokens[0], ssd_input[0], grad_out[0]
    rows, width = feats.shape
    heads = decay_rate.shape[0]
    size = width // heads
    n_dp, n_seq = lax.axis_size("dp"), lax.axis_size("seq")
    part = width // n_dp
    state_n = w_bc.shape[1] // 2
    w_dt = w_dt.T
    rate, bias = decay_rate[None], dt_bias[None]

    pieces = call(split_kernel, [struct((rows, part), BF)] * n_dp, 1.9, feats)
    items = [pieces[0]] + [cyclic(pieces[r], "dp", r) for r in range(1, n_dp)]
    groups = items[:1]
    if n_dp > 1:
        groups.append(items[1] if n_dp == 2 else jnp.concatenate(items[1:], axis=0))
    found = [{} for _ in groups]
    slots = relays(n_seq)
    step = width // CHUNKS
    ride = n_seq == 4 and all(a.shape == (state_n, step) for a in groups)
    second = [(kind, hop) for kind, hop in slots if hop == 2 and not (ride and kind == 0)]
    near = relay(found[0], groups[0], slots[:2])
    partials = [project(items[0], w_bc, w_dt)]
    for r in range(1, n_dp):
        item = after(items[r], partials[0])
        partials.append(cyclic(project(item, w_bc, w_dt), "dp", -r))
    if n_dp > 1:
        near += relay(found[1], groups[1], slots[: 1 if ride else 2])
    partials[1:] = [after(a, *near) for a in partials[1:]]
    proj = partials + [cyclic(a, "head", 1) for a in partials]
    spare = relay(found[1], groups[1], [(1, 1)]) if ride and n_dp > 1 else []
    own, bc, hp, *outs = call(
        functools.partial(state_kernel, 2 * n_dp, size, int(ride)),
        (
            struct((2, CHUNKS, state_n, step), F32),
            struct((2 * rows, state_n), F32),
            struct((5 * heads, rows), F32),
        )
        + (struct((state_n, step), BF),) * CHUNKS
        + (struct((1, step), F32),) * CHUNKS,
        0.1,
        *proj,
        x,
        g,
        rate,
        bias,
        *([found[0][1, 1]] if ride else []),
    )
    first, decay = outs[:CHUNKS], outs[CHUNKS:]
    pairs = width // (2 * size) // PARTS
    span = width // PARTS
    shared = []

    def inner(q, *others):
        held = after(bc, *others) if others else bc
        square = struct((rows, rows), F32)
        block = pl.BlockSpec((rows, span), lambda _: (0, q))
        out = call(
            functools.partial(inner_kernel, q * pairs, pairs, size),
            ([square] if q == 0 else [])
            + [struct((rows, span), F32), square, struct((2, 2 * pairs, rows), F32)],
                2.6,
            held,
            hp,
            x,
            g,
            *shared,
            scratch=(pltpu.VMEM((rows, 2 * span), BF), pltpu.VMEM((rows, 2 * span), BF)),
            specs=[VMEM, VMEM, block, block] + [VMEM] * len(shared),
        )
        if q == 0:
            shared.append(out[0])
            out = out[1:]
        return out

    weights = [w_bc, w_dt]

    def beside(*others):
        for r in range(1, n_dp):
            weights.extend(cyclic(after(a, *others), "dp", r) for a in (w_bc, w_dt))
        return weights[2:] + relay(found[0], groups[0], second, *others)

    def late(*others):
        return relay(found[1], groups[1], second, *others) if n_dp > 1 else []

    first[0] = after(first[0], *spare)
    riders = [f[1, 1] for f in found] if ride else []
    calls = [functools.partial(inner, q) for q in range(PARTS)]
    stores, inners = chains(first, own, decay, calls, beside, riders, late)
    for f, a in zip(found, riders):
        f[0, 2] = a
    done = [relay(f, a, [t for t in slots if t not in f], stores[-1]) for f, a in zip(found, groups)]
    each = PARTS // CHUNKS
    grad_x, back = None, []
    for k in range(CHUNKS):
        last = k == CHUNKS - 1
        block = pl.BlockSpec((rows, step), lambda _, k=k: (0, k))
        made = (k + 1) * (heads // CHUNKS)
        sums = (struct((rows + heads, rows), F32), struct((rows, rows), F32))
        inputs = [stores[k], x, g, bc, hp, rate]
        for q in range(3):
            inputs += [a[q] for a in inners[k * each : (k + 1) * each]]
        specs = [VMEM, block, block] + [VMEM] * (len(inputs) - 3)
        if k > 0:
            inputs += [grad_x] + back
            specs += [HBM, VMEM]
        grad_x, *back = call(
            functools.partial(outer_kernel, k, CHUNKS, size, each),
            (struct((rows, width), BF),)
            + (sums if last else (struct((2 * rows + made, rows), F32),)),
            5.4 / CHUNKS,
            *inputs,
            scratch=(pltpu.VMEM((rows, 2 * step), BF), pltpu.VMEM((rows, 2 * step), BF)),
            specs=specs,
            out_specs=(block,) + (VMEM,) * (2 if last else 1),
            aliases={len(inputs) - 2: 0} if k > 0 else {},
        )
    keep, give = back
    taken = after(cyclic(give, "head", 1), *[a for d in done for a in d])
    count = n_dp * n_seq
    copies = call(low_kernel, struct((count, rows + heads, rows), BF), 1.2, keep, taken)
    mine = copies[0]
    lows = lax.all_to_all(copies, ("seq", "dp"), 0, 0, tiled=True)
    other = cyclic(mine, "head", 1)
    grads = call(
        functools.partial(token_kernel, n_dp),
        struct((rows, width), BF),
        2.9,
        mine,
        other,
        *weights,
    )
    toks = []
    for f, a in zip(found, groups):
        toks += [a] + [f[step] for step in slots]
    slots = [(0, 0)] + slots
    ordered = call(
        functools.partial(order_kernel, n_dp, n_seq, slots),
        struct((n_dp, n_seq * rows, part), BF),
        1.0,
        *after(tuple(toks), copies),
        scratch=[pltpu.SemaphoreType.DMA((n_dp, len(slots)))],
    )
    lows = after(lows, grads, ordered)
    swapped = cyclic(lows, "head", 1)
    cols = 2 * (rows + heads)
    grad_bc, grad_dt = call(
        functools.partial(weight_kernel, 1.0 / (rows * n_seq * n_dp), n_dp, n_seq),
        (struct((part, 2 * state_n), F32), struct((2 * heads, part), F32)),
        4.0,
        ordered,
        lows,
        swapped,
        limit=LIMIT + 2 * n_dp * n_seq * rows * cols,
        scratch=(
            pltpu.VMEM((n_dp, cols, n_seq * rows), BF),
            pltpu.SemaphoreType.DMA((count, 2)),
        ),
    )
    return grad_x[None], grads[None], grad_bc, grad_dt.T


def solution(mesh):
    in_specs = (
        P(("grp", "dp"), "seq", "head"),
        P(("grp", "dp"), "seq", "head"),
        P(("grp", "dp"), "seq", "head"),
        P(("head", "dp"), None),
        P(("head", "dp"), None),
        P("head"),
        P("head"),
    )
    out_specs = (
        P(("grp", "dp"), "seq", "head"),
        P(("grp", "dp"), "seq", "head"),
        P(("grp", "head", "dp"), None),
        P(("grp", "head", "dp"), None),
    )
    return jax.shard_map(body, mesh=mesh, in_specs=in_specs, out_specs=out_specs, check_vma=False)
```

```python
import functools

import jax
import jax.numpy as jnp
from jax import lax
from jax.experimental import pallas as pl
from jax.experimental.pallas import tpu as pltpu
from jax.sharding import PartitionSpec as P

CHUNKS = 2
PARTS = 4
BF = jnp.bfloat16
F32 = jnp.float32
TOP = lax.Precision.HIGHEST
PER_US = 1.15e9
LIMIT = 16 * 1024 * 1024


def cyclic(a, axis, by):
    count = lax.axis_size(axis)
    return lax.ppermute(a, axis, [(i, (i + by) % count) for i in range(count)])


def mm(a, b, ca, cb, precision=None):
    return lax.dot_general(
        a, b, (((ca,), (cb,)), ((), ())), preferred_element_type=F32, precision=precision
    )


def halves(a):
    high = a.astype(BF)
    return high, (a - high.astype(F32)).astype(BF)


def head_lanes(heads, width, size, first=0):
    row = lax.broadcasted_iota(jnp.int32, (heads, width), 0)
    col = lax.broadcasted_iota(jnp.int32, (heads, width), 1) + first
    low = row * size
    return jnp.where((col >= low) & (col < low + size), 1.0, 0.0).astype(F32)


def spread(a, pick):
    high, low = halves(a)
    both = jnp.concatenate([pick, pick], axis=0)
    return mm(jnp.concatenate([high, low], axis=0), both, 0, 0)


VMEM = pl.BlockSpec(memory_space=pltpu.VMEM)
HBM = pl.BlockSpec(memory_space=pltpu.HBM)


def call(kernel, out_shape, span_us, *args, scratch=(), specs=None, out_specs=None, aliases={}, limit=LIMIT):
    size = sum(a.size * a.dtype.itemsize for a in args)
    return pl.pallas_call(
        kernel,
        out_shape=out_shape,
        grid=(1,),
        in_specs=specs or [VMEM] * len(args),
        out_specs=out_specs or jax.tree.map(lambda _: VMEM, out_shape),
        input_output_aliases=aliases,
        scratch_shapes=list(scratch),
        compiler_params=pltpu.CompilerParams(vmem_limit_bytes=limit),
        cost_estimate=pl.CostEstimate(
            flops=int(span_us * PER_US), bytes_accessed=size, transcendentals=0
        ),
    )(*args)


def struct(shape, dtype):
    return jax.ShapeDtypeStruct(shape, dtype)


def after(a, *others):
    return lax.optimization_barrier((a, others))[0]


def matchings(count):
    groups = [[(i, i + 1) for i in range(kind, count - 1, 2)] for kind in (0, 1)]
    pairs = []
    for group in groups:
        to = {i: i for i in range(count)}
        for i, j in group:
            to[i], to[j] = j, i
        pairs.append(sorted(to.items()))
    return groups, pairs


def split_kernel(a_ref, *outs):
    count = len(outs)
    me = lax.axis_index("dp")
    part = outs[0].shape[1]
    for r in range(count):
        at = pl.multiple_of(lax.rem(me + r, count) * part, 128)
        outs[r][...] = a_ref[:, pl.ds(at, part)]


def project_kernel(a_ref, bc_ref, dt_ref, out_ref):
    a = a_ref[...]
    state_n = bc_ref.shape[1] // 2
    rows = a.shape[0]
    heads = dt_ref.shape[0]
    bc = mm(a, bc_ref[...], 1, 0).astype(out_ref.dtype)
    raw = mm(dt_ref[...], a, 1, 1)
    out_ref[0:rows, :] = bc[:, :state_n]
    out_ref[rows : 2 * rows, :] = bc[:, state_n:]
    if out_ref.dtype == BF:
        high, low = halves(raw)
        out_ref[2 * rows : 2 * rows + heads, :] = high
        out_ref[2 * rows + heads :, :] = low
    else:
        out_ref[2 * rows :, :] = raw


def project(a, w_bc, w_dt, dtype):
    rows = a.shape[0]
    total = 2 * rows + w_dt.shape[0] * (2 if dtype == BF else 1)
    return call(
        project_kernel,
        struct((total, w_bc.shape[1] // 2), dtype),
        2.1,
        a,
        w_bc,
        w_dt,
    )


def state_kernel(count, size, ride, *refs):
    proj = refs[:count]
    x_ref, g_ref, rate_ref, bias_ref = refs[count : count + 4]
    riders = refs[count + 4 : count + 4 + ride]
    own_ref, bc_ref, hp_ref = refs[count + 4 + ride : count + 7 + ride]
    outs = refs[count + 7 + ride :]
    firsts, decays = outs[: len(outs) // 2], outs[len(outs) // 2 :]
    heads = rate_ref.shape[1]
    rows = x_ref.shape[0]
    rate, bias = rate_ref[...].T, bias_ref[...].T
    chunks, step = own_ref.shape[1], own_ref.shape[3]
    first = pl.multiple_of(2 * rows + lax.axis_index("head") * heads, 16)
    bc = proj[0][0 : 2 * rows, :]
    pre = proj[0][pl.ds(first, heads), :] + bias
    for ref in proj[1:]:
        bc = bc + ref[0 : 2 * rows, :].astype(F32)
        pre = pre + ref[pl.ds(first, heads), :].astype(F32)
        if ref.dtype == BF:
            low = pl.multiple_of(first + (ref.shape[0] - 2 * rows) // 2, 16)
            pre = pre + ref[pl.ds(low, heads), :].astype(F32)
    bc_ref[...] = bc
    dt = jnp.maximum(pre, 0.0) + jnp.log1p(jnp.exp(-jnp.abs(pre)))
    row = lax.broadcasted_iota(jnp.int32, (rows, rows), 0)
    col = lax.broadcasted_iota(jnp.int32, (rows, rows), 1)
    cum = mm(-dt * rate, jnp.where(row <= col, 1.0, 0.0), 1, 0, TOP)
    last = cum[:, rows - 1 : rows]
    grow = jnp.exp(cum)
    w = jnp.exp(last - cum) * dt
    decay = jnp.exp(last)
    for k, part in enumerate((pre, dt, cum, grow, w)):
        hp_ref[k * heads : (k + 1) * heads, :] = part
    place = lax.axis_index("seq")
    lowest = place == 0
    sides = []
    for vec in (bc[:rows], bc[rows:]):
        high, low = halves(vec.T)
        sides.append((jnp.concatenate([high, low], axis=1), high))
    for k in range(chunks):
        pick = head_lanes(heads, step, size, k * step)
        decays[k][...] = jnp.sum(pick * decay, axis=0, keepdims=True)
        pick = pick.astype(BF)
        both = []
        for kind, (scale, ref) in enumerate(((w, x_ref), (grow, g_ref))):
            wide, high = sides[kind]
            value = spread(scale, pick) * ref[:, k * step : (k + 1) * step].astype(F32)
            top, rest = halves(value)
            value = mm(wide, jnp.concatenate([top, top], axis=0), 1, 0) + mm(high, rest, 1, 0)
            own_ref[kind, k] = value
            both.append(value)
        firsts[k][...] = jnp.where(lowest, both[0], both[1]).astype(BF)
        if k < ride:
            rider = riders[k]

            @pl.when((place > 0) & (place < lax.axis_size("seq") - 1))
            def _():
                firsts[k][...] = rider[...]


def inner_kernel(first, pairs, size, bc_ref, hp_ref, x_ref, g_ref, *refs):
    gx_ref, ds_ref, sums_ref = refs[-5:-2]
    gy_ref, xg_ref = refs[-2:]
    rows = x_ref.shape[0]
    heads = hp_ref.shape[0] // 5
    lanes = 2 * size
    width = pairs * lanes
    if len(refs) == 6 and first > 0:
        scores = refs[0][...]
    else:
        scores = mm(bc_ref[rows : 2 * rows, :], bc_ref[0:rows, :], 1, 1, TOP)
        refs[0][...] = scores
    row = lax.broadcasted_iota(jnp.int32, (rows, rows), 0)
    col = lax.broadcasted_iota(jnp.int32, (rows, rows), 1)
    causal = row >= col
    dt = hp_ref[heads : 2 * heads, :]
    cum = hp_ref[2 * heads : 3 * heads, :]
    cum_t = cum.T
    lane = lax.broadcasted_iota(jnp.int32, (rows, lanes), 1)
    sides = [jnp.where(lane < size, 1.0, 0.0).astype(BF), jnp.where(lane < size, 0.0, 1.0).astype(BF)]
    ds = jnp.zeros((rows, rows), F32)
    for j in range(pairs):
        place = slice(j * lanes, (j + 1) * lanes)
        x, g = x_ref[:, place], g_ref[:, place]
        xs = jnp.concatenate([x * s for s in sides], axis=0)
        gs = jnp.concatenate([g * s for s in sides], axis=0)
        m = mm(gs, x, 1, 1)
        kern = []
        for i in range(2):
            h = 2 * (first + j) + i
            gap = cum_t[:, h : h + 1] - cum[h : h + 1, :]
            fall = jnp.exp(jnp.where(causal, gap, -jnp.inf)) * dt[h : h + 1, :]
            kern.append((fall * scores).astype(BF))
            ds = ds + fall * m[i * rows : (i + 1) * rows]
        y = mm(jnp.concatenate(kern, axis=1), xs, 1, 0)
        gx = mm(jnp.concatenate(kern, axis=0), gs, 0, 0)
        gx_ref[:, place] = gx
        late = slice(width + j * lanes, width + (j + 1) * lanes)
        gy_ref[:, place], gy_ref[:, late] = halves(g.astype(F32) * y)
        xg_ref[:, place], xg_ref[:, late] = halves(x.astype(F32) * gx)
    ds_ref[...] = ds
    pick = head_lanes(2 * pairs, width, size).astype(BF)
    pick = jnp.concatenate([pick, pick], axis=1)
    sums_ref[0] = mm(pick, gy_ref[...], 1, 1)
    sums_ref[1] = mm(pick, xg_ref[...], 1, 1)


def outer_kernel(k, chunks, size, parts, *refs):
    store_ref, x_ref, g_ref, bc_ref, hp_ref, rate_ref = refs[:6]
    gxs, dss, sums = (refs[6 + q * parts : 6 + (q + 1) * parts] for q in range(3))
    rest = refs[6 + 3 * parts :]
    wv_ref, eu_ref = rest[-2:]
    rows, step = x_ref.shape
    all_heads = rate_ref.shape[1]
    heads = all_heads // chunks
    mine = slice(k * heads, (k + 1) * heads)
    piece = step // parts
    b, c = bc_ref[0:rows, :], bc_ref[rows : 2 * rows, :]
    pre, dt, cum, grow, w = (
        hp_ref[q * all_heads + k * heads : q * all_heads + (k + 1) * heads, :] for q in range(5)
    )
    rate = rate_ref[...].T[mine]
    ds = dss[0][...]
    for ref in dss[1:]:
        ds = ds + ref[...]
    db = mm(c, ds, 0, 0, TOP)
    dc = mm(b, ds, 0, 1, TOP)
    b_wide = jnp.concatenate(halves(b), axis=1)
    c_wide = jnp.concatenate(halves(c), axis=1)
    pick = head_lanes(heads, step, size).astype(BF)
    incoming, outgoing = store_ref[0], store_ref[1]
    u = mm(c_wide, jnp.concatenate([incoming, incoming], axis=0), 1, 0)
    v = mm(b_wide, jnp.concatenate([outgoing, outgoing], axis=0), 1, 0)
    scale = spread(w, pick)
    wx = scale * x_ref[...].astype(F32)
    eg = spread(grow, pick) * g_ref[...].astype(F32)
    grad_ref = rest[-5] if k == chunks - 1 else rest[-4]
    for q in range(parts):
        place = slice(q * piece, (q + 1) * piece)
        grad_ref[:, place] = (gxs[q][...] + scale[:, place] * v[:, place]).astype(BF)
    wv_ref[:, :step], wv_ref[:, step:] = halves(wx * v)
    eu_ref[:, :step], eu_ref[:, step:] = halves(eg * u)
    db = db + mm(
        jnp.concatenate([outgoing, outgoing], axis=1), jnp.concatenate(halves(wx), axis=1), 1, 1
    )
    dc = dc + mm(
        jnp.concatenate([incoming, incoming], axis=1), jnp.concatenate(halves(eg), axis=1), 1, 1
    )
    both = jnp.sum(incoming.astype(F32) * outgoing.astype(F32), axis=0, keepdims=True)
    ddecay = jnp.sum(pick.astype(F32) * both, axis=1, keepdims=True)
    pick = jnp.concatenate([pick, pick], axis=1)
    wdw = mm(pick, wv_ref[...], 1, 1)
    egu = mm(pick, eu_ref[...], 1, 1)
    rowsum = jnp.concatenate([s[0] for s in sums], axis=0)
    colsum = jnp.concatenate([s[1] for s in sums], axis=0)
    dcum = rowsum - colsum + egu - wdw
    row = lax.broadcasted_iota(jnp.int32, (rows, rows), 0)
    col = lax.broadcasted_iota(jnp.int32, (rows, rows), 1)
    rev = mm(dcum, jnp.where(row >= col, 1.0, 0.0), 1, 0, TOP)
    decay = grow[:, rows - 1 : rows]
    rev = rev + jnp.sum(wdw, axis=1, keepdims=True) + decay * ddecay
    gate = 1.0 / (1.0 + jnp.exp(-pre))
    small = 1e-30
    ratio = jnp.where(dt > small, gate / jnp.maximum(dt, small), 1.0)
    graw = (colsum + wdw) * ratio - rate * rev * gate
    if k > 0:
        before_ref = rest[1]
        db = db + before_ref[0:rows, :]
        dc = dc + before_ref[rows : 2 * rows, :]
        graw = jnp.concatenate([before_ref[2 * rows :, :], graw], axis=0)
    if k == chunks - 1:
        keep_ref, give_ref = rest[-4], rest[-3]
        core = lax.axis_index("head")
        keep_ref[0:rows, :] = jnp.where(core == 0, db, dc)
        keep_ref[rows:, :] = graw
        give_ref[...] = jnp.where(core == 0, dc, db)
    else:
        back_ref = rest[-3]
        back_ref[0:rows, :] = db
        back_ref[rows : 2 * rows, :] = dc
        back_ref[2 * rows :, :] = graw


def low_kernel(keep_ref, taken_ref, out_ref):
    rows = taken_ref.shape[0]
    low = keep_ref[0:rows, :] + taken_ref[...]
    low = jnp.concatenate([low, keep_ref[rows:, :]], axis=0).astype(BF)
    for k in range(out_ref.shape[0]):
        out_ref[k] = low


def token_kernel(count, mine_ref, other_ref, *refs):
    out_ref = refs[2 * count]
    me, core = lax.axis_index("dp"), lax.axis_index("head")
    part, cols = refs[0].shape
    half = cols // 2
    heads = refs[1].shape[0] // 2
    for r in range(count):
        at = pl.multiple_of(lax.rem(me - r + count, count) * part, 128)
        total = None
        for k, ref in enumerate((mine_ref, other_ref)):
            at_col = pl.multiple_of(lax.rem(core + k, 2) * half, 128)
            at_row = pl.multiple_of(lax.rem(core + k, 2) * heads, 16)
            term = mm(ref[0:half, :], refs[2 * r][:, pl.ds(at_col, half)], 0, 1)
            term = term + mm(ref[half:, :], refs[2 * r + 1][pl.ds(at_row, heads), :], 0, 0)
            total = term if total is None else total + term
        out_ref[:, pl.ds(at, part)] = total.astype(BF)


def order_kernel(n_dp, n_seq, slots, *refs):
    out_ref, sem = refs[-2:]
    toks = refs[:-2]
    rows = toks[0].shape[0]
    place = lax.axis_index("seq")
    even = lax.rem(place, 2) == 0
    copies = []
    for r in range(n_dp):
        for k, (kind, hop) in enumerate(slots):
            above = even if kind == 0 else ~even
            block = jnp.where(above, place + hop, place - hop)
            fits = (block >= 0) & (block < n_seq)
            if hop > 0 and kind == 1:
                fits = fits & jnp.where(above, place < n_seq - 1, place > 0)
            at = pl.multiple_of(jnp.clip(block, 0, n_seq - 1) * rows, 128)
            source = toks[k] if r == 0 else toks[len(slots) + k].at[pl.ds((r - 1) * rows, rows)]
            copy = pltpu.make_async_copy(source, out_ref.at[r, pl.ds(at, rows)], sem.at[r, k])
            copies.append((fits, copy))
    for fits, copy in copies:
        pl.when(fits)(copy.start)
    for fits, copy in copies:
        pl.when(fits)(copy.wait)


def weight_kernel(scale, n_dp, n_seq, tok_ref, *refs):
    lows = refs[:2]
    bc_ref, dt_ref, low_ref, low_sem = refs[2:]
    rows = tok_ref.shape[1] // n_seq
    share = lows[0].shape[1]
    core, me = lax.axis_index("head"), lax.axis_index("dp")
    copies = []
    for r in range(n_dp):
        for s in range(n_seq):
            index = s * n_dp + lax.rem(me - r + n_dp, n_dp)
            for k in range(2):
                row = pl.multiple_of(lax.rem(core + k, 2) * share, 16)
                copies.append(
                    pltpu.make_async_copy(
                        lows[k].at[index],
                        low_ref.at[r, pl.ds(row, share), pl.ds(s * rows, rows)],
                        low_sem.at[r * n_seq + s, k],
                    )
                )
    for copy in copies:
        copy.start()
    for copy in copies:
        copy.wait()
    total = mm(low_ref[0], tok_ref[0], 1, 0)
    for r in range(1, n_dp):
        total = total + mm(low_ref[r], tok_ref[r], 1, 0)
    total = total * scale
    half = bc_ref.shape[1] // 2
    heads = dt_ref.shape[0] // 2
    for k in range(2):
        bc_ref[:, k * half : (k + 1) * half] = total[k * share : k * share + half].T
        dt_ref[k * heads : (k + 1) * heads, :] = total[k * share + half : (k + 1) * share]


def relays(count):
    groups, _ = matchings(count)
    return [
        (kind, hop)
        for hop in range(1, count)
        for kind in (0, 1)
        if any(i - hop + 1 >= 0 or j + hop - 1 < count for i, j in groups[kind])
    ]


def relay(found, block, steps, *others):
    count = lax.axis_size("seq")
    _, pairs = matchings(count)
    for kind, hop in steps:
        source = block if hop == 1 else found[1 - kind, hop - 1]
        source = after(source, *others) if others else source
        found[kind, hop] = lax.ppermute(source, "seq", pairs[kind])
    return [found[step] for step in steps]


def chains(first, own, decay, inner, beside, riders, late):
    count = lax.axis_size("seq")
    place = lax.axis_index("seq")
    chunks = len(first)
    stores = [jnp.zeros((3,) + own.shape[2:], BF) for _ in range(chunks)]
    got = list(first)
    done, todo, extra = [], list(inner), []
    last = count + chunks - 2
    for slot in range(1, last + 1):
        steps = [(hop, slot - hop) for hop in range(1, count) if 0 <= slot - hop < chunks]
        sent = []
        for hop, k in steps:
            value = got[k]
            if hop == 1 and 0 < k < len(riders):
                value = jnp.where((place == 0) | (place == count - 1), value, riders[k])
            if hop > 1:
                value = jnp.where(place == hop - 1, own[0, k], own[1, k])
                value = (value + decay[k] * got[k].astype(F32)).astype(BF)
            sent.append(value)
        for (hop, k), value in zip(steps, sent):
            to = {i: i for i in range(count)}
            for i in (hop - 1, count - hop - 1):
                to[i], to[i + 1] = i + 1, i
            got[k] = lax.ppermute(value, "seq", sorted(to.items()))
            if hop == 1 and k < len(riders):
                riders[k] = got[k]
        for _ in range(-(-len(todo) // (last + 1 - slot))):
            done.append(todo.pop(0)(*sent))
        if slot == 1:
            extra = beside(*sent)
        if slot == last:
            k = steps[-1][1]
            got[k] = after(got[k], *late(*sent))
        if slot < last:
            held = [got[k] for _, k in steps] + [d[0] for d in done[-1:]]
            if slot == last - 1:
                held += extra
            new = slot < chunks
            if new:
                held.append(got[slot])
            kept = lax.optimization_barrier(tuple(held))
            for (_, k), a in zip(steps, kept):
                got[k] = a
            if new:
                got[slot] = kept[-1]
        for hop, k in steps:
            kind = jnp.where(place == hop, 0, jnp.where(place == count - hop - 1, 1, 2))
            zero = jnp.zeros_like(kind)
            stores[k] = lax.dynamic_update_slice(stores[k], got[k][None], (kind, zero, zero))
    done += [make() for make in todo]
    return stores, done


def body(tokens, ssd_input, grad_out, w_bc, w_dt, decay_rate, dt_bias):
    feats, x, g = tokens[0], ssd_input[0], grad_out[0]
    rows, width = feats.shape
    heads = decay_rate.shape[0]
    size = width // heads
    n_dp, n_seq = lax.axis_size("dp"), lax.axis_size("seq")
    part = width // n_dp
    state_n = w_bc.shape[1] // 2
    w_dt = w_dt.T
    rate, bias = decay_rate[None], dt_bias[None]

    pieces = call(split_kernel, [struct((rows, part), BF)] * n_dp, 1.9, feats)
    items = [pieces[0]] + [cyclic(pieces[r], "dp", r) for r in range(1, n_dp)]
    groups = items[:1]
    if n_dp > 1:
        groups.append(items[1] if n_dp == 2 else jnp.concatenate(items[1:], axis=0))
    found = [{} for _ in groups]
    slots = relays(n_seq)
    step = width // CHUNKS
    ride = n_seq == 4 and all(a.shape == (state_n, step) for a in groups)
    second = [(kind, hop) for kind, hop in slots if hop == 2 and not (ride and kind == 0)]
    near = relay(found[0], groups[0], slots[:2])
    partials = [project(items[0], w_bc, w_dt, F32)]
    for r in range(1, n_dp):
        item = after(items[r], partials[0])
        partials.append(cyclic(project(item, w_bc, w_dt, BF), "dp", -r))
    if n_dp > 1:
        near += relay(found[1], groups[1], slots[: 1 if ride else 2])
    partials[1:] = [after(a, *near) for a in partials[1:]]
    proj = partials + [cyclic(a, "head", 1) for a in partials]
    spare = relay(found[1], groups[1], [(1, 1)]) if ride and n_dp > 1 else []
    own, bc, hp, *outs = call(
        functools.partial(state_kernel, 2 * n_dp, size, int(ride)),
        (
            struct((2, CHUNKS, state_n, step), F32),
            struct((2 * rows, state_n), F32),
            struct((5 * heads, rows), F32),
        )
        + (struct((state_n, step), BF),) * CHUNKS
        + (struct((1, step), F32),) * CHUNKS,
        0.1,
        *proj,
        x,
        g,
        rate,
        bias,
        *([found[0][1, 1]] if ride else []),
    )
    first, decay = outs[:CHUNKS], outs[CHUNKS:]
    pairs = width // (2 * size) // PARTS
    span = width // PARTS
    shared = []

    def inner(q, *others):
        held = after(bc, *others) if others else bc
        square = struct((rows, rows), F32)
        block = pl.BlockSpec((rows, span), lambda _: (0, q))
        out = call(
            functools.partial(inner_kernel, q * pairs, pairs, size),
            ([square] if q == 0 else [])
            + [struct((rows, span), F32), square, struct((2, 2 * pairs, rows), F32)],
                2.6,
            held,
            hp,
            x,
            g,
            *shared,
            scratch=(pltpu.VMEM((rows, 2 * span), BF), pltpu.VMEM((rows, 2 * span), BF)),
            specs=[VMEM, VMEM, block, block] + [VMEM] * len(shared),
        )
        if q == 0:
            shared.append(out[0])
            out = out[1:]
        return out

    weights = [w_bc, w_dt]

    def beside(*others):
        for r in range(1, n_dp):
            weights.extend(cyclic(after(a, *others), "dp", r) for a in (w_bc, w_dt))
        return weights[2:] + relay(found[0], groups[0], second, *others)

    def late(*others):
        return relay(found[1], groups[1], second, *others) if n_dp > 1 else []

    first[0] = after(first[0], *spare)
    riders = [f[1, 1] for f in found] if ride else []
    calls = [functools.partial(inner, q) for q in range(PARTS)]
    stores, inners = chains(first, own, decay, calls, beside, riders, late)
    for f, a in zip(found, riders):
        f[0, 2] = a
    each = PARTS // CHUNKS
    grad_x, back = None, []
    for k in range(CHUNKS):
        last = k == CHUNKS - 1
        block = pl.BlockSpec((rows, step), lambda _, k=k: (0, k))
        made = (k + 1) * (heads // CHUNKS)
        sums = (struct((rows + heads, rows), F32), struct((rows, rows), F32))
        inputs = [stores[k], x, g, bc, hp, rate]
        for q in range(3):
            inputs += [a[q] for a in inners[k * each : (k + 1) * each]]
        specs = [VMEM, block, block] + [VMEM] * (len(inputs) - 3)
        if k > 0:
            inputs += [grad_x] + back
            specs += [HBM, VMEM]
        grad_x, *back = call(
            functools.partial(outer_kernel, k, CHUNKS, size, each),
            (struct((rows, width), BF),)
            + (sums if last else (struct((2 * rows + made, rows), F32),)),
            5.4 / CHUNKS,
            *inputs,
            scratch=(pltpu.VMEM((rows, 2 * step), BF), pltpu.VMEM((rows, 2 * step), BF)),
            specs=specs,
            out_specs=(block,) + (VMEM,) * (2 if last else 1),
            aliases={len(inputs) - 2: 0} if k > 0 else {},
        )
    keep, give = back
    taken = cyclic(give, "head", 1)
    count = n_dp * n_seq
    copies = call(low_kernel, struct((count, rows + heads, rows), BF), 1.2, keep, taken)
    mine = copies[0]
    for f, a in zip(found, groups):
        relay(f, a, [t for t in slots if t not in f], copies)
    lows = lax.all_to_all(copies, ("seq", "dp"), 0, 0, tiled=True)
    other = cyclic(mine, "head", 1)
    grads = call(
        functools.partial(token_kernel, n_dp),
        struct((rows, width), BF),
        2.9,
        mine,
        other,
        *weights,
    )
    toks = []
    for f, a in zip(found, groups):
        toks += [a] + [f[step] for step in slots]
    slots = [(0, 0)] + slots
    ordered = call(
        functools.partial(order_kernel, n_dp, n_seq, slots),
        struct((n_dp, n_seq * rows, part), BF),
        1.0,
        *after(tuple(toks), copies),
        scratch=[pltpu.SemaphoreType.DMA((n_dp, len(slots)))],
    )
    lows = after(lows, grads, ordered)
    swapped = cyclic(lows, "head", 1)
    cols = 2 * (rows + heads)
    grad_bc, grad_dt = call(
        functools.partial(weight_kernel, 1.0 / (rows * n_seq * n_dp), n_dp, n_seq),
        (struct((part, 2 * state_n), F32), struct((2 * heads, part), F32)),
        4.0,
        ordered,
        lows,
        swapped,
        limit=LIMIT + 2 * n_dp * n_seq * rows * cols,
        scratch=(
            pltpu.VMEM((n_dp, cols, n_seq * rows), BF),
            pltpu.SemaphoreType.DMA((count, 2)),
        ),
    )
    return grad_x[None], grads[None], grad_bc, grad_dt.T


def solution(mesh):
    in_specs = (
        P(("grp", "dp"), "seq", "head"),
        P(("grp", "dp"), "seq", "head"),
        P(("grp", "dp"), "seq", "head"),
        P(("head", "dp"), None),
        P(("head", "dp"), None),
        P("head"),
        P("head"),
    )
    out_specs = (
        P(("grp", "dp"), "seq", "head"),
        P(("grp", "dp"), "seq", "head"),
        P(("grp", "head", "dp"), None),
        P(("grp", "head", "dp"), None),
    )
    return jax.shard_map(body, mesh=mesh, in_specs=in_specs, out_specs=out_specs, check_vma=False)
```

```python
import functools

import jax
import jax.numpy as jnp
from jax import lax
from jax.experimental import pallas as pl
from jax.experimental.pallas import tpu as pltpu
from jax.sharding import PartitionSpec as P

CHUNKS = 2
PARTS = 4
BF = jnp.bfloat16
F32 = jnp.float32
TOP = lax.Precision.HIGHEST
PER_US = 1.15e9
LIMIT = 16 * 1024 * 1024


def cyclic(a, axis, by):
    count = lax.axis_size(axis)
    return lax.ppermute(a, axis, [(i, (i + by) % count) for i in range(count)])


def mm(a, b, ca, cb, precision=None):
    return lax.dot_general(
        a, b, (((ca,), (cb,)), ((), ())), preferred_element_type=F32, precision=precision
    )


def halves(a):
    high = a.astype(BF)
    return high, (a - high.astype(F32)).astype(BF)


def head_lanes(heads, width, size, first=0):
    row = lax.broadcasted_iota(jnp.int32, (heads, width), 0)
    col = lax.broadcasted_iota(jnp.int32, (heads, width), 1) + first
    low = row * size
    return jnp.where((col >= low) & (col < low + size), 1.0, 0.0).astype(F32)


def spread(a, pick):
    high, low = halves(a)
    both = jnp.concatenate([pick, pick], axis=0)
    return mm(jnp.concatenate([high, low], axis=0), both, 0, 0)


VMEM = pl.BlockSpec(memory_space=pltpu.VMEM)
HBM = pl.BlockSpec(memory_space=pltpu.HBM)


def call(kernel, out_shape, span_us, *args, scratch=(), specs=None, out_specs=None, aliases={}, limit=LIMIT):
    size = sum(a.size * a.dtype.itemsize for a in args)
    return pl.pallas_call(
        kernel,
        out_shape=out_shape,
        grid=(1,),
        in_specs=specs or [VMEM] * len(args),
        out_specs=out_specs or jax.tree.map(lambda _: VMEM, out_shape),
        input_output_aliases=aliases,
        scratch_shapes=list(scratch),
        compiler_params=pltpu.CompilerParams(vmem_limit_bytes=limit),
        cost_estimate=pl.CostEstimate(
            flops=int(span_us * PER_US), bytes_accessed=size, transcendentals=0
        ),
    )(*args)


def struct(shape, dtype):
    return jax.ShapeDtypeStruct(shape, dtype)


def after(a, *others):
    return lax.optimization_barrier((a, others))[0]


def matchings(count):
    groups = [[(i, i + 1) for i in range(kind, count - 1, 2)] for kind in (0, 1)]
    pairs = []
    for group in groups:
        to = {i: i for i in range(count)}
        for i, j in group:
            to[i], to[j] = j, i
        pairs.append(sorted(to.items()))
    return groups, pairs


def split_kernel(a_ref, *outs):
    count = len(outs)
    me = lax.axis_index("dp")
    part = outs[0].shape[1]
    for r in range(count):
        at = pl.multiple_of(lax.rem(me + r, count) * part, 128)
        outs[r][...] = a_ref[:, pl.ds(at, part)]


def project_kernel(a_ref, bc_ref, dt_ref, out_ref):
    a = a_ref[...]
    state_n = bc_ref.shape[1] // 2
    rows = a.shape[0]
    bc = mm(a, bc_ref[...], 1, 0)
    out_ref[0:rows, :] = bc[:, :state_n]
    out_ref[rows : 2 * rows, :] = bc[:, state_n:]
    out_ref[2 * rows :, :] = mm(dt_ref[...], a, 1, 1)


def project(a, w_bc, w_dt):
    rows = a.shape[0]
    total = 2 * rows + w_dt.shape[0]
    return call(
        project_kernel,
        struct((total, w_bc.shape[1] // 2), F32),
        2.1,
        a,
        w_bc,
        w_dt,
    )


def state_kernel(count, size, ride, *refs):
    proj = refs[:count]
    x_ref, g_ref, rate_ref, bias_ref = refs[count : count + 4]
    riders = refs[count + 4 : count + 4 + ride]
    own_ref, bc_ref, hp_ref = refs[count + 4 + ride : count + 7 + ride]
    outs = refs[count + 7 + ride :]
    firsts, decays = outs[: len(outs) // 2], outs[len(outs) // 2 :]
    heads = rate_ref.shape[1]
    rows = x_ref.shape[0]
    rate, bias = rate_ref[...].T, bias_ref[...].T
    chunks, step = own_ref.shape[1], own_ref.shape[3]
    first = pl.multiple_of(2 * rows + lax.axis_index("head") * heads, 8)
    bc = proj[0][0 : 2 * rows, :]
    pre = proj[0][pl.ds(first, heads), :] + bias
    for ref in proj[1:]:
        bc = bc + ref[0 : 2 * rows, :]
        pre = pre + ref[pl.ds(first, heads), :]
    bc_ref[...] = bc
    dt = jnp.maximum(pre, 0.0) + jnp.log1p(jnp.exp(-jnp.abs(pre)))
    row = lax.broadcasted_iota(jnp.int32, (rows, rows), 0)
    col = lax.broadcasted_iota(jnp.int32, (rows, rows), 1)
    cum = mm(-dt * rate, jnp.where(row <= col, 1.0, 0.0), 1, 0, TOP)
    last = cum[:, rows - 1 : rows]
    grow = jnp.exp(cum)
    w = jnp.exp(last - cum) * dt
    decay = jnp.exp(last)
    for k, part in enumerate((pre, dt, cum, grow, w)):
        hp_ref[k * heads : (k + 1) * heads, :] = part
    place = lax.axis_index("seq")
    lowest = place == 0
    sides = []
    for vec in (bc[:rows], bc[rows:]):
        high, low = halves(vec.T)
        sides.append((jnp.concatenate([high, low], axis=1), high))
    for k in range(chunks):
        pick = head_lanes(heads, step, size, k * step)
        decays[k][...] = jnp.sum(pick * decay, axis=0, keepdims=True)
        pick = pick.astype(BF)
        both = []
        for kind, (scale, ref) in enumerate(((w, x_ref), (grow, g_ref))):
            wide, high = sides[kind]
            value = spread(scale, pick) * ref[:, k * step : (k + 1) * step].astype(F32)
            top, rest = halves(value)
            value = mm(wide, jnp.concatenate([top, top], axis=0), 1, 0) + mm(high, rest, 1, 0)
            own_ref[kind, k] = value
            both.append(value)
        firsts[k][...] = jnp.where(lowest, both[0], both[1]).astype(BF)
        if k < ride:
            rider = riders[k]

            @pl.when((place > 0) & (place < lax.axis_size("seq") - 1))
            def _():
                firsts[k][...] = rider[...]


def inner_kernel(first, pairs, size, bc_ref, hp_ref, x_ref, g_ref, *refs):
    gx_ref, ds_ref, sums_ref = refs[-5:-2]
    gy_ref, xg_ref = refs[-2:]
    rows = x_ref.shape[0]
    heads = hp_ref.shape[0] // 5
    lanes = 2 * size
    width = pairs * lanes
    if len(refs) == 6 and first > 0:
        scores = refs[0][...]
    else:
        scores = mm(bc_ref[rows : 2 * rows, :], bc_ref[0:rows, :], 1, 1, TOP)
        refs[0][...] = scores
    row = lax.broadcasted_iota(jnp.int32, (rows, rows), 0)
    col = lax.broadcasted_iota(jnp.int32, (rows, rows), 1)
    causal = row >= col
    dt = hp_ref[heads : 2 * heads, :]
    cum = hp_ref[2 * heads : 3 * heads, :]
    cum_t = cum.T
    lane = lax.broadcasted_iota(jnp.int32, (rows, lanes), 1)
    sides = [jnp.where(lane < size, 1.0, 0.0).astype(BF), jnp.where(lane < size, 0.0, 1.0).astype(BF)]
    ds = jnp.zeros((rows, rows), F32)
    for j in range(pairs):
        place = slice(j * lanes, (j + 1) * lanes)
        x, g = x_ref[:, place], g_ref[:, place]
        xs = jnp.concatenate([x * s for s in sides], axis=0)
        gs = jnp.concatenate([g * s for s in sides], axis=0)
        m = mm(gs, x, 1, 1)
        kern = []
        for i in range(2):
            h = 2 * (first + j) + i
            gap = cum_t[:, h : h + 1] - cum[h : h + 1, :]
            fall = jnp.exp(jnp.where(causal, gap, -jnp.inf)) * dt[h : h + 1, :]
            kern.append((fall * scores).astype(BF))
            ds = ds + fall * m[i * rows : (i + 1) * rows]
        y = mm(jnp.concatenate(kern, axis=1), xs, 1, 0)
        gx = mm(jnp.concatenate(kern, axis=0), gs, 0, 0)
        gx_ref[:, place] = gx
        late = slice(width + j * lanes, width + (j + 1) * lanes)
        gy_ref[:, place], gy_ref[:, late] = halves(g.astype(F32) * y)
        xg_ref[:, place], xg_ref[:, late] = halves(x.astype(F32) * gx)
    ds_ref[...] = ds
    pick = head_lanes(2 * pairs, width, size).astype(BF)
    pick = jnp.concatenate([pick, pick], axis=1)
    sums_ref[0] = mm(pick, gy_ref[...], 1, 1)
    sums_ref[1] = mm(pick, xg_ref[...], 1, 1)


def outer_kernel(k, chunks, size, parts, *refs):
    store_ref, x_ref, g_ref, bc_ref, hp_ref, rate_ref = refs[:6]
    gxs, dss, sums = (refs[6 + q * parts : 6 + (q + 1) * parts] for q in range(3))
    rest = refs[6 + 3 * parts :]
    wv_ref, eu_ref = rest[-2:]
    rows, step = x_ref.shape
    all_heads = rate_ref.shape[1]
    heads = all_heads // chunks
    mine = slice(k * heads, (k + 1) * heads)
    piece = step // parts
    b, c = bc_ref[0:rows, :], bc_ref[rows : 2 * rows, :]
    pre, dt, cum, grow, w = (
        hp_ref[q * all_heads + k * heads : q * all_heads + (k + 1) * heads, :] for q in range(5)
    )
    rate = rate_ref[...].T[mine]
    ds = dss[0][...]
    for ref in dss[1:]:
        ds = ds + ref[...]
    db = mm(c, ds, 0, 0, TOP)
    dc = mm(b, ds, 0, 1, TOP)
    b_wide = jnp.concatenate(halves(b), axis=1)
    c_wide = jnp.concatenate(halves(c), axis=1)
    pick = head_lanes(heads, step, size).astype(BF)
    incoming, outgoing = store_ref[0], store_ref[1]
    u = mm(c_wide, jnp.concatenate([incoming, incoming], axis=0), 1, 0)
    v = mm(b_wide, jnp.concatenate([outgoing, outgoing], axis=0), 1, 0)
    scale = spread(w, pick)
    wx = scale * x_ref[...].astype(F32)
    eg = spread(grow, pick) * g_ref[...].astype(F32)
    grad_ref = rest[-5] if k == chunks - 1 else rest[-4]
    for q in range(parts):
        place = slice(q * piece, (q + 1) * piece)
        grad_ref[:, place] = (gxs[q][...] + scale[:, place] * v[:, place]).astype(BF)
    wv_ref[:, :step], wv_ref[:, step:] = halves(wx * v)
    eu_ref[:, :step], eu_ref[:, step:] = halves(eg * u)
    db = db + mm(
        jnp.concatenate([outgoing, outgoing], axis=1), jnp.concatenate(halves(wx), axis=1), 1, 1
    )
    dc = dc + mm(
        jnp.concatenate([incoming, incoming], axis=1), jnp.concatenate(halves(eg), axis=1), 1, 1
    )
    both = jnp.sum(incoming.astype(F32) * outgoing.astype(F32), axis=0, keepdims=True)
    ddecay = jnp.sum(pick.astype(F32) * both, axis=1, keepdims=True)
    pick = jnp.concatenate([pick, pick], axis=1)
    wdw = mm(pick, wv_ref[...], 1, 1)
    egu = mm(pick, eu_ref[...], 1, 1)
    rowsum = jnp.concatenate([s[0] for s in sums], axis=0)
    colsum = jnp.concatenate([s[1] for s in sums], axis=0)
    dcum = rowsum - colsum + egu - wdw
    row = lax.broadcasted_iota(jnp.int32, (rows, rows), 0)
    col = lax.broadcasted_iota(jnp.int32, (rows, rows), 1)
    rev = mm(dcum, jnp.where(row >= col, 1.0, 0.0), 1, 0, TOP)
    decay = grow[:, rows - 1 : rows]
    rev = rev + jnp.sum(wdw, axis=1, keepdims=True) + decay * ddecay
    gate = 1.0 / (1.0 + jnp.exp(-pre))
    small = 1e-30
    ratio = jnp.where(dt > small, gate / jnp.maximum(dt, small), 1.0)
    graw = (colsum + wdw) * ratio - rate * rev * gate
    if k > 0:
        before_ref = rest[1]
        db = db + before_ref[0:rows, :]
        dc = dc + before_ref[rows : 2 * rows, :]
        graw = jnp.concatenate([before_ref[2 * rows :, :], graw], axis=0)
    if k == chunks - 1:
        keep_ref, give_ref = rest[-4], rest[-3]
        core = lax.axis_index("head")
        keep_ref[0:rows, :] = jnp.where(core == 0, db, dc)
        keep_ref[rows:, :] = graw
        give_ref[...] = jnp.where(core == 0, dc, db)
    else:
        back_ref = rest[-3]
        back_ref[0:rows, :] = db
        back_ref[rows : 2 * rows, :] = dc
        back_ref[2 * rows :, :] = graw


def low_kernel(keep_ref, taken_ref, out_ref):
    rows = taken_ref.shape[0]
    low = keep_ref[0:rows, :] + taken_ref[...]
    low = jnp.concatenate([low, keep_ref[rows:, :]], axis=0).astype(BF)
    for k in range(out_ref.shape[0]):
        out_ref[k] = low


def token_kernel(count, mine_ref, other_ref, *refs):
    out_ref = refs[2 * count]
    me, core = lax.axis_index("dp"), lax.axis_index("head")
    part, cols = refs[0].shape
    half = cols // 2
    heads = refs[1].shape[0] // 2
    for r in range(count):
        at = pl.multiple_of(lax.rem(me - r + count, count) * part, 128)
        total = None
        for k, ref in enumerate((mine_ref, other_ref)):
            at_col = pl.multiple_of(lax.rem(core + k, 2) * half, 128)
            at_row = pl.multiple_of(lax.rem(core + k, 2) * heads, 16)
            term = mm(ref[0:half, :], refs[2 * r][:, pl.ds(at_col, half)], 0, 1)
            term = term + mm(ref[half:, :], refs[2 * r + 1][pl.ds(at_row, heads), :], 0, 0)
            total = term if total is None else total + term
        out_ref[:, pl.ds(at, part)] = total.astype(BF)


def order_kernel(n_dp, n_seq, slots, *refs):
    out_ref, sem = refs[-2:]
    toks = refs[:-2]
    rows = toks[0].shape[0]
    place = lax.axis_index("seq")
    even = lax.rem(place, 2) == 0
    copies = []
    for r in range(n_dp):
        for k, (kind, hop) in enumerate(slots):
            above = even if kind == 0 else ~even
            block = jnp.where(above, place + hop, place - hop)
            fits = (block >= 0) & (block < n_seq)
            if hop > 0 and kind == 1:
                fits = fits & jnp.where(above, place < n_seq - 1, place > 0)
            at = pl.multiple_of(jnp.clip(block, 0, n_seq - 1) * rows, 128)
            source = toks[k] if r == 0 else toks[len(slots) + k].at[pl.ds((r - 1) * rows, rows)]
            copy = pltpu.make_async_copy(source, out_ref.at[r, pl.ds(at, rows)], sem.at[r, k])
            copies.append((fits, copy))
    for fits, copy in copies:
        pl.when(fits)(copy.start)
    for fits, copy in copies:
        pl.when(fits)(copy.wait)


def weight_kernel(scale, n_dp, n_seq, tok_ref, *refs):
    lows = refs[:2]
    bc_ref, dt_ref, low_ref, low_sem = refs[2:]
    rows = tok_ref.shape[1] // n_seq
    share = lows[0].shape[1]
    core, me = lax.axis_index("head"), lax.axis_index("dp")
    copies = []
    for r in range(n_dp):
        for s in range(n_seq):
            index = s * n_dp + lax.rem(me - r + n_dp, n_dp)
            for k in range(2):
                row = pl.multiple_of(lax.rem(core + k, 2) * share, 16)
                copies.append(
                    pltpu.make_async_copy(
                        lows[k].at[index],
                        low_ref.at[r, pl.ds(row, share), pl.ds(s * rows, rows)],
                        low_sem.at[r * n_seq + s, k],
                    )
                )
    for copy in copies:
        copy.start()
    for copy in copies:
        copy.wait()
    total = mm(low_ref[0], tok_ref[0], 1, 0)
    for r in range(1, n_dp):
        total = total + mm(low_ref[r], tok_ref[r], 1, 0)
    total = total * scale
    half = bc_ref.shape[1] // 2
    heads = dt_ref.shape[0] // 2
    for k in range(2):
        bc_ref[:, k * half : (k + 1) * half] = total[k * share : k * share + half].T
        dt_ref[k * heads : (k + 1) * heads, :] = total[k * share + half : (k + 1) * share]


def relays(count):
    groups, _ = matchings(count)
    return [
        (kind, hop)
        for hop in range(1, count)
        for kind in (0, 1)
        if any(i - hop + 1 >= 0 or j + hop - 1 < count for i, j in groups[kind])
    ]


def relay(found, block, steps, *others):
    count = lax.axis_size("seq")
    _, pairs = matchings(count)
    for kind, hop in steps:
        source = block if hop == 1 else found[1 - kind, hop - 1]
        source = after(source, *others) if others else source
        found[kind, hop] = lax.ppermute(source, "seq", pairs[kind])
    return [found[step] for step in steps]


def chains(first, own, decay, inner, beside, riders, late):
    count = lax.axis_size("seq")
    place = lax.axis_index("seq")
    chunks = len(first)
    stores = [jnp.zeros((3,) + own.shape[2:], BF) for _ in range(chunks)]
    got = list(first)
    done, todo, extra = [], list(inner), []
    last = count + chunks - 2
    for slot in range(1, last + 1):
        steps = [(hop, slot - hop) for hop in range(1, count) if 0 <= slot - hop < chunks]
        sent = []
        for hop, k in steps:
            value = got[k]
            if hop == 1 and 0 < k < len(riders):
                value = jnp.where((place == 0) | (place == count - 1), value, riders[k])
            if hop > 1:
                value = jnp.where(place == hop - 1, own[0, k], own[1, k])
                value = (value + decay[k] * got[k].astype(F32)).astype(BF)
            sent.append(value)
        for (hop, k), value in zip(steps, sent):
            to = {i: i for i in range(count)}
            for i in (hop - 1, count - hop - 1):
                to[i], to[i + 1] = i + 1, i
            got[k] = lax.ppermute(value, "seq", sorted(to.items()))
            if hop == 1 and k < len(riders):
                riders[k] = got[k]
        for _ in range(-(-len(todo) // (last + 1 - slot))):
            done.append(todo.pop(0)(*sent))
        if slot == 1:
            extra = beside(*sent)
        if slot == last:
            k = steps[-1][1]
            got[k] = after(got[k], *late(*sent))
        if slot < last:
            held = [got[k] for _, k in steps] + [d[0] for d in done[-1:]]
            if slot == last - 1:
                held += extra
            new = slot < chunks
            if new:
                held.append(got[slot])
            kept = lax.optimization_barrier(tuple(held))
            for (_, k), a in zip(steps, kept):
                got[k] = a
            if new:
                got[slot] = kept[-1]
        for hop, k in steps:
            kind = jnp.where(place == hop, 0, jnp.where(place == count - hop - 1, 1, 2))
            zero = jnp.zeros_like(kind)
            stores[k] = lax.dynamic_update_slice(stores[k], got[k][None], (kind, zero, zero))
    done += [make() for make in todo]
    return stores, done


def body(tokens, ssd_input, grad_out, w_bc, w_dt, decay_rate, dt_bias):
    feats, x, g = tokens[0], ssd_input[0], grad_out[0]
    rows, width = feats.shape
    heads = decay_rate.shape[0]
    size = width // heads
    n_dp, n_seq = lax.axis_size("dp"), lax.axis_size("seq")
    part = width // n_dp
    state_n = w_bc.shape[1] // 2
    w_dt = w_dt.T
    rate, bias = decay_rate[None], dt_bias[None]

    pieces = call(split_kernel, [struct((rows, part), BF)] * n_dp, 1.9, feats)
    items = [pieces[0]] + [cyclic(pieces[r], "dp", r) for r in range(1, n_dp)]
    groups = items[:1]
    if n_dp > 1:
        groups.append(items[1] if n_dp == 2 else jnp.concatenate(items[1:], axis=0))
    found = [{} for _ in groups]
    slots = relays(n_seq)
    step = width // CHUNKS
    ride = n_seq == 4 and all(a.shape == (state_n, step) for a in groups)
    second = [(kind, hop) for kind, hop in slots if hop == 2 and not (ride and kind == 0)]
    near = relay(found[0], groups[0], slots[:2])
    partials = [project(items[0], w_bc, w_dt)]
    for r in range(1, n_dp):
        item = after(items[r], partials[0])
        partials.append(cyclic(project(item, w_bc, w_dt), "dp", -r))
    if n_dp > 1:
        near += relay(found[1], groups[1], slots[: 1 if ride else 2])
    partials[1:] = [after(a, *near) for a in partials[1:]]
    proj = partials + [cyclic(a, "head", 1) for a in partials]
    spare = relay(found[1], groups[1], [(1, 1)]) if ride and n_dp > 1 else []
    own, bc, hp, *outs = call(
        functools.partial(state_kernel, 2 * n_dp, size, int(ride)),
        (
            struct((2, CHUNKS, state_n, step), F32),
            struct((2 * rows, state_n), F32),
            struct((5 * heads, rows), F32),
        )
        + (struct((state_n, step), BF),) * CHUNKS
        + (struct((1, step), F32),) * CHUNKS,
        0.1,
        *proj,
        x,
        g,
        rate,
        bias,
        *([found[0][1, 1]] if ride else []),
    )
    first, decay = outs[:CHUNKS], outs[CHUNKS:]
    pairs = width // (2 * size) // PARTS
    span = width // PARTS
    shared = []

    def inner(q, *others):
        held = after(bc, *others) if others else bc
        square = struct((rows, rows), F32)
        block = pl.BlockSpec((rows, span), lambda _: (0, q))
        out = call(
            functools.partial(inner_kernel, q * pairs, pairs, size),
            ([square] if q == 0 else [])
            + [struct((rows, span), F32), square, struct((2, 2 * pairs, rows), F32)],
                2.6,
            held,
            hp,
            x,
            g,
            *shared,
            scratch=(pltpu.VMEM((rows, 2 * span), BF), pltpu.VMEM((rows, 2 * span), BF)),
            specs=[VMEM, VMEM, block, block] + [VMEM] * len(shared),
        )
        if q == 0:
            shared.append(out[0])
            out = out[1:]
        return out

    weights = [w_bc, w_dt]

    def beside(*others):
        for r in range(1, n_dp):
            weights.extend(cyclic(after(a, *others), "dp", r) for a in (w_bc, w_dt))
        return weights[2:] + relay(found[0], groups[0], second, *others)

    def late(*others):
        return relay(found[1], groups[1], second, *others) if n_dp > 1 else []

    first[0] = after(first[0], *spare)
    riders = [f[1, 1] for f in found] if ride else []
    calls = [functools.partial(inner, q) for q in range(PARTS)]
    stores, inners = chains(first, own, decay, calls, beside, riders, late)
    for f, a in zip(found, riders):
        f[0, 2] = a
    done = [relay(f, a, [t for t in slots if t not in f], stores[-1]) for f, a in zip(found, groups)]
    each = PARTS // CHUNKS
    grad_x, back = None, []
    for k in range(CHUNKS):
        last = k == CHUNKS - 1
        block = pl.BlockSpec((rows, step), lambda _, k=k: (0, k))
        made = (k + 1) * (heads // CHUNKS)
        sums = (struct((rows + heads, rows), F32), struct((rows, rows), F32))
        inputs = [stores[k], x, g, bc, hp, rate]
        for q in range(3):
            inputs += [a[q] for a in inners[k * each : (k + 1) * each]]
        specs = [VMEM, block, block] + [VMEM] * (len(inputs) - 3)
        if k > 0:
            inputs += [grad_x] + back
            specs += [HBM, VMEM]
        grad_x, *back = call(
            functools.partial(outer_kernel, k, CHUNKS, size, each),
            (struct((rows, width), BF),)
            + (sums if last else (struct((2 * rows + made, rows), F32),)),
            5.4 / CHUNKS,
            *inputs,
            scratch=(pltpu.VMEM((rows, 2 * step), BF), pltpu.VMEM((rows, 2 * step), BF)),
            specs=specs,
            out_specs=(block,) + (VMEM,) * (2 if last else 1),
            aliases={len(inputs) - 2: 0} if k > 0 else {},
        )
    keep, give = back
    taken = after(cyclic(give, "head", 1), *[a for d in done for a in d])
    count = n_dp * n_seq
    copies = call(low_kernel, struct((count, rows + heads, rows), BF), 1.2, keep, taken)
    mine = copies[0]
    lows = lax.all_to_all(copies, ("seq", "dp"), 0, 0, tiled=True)
    other = cyclic(mine, "head", 1)
    grads = call(
        functools.partial(token_kernel, n_dp),
        struct((rows, width), BF),
        2.9,
        mine,
        other,
        *weights,
    )
    toks = []
    for f, a in zip(found, groups):
        toks += [a] + [f[step] for step in slots]
    slots = [(0, 0)] + slots
    ordered = call(
        functools.partial(order_kernel, n_dp, n_seq, slots),
        struct((n_dp, n_seq * rows, part), BF),
        1.0,
        *after(tuple(toks), grads),
        scratch=[pltpu.SemaphoreType.DMA((n_dp, len(slots)))],
    )
    lows = after(lows, grads, ordered)
    swapped = cyclic(lows, "head", 1)
    cols = 2 * (rows + heads)
    grad_bc, grad_dt = call(
        functools.partial(weight_kernel, 1.0 / (rows * n_seq * n_dp), n_dp, n_seq),
        (struct((part, 2 * state_n), F32), struct((2 * heads, part), F32)),
        4.0,
        ordered,
        lows,
        swapped,
        limit=LIMIT + 2 * n_dp * n_seq * rows * cols,
        scratch=(
            pltpu.VMEM((n_dp, cols, n_seq * rows), BF),
            pltpu.SemaphoreType.DMA((count, 2)),
        ),
    )
    return grad_x[None], grads[None], grad_bc, grad_dt.T


def solution(mesh):
    in_specs = (
        P(("grp", "dp"), "seq", "head"),
        P(("grp", "dp"), "seq", "head"),
        P(("grp", "dp"), "seq", "head"),
        P(("head", "dp"), None),
        P(("head", "dp"), None),
        P("head"),
        P("head"),
    )
    out_specs = (
        P(("grp", "dp"), "seq", "head"),
        P(("grp", "dp"), "seq", "head"),
        P(("grp", "head", "dp"), None),
        P(("grp", "head", "dp"), None),
    )
    return jax.shard_map(body, mesh=mesh, in_specs=in_specs, out_specs=out_specs, check_vma=False)
```

```python
import functools

import jax
import jax.numpy as jnp
from jax import lax
from jax.experimental import pallas as pl
from jax.experimental.pallas import tpu as pltpu
from jax.sharding import PartitionSpec as P

CHUNKS = 2
PARTS = 4
BF = jnp.bfloat16
F32 = jnp.float32
TOP = lax.Precision.HIGHEST
PER_US = 1.15e9
LIMIT = 16 * 1024 * 1024


def cyclic(a, axis, by):
    count = lax.axis_size(axis)
    return lax.ppermute(a, axis, [(i, (i + by) % count) for i in range(count)])


def mm(a, b, ca, cb, precision=None):
    return lax.dot_general(
        a, b, (((ca,), (cb,)), ((), ())), preferred_element_type=F32, precision=precision
    )


def halves(a):
    high = a.astype(BF)
    return high, (a - high.astype(F32)).astype(BF)


def head_lanes(heads, width, size, first=0):
    row = lax.broadcasted_iota(jnp.int32, (heads, width), 0)
    col = lax.broadcasted_iota(jnp.int32, (heads, width), 1) + first
    low = row * size
    return jnp.where((col >= low) & (col < low + size), 1.0, 0.0).astype(F32)


def spread(a, pick):
    high, low = halves(a)
    both = jnp.concatenate([pick, pick], axis=0)
    return mm(jnp.concatenate([high, low], axis=0), both, 0, 0)


VMEM = pl.BlockSpec(memory_space=pltpu.VMEM)
HBM = pl.BlockSpec(memory_space=pltpu.HBM)


def call(kernel, out_shape, span_us, *args, scratch=(), specs=None, out_specs=None, aliases={}, limit=LIMIT):
    size = sum(a.size * a.dtype.itemsize for a in args)
    return pl.pallas_call(
        kernel,
        out_shape=out_shape,
        grid=(1,),
        in_specs=specs or [VMEM] * len(args),
        out_specs=out_specs or jax.tree.map(lambda _: VMEM, out_shape),
        input_output_aliases=aliases,
        scratch_shapes=list(scratch),
        compiler_params=pltpu.CompilerParams(vmem_limit_bytes=limit),
        cost_estimate=pl.CostEstimate(
            flops=int(span_us * PER_US), bytes_accessed=size, transcendentals=0
        ),
    )(*args)


def struct(shape, dtype):
    return jax.ShapeDtypeStruct(shape, dtype)


def after(a, *others):
    return lax.optimization_barrier((a, others))[0]


def matchings(count):
    groups = [[(i, i + 1) for i in range(kind, count - 1, 2)] for kind in (0, 1)]
    pairs = []
    for group in groups:
        to = {i: i for i in range(count)}
        for i, j in group:
            to[i], to[j] = j, i
        pairs.append(sorted(to.items()))
    return groups, pairs


def split_kernel(a_ref, *outs):
    count = len(outs)
    me = lax.axis_index("dp")
    part = outs[0].shape[1]
    for r in range(count):
        at = pl.multiple_of(lax.rem(me + r, count) * part, 128)
        outs[r][...] = a_ref[:, pl.ds(at, part)]


def project_kernel(a_ref, bc_ref, dt_ref, out_ref):
    a = a_ref[...]
    state_n = bc_ref.shape[1] // 2
    rows = a.shape[0]
    bc = mm(a, bc_ref[...], 1, 0)
    out_ref[0:rows, :] = bc[:, :state_n]
    out_ref[rows : 2 * rows, :] = bc[:, state_n:]
    out_ref[2 * rows :, :] = mm(dt_ref[...], a, 1, 1)


def project(a, w_bc, w_dt):
    rows = a.shape[0]
    total = 2 * rows + w_dt.shape[0]
    return call(
        project_kernel,
        struct((total, w_bc.shape[1] // 2), F32),
        2.1,
        a,
        w_bc,
        w_dt,
    )


def state_kernel(count, size, ride, *refs):
    proj = refs[:count]
    x_ref, g_ref, rate_ref, bias_ref = refs[count : count + 4]
    riders = refs[count + 4 : count + 4 + ride]
    own_ref, bc_ref, hp_ref = refs[count + 4 + ride : count + 7 + ride]
    outs = refs[count + 7 + ride :]
    firsts, decays = outs[: len(outs) // 2], outs[len(outs) // 2 :]
    heads = rate_ref.shape[1]
    rows = x_ref.shape[0]
    rate, bias = rate_ref[...].T, bias_ref[...].T
    chunks, step = own_ref.shape[1], own_ref.shape[3]
    first = pl.multiple_of(2 * rows + lax.axis_index("head") * heads, 8)
    bc = proj[0][0 : 2 * rows, :]
    pre = proj[0][pl.ds(first, heads), :] + bias
    for ref in proj[1:]:
        bc = bc + ref[0 : 2 * rows, :]
        pre = pre + ref[pl.ds(first, heads), :]
    bc_ref[...] = bc
    dt = jnp.maximum(pre, 0.0) + jnp.log1p(jnp.exp(-jnp.abs(pre)))
    row = lax.broadcasted_iota(jnp.int32, (rows, rows), 0)
    col = lax.broadcasted_iota(jnp.int32, (rows, rows), 1)
    cum = mm(-dt * rate, jnp.where(row <= col, 1.0, 0.0), 1, 0, TOP)
    last = cum[:, rows - 1 : rows]
    grow = jnp.exp(cum)
    w = jnp.exp(last - cum) * dt
    decay = jnp.exp(last)
    for k, part in enumerate((pre, dt, cum, grow, w)):
        hp_ref[k * heads : (k + 1) * heads, :] = part
    place = lax.axis_index("seq")
    lowest = place == 0
    sides = []
    for vec in (bc[:rows], bc[rows:]):
        high, low = halves(vec.T)
        sides.append((jnp.concatenate([high, low], axis=1), high))
    for k in range(chunks):
        pick = head_lanes(heads, step, size, k * step)
        decays[k][...] = jnp.sum(pick * decay, axis=0, keepdims=True)
        pick = pick.astype(BF)
        both = []
        for kind, (scale, ref) in enumerate(((w, x_ref), (grow, g_ref))):
            wide, high = sides[kind]
            value = spread(scale, pick) * ref[:, k * step : (k + 1) * step].astype(F32)
            top, rest = halves(value)
            value = mm(wide, jnp.concatenate([top, top], axis=0), 1, 0) + mm(high, rest, 1, 0)
            own_ref[kind, k] = value
            both.append(value)
        firsts[k][...] = jnp.where(lowest, both[0], both[1]).astype(BF)
        if k < ride:
            rider = riders[k]

            @pl.when((place > 0) & (place < lax.axis_size("seq") - 1))
            def _():
                firsts[k][...] = rider[...]


def inner_kernel(first, pairs, size, bc_ref, hp_ref, x_ref, g_ref, *refs):
    gx_ref, ds_ref, sums_ref = refs[-5:-2]
    gy_ref, xg_ref = refs[-2:]
    rows = x_ref.shape[0]
    heads = hp_ref.shape[0] // 5
    lanes = 2 * size
    width = pairs * lanes
    if len(refs) == 6 and first > 0:
        scores = refs[0][...]
    else:
        scores = mm(bc_ref[rows : 2 * rows, :], bc_ref[0:rows, :], 1, 1, TOP)
        refs[0][...] = scores
    row = lax.broadcasted_iota(jnp.int32, (rows, rows), 0)
    col = lax.broadcasted_iota(jnp.int32, (rows, rows), 1)
    causal = row >= col
    dt = hp_ref[heads : 2 * heads, :]
    cum = hp_ref[2 * heads : 3 * heads, :]
    cum_t = cum.T
    lane = lax.broadcasted_iota(jnp.int32, (rows, lanes), 1)
    sides = [jnp.where(lane < size, 1.0, 0.0).astype(BF), jnp.where(lane < size, 0.0, 1.0).astype(BF)]
    ds = jnp.zeros((rows, rows), F32)
    for j in range(pairs):
        place = slice(j * lanes, (j + 1) * lanes)
        x, g = x_ref[:, place], g_ref[:, place]
        xs = jnp.concatenate([x * s for s in sides], axis=0)
        gs = jnp.concatenate([g * s for s in sides], axis=0)
        m = mm(gs, x, 1, 1)
        kern = []
        for i in range(2):
            h = 2 * (first + j) + i
            gap = cum_t[:, h : h + 1] - cum[h : h + 1, :]
            fall = jnp.exp(jnp.where(causal, gap, -jnp.inf)) * dt[h : h + 1, :]
            kern.append((fall * scores).astype(BF))
            ds = ds + fall * m[i * rows : (i + 1) * rows]
        y = mm(jnp.concatenate(kern, axis=1), xs, 1, 0)
        gx = mm(jnp.concatenate(kern, axis=0), gs, 0, 0)
        gx_ref[:, place] = gx
        late = slice(width + j * lanes, width + (j + 1) * lanes)
        gy_ref[:, place], gy_ref[:, late] = halves(g.astype(F32) * y)
        xg_ref[:, place], xg_ref[:, late] = halves(x.astype(F32) * gx)
    ds_ref[...] = ds
    pick = head_lanes(2 * pairs, width, size).astype(BF)
    pick = jnp.concatenate([pick, pick], axis=1)
    sums_ref[0] = mm(pick, gy_ref[...], 1, 1)
    sums_ref[1] = mm(pick, xg_ref[...], 1, 1)


def outer_kernel(k, chunks, size, parts, *refs):
    store_ref, x_ref, g_ref, bc_ref, hp_ref, rate_ref = refs[:6]
    gxs, dss, sums = (refs[6 + q * parts : 6 + (q + 1) * parts] for q in range(3))
    rest = refs[6 + 3 * parts :]
    wv_ref, eu_ref = rest[-2:]
    rows, step = x_ref.shape
    all_heads = rate_ref.shape[1]
    heads = all_heads // chunks
    mine = slice(k * heads, (k + 1) * heads)
    piece = step // parts
    b, c = bc_ref[0:rows, :], bc_ref[rows : 2 * rows, :]
    pre, dt, cum, grow, w = (
        hp_ref[q * all_heads + k * heads : q * all_heads + (k + 1) * heads, :] for q in range(5)
    )
    rate = rate_ref[...].T[mine]
    ds = dss[0][...]
    for ref in dss[1:]:
        ds = ds + ref[...]
    db = mm(c, ds, 0, 0, TOP)
    dc = mm(b, ds, 0, 1, TOP)
    b_wide = jnp.concatenate(halves(b), axis=1)
    c_wide = jnp.concatenate(halves(c), axis=1)
    pick = head_lanes(heads, step, size).astype(BF)
    incoming, outgoing = store_ref[0], store_ref[1]
    u = mm(c_wide, jnp.concatenate([incoming, incoming], axis=0), 1, 0)
    v = mm(b_wide, jnp.concatenate([outgoing, outgoing], axis=0), 1, 0)
    scale = spread(w, pick)
    wx = scale * x_ref[...].astype(F32)
    eg = spread(grow, pick) * g_ref[...].astype(F32)
    grad_ref = rest[-5] if k == chunks - 1 else rest[-4]
    for q in range(parts):
        place = slice(q * piece, (q + 1) * piece)
        grad_ref[:, place] = (gxs[q][...] + scale[:, place] * v[:, place]).astype(BF)
    wv_ref[:, :step], wv_ref[:, step:] = halves(wx * v)
    eu_ref[:, :step], eu_ref[:, step:] = halves(eg * u)
    db = db + mm(
        jnp.concatenate([outgoing, outgoing], axis=1), jnp.concatenate(halves(wx), axis=1), 1, 1
    )
    dc = dc + mm(
        jnp.concatenate([incoming, incoming], axis=1), jnp.concatenate(halves(eg), axis=1), 1, 1
    )
    both = jnp.sum(incoming.astype(F32) * outgoing.astype(F32), axis=0, keepdims=True)
    ddecay = jnp.sum(pick.astype(F32) * both, axis=1, keepdims=True)
    pick = jnp.concatenate([pick, pick], axis=1)
    wdw = mm(pick, wv_ref[...], 1, 1)
    egu = mm(pick, eu_ref[...], 1, 1)
    rowsum = jnp.concatenate([s[0] for s in sums], axis=0)
    colsum = jnp.concatenate([s[1] for s in sums], axis=0)
    dcum = rowsum - colsum + egu - wdw
    row = lax.broadcasted_iota(jnp.int32, (rows, rows), 0)
    col = lax.broadcasted_iota(jnp.int32, (rows, rows), 1)
    rev = mm(dcum, jnp.where(row >= col, 1.0, 0.0), 1, 0, TOP)
    decay = grow[:, rows - 1 : rows]
    rev = rev + jnp.sum(wdw, axis=1, keepdims=True) + decay * ddecay
    gate = 1.0 / (1.0 + jnp.exp(-pre))
    small = 1e-30
    ratio = jnp.where(dt > small, gate / jnp.maximum(dt, small), 1.0)
    graw = (colsum + wdw) * ratio - rate * rev * gate
    if k > 0:
        before_ref = rest[1]
        db = db + before_ref[0:rows, :]
        dc = dc + before_ref[rows : 2 * rows, :]
        graw = jnp.concatenate([before_ref[2 * rows :, :], graw], axis=0)
    if k == chunks - 1:
        keep_ref, give_ref = rest[-4], rest[-3]
        core = lax.axis_index("head")
        keep_ref[0:rows, :] = jnp.where(core == 0, db, dc)
        keep_ref[rows:, :] = graw
        give_ref[...] = jnp.where(core == 0, dc, db)
    else:
        back_ref = rest[-3]
        back_ref[0:rows, :] = db
        back_ref[rows : 2 * rows, :] = dc
        back_ref[2 * rows :, :] = graw


def low_kernel(keep_ref, taken_ref, out_ref):
    rows = taken_ref.shape[0]
    low = keep_ref[0:rows, :] + taken_ref[...]
    low = jnp.concatenate([low, keep_ref[rows:, :]], axis=0).astype(BF)
    for k in range(out_ref.shape[0]):
        out_ref[k] = low


def token_kernel(count, mine_ref, other_ref, *refs):
    out_ref = refs[2 * count]
    me, core = lax.axis_index("dp"), lax.axis_index("head")
    part, cols = refs[0].shape
    half = cols // 2
    heads = refs[1].shape[0] // 2
    for r in range(count):
        at = pl.multiple_of(lax.rem(me - r + count, count) * part, 128)
        total = None
        for k, ref in enumerate((mine_ref, other_ref)):
            at_col = pl.multiple_of(lax.rem(core + k, 2) * half, 128)
            at_row = pl.multiple_of(lax.rem(core + k, 2) * heads, 16)
            term = mm(ref[0:half, :], refs[2 * r][:, pl.ds(at_col, half)], 0, 1)
            term = term + mm(ref[half:, :], refs[2 * r + 1][pl.ds(at_row, heads), :], 0, 0)
            total = term if total is None else total + term
        out_ref[:, pl.ds(at, part)] = total.astype(BF)


def order_kernel(n_dp, n_seq, slots, *refs):
    out_ref, sem = refs[-2:]
    toks = refs[:-2]
    rows = toks[0].shape[0]
    place = lax.axis_index("seq")
    even = lax.rem(place, 2) == 0
    copies = []
    for r in range(n_dp):
        for k, (kind, hop) in enumerate(slots):
            above = even if kind == 0 else ~even
            block = jnp.where(above, place + hop, place - hop)
            fits = (block >= 0) & (block < n_seq)
            if hop > 0 and kind == 1:
                fits = fits & jnp.where(above, place < n_seq - 1, place > 0)
            at = pl.multiple_of(jnp.clip(block, 0, n_seq - 1) * rows, 128)
            source = toks[k] if r == 0 else toks[len(slots) + k].at[pl.ds((r - 1) * rows, rows)]
            copy = pltpu.make_async_copy(source, out_ref.at[r, pl.ds(at, rows)], sem.at[r, k])
            copies.append((fits, copy))
    for fits, copy in copies:
        pl.when(fits)(copy.start)
    for fits, copy in copies:
        pl.when(fits)(copy.wait)


def weight_kernel(scale, n_dp, n_seq, tok_ref, *refs):
    lows = refs[:2]
    bc_ref, dt_ref, low_ref, low_sem = refs[2:]
    rows = tok_ref.shape[1] // n_seq
    share = lows[0].shape[1]
    core, me = lax.axis_index("head"), lax.axis_index("dp")
    copies = []
    for r in range(n_dp):
        for s in range(n_seq):
            index = s * n_dp + lax.rem(me - r + n_dp, n_dp)
            for k in range(2):
                row = pl.multiple_of(lax.rem(core + k, 2) * share, 16)
                copies.append(
                    pltpu.make_async_copy(
                        lows[k].at[index],
                        low_ref.at[r, pl.ds(row, share), pl.ds(s * rows, rows)],
                        low_sem.at[r * n_seq + s, k],
                    )
                )
    for copy in copies:
        copy.start()
    for copy in copies:
        copy.wait()
    total = mm(low_ref[0], tok_ref[0], 1, 0)
    for r in range(1, n_dp):
        total = total + mm(low_ref[r], tok_ref[r], 1, 0)
    total = total * scale
    half = bc_ref.shape[1] // 2
    heads = dt_ref.shape[0] // 2
    for k in range(2):
        bc_ref[:, k * half : (k + 1) * half] = total[k * share : k * share + half].T
        dt_ref[k * heads : (k + 1) * heads, :] = total[k * share + half : (k + 1) * share]


def relays(count):
    groups, _ = matchings(count)
    return [
        (kind, hop)
        for hop in range(1, count)
        for kind in (0, 1)
        if any(i - hop + 1 >= 0 or j + hop - 1 < count for i, j in groups[kind])
    ]


def relay(found, block, steps, *others):
    count = lax.axis_size("seq")
    _, pairs = matchings(count)
    for kind, hop in steps:
        source = block if hop == 1 else found[1 - kind, hop - 1]
        source = after(source, *others) if others else source
        found[kind, hop] = lax.ppermute(source, "seq", pairs[kind])
    return [found[step] for step in steps]


def chains(first, own, decay, inner, beside, riders, cross, late):
    count = lax.axis_size("seq")
    place = lax.axis_index("seq")
    chunks = len(first)
    stores = [jnp.zeros((3,) + own.shape[2:], BF) for _ in range(chunks)]
    got = list(first)
    done, todo, extra = [], list(inner), []
    last = count + chunks - 2
    for slot in range(1, last + 1):
        steps = [(hop, slot - hop) for hop in range(1, count) if 0 <= slot - hop < chunks]
        sent = []
        for hop, k in steps:
            value = got[k]
            if hop == 1 and 0 < k < len(riders):
                value = jnp.where((place == 0) | (place == count - 1), value, riders[k])
            if hop > 1:
                value = jnp.where(place == hop - 1, own[0, k], own[1, k])
                value = (value + decay[k] * got[k].astype(F32)).astype(BF)
            sent.append(value)
        for (hop, k), value in zip(steps, sent):
            to = {i: i for i in range(count)}
            for i in (hop - 1, count - hop - 1):
                to[i], to[i + 1] = i + 1, i
            got[k] = lax.ppermute(value, "seq", sorted(to.items()))
            if hop == 1 and k < len(riders):
                riders[k] = got[k]
        for _ in range(-(-len(todo) // (last + 1 - slot))):
            done.append(todo.pop(0)(*sent))
        if slot == 1:
            extra = beside(*sent)
        if slot == max(last - 1, 1):
            crossed = cross(*sent)
        if slot == last:
            k = steps[-1][1]
            got[k] = after(got[k], *late(*sent), *crossed)
        if slot < last:
            held = [got[k] for _, k in steps] + [d[0] for d in done[-1:]]
            if slot == last - 1:
                held += extra
            new = slot < chunks
            if new:
                held.append(got[slot])
            kept = lax.optimization_barrier(tuple(held))
            for (_, k), a in zip(steps, kept):
                got[k] = a
            if new:
                got[slot] = kept[-1]
        for hop, k in steps:
            kind = jnp.where(place == hop, 0, jnp.where(place == count - hop - 1, 1, 2))
            zero = jnp.zeros_like(kind)
            stores[k] = lax.dynamic_update_slice(stores[k], got[k][None], (kind, zero, zero))
    done += [make() for make in todo]
    return stores, done


def body(tokens, ssd_input, grad_out, w_bc, w_dt, decay_rate, dt_bias):
    feats, x, g = tokens[0], ssd_input[0], grad_out[0]
    rows, width = feats.shape
    heads = decay_rate.shape[0]
    size = width // heads
    n_dp, n_seq = lax.axis_size("dp"), lax.axis_size("seq")
    part = width // n_dp
    state_n = w_bc.shape[1] // 2
    w_dt = w_dt.T
    rate, bias = decay_rate[None], dt_bias[None]

    pieces = call(split_kernel, [struct((rows, part), BF)] * n_dp, 1.9, feats)
    items = [pieces[0]] + [cyclic(pieces[r], "dp", r) for r in range(1, n_dp)]
    groups = items[:1]
    if n_dp > 1:
        groups.append(items[1] if n_dp == 2 else jnp.concatenate(items[1:], axis=0))
    found = [{} for _ in groups]
    slots = relays(n_seq)
    step = width // CHUNKS
    ride = n_seq == 4 and all(a.shape == (state_n, step) for a in groups)
    second = [(kind, hop) for kind, hop in slots if hop == 2 and not (ride and kind == 0)]
    near = relay(found[0], groups[0], slots[:2])
    partials = [project(items[0], w_bc, w_dt)]
    for r in range(1, n_dp):
        item = after(items[r], partials[0])
        partials.append(cyclic(project(item, w_bc, w_dt), "dp", -r))
    if n_dp > 1:
        near += relay(found[1], groups[1], slots[: 1 if ride else 2])
    partials[1:] = [after(a, *near) for a in partials[1:]]
    proj = partials + [cyclic(a, "head", 1) for a in partials]
    spare = relay(found[1], groups[1], [(1, 1)]) if ride and n_dp > 1 else []
    own, bc, hp, *outs = call(
        functools.partial(state_kernel, 2 * n_dp, size, int(ride)),
        (
            struct((2, CHUNKS, state_n, step), F32),
            struct((2 * rows, state_n), F32),
            struct((5 * heads, rows), F32),
        )
        + (struct((state_n, step), BF),) * CHUNKS
        + (struct((1, step), F32),) * CHUNKS,
        0.1,
        *proj,
        x,
        g,
        rate,
        bias,
        *([found[0][1, 1]] if ride else []),
    )
    first, decay = outs[:CHUNKS], outs[CHUNKS:]
    pairs = width // (2 * size) // PARTS
    span = width // PARTS
    shared = []

    def inner(q, *others):
        held = after(bc, *others) if others else bc
        square = struct((rows, rows), F32)
        block = pl.BlockSpec((rows, span), lambda _: (0, q))
        out = call(
            functools.partial(inner_kernel, q * pairs, pairs, size),
            ([square] if q == 0 else [])
            + [struct((rows, span), F32), square, struct((2, 2 * pairs, rows), F32)],
                2.6,
            held,
            hp,
            x,
            g,
            *shared,
            scratch=(pltpu.VMEM((rows, 2 * span), BF), pltpu.VMEM((rows, 2 * span), BF)),
            specs=[VMEM, VMEM, block, block] + [VMEM] * len(shared),
        )
        if q == 0:
            shared.append(out[0])
            out = out[1:]
        return out

    weights = [w_bc, w_dt]

    def beside(*others):
        return relay(found[0], groups[0], second, *others)

    def cross(*others):
        for r in range(1, n_dp):
            weights.extend(cyclic(after(a, *others), "dp", r) for a in (w_bc, w_dt))
        return weights[2:]

    def late(*others):
        return relay(found[1], groups[1], second, *others) if n_dp > 1 else []

    first[0] = after(first[0], *spare)
    riders = [f[1, 1] for f in found] if ride else []
    calls = [functools.partial(inner, q) for q in range(PARTS)]
    stores, inners = chains(first, own, decay, calls, beside, riders, cross, late)
    for f, a in zip(found, riders):
        f[0, 2] = a
    done = [relay(f, a, [t for t in slots if t not in f], stores[-1]) for f, a in zip(found, groups)]
    each = PARTS // CHUNKS
    grad_x, back = None, []
    for k in range(CHUNKS):
        last = k == CHUNKS - 1
        block = pl.BlockSpec((rows, step), lambda _, k=k: (0, k))
        made = (k + 1) * (heads // CHUNKS)
        sums = (struct((rows + heads, rows), F32), struct((rows, rows), F32))
        inputs = [stores[k], x, g, bc, hp, rate]
        for q in range(3):
            inputs += [a[q] for a in inners[k * each : (k + 1) * each]]
        specs = [VMEM, block, block] + [VMEM] * (len(inputs) - 3)
        if k > 0:
            inputs += [grad_x] + back
            specs += [HBM, VMEM]
        grad_x, *back = call(
            functools.partial(outer_kernel, k, CHUNKS, size, each),
            (struct((rows, width), BF),)
            + (sums if last else (struct((2 * rows + made, rows), F32),)),
            5.4 / CHUNKS,
            *inputs,
            scratch=(pltpu.VMEM((rows, 2 * step), BF), pltpu.VMEM((rows, 2 * step), BF)),
            specs=specs,
            out_specs=(block,) + (VMEM,) * (2 if last else 1),
            aliases={len(inputs) - 2: 0} if k > 0 else {},
        )
    keep, give = back
    taken = after(cyclic(give, "head", 1), *[a for d in done for a in d])
    count = n_dp * n_seq
    copies = call(low_kernel, struct((count, rows + heads, rows), BF), 1.2, keep, taken)
    mine = copies[0]
    lows = lax.all_to_all(copies, ("seq", "dp"), 0, 0, tiled=True)
    other = cyclic(mine, "head", 1)
    grads = call(
        functools.partial(token_kernel, n_dp),
        struct((rows, width), BF),
        2.9,
        mine,
        other,
        *weights,
    )
    toks = []
    for f, a in zip(found, groups):
        toks += [a] + [f[step] for step in slots]
    slots = [(0, 0)] + slots
    ordered = call(
        functools.partial(order_kernel, n_dp, n_seq, slots),
        struct((n_dp, n_seq * rows, part), BF),
        1.0,
        *after(tuple(toks), grads),
        scratch=[pltpu.SemaphoreType.DMA((n_dp, len(slots)))],
    )
    lows = after(lows, grads, ordered)
    swapped = cyclic(lows, "head", 1)
    cols = 2 * (rows + heads)
    grad_bc, grad_dt = call(
        functools.partial(weight_kernel, 1.0 / (rows * n_seq * n_dp), n_dp, n_seq),
        (struct((part, 2 * state_n), F32), struct((2 * heads, part), F32)),
        4.0,
        ordered,
        lows,
        swapped,
        limit=LIMIT + 2 * n_dp * n_seq * rows * cols,
        scratch=(
            pltpu.VMEM((n_dp, cols, n_seq * rows), BF),
            pltpu.SemaphoreType.DMA((count, 2)),
        ),
    )
    return grad_x[None], grads[None], grad_bc, grad_dt.T


def solution(mesh):
    in_specs = (
        P(("grp", "dp"), "seq", "head"),
        P(("grp", "dp"), "seq", "head"),
        P(("grp", "dp"), "seq", "head"),
        P(("head", "dp"), None),
        P(("head", "dp"), None),
        P("head"),
        P("head"),
    )
    out_specs = (
        P(("grp", "dp"), "seq", "head"),
        P(("grp", "dp"), "seq", "head"),
        P(("grp", "head", "dp"), None),
        P(("grp", "head", "dp"), None),
    )
    return jax.shard_map(body, mesh=mesh, in_specs=in_specs, out_specs=out_specs, check_vma=False)
```

```python
import functools

import jax
import jax.numpy as jnp
from jax import lax
from jax.experimental import pallas as pl
from jax.experimental.pallas import tpu as pltpu
from jax.sharding import PartitionSpec as P

CHUNKS = 2
PARTS = 4
BF = jnp.bfloat16
F32 = jnp.float32
TOP = lax.Precision.HIGHEST
PER_US = 1.15e9
LIMIT = 16 * 1024 * 1024


def cyclic(a, axis, by):
    count = lax.axis_size(axis)
    return lax.ppermute(a, axis, [(i, (i + by) % count) for i in range(count)])


def mm(a, b, ca, cb, precision=None):
    return lax.dot_general(
        a, b, (((ca,), (cb,)), ((), ())), preferred_element_type=F32, precision=precision
    )


def halves(a):
    high = a.astype(BF)
    return high, (a - high.astype(F32)).astype(BF)


def head_lanes(heads, width, size, first=0):
    row = lax.broadcasted_iota(jnp.int32, (heads, width), 0)
    col = lax.broadcasted_iota(jnp.int32, (heads, width), 1) + first
    low = row * size
    return jnp.where((col >= low) & (col < low + size), 1.0, 0.0).astype(F32)


def spread(a, pick):
    high, low = halves(a)
    both = jnp.concatenate([pick, pick], axis=0)
    return mm(jnp.concatenate([high, low], axis=0), both, 0, 0)


VMEM = pl.BlockSpec(memory_space=pltpu.VMEM)
HBM = pl.BlockSpec(memory_space=pltpu.HBM)


def call(kernel, out_shape, span_us, *args, scratch=(), specs=None, out_specs=None, aliases={}, limit=LIMIT):
    size = sum(a.size * a.dtype.itemsize for a in args)
    return pl.pallas_call(
        kernel,
        out_shape=out_shape,
        grid=(1,),
        in_specs=specs or [VMEM] * len(args),
        out_specs=out_specs or jax.tree.map(lambda _: VMEM, out_shape),
        input_output_aliases=aliases,
        scratch_shapes=list(scratch),
        compiler_params=pltpu.CompilerParams(vmem_limit_bytes=limit),
        cost_estimate=pl.CostEstimate(
            flops=int(span_us * PER_US), bytes_accessed=size, transcendentals=0
        ),
    )(*args)


def struct(shape, dtype):
    return jax.ShapeDtypeStruct(shape, dtype)


def after(a, *others):
    return lax.optimization_barrier((a, others))[0]


def matchings(count):
    groups = [[(i, i + 1) for i in range(kind, count - 1, 2)] for kind in (0, 1)]
    pairs = []
    for group in groups:
        to = {i: i for i in range(count)}
        for i, j in group:
            to[i], to[j] = j, i
        pairs.append(sorted(to.items()))
    return groups, pairs


def split_kernel(a_ref, *outs):
    count = len(outs)
    me = lax.axis_index("dp")
    part = outs[0].shape[1]
    for r in range(count):
        at = pl.multiple_of(lax.rem(me + r, count) * part, 128)
        outs[r][...] = a_ref[:, pl.ds(at, part)]


def project_kernel(a_ref, bc_ref, dt_ref, out_ref):
    a = a_ref[...]
    state_n = bc_ref.shape[1] // 2
    rows = a.shape[0]
    bc = mm(a, bc_ref[...], 1, 0)
    out_ref[0:rows, :] = bc[:, :state_n]
    out_ref[rows : 2 * rows, :] = bc[:, state_n:]
    out_ref[2 * rows :, :] = mm(dt_ref[...], a, 1, 1)


def project(a, w_bc, w_dt):
    rows = a.shape[0]
    total = 2 * rows + w_dt.shape[0]
    return call(
        project_kernel,
        struct((total, w_bc.shape[1] // 2), F32),
        2.1,
        a,
        w_bc,
        w_dt,
    )


def state_kernel(count, size, ride, *refs):
    proj = refs[:count]
    x_ref, g_ref, rate_ref, bias_ref = refs[count : count + 4]
    riders = refs[count + 4 : count + 4 + ride]
    own_ref, bc_ref, hp_ref = refs[count + 4 + ride : count + 7 + ride]
    outs = refs[count + 7 + ride :]
    firsts, decays = outs[: len(outs) // 2], outs[len(outs) // 2 :]
    heads = rate_ref.shape[1]
    rows = x_ref.shape[0]
    rate, bias = rate_ref[...].T, bias_ref[...].T
    chunks, step = own_ref.shape[1], own_ref.shape[3]
    first = pl.multiple_of(2 * rows + lax.axis_index("head") * heads, 8)
    bc = proj[0][0 : 2 * rows, :]
    pre = proj[0][pl.ds(first, heads), :] + bias
    for ref in proj[1:]:
        bc = bc + ref[0 : 2 * rows, :]
        pre = pre + ref[pl.ds(first, heads), :]
    bc_ref[...] = bc
    dt = jnp.maximum(pre, 0.0) + jnp.log1p(jnp.exp(-jnp.abs(pre)))
    row = lax.broadcasted_iota(jnp.int32, (rows, rows), 0)
    col = lax.broadcasted_iota(jnp.int32, (rows, rows), 1)
    cum = mm(-dt * rate, jnp.where(row <= col, 1.0, 0.0), 1, 0, TOP)
    last = cum[:, rows - 1 : rows]
    grow = jnp.exp(cum)
    w = jnp.exp(last - cum) * dt
    decay = jnp.exp(last)
    for k, part in enumerate((pre, dt, cum, grow, w)):
        hp_ref[k * heads : (k + 1) * heads, :] = part
    place = lax.axis_index("seq")
    lowest = place == 0
    sides = []
    for vec in (bc[:rows], bc[rows:]):
        high, low = halves(vec.T)
        sides.append((jnp.concatenate([high, low], axis=1), high))
    for k in range(chunks):
        pick = head_lanes(heads, step, size, k * step)
        decays[k][...] = jnp.sum(pick * decay, axis=0, keepdims=True)
        pick = pick.astype(BF)
        both = []
        for kind, (scale, ref) in enumerate(((w, x_ref), (grow, g_ref))):
            wide, high = sides[kind]
            value = spread(scale, pick) * ref[:, k * step : (k + 1) * step].astype(F32)
            top, rest = halves(value)
            value = mm(wide, jnp.concatenate([top, top], axis=0), 1, 0) + mm(high, rest, 1, 0)
            own_ref[kind, k] = value
            both.append(value)
        firsts[k][...] = jnp.where(lowest, both[0], both[1]).astype(BF)
        if k < ride:
            rider = riders[k]

            @pl.when((place > 0) & (place < lax.axis_size("seq") - 1))
            def _():
                firsts[k][...] = rider[...]


def inner_kernel(first, pairs, size, bc_ref, hp_ref, x_ref, g_ref, *refs):
    gx_ref, ds_ref, sums_ref = refs[-5:-2]
    gy_ref, xg_ref = refs[-2:]
    rows = x_ref.shape[0]
    heads = hp_ref.shape[0] // 5
    lanes = 2 * size
    width = pairs * lanes
    if len(refs) == 6 and first > 0:
        scores = refs[0][...]
    else:
        scores = mm(bc_ref[rows : 2 * rows, :], bc_ref[0:rows, :], 1, 1, TOP)
        refs[0][...] = scores
    row = lax.broadcasted_iota(jnp.int32, (rows, rows), 0)
    col = lax.broadcasted_iota(jnp.int32, (rows, rows), 1)
    causal = row >= col
    dt = hp_ref[heads : 2 * heads, :]
    cum = hp_ref[2 * heads : 3 * heads, :]
    cum_t = cum.T
    lane = lax.broadcasted_iota(jnp.int32, (rows, lanes), 1)
    sides = [jnp.where(lane < size, 1.0, 0.0).astype(BF), jnp.where(lane < size, 0.0, 1.0).astype(BF)]
    ds = jnp.zeros((rows, rows), F32)
    for j in range(pairs):
        place = slice(j * lanes, (j + 1) * lanes)
        x, g = x_ref[:, place], g_ref[:, place]
        xs = jnp.concatenate([x * s for s in sides], axis=0)
        gs = jnp.concatenate([g * s for s in sides], axis=0)
        m = mm(gs, x, 1, 1)
        kern = []
        for i in range(2):
            h = 2 * (first + j) + i
            gap = cum_t[:, h : h + 1] - cum[h : h + 1, :]
            fall = jnp.exp(jnp.where(causal, gap, -jnp.inf)) * dt[h : h + 1, :]
            kern.append((fall * scores).astype(BF))
            ds = ds + fall * m[i * rows : (i + 1) * rows]
        y = mm(jnp.concatenate(kern, axis=1), xs, 1, 0)
        gx = mm(jnp.concatenate(kern, axis=0), gs, 0, 0)
        gx_ref[:, place] = gx
        late = slice(width + j * lanes, width + (j + 1) * lanes)
        gy_ref[:, place], gy_ref[:, late] = halves(g.astype(F32) * y)
        xg_ref[:, place], xg_ref[:, late] = halves(x.astype(F32) * gx)
    ds_ref[...] = ds
    pick = head_lanes(2 * pairs, width, size).astype(BF)
    pick = jnp.concatenate([pick, pick], axis=1)
    sums_ref[0] = mm(pick, gy_ref[...], 1, 1)
    sums_ref[1] = mm(pick, xg_ref[...], 1, 1)


def outer_kernel(k, chunks, size, parts, *refs):
    store_ref, x_ref, g_ref, bc_ref, hp_ref, rate_ref = refs[:6]
    gxs, dss, sums = (refs[6 + q * parts : 6 + (q + 1) * parts] for q in range(3))
    rest = refs[6 + 3 * parts :]
    wv_ref, eu_ref = rest[-2:]
    rows, step = x_ref.shape
    all_heads = rate_ref.shape[1]
    heads = all_heads // chunks
    mine = slice(k * heads, (k + 1) * heads)
    piece = step // parts
    b, c = bc_ref[0:rows, :], bc_ref[rows : 2 * rows, :]
    pre, dt, cum, grow, w = (
        hp_ref[q * all_heads + k * heads : q * all_heads + (k + 1) * heads, :] for q in range(5)
    )
    rate = rate_ref[...].T[mine]
    ds = dss[0][...]
    for ref in dss[1:]:
        ds = ds + ref[...]
    db = mm(c, ds, 0, 0, TOP)
    dc = mm(b, ds, 0, 1, TOP)
    b_wide = jnp.concatenate(halves(b), axis=1)
    c_wide = jnp.concatenate(halves(c), axis=1)
    pick = head_lanes(heads, step, size).astype(BF)
    incoming, outgoing = store_ref[0], store_ref[1]
    u = mm(c_wide, jnp.concatenate([incoming, incoming], axis=0), 1, 0)
    v = mm(b_wide, jnp.concatenate([outgoing, outgoing], axis=0), 1, 0)
    scale = spread(w, pick)
    wx = scale * x_ref[...].astype(F32)
    eg = spread(grow, pick) * g_ref[...].astype(F32)
    grad_ref = rest[-5] if k == chunks - 1 else rest[-4]
    for q in range(parts):
        place = slice(q * piece, (q + 1) * piece)
        grad_ref[:, place] = (gxs[q][...] + scale[:, place] * v[:, place]).astype(BF)
    wv_ref[:, :step], wv_ref[:, step:] = halves(wx * v)
    eu_ref[:, :step], eu_ref[:, step:] = halves(eg * u)
    db = db + mm(
        jnp.concatenate([outgoing, outgoing], axis=1), jnp.concatenate(halves(wx), axis=1), 1, 1
    )
    dc = dc + mm(
        jnp.concatenate([incoming, incoming], axis=1), jnp.concatenate(halves(eg), axis=1), 1, 1
    )
    both = jnp.sum(incoming.astype(F32) * outgoing.astype(F32), axis=0, keepdims=True)
    ddecay = jnp.sum(pick.astype(F32) * both, axis=1, keepdims=True)
    pick = jnp.concatenate([pick, pick], axis=1)
    wdw = mm(pick, wv_ref[...], 1, 1)
    egu = mm(pick, eu_ref[...], 1, 1)
    rowsum = jnp.concatenate([s[0] for s in sums], axis=0)
    colsum = jnp.concatenate([s[1] for s in sums], axis=0)
    dcum = rowsum - colsum + egu - wdw
    row = lax.broadcasted_iota(jnp.int32, (rows, rows), 0)
    col = lax.broadcasted_iota(jnp.int32, (rows, rows), 1)
    rev = mm(dcum, jnp.where(row >= col, 1.0, 0.0), 1, 0, TOP)
    decay = grow[:, rows - 1 : rows]
    rev = rev + jnp.sum(wdw, axis=1, keepdims=True) + decay * ddecay
    gate = 1.0 / (1.0 + jnp.exp(-pre))
    small = 1e-30
    ratio = jnp.where(dt > small, gate / jnp.maximum(dt, small), 1.0)
    graw = (colsum + wdw) * ratio - rate * rev * gate
    if k > 0:
        before_ref = rest[1]
        db = db + before_ref[0:rows, :]
        dc = dc + before_ref[rows : 2 * rows, :]
        graw = jnp.concatenate([before_ref[2 * rows :, :], graw], axis=0)
    if k == chunks - 1:
        keep_ref, give_ref = rest[-4], rest[-3]
        core = lax.axis_index("head")
        keep_ref[0:rows, :] = jnp.where(core == 0, db, dc)
        keep_ref[rows:, :] = graw
        give_ref[...] = jnp.where(core == 0, dc, db)
    else:
        back_ref = rest[-3]
        back_ref[0:rows, :] = db
        back_ref[rows : 2 * rows, :] = dc
        back_ref[2 * rows :, :] = graw


def low_kernel(keep_ref, taken_ref, out_ref):
    rows = taken_ref.shape[0]
    low = keep_ref[0:rows, :] + taken_ref[...]
    low = jnp.concatenate([low, keep_ref[rows:, :]], axis=0).astype(BF)
    for k in range(out_ref.shape[0]):
        out_ref[k] = low


def token_kernel(count, mine_ref, other_ref, *refs):
    out_ref = refs[2 * count]
    me, core = lax.axis_index("dp"), lax.axis_index("head")
    part, cols = refs[0].shape
    half = cols // 2
    heads = refs[1].shape[0] // 2
    for r in range(count):
        at = pl.multiple_of(lax.rem(me - r + count, count) * part, 128)
        total = None
        for k, ref in enumerate((mine_ref, other_ref)):
            at_col = pl.multiple_of(lax.rem(core + k, 2) * half, 128)
            at_row = pl.multiple_of(lax.rem(core + k, 2) * heads, 16)
            term = mm(ref[0:half, :], refs[2 * r][:, pl.ds(at_col, half)], 0, 1)
            term = term + mm(ref[half:, :], refs[2 * r + 1][pl.ds(at_row, heads), :], 0, 0)
            total = term if total is None else total + term
        out_ref[:, pl.ds(at, part)] = total.astype(BF)


def order_kernel(n_dp, n_seq, slots, *refs):
    out_ref, sem = refs[-2:]
    toks = refs[:-2]
    rows = toks[0].shape[0]
    place = lax.axis_index("seq")
    even = lax.rem(place, 2) == 0
    copies = []
    for r in range(n_dp):
        for k, (kind, hop) in enumerate(slots):
            above = even if kind == 0 else ~even
            block = jnp.where(above, place + hop, place - hop)
            fits = (block >= 0) & (block < n_seq)
            if hop > 0 and kind == 1:
                fits = fits & jnp.where(above, place < n_seq - 1, place > 0)
            at = pl.multiple_of(jnp.clip(block, 0, n_seq - 1) * rows, 128)
            source = toks[k] if r == 0 else toks[len(slots) + k].at[pl.ds((r - 1) * rows, rows)]
            copy = pltpu.make_async_copy(source, out_ref.at[r, pl.ds(at, rows)], sem.at[r, k])
            copies.append((fits, copy))
    for fits, copy in copies:
        pl.when(fits)(copy.start)
    for fits, copy in copies:
        pl.when(fits)(copy.wait)


def weight_kernel(scale, n_dp, n_seq, tok_ref, *refs):
    lows = refs[:2]
    bc_ref, dt_ref, low_ref, low_sem = refs[2:]
    rows = tok_ref.shape[1] // n_seq
    share = lows[0].shape[1]
    core, me = lax.axis_index("head"), lax.axis_index("dp")
    copies = []
    for r in range(n_dp):
        for s in range(n_seq):
            index = s * n_dp + lax.rem(me - r + n_dp, n_dp)
            for k in range(2):
                row = pl.multiple_of(lax.rem(core + k, 2) * share, 16)
                copies.append(
                    pltpu.make_async_copy(
                        lows[k].at[index],
                        low_ref.at[r, pl.ds(row, share), pl.ds(s * rows, rows)],
                        low_sem.at[r * n_seq + s, k],
                    )
                )
    for copy in copies:
        copy.start()
    for copy in copies:
        copy.wait()
    total = mm(low_ref[0], tok_ref[0], 1, 0)
    for r in range(1, n_dp):
        total = total + mm(low_ref[r], tok_ref[r], 1, 0)
    total = total * scale
    half = bc_ref.shape[1] // 2
    heads = dt_ref.shape[0] // 2
    for k in range(2):
        bc_ref[:, k * half : (k + 1) * half] = total[k * share : k * share + half].T
        dt_ref[k * heads : (k + 1) * heads, :] = total[k * share + half : (k + 1) * share]


def relays(count):
    groups, _ = matchings(count)
    return [
        (kind, hop)
        for hop in range(1, count)
        for kind in (0, 1)
        if any(i - hop + 1 >= 0 or j + hop - 1 < count for i, j in groups[kind])
    ]


def relay(found, block, steps, *others):
    count = lax.axis_size("seq")
    _, pairs = matchings(count)
    for kind, hop in steps:
        source = block if hop == 1 else found[1 - kind, hop - 1]
        source = after(source, *others) if others else source
        found[kind, hop] = lax.ppermute(source, "seq", pairs[kind])
    return [found[step] for step in steps]


def chains(first, own, decay, inner, beside, riders, late):
    count = lax.axis_size("seq")
    place = lax.axis_index("seq")
    chunks = len(first)
    stores = [jnp.zeros((3,) + own.shape[2:], BF) for _ in range(chunks)]
    got = list(first)
    done, todo, extra = [], list(inner), []
    last = count + chunks - 2
    for slot in range(1, last + 1):
        steps = [(hop, slot - hop) for hop in range(1, count) if 0 <= slot - hop < chunks]
        sent = []
        for hop, k in steps:
            value = got[k]
            if hop == 1 and 0 < k < len(riders):
                value = jnp.where((place == 0) | (place == count - 1), value, riders[k])
            if hop > 1:
                value = jnp.where(place == hop - 1, own[0, k], own[1, k])
                value = (value + decay[k] * got[k].astype(F32)).astype(BF)
            sent.append(value)
        for (hop, k), value in zip(steps, sent):
            to = {i: i for i in range(count)}
            for i in (hop - 1, count - hop - 1):
                to[i], to[i + 1] = i + 1, i
            got[k] = lax.ppermute(value, "seq", sorted(to.items()))
            if hop == 1 and k < len(riders):
                riders[k] = got[k]
        for _ in range(-(-len(todo) // (last + 1 - slot))):
            done.append(todo.pop(0)(*sent))
        if slot == 1:
            extra = beside(*sent)
        if slot == last:
            k = steps[-1][1]
            got[k] = after(got[k], *late(*sent))
        if slot < last:
            held = [got[k] for _, k in steps] + [d[0] for d in done[-1:]]
            if slot == last - 1:
                held += extra
            new = slot < chunks
            if new:
                held.append(got[slot])
            kept = lax.optimization_barrier(tuple(held))
            for (_, k), a in zip(steps, kept):
                got[k] = a
            if new:
                got[slot] = kept[-1]
        for hop, k in steps:
            kind = jnp.where(place == hop, 0, jnp.where(place == count - hop - 1, 1, 2))
            zero = jnp.zeros_like(kind)
            stores[k] = lax.dynamic_update_slice(stores[k], got[k][None], (kind, zero, zero))
    done += [make() for make in todo]
    return stores, done


def body(tokens, ssd_input, grad_out, w_bc, w_dt, decay_rate, dt_bias):
    feats, x, g = tokens[0], ssd_input[0], grad_out[0]
    rows, width = feats.shape
    heads = decay_rate.shape[0]
    size = width // heads
    n_dp, n_seq = lax.axis_size("dp"), lax.axis_size("seq")
    part = width // n_dp
    state_n = w_bc.shape[1] // 2
    w_dt = w_dt.T
    rate, bias = decay_rate[None], dt_bias[None]

    pieces = call(split_kernel, [struct((rows, part), BF)] * n_dp, 1.9, feats)
    items = [pieces[0]] + [cyclic(pieces[r], "dp", r) for r in range(1, n_dp)]
    groups = items[:1]
    if n_dp > 1:
        groups.append(items[1] if n_dp == 2 else jnp.concatenate(items[1:], axis=0))
    found = [{} for _ in groups]
    slots = relays(n_seq)
    step = width // CHUNKS
    ride = n_seq == 4 and all(a.shape == (state_n, step) for a in groups)
    second = [(kind, hop) for kind, hop in slots if hop == 2 and not (ride and kind == 0)]
    near = relay(found[0], groups[0], slots[:2])
    partials, local = [project(items[0], w_bc, w_dt)], []
    for r in range(1, n_dp):
        item = after(items[r], partials[0])
        local.append(project(item, w_bc, w_dt))
        partials.append(cyclic(local[-1], "dp", -r))
    spare = relay(found[1], groups[1], slots[:2], *local) if n_dp > 1 else []
    partials[1:] = [after(a, *near) for a in partials[1:]]
    proj = partials + [cyclic(a, "head", 1) for a in partials]
    own, bc, hp, *outs = call(
        functools.partial(state_kernel, 2 * n_dp, size, int(ride)),
        (
            struct((2, CHUNKS, state_n, step), F32),
            struct((2 * rows, state_n), F32),
            struct((5 * heads, rows), F32),
        )
        + (struct((state_n, step), BF),) * CHUNKS
        + (struct((1, step), F32),) * CHUNKS,
        0.1,
        *proj,
        x,
        g,
        rate,
        bias,
        *([found[0][1, 1]] if ride else []),
    )
    first, decay = outs[:CHUNKS], outs[CHUNKS:]
    pairs = width // (2 * size) // PARTS
    span = width // PARTS
    shared = []

    def inner(q, *others):
        held = after(bc, *others) if others else bc
        square = struct((rows, rows), F32)
        block = pl.BlockSpec((rows, span), lambda _: (0, q))
        out = call(
            functools.partial(inner_kernel, q * pairs, pairs, size),
            ([square] if q == 0 else [])
            + [struct((rows, span), F32), square, struct((2, 2 * pairs, rows), F32)],
                2.6,
            held,
            hp,
            x,
            g,
            *shared,
            scratch=(pltpu.VMEM((rows, 2 * span), BF), pltpu.VMEM((rows, 2 * span), BF)),
            specs=[VMEM, VMEM, block, block] + [VMEM] * len(shared),
        )
        if q == 0:
            shared.append(out[0])
            out = out[1:]
        return out

    weights = [w_bc, w_dt]

    def beside(*others):
        for r in range(1, n_dp):
            weights.extend(cyclic(after(a, *others), "dp", r) for a in (w_bc, w_dt))
        return weights[2:] + relay(found[0], groups[0], second, *others)

    def late(*others):
        return relay(found[1], groups[1], second, *others) if n_dp > 1 else []

    first[0] = after(first[0], *spare)
    riders = [f[1, 1] for f in found] if ride else []
    calls = [functools.partial(inner, q) for q in range(PARTS)]
    stores, inners = chains(first, own, decay, calls, beside, riders, late)
    for f, a in zip(found, riders):
        f[0, 2] = a
    done = [relay(f, a, [t for t in slots if t not in f], stores[-1]) for f, a in zip(found, groups)]
    each = PARTS // CHUNKS
    grad_x, back = None, []
    for k in range(CHUNKS):
        last = k == CHUNKS - 1
        block = pl.BlockSpec((rows, step), lambda _, k=k: (0, k))
        made = (k + 1) * (heads // CHUNKS)
        sums = (struct((rows + heads, rows), F32), struct((rows, rows), F32))
        inputs = [stores[k], x, g, bc, hp, rate]
        for q in range(3):
            inputs += [a[q] for a in inners[k * each : (k + 1) * each]]
        specs = [VMEM, block, block] + [VMEM] * (len(inputs) - 3)
        if k > 0:
            inputs += [grad_x] + back
            specs += [HBM, VMEM]
        grad_x, *back = call(
            functools.partial(outer_kernel, k, CHUNKS, size, each),
            (struct((rows, width), BF),)
            + (sums if last else (struct((2 * rows + made, rows), F32),)),
            5.4 / CHUNKS,
            *inputs,
            scratch=(pltpu.VMEM((rows, 2 * step), BF), pltpu.VMEM((rows, 2 * step), BF)),
            specs=specs,
            out_specs=(block,) + (VMEM,) * (2 if last else 1),
            aliases={len(inputs) - 2: 0} if k > 0 else {},
        )
    keep, give = back
    toks = []
    for f, a in zip(found, groups):
        toks += [a] + [f[step] for step in slots]
    slots = [(0, 0)] + slots
    ordered = call(
        functools.partial(order_kernel, n_dp, n_seq, slots),
        struct((n_dp, n_seq * rows, part), BF),
        1.0,
        *toks,
        scratch=[pltpu.SemaphoreType.DMA((n_dp, len(slots)))],
    )
    taken = after(cyclic(give, "head", 1), ordered)
    count = n_dp * n_seq
    copies = call(low_kernel, struct((count, rows + heads, rows), BF), 1.2, keep, taken)
    mine = copies[0]
    lows = lax.all_to_all(copies, ("seq", "dp"), 0, 0, tiled=True)
    other = cyclic(mine, "head", 1)
    grads = call(
        functools.partial(token_kernel, n_dp),
        struct((rows, width), BF),
        2.9,
        mine,
        other,
        *weights,
    )
    lows = after(lows, grads)
    swapped = cyclic(lows, "head", 1)
    cols = 2 * (rows + heads)
    grad_bc, grad_dt = call(
        functools.partial(weight_kernel, 1.0 / (rows * n_seq * n_dp), n_dp, n_seq),
        (struct((part, 2 * state_n), F32), struct((2 * heads, part), F32)),
        4.0,
        ordered,
        lows,
        swapped,
        limit=LIMIT + 2 * n_dp * n_seq * rows * cols,
        scratch=(
            pltpu.VMEM((n_dp, cols, n_seq * rows), BF),
            pltpu.SemaphoreType.DMA((count, 2)),
        ),
    )
    return grad_x[None], grads[None], grad_bc, grad_dt.T


def solution(mesh):
    in_specs = (
        P(("grp", "dp"), "seq", "head"),
        P(("grp", "dp"), "seq", "head"),
        P(("grp", "dp"), "seq", "head"),
        P(("head", "dp"), None),
        P(("head", "dp"), None),
        P("head"),
        P("head"),
    )
    out_specs = (
        P(("grp", "dp"), "seq", "head"),
        P(("grp", "dp"), "seq", "head"),
        P(("grp", "head", "dp"), None),
        P(("grp", "head", "dp"), None),
    )
    return jax.shard_map(body, mesh=mesh, in_specs=in_specs, out_specs=out_specs, check_vma=False)
```

```python
import functools

import jax
import jax.numpy as jnp
from jax import lax
from jax.experimental import pallas as pl
from jax.experimental.pallas import tpu as pltpu
from jax.sharding import PartitionSpec as P

CHUNKS = 2
PARTS = 4
BF = jnp.bfloat16
F32 = jnp.float32
TOP = lax.Precision.HIGHEST
PER_US = 1.15e9
LIMIT = 16 * 1024 * 1024


def cyclic(a, axis, by):
    count = lax.axis_size(axis)
    return lax.ppermute(a, axis, [(i, (i + by) % count) for i in range(count)])


def mm(a, b, ca, cb, precision=None):
    return lax.dot_general(
        a, b, (((ca,), (cb,)), ((), ())), preferred_element_type=F32, precision=precision
    )


def halves(a):
    high = a.astype(BF)
    return high, (a - high.astype(F32)).astype(BF)


def head_lanes(heads, width, size, first=0):
    row = lax.broadcasted_iota(jnp.int32, (heads, width), 0)
    col = lax.broadcasted_iota(jnp.int32, (heads, width), 1) + first
    low = row * size
    return jnp.where((col >= low) & (col < low + size), 1.0, 0.0).astype(F32)


def spread(a, pick):
    high, low = halves(a)
    both = jnp.concatenate([pick, pick], axis=0)
    return mm(jnp.concatenate([high, low], axis=0), both, 0, 0)


VMEM = pl.BlockSpec(memory_space=pltpu.VMEM)
HBM = pl.BlockSpec(memory_space=pltpu.HBM)


def call(kernel, out_shape, span_us, *args, scratch=(), specs=None, out_specs=None, aliases={}, limit=LIMIT):
    size = sum(a.size * a.dtype.itemsize for a in args)
    return pl.pallas_call(
        kernel,
        out_shape=out_shape,
        grid=(1,),
        in_specs=specs or [VMEM] * len(args),
        out_specs=out_specs or jax.tree.map(lambda _: VMEM, out_shape),
        input_output_aliases=aliases,
        scratch_shapes=list(scratch),
        compiler_params=pltpu.CompilerParams(vmem_limit_bytes=limit),
        cost_estimate=pl.CostEstimate(
            flops=int(span_us * PER_US), bytes_accessed=size, transcendentals=0
        ),
    )(*args)


def struct(shape, dtype):
    return jax.ShapeDtypeStruct(shape, dtype)


def after(a, *others):
    return lax.optimization_barrier((a, others))[0]


def matchings(count):
    groups = [[(i, i + 1) for i in range(kind, count - 1, 2)] for kind in (0, 1)]
    pairs = []
    for group in groups:
        to = {i: i for i in range(count)}
        for i, j in group:
            to[i], to[j] = j, i
        pairs.append(sorted(to.items()))
    return groups, pairs


def split_kernel(a_ref, *refs):
    outs, sem = refs[:-1], refs[-1]
    count = len(outs)
    me = lax.axis_index("dp")
    part = outs[0].shape[1]
    copies = []
    for r in range(count):
        at = pl.multiple_of(lax.rem(me + r, count) * part, 128)
        copies.append(pltpu.make_async_copy(a_ref.at[:, pl.ds(at, part)], outs[r], sem.at[r]))
    for copy in copies:
        copy.start()
    for copy in copies:
        copy.wait()


def project_kernel(a_ref, bc_ref, dt_ref, out_ref):
    a = a_ref[...]
    state_n = bc_ref.shape[1] // 2
    rows = a.shape[0]
    bc = mm(a, bc_ref[...], 1, 0)
    out_ref[0:rows, :] = bc[:, :state_n]
    out_ref[rows : 2 * rows, :] = bc[:, state_n:]
    out_ref[2 * rows :, :] = mm(dt_ref[...], a, 1, 1)


def project(a, w_bc, w_dt):
    rows = a.shape[0]
    total = 2 * rows + w_dt.shape[0]
    return call(
        project_kernel,
        struct((total, w_bc.shape[1] // 2), F32),
        2.1,
        a,
        w_bc,
        w_dt,
    )


def state_kernel(count, size, ride, *refs):
    proj = refs[:count]
    x_ref, g_ref, rate_ref, bias_ref = refs[count : count + 4]
    riders = refs[count + 4 : count + 4 + ride]
    own_ref, bc_ref, hp_ref = refs[count + 4 + ride : count + 7 + ride]
    outs = refs[count + 7 + ride :]
    firsts, decays = outs[: len(outs) // 2], outs[len(outs) // 2 :]
    heads = rate_ref.shape[1]
    rows = x_ref.shape[0]
    rate, bias = rate_ref[...].T, bias_ref[...].T
    chunks, step = own_ref.shape[1], own_ref.shape[3]
    first = pl.multiple_of(2 * rows + lax.axis_index("head") * heads, 8)
    bc = proj[0][0 : 2 * rows, :]
    pre = proj[0][pl.ds(first, heads), :] + bias
    for ref in proj[1:]:
        bc = bc + ref[0 : 2 * rows, :]
        pre = pre + ref[pl.ds(first, heads), :]
    bc_ref[...] = bc
    dt = jnp.maximum(pre, 0.0) + jnp.log1p(jnp.exp(-jnp.abs(pre)))
    row = lax.broadcasted_iota(jnp.int32, (rows, rows), 0)
    col = lax.broadcasted_iota(jnp.int32, (rows, rows), 1)
    cum = mm(-dt * rate, jnp.where(row <= col, 1.0, 0.0), 1, 0, TOP)
    last = cum[:, rows - 1 : rows]
    grow = jnp.exp(cum)
    w = jnp.exp(last - cum) * dt
    decay = jnp.exp(last)
    for k, part in enumerate((pre, dt, cum, grow, w)):
        hp_ref[k * heads : (k + 1) * heads, :] = part
    place = lax.axis_index("seq")
    lowest = place == 0
    sides = []
    for vec in (bc[:rows], bc[rows:]):
        high, low = halves(vec.T)
        sides.append((jnp.concatenate([high, low], axis=1), high))
    for k in range(chunks):
        pick = head_lanes(heads, step, size, k * step)
        decays[k][...] = jnp.sum(pick * decay, axis=0, keepdims=True)
        pick = pick.astype(BF)
        both = []
        for kind, (scale, ref) in enumerate(((w, x_ref), (grow, g_ref))):
            wide, high = sides[kind]
            value = spread(scale, pick) * ref[:, k * step : (k + 1) * step].astype(F32)
            top, rest = halves(value)
            value = mm(wide, jnp.concatenate([top, top], axis=0), 1, 0) + mm(high, rest, 1, 0)
            own_ref[kind, k] = value
            both.append(value)
        firsts[k][...] = jnp.where(lowest, both[0], both[1]).astype(BF)
        if k < ride:
            rider = riders[k]

            @pl.when((place > 0) & (place < lax.axis_size("seq") - 1))
            def _():
                firsts[k][...] = rider[...]


def inner_kernel(first, pairs, size, bc_ref, hp_ref, x_ref, g_ref, *refs):
    gx_ref, ds_ref, sums_ref = refs[-5:-2]
    gy_ref, xg_ref = refs[-2:]
    rows = x_ref.shape[0]
    heads = hp_ref.shape[0] // 5
    lanes = 2 * size
    width = pairs * lanes
    if len(refs) == 6 and first > 0:
        scores = refs[0][...]
    else:
        scores = mm(bc_ref[rows : 2 * rows, :], bc_ref[0:rows, :], 1, 1, TOP)
        refs[0][...] = scores
    row = lax.broadcasted_iota(jnp.int32, (rows, rows), 0)
    col = lax.broadcasted_iota(jnp.int32, (rows, rows), 1)
    causal = row >= col
    dt = hp_ref[heads : 2 * heads, :]
    cum = hp_ref[2 * heads : 3 * heads, :]
    cum_t = cum.T
    lane = lax.broadcasted_iota(jnp.int32, (rows, lanes), 1)
    sides = [jnp.where(lane < size, 1.0, 0.0).astype(BF), jnp.where(lane < size, 0.0, 1.0).astype(BF)]
    ds = jnp.zeros((rows, rows), F32)
    for j in range(pairs):
        place = slice(j * lanes, (j + 1) * lanes)
        x, g = x_ref[:, place], g_ref[:, place]
        xs = jnp.concatenate([x * s for s in sides], axis=0)
        gs = jnp.concatenate([g * s for s in sides], axis=0)
        m = mm(gs, x, 1, 1)
        kern = []
        for i in range(2):
            h = 2 * (first + j) + i
            gap = cum_t[:, h : h + 1] - cum[h : h + 1, :]
            fall = jnp.exp(jnp.where(causal, gap, -jnp.inf)) * dt[h : h + 1, :]
            kern.append((fall * scores).astype(BF))
            ds = ds + fall * m[i * rows : (i + 1) * rows]
        y = mm(jnp.concatenate(kern, axis=1), xs, 1, 0)
        gx = mm(jnp.concatenate(kern, axis=0), gs, 0, 0)
        gx_ref[:, place] = gx
        late = slice(width + j * lanes, width + (j + 1) * lanes)
        gy_ref[:, place], gy_ref[:, late] = halves(g.astype(F32) * y)
        xg_ref[:, place], xg_ref[:, late] = halves(x.astype(F32) * gx)
    ds_ref[...] = ds
    pick = head_lanes(2 * pairs, width, size).astype(BF)
    pick = jnp.concatenate([pick, pick], axis=1)
    sums_ref[0] = mm(pick, gy_ref[...], 1, 1)
    sums_ref[1] = mm(pick, xg_ref[...], 1, 1)


def outer_kernel(k, chunks, size, parts, *refs):
    store_ref, x_ref, g_ref, bc_ref, hp_ref, rate_ref = refs[:6]
    gxs, dss, sums = (refs[6 + q * parts : 6 + (q + 1) * parts] for q in range(3))
    rest = refs[6 + 3 * parts :]
    wv_ref, eu_ref = rest[-2:]
    rows, step = x_ref.shape
    all_heads = rate_ref.shape[1]
    heads = all_heads // chunks
    mine = slice(k * heads, (k + 1) * heads)
    piece = step // parts
    b, c = bc_ref[0:rows, :], bc_ref[rows : 2 * rows, :]
    pre, dt, cum, grow, w = (
        hp_ref[q * all_heads + k * heads : q * all_heads + (k + 1) * heads, :] for q in range(5)
    )
    rate = rate_ref[...].T[mine]
    ds = dss[0][...]
    for ref in dss[1:]:
        ds = ds + ref[...]
    db = mm(c, ds, 0, 0, TOP)
    dc = mm(b, ds, 0, 1, TOP)
    b_wide = jnp.concatenate(halves(b), axis=1)
    c_wide = jnp.concatenate(halves(c), axis=1)
    pick = head_lanes(heads, step, size).astype(BF)
    incoming, outgoing = store_ref[0], store_ref[1]
    u = mm(c_wide, jnp.concatenate([incoming, incoming], axis=0), 1, 0)
    v = mm(b_wide, jnp.concatenate([outgoing, outgoing], axis=0), 1, 0)
    scale = spread(w, pick)
    wx = scale * x_ref[...].astype(F32)
    eg = spread(grow, pick) * g_ref[...].astype(F32)
    grad_ref = rest[-5] if k == chunks - 1 else rest[-4]
    for q in range(parts):
        place = slice(q * piece, (q + 1) * piece)
        grad_ref[:, place] = (gxs[q][...] + scale[:, place] * v[:, place]).astype(BF)
    wv_ref[:, :step], wv_ref[:, step:] = halves(wx * v)
    eu_ref[:, :step], eu_ref[:, step:] = halves(eg * u)
    db = db + mm(
        jnp.concatenate([outgoing, outgoing], axis=1), jnp.concatenate(halves(wx), axis=1), 1, 1
    )
    dc = dc + mm(
        jnp.concatenate([incoming, incoming], axis=1), jnp.concatenate(halves(eg), axis=1), 1, 1
    )
    both = jnp.sum(incoming.astype(F32) * outgoing.astype(F32), axis=0, keepdims=True)
    ddecay = jnp.sum(pick.astype(F32) * both, axis=1, keepdims=True)
    pick = jnp.concatenate([pick, pick], axis=1)
    wdw = mm(pick, wv_ref[...], 1, 1)
    egu = mm(pick, eu_ref[...], 1, 1)
    rowsum = jnp.concatenate([s[0] for s in sums], axis=0)
    colsum = jnp.concatenate([s[1] for s in sums], axis=0)
    dcum = rowsum - colsum + egu - wdw
    row = lax.broadcasted_iota(jnp.int32, (rows, rows), 0)
    col = lax.broadcasted_iota(jnp.int32, (rows, rows), 1)
    rev = mm(dcum, jnp.where(row >= col, 1.0, 0.0), 1, 0, TOP)
    decay = grow[:, rows - 1 : rows]
    rev = rev + jnp.sum(wdw, axis=1, keepdims=True) + decay * ddecay
    gate = 1.0 / (1.0 + jnp.exp(-pre))
    small = 1e-30
    ratio = jnp.where(dt > small, gate / jnp.maximum(dt, small), 1.0)
    graw = (colsum + wdw) * ratio - rate * rev * gate
    if k > 0:
        before_ref = rest[1]
        db = db + before_ref[0:rows, :]
        dc = dc + before_ref[rows : 2 * rows, :]
        graw = jnp.concatenate([before_ref[2 * rows :, :], graw], axis=0)
    if k == chunks - 1:
        keep_ref, give_ref = rest[-4], rest[-3]
        core = lax.axis_index("head")
        keep_ref[0:rows, :] = jnp.where(core == 0, db, dc)
        keep_ref[rows:, :] = graw
        give_ref[...] = jnp.where(core == 0, dc, db)
    else:
        back_ref = rest[-3]
        back_ref[0:rows, :] = db
        back_ref[rows : 2 * rows, :] = dc
        back_ref[2 * rows :, :] = graw


def low_kernel(keep_ref, taken_ref, out_ref):
    rows = taken_ref.shape[0]
    low = keep_ref[0:rows, :] + taken_ref[...]
    low = jnp.concatenate([low, keep_ref[rows:, :]], axis=0).astype(BF)
    for k in range(out_ref.shape[0]):
        out_ref[k] = low


def token_kernel(count, mine_ref, other_ref, *refs):
    out_ref = refs[2 * count]
    me, core = lax.axis_index("dp"), lax.axis_index("head")
    part, cols = refs[0].shape
    half = cols // 2
    heads = refs[1].shape[0] // 2
    for r in range(count):
        at = pl.multiple_of(lax.rem(me - r + count, count) * part, 128)
        total = None
        for k, ref in enumerate((mine_ref, other_ref)):
            at_col = pl.multiple_of(lax.rem(core + k, 2) * half, 128)
            at_row = pl.multiple_of(lax.rem(core + k, 2) * heads, 16)
            term = mm(ref[0:half, :], refs[2 * r][:, pl.ds(at_col, half)], 0, 1)
            term = term + mm(ref[half:, :], refs[2 * r + 1][pl.ds(at_row, heads), :], 0, 0)
            total = term if total is None else total + term
        out_ref[:, pl.ds(at, part)] = total.astype(BF)


def order_kernel(n_dp, n_seq, slots, *refs):
    out_ref, sem = refs[-2:]
    toks = refs[:-2]
    rows = toks[0].shape[0]
    place = lax.axis_index("seq")
    even = lax.rem(place, 2) == 0
    copies = []
    for r in range(n_dp):
        for k, (kind, hop) in enumerate(slots):
            above = even if kind == 0 else ~even
            block = jnp.where(above, place + hop, place - hop)
            fits = (block >= 0) & (block < n_seq)
            if hop > 0 and kind == 1:
                fits = fits & jnp.where(above, place < n_seq - 1, place > 0)
            at = pl.multiple_of(jnp.clip(block, 0, n_seq - 1) * rows, 128)
            source = toks[k] if r == 0 else toks[len(slots) + k].at[pl.ds((r - 1) * rows, rows)]
            copy = pltpu.make_async_copy(source, out_ref.at[r, pl.ds(at, rows)], sem.at[r, k])
            copies.append((fits, copy))
    for fits, copy in copies:
        pl.when(fits)(copy.start)
    for fits, copy in copies:
        pl.when(fits)(copy.wait)


def weight_kernel(scale, n_dp, n_seq, tok_ref, *refs):
    lows = refs[:2]
    bc_ref, dt_ref, low_ref, low_sem = refs[2:]
    rows = tok_ref.shape[1] // n_seq
    share = lows[0].shape[1]
    core, me = lax.axis_index("head"), lax.axis_index("dp")
    copies = []
    for r in range(n_dp):
        for s in range(n_seq):
            index = s * n_dp + lax.rem(me - r + n_dp, n_dp)
            for k in range(2):
                row = pl.multiple_of(lax.rem(core + k, 2) * share, 16)
                copies.append(
                    pltpu.make_async_copy(
                        lows[k].at[index],
                        low_ref.at[r, pl.ds(row, share), pl.ds(s * rows, rows)],
                        low_sem.at[r * n_seq + s, k],
                    )
                )
    for copy in copies:
        copy.start()
    for copy in copies:
        copy.wait()
    total = mm(low_ref[0], tok_ref[0], 1, 0)
    for r in range(1, n_dp):
        total = total + mm(low_ref[r], tok_ref[r], 1, 0)
    total = total * scale
    half = bc_ref.shape[1] // 2
    heads = dt_ref.shape[0] // 2
    for k in range(2):
        bc_ref[:, k * half : (k + 1) * half] = total[k * share : k * share + half].T
        dt_ref[k * heads : (k + 1) * heads, :] = total[k * share + half : (k + 1) * share]


def relays(count):
    groups, _ = matchings(count)
    return [
        (kind, hop)
        for hop in range(1, count)
        for kind in (0, 1)
        if any(i - hop + 1 >= 0 or j + hop - 1 < count for i, j in groups[kind])
    ]


def relay(found, block, steps, *others):
    count = lax.axis_size("seq")
    _, pairs = matchings(count)
    for kind, hop in steps:
        source = block if hop == 1 else found[1 - kind, hop - 1]
        source = after(source, *others) if others else source
        found[kind, hop] = lax.ppermute(source, "seq", pairs[kind])
    return [found[step] for step in steps]


def chains(first, own, decay, inner, beside, riders):
    count = lax.axis_size("seq")
    place = lax.axis_index("seq")
    chunks = len(first)
    stores = [jnp.zeros((3,) + own.shape[2:], BF) for _ in range(chunks)]
    got = list(first)
    done, todo, extra = [], list(inner), []
    last = count + chunks - 2
    for slot in range(1, last + 1):
        steps = [(hop, slot - hop) for hop in range(1, count) if 0 <= slot - hop < chunks]
        sent = []
        for hop, k in steps:
            value = got[k]
            if hop == 1 and 0 < k < len(riders):
                value = jnp.where((place == 0) | (place == count - 1), value, riders[k])
            if hop > 1:
                value = jnp.where(place == hop - 1, own[0, k], own[1, k])
                value = (value + decay[k] * got[k].astype(F32)).astype(BF)
            sent.append(value)
        for (hop, k), value in zip(steps, sent):
            to = {i: i for i in range(count)}
            for i in (hop - 1, count - hop - 1):
                to[i], to[i + 1] = i + 1, i
            got[k] = lax.ppermute(value, "seq", sorted(to.items()))
            if hop == 1 and k < len(riders):
                riders[k] = got[k]
        for _ in range(-(-len(todo) // (last + 1 - slot))):
            done.append(todo.pop(0)(*sent))
        if slot == 1:
            extra = beside(*sent)
        if slot < last:
            held = [got[k] for _, k in steps] + [d[0] for d in done[-1:]]
            if slot == last - 1:
                held += extra
            new = slot < chunks
            if new:
                held.append(got[slot])
            kept = lax.optimization_barrier(tuple(held))
            for (_, k), a in zip(steps, kept):
                got[k] = a
            if new:
                got[slot] = kept[-1]
        for hop, k in steps:
            kind = jnp.where(place == hop, 0, jnp.where(place == count - hop - 1, 1, 2))
            zero = jnp.zeros_like(kind)
            stores[k] = lax.dynamic_update_slice(stores[k], got[k][None], (kind, zero, zero))
    done += [make() for make in todo]
    return stores, done


def body(tokens, ssd_input, grad_out, w_bc, w_dt, decay_rate, dt_bias):
    feats, x, g = tokens[0], ssd_input[0], grad_out[0]
    rows, width = feats.shape
    heads = decay_rate.shape[0]
    size = width // heads
    n_dp, n_seq = lax.axis_size("dp"), lax.axis_size("seq")
    part = width // n_dp
    state_n = w_bc.shape[1] // 2
    w_dt = w_dt.T
    rate, bias = decay_rate[None], dt_bias[None]

    pieces = call(
        split_kernel,
        [struct((rows, part), BF)] * n_dp,
        1.9,
        feats,
        scratch=[pltpu.SemaphoreType.DMA((n_dp,))],
        specs=[HBM],
    )
    items = [pieces[0]] + [cyclic(pieces[r], "dp", r) for r in range(1, n_dp)]
    groups = items[:1]
    if n_dp > 1:
        groups.append(items[1] if n_dp == 2 else jnp.concatenate(items[1:], axis=0))
    found = [{} for _ in groups]
    slots = relays(n_seq)
    step = width // CHUNKS
    ride = n_seq == 4 and all(a.shape == (state_n, step) for a in groups)
    second = [(kind, hop) for kind, hop in slots if hop == 2 and not (ride and kind == 0)]
    near = relay(found[0], groups[0], slots[:2])
    partials, local = [project(items[0], w_bc, w_dt)], []
    for r in range(1, n_dp):
        item = after(items[r], partials[0])
        local.append(project(item, w_bc, w_dt))
        partials.append(cyclic(local[-1], "dp", -r))
    spare = relay(found[1], groups[1], slots[:2], *local) if n_dp > 1 else []
    partials[1:] = [after(a, *near) for a in partials[1:]]
    proj = partials + [cyclic(a, "head", 1) for a in partials]
    own, bc, hp, *outs = call(
        functools.partial(state_kernel, 2 * n_dp, size, int(ride)),
        (
            struct((2, CHUNKS, state_n, step), F32),
            struct((2 * rows, state_n), F32),
            struct((5 * heads, rows), F32),
        )
        + (struct((state_n, step), BF),) * CHUNKS
        + (struct((1, step), F32),) * CHUNKS,
        0.1,
        *proj,
        x,
        g,
        rate,
        bias,
        *([found[0][1, 1]] if ride else []),
    )
    first, decay = outs[:CHUNKS], outs[CHUNKS:]
    pairs = width // (2 * size) // PARTS
    span = width // PARTS
    shared = []

    def inner(q, *others):
        held = after(bc, *others) if others else bc
        square = struct((rows, rows), F32)
        block = pl.BlockSpec((rows, span), lambda _: (0, q))
        out = call(
            functools.partial(inner_kernel, q * pairs, pairs, size),
            ([square] if q == 0 else [])
            + [struct((rows, span), F32), square, struct((2, 2 * pairs, rows), F32)],
                2.6,
            held,
            hp,
            x,
            g,
            *shared,
            scratch=(pltpu.VMEM((rows, 2 * span), BF), pltpu.VMEM((rows, 2 * span), BF)),
            specs=[VMEM, VMEM, block, block] + [VMEM] * len(shared),
        )
        if q == 0:
            shared.append(out[0])
            out = out[1:]
        return out

    weights = [w_bc, w_dt]

    def beside(*others):
        for r in range(1, n_dp):
            weights.extend(cyclic(after(a, *others), "dp", r) for a in (w_bc, w_dt))
        return weights[2:] + [a for f, b in zip(found, groups) for a in relay(f, b, second, *others)]

    first[0] = after(first[0], *spare)
    riders = [f[1, 1] for f in found] if ride else []
    calls = [functools.partial(inner, q) for q in range(PARTS)]
    stores, inners = chains(first, own, decay, calls, beside, riders)
    for f, a in zip(found, riders):
        f[0, 2] = a
    done = [relay(f, a, [t for t in slots if t not in f], stores[-1]) for f, a in zip(found, groups)]
    each = PARTS // CHUNKS
    grad_x, back = None, []
    for k in range(CHUNKS):
        last = k == CHUNKS - 1
        block = pl.BlockSpec((rows, step), lambda _, k=k: (0, k))
        made = (k + 1) * (heads // CHUNKS)
        sums = (struct((rows + heads, rows), F32), struct((rows, rows), F32))
        inputs = [stores[k], x, g, bc, hp, rate]
        for q in range(3):
            inputs += [a[q] for a in inners[k * each : (k + 1) * each]]
        specs = [VMEM, block, block] + [VMEM] * (len(inputs) - 3)
        if k > 0:
            inputs += [grad_x] + back
            specs += [HBM, VMEM]
        grad_x, *back = call(
            functools.partial(outer_kernel, k, CHUNKS, size, each),
            (struct((rows, width), BF),)
            + (sums if last else (struct((2 * rows + made, rows), F32),)),
            5.4 / CHUNKS,
            *inputs,
            scratch=(pltpu.VMEM((rows, 2 * step), BF), pltpu.VMEM((rows, 2 * step), BF)),
            specs=specs,
            out_specs=(block,) + (VMEM,) * (2 if last else 1),
            aliases={len(inputs) - 2: 0} if k > 0 else {},
        )
    keep, give = back
    toks = []
    for f, a in zip(found, groups):
        toks += [a] + [f[step] for step in slots]
    slots = [(0, 0)] + slots
    ordered = call(
        functools.partial(order_kernel, n_dp, n_seq, slots),
        struct((n_dp, n_seq * rows, part), BF),
        1.0,
        *toks,
        scratch=[pltpu.SemaphoreType.DMA((n_dp, len(slots)))],
    )
    taken = after(cyclic(give, "head", 1), ordered)
    count = n_dp * n_seq
    copies = call(low_kernel, struct((count, rows + heads, rows), BF), 1.2, keep, taken)
    mine = copies[0]
    lows = lax.all_to_all(copies, ("seq", "dp"), 0, 0, tiled=True)
    other = cyclic(mine, "head", 1)
    grads = call(
        functools.partial(token_kernel, n_dp),
        struct((rows, width), BF),
        2.9,
        mine,
        other,
        *weights,
    )
    lows = after(lows, grads)
    swapped = cyclic(lows, "head", 1)
    cols = 2 * (rows + heads)
    grad_bc, grad_dt = call(
        functools.partial(weight_kernel, 1.0 / (rows * n_seq * n_dp), n_dp, n_seq),
        (struct((part, 2 * state_n), F32), struct((2 * heads, part), F32)),
        4.0,
        ordered,
        lows,
        swapped,
        limit=LIMIT + 2 * n_dp * n_seq * rows * cols,
        scratch=(
            pltpu.VMEM((n_dp, cols, n_seq * rows), BF),
            pltpu.SemaphoreType.DMA((count, 2)),
        ),
    )
    return grad_x[None], grads[None], grad_bc, grad_dt.T


def solution(mesh):
    in_specs = (
        P(("grp", "dp"), "seq", "head"),
        P(("grp", "dp"), "seq", "head"),
        P(("grp", "dp"), "seq", "head"),
        P(("head", "dp"), None),
        P(("head", "dp"), None),
        P("head"),
        P("head"),
    )
    out_specs = (
        P(("grp", "dp"), "seq", "head"),
        P(("grp", "dp"), "seq", "head"),
        P(("grp", "head", "dp"), None),
        P(("grp", "head", "dp"), None),
    )
    return jax.shard_map(body, mesh=mesh, in_specs=in_specs, out_specs=out_specs, check_vma=False)
```

```python
import functools

import jax
import jax.numpy as jnp
from jax import lax
from jax.experimental import pallas as pl
from jax.experimental.pallas import tpu as pltpu
from jax.sharding import PartitionSpec as P

CHUNKS = 2
PARTS = 4
BF = jnp.bfloat16
F32 = jnp.float32
TOP = lax.Precision.HIGHEST
PER_US = 1.15e9
LIMIT = 16 * 1024 * 1024


def cyclic(a, axis, by):
    count = lax.axis_size(axis)
    return lax.ppermute(a, axis, [(i, (i + by) % count) for i in range(count)])


def mm(a, b, ca, cb, precision=None):
    return lax.dot_general(
        a, b, (((ca,), (cb,)), ((), ())), preferred_element_type=F32, precision=precision
    )


def halves(a):
    high = a.astype(BF)
    return high, (a - high.astype(F32)).astype(BF)


def head_lanes(heads, width, size, first=0):
    row = lax.broadcasted_iota(jnp.int32, (heads, width), 0)
    col = lax.broadcasted_iota(jnp.int32, (heads, width), 1) + first
    low = row * size
    return jnp.where((col >= low) & (col < low + size), 1.0, 0.0).astype(F32)


def spread(a, pick):
    high, low = halves(a)
    both = jnp.concatenate([pick, pick], axis=0)
    return mm(jnp.concatenate([high, low], axis=0), both, 0, 0)


VMEM = pl.BlockSpec(memory_space=pltpu.VMEM)
HBM = pl.BlockSpec(memory_space=pltpu.HBM)


def call(kernel, out_shape, span_us, *args, scratch=(), specs=None, out_specs=None, aliases={}, limit=LIMIT):
    size = sum(a.size * a.dtype.itemsize for a in args)
    return pl.pallas_call(
        kernel,
        out_shape=out_shape,
        grid=(1,),
        in_specs=specs or [VMEM] * len(args),
        out_specs=out_specs or jax.tree.map(lambda _: VMEM, out_shape),
        input_output_aliases=aliases,
        scratch_shapes=list(scratch),
        compiler_params=pltpu.CompilerParams(vmem_limit_bytes=limit),
        cost_estimate=pl.CostEstimate(
            flops=int(span_us * PER_US), bytes_accessed=size, transcendentals=0
        ),
    )(*args)


def struct(shape, dtype):
    return jax.ShapeDtypeStruct(shape, dtype)


def after(a, *others):
    return lax.optimization_barrier((a, others))[0]


def matchings(count):
    groups = [[(i, i + 1) for i in range(kind, count - 1, 2)] for kind in (0, 1)]
    pairs = []
    for group in groups:
        to = {i: i for i in range(count)}
        for i, j in group:
            to[i], to[j] = j, i
        pairs.append(sorted(to.items()))
    return groups, pairs


def split_kernel(a_ref, *outs):
    count = len(outs)
    me = lax.axis_index("dp")
    part = outs[0].shape[1]
    for r in range(count):
        at = pl.multiple_of(lax.rem(me + r, count) * part, 128)
        outs[r][...] = a_ref[:, pl.ds(at, part)]


def project_kernel(a_ref, bc_ref, dt_ref, out_ref):
    a = a_ref[...]
    state_n = bc_ref.shape[1] // 2
    rows = a.shape[0]
    bc = mm(a, bc_ref[...], 1, 0)
    out_ref[0:rows, :] = bc[:, :state_n]
    out_ref[rows : 2 * rows, :] = bc[:, state_n:]
    out_ref[2 * rows :, :] = mm(dt_ref[...], a, 1, 1)


def project(a, w_bc, w_dt):
    rows = a.shape[0]
    total = 2 * rows + w_dt.shape[0]
    return call(
        project_kernel,
        struct((total, w_bc.shape[1] // 2), F32),
        2.1,
        a,
        w_bc,
        w_dt,
    )


def state_kernel(count, size, ride, *refs):
    proj = refs[:count]
    x_ref, g_ref, rate_ref, bias_ref = refs[count : count + 4]
    riders = refs[count + 4 : count + 4 + ride]
    own_ref, bc_ref, hp_ref = refs[count + 4 + ride : count + 7 + ride]
    outs = refs[count + 7 + ride :]
    firsts, decays = outs[: len(outs) // 2], outs[len(outs) // 2 :]
    heads = rate_ref.shape[1]
    rows = x_ref.shape[0]
    rate, bias = rate_ref[...].T, bias_ref[...].T
    chunks, step = own_ref.shape[1], own_ref.shape[3]
    first = pl.multiple_of(2 * rows + lax.axis_index("head") * heads, 8)
    bc = proj[0][0 : 2 * rows, :]
    pre = proj[0][pl.ds(first, heads), :] + bias
    for ref in proj[1:]:
        bc = bc + ref[0 : 2 * rows, :]
        pre = pre + ref[pl.ds(first, heads), :]
    bc_ref[...] = bc
    dt = jnp.maximum(pre, 0.0) + jnp.log1p(jnp.exp(-jnp.abs(pre)))
    row = lax.broadcasted_iota(jnp.int32, (rows, rows), 0)
    col = lax.broadcasted_iota(jnp.int32, (rows, rows), 1)
    cum = mm(-dt * rate, jnp.where(row <= col, 1.0, 0.0), 1, 0, TOP)
    last = cum[:, rows - 1 : rows]
    grow = jnp.exp(cum)
    w = jnp.exp(last - cum) * dt
    decay = jnp.exp(last)
    for k, part in enumerate((pre, dt, cum, grow, w)):
        hp_ref[k * heads : (k + 1) * heads, :] = part
    place = lax.axis_index("seq")
    lowest = place == 0
    sides = []
    for vec in (bc[:rows], bc[rows:]):
        high, low = halves(vec.T)
        sides.append((jnp.concatenate([high, low], axis=1), high))
    for k in range(chunks):
        pick = head_lanes(heads, step, size, k * step)
        decays[k][...] = jnp.sum(pick * decay, axis=0, keepdims=True)
        pick = pick.astype(BF)
        both = []
        for kind, (scale, ref) in enumerate(((w, x_ref), (grow, g_ref))):
            wide, high = sides[kind]
            value = spread(scale, pick) * ref[:, k * step : (k + 1) * step].astype(F32)
            top, rest = halves(value)
            value = mm(wide, jnp.concatenate([top, top], axis=0), 1, 0) + mm(high, rest, 1, 0)
            own_ref[kind, k] = value
            both.append(value)
        firsts[k][...] = jnp.where(lowest, both[0], both[1]).astype(BF)
        if k < ride:
            rider = riders[k]

            @pl.when((place > 0) & (place < lax.axis_size("seq") - 1))
            def _():
                firsts[k][...] = rider[...]


def inner_kernel(first, pairs, size, bc_ref, hp_ref, x_ref, g_ref, *refs):
    gx_ref, ds_ref, sums_ref = refs[-5:-2]
    gy_ref, xg_ref = refs[-2:]
    rows = x_ref.shape[0]
    heads = hp_ref.shape[0] // 5
    lanes = 2 * size
    width = pairs * lanes
    if len(refs) == 6 and first > 0:
        scores = refs[0][...]
    else:
        scores = mm(bc_ref[rows : 2 * rows, :], bc_ref[0:rows, :], 1, 1, TOP)
        refs[0][...] = scores
    row = lax.broadcasted_iota(jnp.int32, (rows, rows), 0)
    col = lax.broadcasted_iota(jnp.int32, (rows, rows), 1)
    causal = row >= col
    dt = hp_ref[heads : 2 * heads, :]
    cum = hp_ref[2 * heads : 3 * heads, :]
    cum_t = cum.T
    lane = lax.broadcasted_iota(jnp.int32, (rows, lanes), 1)
    sides = [jnp.where(lane < size, 1.0, 0.0).astype(BF), jnp.where(lane < size, 0.0, 1.0).astype(BF)]
    ds = jnp.zeros((rows, rows), F32)
    for j in range(pairs):
        place = slice(j * lanes, (j + 1) * lanes)
        x, g = x_ref[:, place], g_ref[:, place]
        xs = jnp.concatenate([x * s for s in sides], axis=0)
        gs = jnp.concatenate([g * s for s in sides], axis=0)
        m = mm(gs, x, 1, 1)
        kern = []
        for i in range(2):
            h = 2 * (first + j) + i
            gap = cum_t[:, h : h + 1] - cum[h : h + 1, :]
            fall = jnp.exp(jnp.where(causal, gap, -jnp.inf)) * dt[h : h + 1, :]
            kern.append((fall * scores).astype(BF))
            ds = ds + fall * m[i * rows : (i + 1) * rows]
        y = mm(jnp.concatenate(kern, axis=1), xs, 1, 0)
        gx = mm(jnp.concatenate(kern, axis=0), gs, 0, 0)
        gx_ref[:, place] = gx
        late = slice(width + j * lanes, width + (j + 1) * lanes)
        gy_ref[:, place], gy_ref[:, late] = halves(g.astype(F32) * y)
        xg_ref[:, place], xg_ref[:, late] = halves(x.astype(F32) * gx)
    ds_ref[...] = ds
    pick = head_lanes(2 * pairs, width, size).astype(BF)
    pick = jnp.concatenate([pick, pick], axis=1)
    sums_ref[0] = mm(pick, gy_ref[...], 1, 1)
    sums_ref[1] = mm(pick, xg_ref[...], 1, 1)


def outer_kernel(k, chunks, size, parts, *refs):
    store_ref, x_ref, g_ref, bc_ref, hp_ref, rate_ref = refs[:6]
    gxs, dss, sums = (refs[6 + q * parts : 6 + (q + 1) * parts] for q in range(3))
    rest = refs[6 + 3 * parts :]
    wv_ref, eu_ref = rest[-2:]
    rows, step = x_ref.shape
    all_heads = rate_ref.shape[1]
    heads = all_heads // chunks
    mine = slice(k * heads, (k + 1) * heads)
    piece = step // parts
    b, c = bc_ref[0:rows, :], bc_ref[rows : 2 * rows, :]
    pre, dt, cum, grow, w = (
        hp_ref[q * all_heads + k * heads : q * all_heads + (k + 1) * heads, :] for q in range(5)
    )
    rate = rate_ref[...].T[mine]
    ds = dss[0][...]
    for ref in dss[1:]:
        ds = ds + ref[...]
    db = mm(c, ds, 0, 0, TOP)
    dc = mm(b, ds, 0, 1, TOP)
    b_wide = jnp.concatenate(halves(b), axis=1)
    c_wide = jnp.concatenate(halves(c), axis=1)
    pick = head_lanes(heads, step, size).astype(BF)
    incoming, outgoing = store_ref[0], store_ref[1]
    u = mm(c_wide, jnp.concatenate([incoming, incoming], axis=0), 1, 0)
    v = mm(b_wide, jnp.concatenate([outgoing, outgoing], axis=0), 1, 0)
    scale = spread(w, pick)
    wx = scale * x_ref[...].astype(F32)
    eg = spread(grow, pick) * g_ref[...].astype(F32)
    grad_ref = rest[-5] if k == chunks - 1 else rest[-4]
    for q in range(parts):
        place = slice(q * piece, (q + 1) * piece)
        grad_ref[:, place] = (gxs[q][...] + scale[:, place] * v[:, place]).astype(BF)
    wv_ref[:, :step], wv_ref[:, step:] = halves(wx * v)
    eu_ref[:, :step], eu_ref[:, step:] = halves(eg * u)
    db = db + mm(
        jnp.concatenate([outgoing, outgoing], axis=1), jnp.concatenate(halves(wx), axis=1), 1, 1
    )
    dc = dc + mm(
        jnp.concatenate([incoming, incoming], axis=1), jnp.concatenate(halves(eg), axis=1), 1, 1
    )
    both = jnp.sum(incoming.astype(F32) * outgoing.astype(F32), axis=0, keepdims=True)
    ddecay = jnp.sum(pick.astype(F32) * both, axis=1, keepdims=True)
    pick = jnp.concatenate([pick, pick], axis=1)
    wdw = mm(pick, wv_ref[...], 1, 1)
    egu = mm(pick, eu_ref[...], 1, 1)
    rowsum = jnp.concatenate([s[0] for s in sums], axis=0)
    colsum = jnp.concatenate([s[1] for s in sums], axis=0)
    dcum = rowsum - colsum + egu - wdw
    row = lax.broadcasted_iota(jnp.int32, (rows, rows), 0)
    col = lax.broadcasted_iota(jnp.int32, (rows, rows), 1)
    rev = mm(dcum, jnp.where(row >= col, 1.0, 0.0), 1, 0, TOP)
    decay = grow[:, rows - 1 : rows]
    rev = rev + jnp.sum(wdw, axis=1, keepdims=True) + decay * ddecay
    gate = 1.0 / (1.0 + jnp.exp(-pre))
    small = 1e-30
    ratio = jnp.where(dt > small, gate / jnp.maximum(dt, small), 1.0)
    graw = (colsum + wdw) * ratio - rate * rev * gate
    if k > 0:
        before_ref = rest[1]
        db = db + before_ref[0:rows, :]
        dc = dc + before_ref[rows : 2 * rows, :]
        graw = jnp.concatenate([before_ref[2 * rows :, :], graw], axis=0)
    if k == chunks - 1:
        keep_ref, give_ref = rest[-4], rest[-3]
        core = lax.axis_index("head")
        keep_ref[0:rows, :] = jnp.where(core == 0, db, dc)
        keep_ref[rows:, :] = graw
        give_ref[...] = jnp.where(core == 0, dc, db)
    else:
        back_ref = rest[-3]
        back_ref[0:rows, :] = db
        back_ref[rows : 2 * rows, :] = dc
        back_ref[2 * rows :, :] = graw


def low_kernel(keep_ref, taken_ref, out_ref):
    rows = taken_ref.shape[0]
    low = keep_ref[0:rows, :] + taken_ref[...]
    low = jnp.concatenate([low, keep_ref[rows:, :]], axis=0).astype(BF)
    for k in range(out_ref.shape[0]):
        out_ref[k] = low


def token_kernel(count, mine_ref, other_ref, *refs):
    out_ref = refs[2 * count]
    me, core = lax.axis_index("dp"), lax.axis_index("head")
    part, cols = refs[0].shape
    half = cols // 2
    heads = refs[1].shape[0] // 2
    for r in range(count):
        at = pl.multiple_of(lax.rem(me - r + count, count) * part, 128)
        total = None
        for k, ref in enumerate((mine_ref, other_ref)):
            at_col = pl.multiple_of(lax.rem(core + k, 2) * half, 128)
            at_row = pl.multiple_of(lax.rem(core + k, 2) * heads, 16)
            term = mm(ref[0:half, :], refs[2 * r][:, pl.ds(at_col, half)], 0, 1)
            term = term + mm(ref[half:, :], refs[2 * r + 1][pl.ds(at_row, heads), :], 0, 0)
            total = term if total is None else total + term
        out_ref[:, pl.ds(at, part)] = total.astype(BF)


def order_kernel(n_dp, n_seq, slots, *refs):
    out_ref, sem = refs[-2:]
    toks = refs[:-2]
    rows = toks[0].shape[0]
    place = lax.axis_index("seq")
    even = lax.rem(place, 2) == 0
    copies = []
    for r in range(n_dp):
        for k, (kind, hop) in enumerate(slots):
            above = even if kind == 0 else ~even
            block = jnp.where(above, place + hop, place - hop)
            fits = (block >= 0) & (block < n_seq)
            if hop > 0 and kind == 1:
                fits = fits & jnp.where(above, place < n_seq - 1, place > 0)
            at = pl.multiple_of(jnp.clip(block, 0, n_seq - 1) * rows, 128)
            source = toks[k] if r == 0 else toks[len(slots) + k].at[pl.ds((r - 1) * rows, rows)]
            copy = pltpu.make_async_copy(source, out_ref.at[r, pl.ds(at, rows)], sem.at[r, k])
            copies.append((fits, copy))
    for fits, copy in copies:
        pl.when(fits)(copy.start)
    for fits, copy in copies:
        pl.when(fits)(copy.wait)


def weight_kernel(scale, n_dp, n_seq, tok_ref, *refs):
    lows = refs[:2]
    bc_ref, dt_ref, low_ref, low_sem = refs[2:]
    rows = tok_ref.shape[1] // n_seq
    share = lows[0].shape[1]
    core, me = lax.axis_index("head"), lax.axis_index("dp")
    copies = []
    for r in range(n_dp):
        for s in range(n_seq):
            index = s * n_dp + lax.rem(me - r + n_dp, n_dp)
            for k in range(2):
                row = pl.multiple_of(lax.rem(core + k, 2) * share, 16)
                copies.append(
                    pltpu.make_async_copy(
                        lows[k].at[index],
                        low_ref.at[r, pl.ds(row, share), pl.ds(s * rows, rows)],
                        low_sem.at[r * n_seq + s, k],
                    )
                )
    for copy in copies:
        copy.start()
    for copy in copies:
        copy.wait()
    total = mm(low_ref[0], tok_ref[0], 1, 0)
    for r in range(1, n_dp):
        total = total + mm(low_ref[r], tok_ref[r], 1, 0)
    total = total * scale
    half = bc_ref.shape[1] // 2
    heads = dt_ref.shape[0] // 2
    for k in range(2):
        bc_ref[:, k * half : (k + 1) * half] = total[k * share : k * share + half].T
        dt_ref[k * heads : (k + 1) * heads, :] = total[k * share + half : (k + 1) * share]


def relays(count):
    groups, _ = matchings(count)
    return [
        (kind, hop)
        for hop in range(1, count)
        for kind in (0, 1)
        if any(i - hop + 1 >= 0 or j + hop - 1 < count for i, j in groups[kind])
    ]


def relay(found, block, steps, *others):
    count = lax.axis_size("seq")
    _, pairs = matchings(count)
    for kind, hop in steps:
        source = block if hop == 1 else found[1 - kind, hop - 1]
        source = after(source, *others) if others else source
        found[kind, hop] = lax.ppermute(source, "seq", pairs[kind])
    return [found[step] for step in steps]


def chains(first, own, decay, inner, beside, riders, late):
    count = lax.axis_size("seq")
    place = lax.axis_index("seq")
    chunks = len(first)
    stores = [jnp.zeros((3,) + own.shape[2:], BF) for _ in range(chunks)]
    got = list(first)
    done, todo, extra = [], list(inner), []
    last = count + chunks - 2
    for slot in range(1, last + 1):
        steps = [(hop, slot - hop) for hop in range(1, count) if 0 <= slot - hop < chunks]
        sent = []
        for hop, k in steps:
            value = got[k]
            if hop == 1 and 0 < k < len(riders):
                value = jnp.where((place == 0) | (place == count - 1), value, riders[k])
            if hop > 1:
                value = jnp.where(place == hop - 1, own[0, k], own[1, k])
                value = (value + decay[k] * got[k].astype(F32)).astype(BF)
            sent.append(value)
        for (hop, k), value in zip(steps, sent):
            to = {i: i for i in range(count)}
            for i in (hop - 1, count - hop - 1):
                to[i], to[i + 1] = i + 1, i
            got[k] = lax.ppermute(value, "seq", sorted(to.items()))
            if hop == 1 and k < len(riders):
                riders[k] = got[k]
        for _ in range(-(-len(todo) // (last + 1 - slot))):
            done.append(todo.pop(0)(*sent))
        if slot == 1:
            extra = beside(*sent)
        if slot == last:
            k = steps[-1][1]
            got[k] = after(got[k], *late(*sent))
        if slot < last:
            held = [got[k] for _, k in steps] + [d[0] for d in done[-1:]]
            if slot == last - 1:
                held += extra
            new = slot < chunks
            if new:
                held.append(got[slot])
            kept = lax.optimization_barrier(tuple(held))
            for (_, k), a in zip(steps, kept):
                got[k] = a
            if new:
                got[slot] = kept[-1]
        for hop, k in steps:
            kind = jnp.where(place == hop, 0, jnp.where(place == count - hop - 1, 1, 2))
            zero = jnp.zeros_like(kind)
            stores[k] = lax.dynamic_update_slice(stores[k], got[k][None], (kind, zero, zero))
    done += [make() for make in todo]
    return stores, done


def body(tokens, ssd_input, grad_out, w_bc, w_dt, decay_rate, dt_bias):
    feats, x, g = tokens[0], ssd_input[0], grad_out[0]
    rows, width = feats.shape
    heads = decay_rate.shape[0]
    size = width // heads
    n_dp, n_seq = lax.axis_size("dp"), lax.axis_size("seq")
    part = width // n_dp
    state_n = w_bc.shape[1] // 2
    w_dt = w_dt.T
    rate, bias = decay_rate[None], dt_bias[None]

    pieces = call(split_kernel, [struct((rows, part), BF)] * n_dp, 1.9, feats)
    items = [pieces[0]] + [cyclic(pieces[r], "dp", r) for r in range(1, n_dp)]
    groups = items[:1]
    if n_dp > 1:
        groups.append(items[1] if n_dp == 2 else jnp.concatenate(items[1:], axis=0))
    found = [{} for _ in groups]
    slots = relays(n_seq)
    step = width // CHUNKS
    ride = n_seq == 4 and all(a.shape == (state_n, step) for a in groups)
    second = [(kind, hop) for kind, hop in slots if hop == 2 and not (ride and kind == 0)]
    near = relay(found[0], groups[0], slots[:2])
    partials, local = [project(items[0], w_bc, w_dt)], []
    for r in range(1, n_dp):
        item = after(items[r], partials[0])
        local.append(project(item, w_bc, w_dt))
        partials.append(cyclic(local[-1], "dp", -r))
    spare = relay(found[1], groups[1], slots[:2], *local) if n_dp > 1 else []
    partials[1:] = [after(a, *near) for a in partials[1:]]
    proj = partials + [cyclic(a, "head", 1) for a in partials]
    own, bc, hp, *outs = call(
        functools.partial(state_kernel, 2 * n_dp, size, int(ride)),
        (
            struct((2, CHUNKS, state_n, step), F32),
            struct((2 * rows, state_n), F32),
            struct((5 * heads, rows), F32),
        )
        + (struct((state_n, step), BF),) * CHUNKS
        + (struct((1, step), F32),) * CHUNKS,
        0.1,
        *proj,
        x,
        g,
        rate,
        bias,
        *([found[0][1, 1]] if ride else []),
    )
    first, decay = outs[:CHUNKS], outs[CHUNKS:]
    pairs = width // (2 * size) // PARTS
    span = width // PARTS
    shared = []

    def inner(q, *others):
        held = after(bc, *others) if others else bc
        square = struct((rows, rows), F32)
        block = pl.BlockSpec((rows, span), lambda _: (0, q))
        out = call(
            functools.partial(inner_kernel, q * pairs, pairs, size),
            ([square] if q == 0 else [])
            + [struct((rows, span), F32), square, struct((2, 2 * pairs, rows), F32)],
                2.6,
            held,
            hp,
            x,
            g,
            *shared,
            scratch=(pltpu.VMEM((rows, 2 * span), BF), pltpu.VMEM((rows, 2 * span), BF)),
            specs=[VMEM, VMEM, block, block] + [VMEM] * len(shared),
        )
        if q == 0:
            shared.append(out[0])
            out = out[1:]
        return out

    weights = [w_bc, w_dt]

    def beside(*others):
        for r in range(1, n_dp):
            weights.extend(cyclic(after(a, *others), "dp", r) for a in (w_bc, w_dt))
        return weights[2:] + relay(found[0], groups[0], second, *others)

    def late(*others):
        return relay(found[1], groups[1], second, *others) if n_dp > 1 else []

    first[0] = after(first[0], *spare)
    riders = [f[1, 1] for f in found] if ride else []
    calls = [functools.partial(inner, q) for q in range(PARTS)]
    stores, inners = chains(first, own, decay, calls, beside, riders, late)
    for f, a in zip(found, riders):
        f[0, 2] = a
    done = [relay(f, a, [t for t in slots if t not in f], stores[-1]) for f, a in zip(found, groups)]
    each = PARTS // CHUNKS
    grad_x, back = None, []
    for k in range(CHUNKS):
        last = k == CHUNKS - 1
        block = pl.BlockSpec((rows, step), lambda _, k=k: (0, k))
        made = (k + 1) * (heads // CHUNKS)
        sums = (struct((rows + heads, rows), F32), struct((rows, rows), F32))
        inputs = [stores[k], x, g, bc, hp, rate]
        for q in range(3):
            inputs += [a[q] for a in inners[k * each : (k + 1) * each]]
        specs = [VMEM, block, block] + [VMEM] * (len(inputs) - 3)
        if k > 0:
            inputs += [grad_x] + back
            specs += [HBM, VMEM]
        grad_x, *back = call(
            functools.partial(outer_kernel, k, CHUNKS, size, each),
            (struct((rows, width), BF),)
            + (sums if last else (struct((2 * rows + made, rows), F32),)),
            5.4 / CHUNKS,
            *inputs,
            scratch=(pltpu.VMEM((rows, 2 * step), BF), pltpu.VMEM((rows, 2 * step), BF)),
            specs=specs,
            out_specs=(block,) + (VMEM,) * (2 if last else 1),
            aliases={len(inputs) - 2: 0} if k > 0 else {},
        )
    keep, give = back
    toks = []
    for f, a in zip(found, groups):
        toks += [a] + [f[step] for step in slots]
    slots = [(0, 0)] + slots
    ordered = call(
        functools.partial(order_kernel, n_dp, n_seq, slots),
        struct((n_dp, n_seq * rows, part), BF),
        1.0,
        *toks,
        scratch=[pltpu.SemaphoreType.DMA((n_dp, len(slots)))],
    )
    taken = cyclic(give, "head", 1)
    count = n_dp * n_seq
    copies = call(low_kernel, struct((count, rows + heads, rows), BF), 1.2, keep, taken)
    mine = copies[0]
    lows = lax.all_to_all(copies, ("seq", "dp"), 0, 0, tiled=True)
    other = cyclic(after(mine, ordered), "head", 1)
    grads = call(
        functools.partial(token_kernel, n_dp),
        struct((rows, width), BF),
        2.9,
        mine,
        other,
        *weights,
    )
    lows = after(lows, grads)
    swapped = cyclic(lows, "head", 1)
    cols = 2 * (rows + heads)
    grad_bc, grad_dt = call(
        functools.partial(weight_kernel, 1.0 / (rows * n_seq * n_dp), n_dp, n_seq),
        (struct((part, 2 * state_n), F32), struct((2 * heads, part), F32)),
        4.0,
        ordered,
        lows,
        swapped,
        limit=LIMIT + 2 * n_dp * n_seq * rows * cols,
        scratch=(
            pltpu.VMEM((n_dp, cols, n_seq * rows), BF),
            pltpu.SemaphoreType.DMA((count, 2)),
        ),
    )
    return grad_x[None], grads[None], grad_bc, grad_dt.T


def solution(mesh):
    in_specs = (
        P(("grp", "dp"), "seq", "head"),
        P(("grp", "dp"), "seq", "head"),
        P(("grp", "dp"), "seq", "head"),
        P(("head", "dp"), None),
        P(("head", "dp"), None),
        P("head"),
        P("head"),
    )
    out_specs = (
        P(("grp", "dp"), "seq", "head"),
        P(("grp", "dp"), "seq", "head"),
        P(("grp", "head", "dp"), None),
        P(("grp", "head", "dp"), None),
    )
    return jax.shard_map(body, mesh=mesh, in_specs=in_specs, out_specs=out_specs, check_vma=False)
```

```python
import functools

import jax
import jax.numpy as jnp
from jax import lax
from jax.experimental import pallas as pl
from jax.experimental.pallas import tpu as pltpu
from jax.sharding import PartitionSpec as P

CHUNKS = 2
PARTS = 4
BF = jnp.bfloat16
F32 = jnp.float32
TOP = lax.Precision.HIGHEST
PER_US = 1.15e9
LIMIT = 16 * 1024 * 1024


def cyclic(a, axis, by):
    count = lax.axis_size(axis)
    return lax.ppermute(a, axis, [(i, (i + by) % count) for i in range(count)])


def mm(a, b, ca, cb, precision=None):
    return lax.dot_general(
        a, b, (((ca,), (cb,)), ((), ())), preferred_element_type=F32, precision=precision
    )


def halves(a):
    high = a.astype(BF)
    return high, (a - high.astype(F32)).astype(BF)


def head_lanes(heads, width, size, first=0):
    row = lax.broadcasted_iota(jnp.int32, (heads, width), 0)
    col = lax.broadcasted_iota(jnp.int32, (heads, width), 1) + first
    low = row * size
    return jnp.where((col >= low) & (col < low + size), 1.0, 0.0).astype(F32)


def spread(a, pick):
    high, low = halves(a)
    both = jnp.concatenate([pick, pick], axis=0)
    return mm(jnp.concatenate([high, low], axis=0), both, 0, 0)


VMEM = pl.BlockSpec(memory_space=pltpu.VMEM)
HBM = pl.BlockSpec(memory_space=pltpu.HBM)


def call(kernel, out_shape, span_us, *args, scratch=(), specs=None, out_specs=None, aliases={}, limit=LIMIT):
    size = sum(a.size * a.dtype.itemsize for a in args)
    return pl.pallas_call(
        kernel,
        out_shape=out_shape,
        grid=(1,),
        in_specs=specs or [VMEM] * len(args),
        out_specs=out_specs or jax.tree.map(lambda _: VMEM, out_shape),
        input_output_aliases=aliases,
        scratch_shapes=list(scratch),
        compiler_params=pltpu.CompilerParams(vmem_limit_bytes=limit),
        cost_estimate=pl.CostEstimate(
            flops=int(span_us * PER_US), bytes_accessed=size, transcendentals=0
        ),
    )(*args)


def struct(shape, dtype):
    return jax.ShapeDtypeStruct(shape, dtype)


def after(a, *others):
    return lax.optimization_barrier((a, others))[0]


def matchings(count):
    groups = [[(i, i + 1) for i in range(kind, count - 1, 2)] for kind in (0, 1)]
    pairs = []
    for group in groups:
        to = {i: i for i in range(count)}
        for i, j in group:
            to[i], to[j] = j, i
        pairs.append(sorted(to.items()))
    return groups, pairs


def split_kernel(a_ref, *outs):
    count = len(outs)
    me = lax.axis_index("dp")
    part = outs[0].shape[1]
    for r in range(count):
        at = pl.multiple_of(lax.rem(me + r, count) * part, 128)
        outs[r][...] = a_ref[:, pl.ds(at, part)]


def project_kernel(a_ref, bc_ref, dt_ref, out_ref):
    a = a_ref[...]
    state_n = bc_ref.shape[1] // 2
    rows = a.shape[0]
    bc = mm(a, bc_ref[...], 1, 0)
    out_ref[0:rows, :] = bc[:, :state_n]
    out_ref[rows : 2 * rows, :] = bc[:, state_n:]
    out_ref[2 * rows :, :] = mm(dt_ref[...], a, 1, 1)


def project(a, w_bc, w_dt):
    rows = a.shape[0]
    total = 2 * rows + w_dt.shape[0]
    return call(
        project_kernel,
        struct((total, w_bc.shape[1] // 2), F32),
        2.1,
        a,
        w_bc,
        w_dt,
    )


def state_kernel(count, size, ride, *refs):
    proj = refs[:count]
    x_ref, g_ref, rate_ref, bias_ref = refs[count : count + 4]
    riders = refs[count + 4 : count + 4 + ride]
    own_ref, bc_ref, hp_ref = refs[count + 4 + ride : count + 7 + ride]
    outs = refs[count + 7 + ride :]
    firsts, decays = outs[: len(outs) // 2], outs[len(outs) // 2 :]
    heads = rate_ref.shape[1]
    rows = x_ref.shape[0]
    rate, bias = rate_ref[...].T, bias_ref[...].T
    chunks, step = own_ref.shape[1], own_ref.shape[3]
    first = pl.multiple_of(2 * rows + lax.axis_index("head") * heads, 8)
    bc = proj[0][0 : 2 * rows, :]
    pre = proj[0][pl.ds(first, heads), :] + bias
    for ref in proj[1:]:
        bc = bc + ref[0 : 2 * rows, :]
        pre = pre + ref[pl.ds(first, heads), :]
    bc_ref[...] = bc
    dt = jnp.maximum(pre, 0.0) + jnp.log1p(jnp.exp(-jnp.abs(pre)))
    row = lax.broadcasted_iota(jnp.int32, (rows, rows), 0)
    col = lax.broadcasted_iota(jnp.int32, (rows, rows), 1)
    cum = mm(-dt * rate, jnp.where(row <= col, 1.0, 0.0), 1, 0, TOP)
    last = cum[:, rows - 1 : rows]
    grow = jnp.exp(cum)
    w = jnp.exp(last - cum) * dt
    decay = jnp.exp(last)
    for k, part in enumerate((pre, dt, cum, grow, w)):
        hp_ref[k * heads : (k + 1) * heads, :] = part
    place = lax.axis_index("seq")
    lowest = place == 0
    sides = []
    for vec in (bc[:rows], bc[rows:]):
        high, low = halves(vec.T)
        sides.append((jnp.concatenate([high, low], axis=1), high))
    for k in range(chunks):
        pick = head_lanes(heads, step, size, k * step)
        decays[k][...] = jnp.sum(pick * decay, axis=0, keepdims=True)
        pick = pick.astype(BF)
        both = []
        for kind, (scale, ref) in enumerate(((w, x_ref), (grow, g_ref))):
            wide, high = sides[kind]
            value = spread(scale, pick) * ref[:, k * step : (k + 1) * step].astype(F32)
            top, rest = halves(value)
            value = mm(wide, jnp.concatenate([top, top], axis=0), 1, 0) + mm(high, rest, 1, 0)
            own_ref[kind, k] = value
            both.append(value)
        firsts[k][...] = jnp.where(lowest, both[0], both[1]).astype(BF)
        if k < ride:
            rider = riders[k]

            @pl.when((place > 0) & (place < lax.axis_size("seq") - 1))
            def _():
                firsts[k][...] = rider[...]


def inner_kernel(first, pairs, size, bc_ref, hp_ref, x_ref, g_ref, *refs):
    gx_ref, ds_ref, sums_ref = refs[-5:-2]
    gy_ref, xg_ref = refs[-2:]
    rows = x_ref.shape[0]
    heads = hp_ref.shape[0] // 5
    lanes = 2 * size
    width = pairs * lanes
    if len(refs) == 6 and first > 0:
        scores = refs[0][...]
    else:
        scores = mm(bc_ref[rows : 2 * rows, :], bc_ref[0:rows, :], 1, 1, TOP)
        refs[0][...] = scores
    row = lax.broadcasted_iota(jnp.int32, (rows, rows), 0)
    col = lax.broadcasted_iota(jnp.int32, (rows, rows), 1)
    causal = row >= col
    dt = hp_ref[heads : 2 * heads, :]
    cum = hp_ref[2 * heads : 3 * heads, :]
    cum_t = cum.T
    lane = lax.broadcasted_iota(jnp.int32, (rows, lanes), 1)
    sides = [jnp.where(lane < size, 1.0, 0.0).astype(BF), jnp.where(lane < size, 0.0, 1.0).astype(BF)]
    ds = jnp.zeros((rows, rows), F32)
    for j in range(pairs):
        place = slice(j * lanes, (j + 1) * lanes)
        x, g = x_ref[:, place], g_ref[:, place]
        xs = jnp.concatenate([x * s for s in sides], axis=0)
        gs = jnp.concatenate([g * s for s in sides], axis=0)
        m = mm(gs, x, 1, 1)
        kern = []
        for i in range(2):
            h = 2 * (first + j) + i
            gap = cum_t[:, h : h + 1] - cum[h : h + 1, :]
            fall = jnp.exp(jnp.where(causal, gap, -jnp.inf)) * dt[h : h + 1, :]
            kern.append((fall * scores).astype(BF))
            ds = ds + fall * m[i * rows : (i + 1) * rows]
        y = mm(jnp.concatenate(kern, axis=1), xs, 1, 0)
        gx = mm(jnp.concatenate(kern, axis=0), gs, 0, 0)
        gx_ref[:, place] = gx
        late = slice(width + j * lanes, width + (j + 1) * lanes)
        gy_ref[:, place], gy_ref[:, late] = halves(g.astype(F32) * y)
        xg_ref[:, place], xg_ref[:, late] = halves(x.astype(F32) * gx)
    ds_ref[...] = ds
    pick = head_lanes(2 * pairs, width, size).astype(BF)
    pick = jnp.concatenate([pick, pick], axis=1)
    sums_ref[0] = mm(pick, gy_ref[...], 1, 1)
    sums_ref[1] = mm(pick, xg_ref[...], 1, 1)


def outer_kernel(k, chunks, size, parts, *refs):
    store_ref, x_ref, g_ref, bc_ref, hp_ref, rate_ref = refs[:6]
    gxs, dss, sums = (refs[6 + q * parts : 6 + (q + 1) * parts] for q in range(3))
    rest = refs[6 + 3 * parts :]
    wv_ref, eu_ref = rest[-2:]
    rows, step = x_ref.shape
    all_heads = rate_ref.shape[1]
    heads = all_heads // chunks
    mine = slice(k * heads, (k + 1) * heads)
    piece = step // parts
    b, c = bc_ref[0:rows, :], bc_ref[rows : 2 * rows, :]
    pre, dt, cum, grow, w = (
        hp_ref[q * all_heads + k * heads : q * all_heads + (k + 1) * heads, :] for q in range(5)
    )
    rate = rate_ref[...].T[mine]
    ds = dss[0][...]
    for ref in dss[1:]:
        ds = ds + ref[...]
    db = mm(c, ds, 0, 0, TOP)
    dc = mm(b, ds, 0, 1, TOP)
    b_wide = jnp.concatenate(halves(b), axis=1)
    c_wide = jnp.concatenate(halves(c), axis=1)
    pick = head_lanes(heads, step, size).astype(BF)
    incoming, outgoing = store_ref[0], store_ref[1]
    u = mm(c_wide, jnp.concatenate([incoming, incoming], axis=0), 1, 0)
    v = mm(b_wide, jnp.concatenate([outgoing, outgoing], axis=0), 1, 0)
    scale = spread(w, pick)
    wx = scale * x_ref[...].astype(F32)
    eg = spread(grow, pick) * g_ref[...].astype(F32)
    grad_ref = rest[-5] if k == chunks - 1 else rest[-4]
    for q in range(parts):
        place = slice(q * piece, (q + 1) * piece)
        grad_ref[:, place] = (gxs[q][...] + scale[:, place] * v[:, place]).astype(BF)
    wv_ref[:, :step], wv_ref[:, step:] = halves(wx * v)
    eu_ref[:, :step], eu_ref[:, step:] = halves(eg * u)
    db = db + mm(
        jnp.concatenate([outgoing, outgoing], axis=1), jnp.concatenate(halves(wx), axis=1), 1, 1
    )
    dc = dc + mm(
        jnp.concatenate([incoming, incoming], axis=1), jnp.concatenate(halves(eg), axis=1), 1, 1
    )
    both = jnp.sum(incoming.astype(F32) * outgoing.astype(F32), axis=0, keepdims=True)
    ddecay = jnp.sum(pick.astype(F32) * both, axis=1, keepdims=True)
    pick = jnp.concatenate([pick, pick], axis=1)
    wdw = mm(pick, wv_ref[...], 1, 1)
    egu = mm(pick, eu_ref[...], 1, 1)
    rowsum = jnp.concatenate([s[0] for s in sums], axis=0)
    colsum = jnp.concatenate([s[1] for s in sums], axis=0)
    dcum = rowsum - colsum + egu - wdw
    row = lax.broadcasted_iota(jnp.int32, (rows, rows), 0)
    col = lax.broadcasted_iota(jnp.int32, (rows, rows), 1)
    rev = mm(dcum, jnp.where(row >= col, 1.0, 0.0), 1, 0, TOP)
    decay = grow[:, rows - 1 : rows]
    rev = rev + jnp.sum(wdw, axis=1, keepdims=True) + decay * ddecay
    gate = 1.0 / (1.0 + jnp.exp(-pre))
    small = 1e-30
    ratio = jnp.where(dt > small, gate / jnp.maximum(dt, small), 1.0)
    graw = (colsum + wdw) * ratio - rate * rev * gate
    if k > 0:
        before_ref = rest[1]
        db = db + before_ref[0:rows, :]
        dc = dc + before_ref[rows : 2 * rows, :]
        graw = jnp.concatenate([before_ref[2 * rows :, :], graw], axis=0)
    if k == chunks - 1:
        keep_ref, give_ref = rest[-4], rest[-3]
        core = lax.axis_index("head")
        keep_ref[0:rows, :] = jnp.where(core == 0, db, dc)
        keep_ref[rows:, :] = graw
        give_ref[...] = jnp.where(core == 0, dc, db)
    else:
        back_ref = rest[-3]
        back_ref[0:rows, :] = db
        back_ref[rows : 2 * rows, :] = dc
        back_ref[2 * rows :, :] = graw


def low_kernel(keep_ref, taken_ref, out_ref):
    rows = taken_ref.shape[0]
    low = keep_ref[0:rows, :] + taken_ref[...]
    low = jnp.concatenate([low, keep_ref[rows:, :]], axis=0).astype(BF)
    for k in range(out_ref.shape[0]):
        out_ref[k] = low


def token_kernel(count, mine_ref, other_ref, *refs):
    out_ref = refs[2 * count]
    me, core = lax.axis_index("dp"), lax.axis_index("head")
    part, cols = refs[0].shape
    half = cols // 2
    heads = refs[1].shape[0] // 2
    for r in range(count):
        at = pl.multiple_of(lax.rem(me - r + count, count) * part, 128)
        total = None
        for k, ref in enumerate((mine_ref, other_ref)):
            at_col = pl.multiple_of(lax.rem(core + k, 2) * half, 128)
            at_row = pl.multiple_of(lax.rem(core + k, 2) * heads, 16)
            term = mm(ref[0:half, :], refs[2 * r][:, pl.ds(at_col, half)], 0, 1)
            term = term + mm(ref[half:, :], refs[2 * r + 1][pl.ds(at_row, heads), :], 0, 0)
            total = term if total is None else total + term
        out_ref[:, pl.ds(at, part)] = total.astype(BF)


def order_kernel(n_dp, n_seq, slots, *refs):
    out_ref, sem = refs[-2:]
    toks = refs[:-2]
    rows = toks[0].shape[0]
    place = lax.axis_index("seq")
    even = lax.rem(place, 2) == 0
    copies = []
    for r in range(n_dp):
        for k, (kind, hop) in enumerate(slots):
            above = even if kind == 0 else ~even
            block = jnp.where(above, place + hop, place - hop)
            fits = (block >= 0) & (block < n_seq)
            if hop > 0 and kind == 1:
                fits = fits & jnp.where(above, place < n_seq - 1, place > 0)
            at = pl.multiple_of(jnp.clip(block, 0, n_seq - 1) * rows, 128)
            source = toks[k] if r == 0 else toks[len(slots) + k].at[pl.ds((r - 1) * rows, rows)]
            copy = pltpu.make_async_copy(source, out_ref.at[r, pl.ds(at, rows)], sem.at[r, k])
            copies.append((fits, copy))
    for fits, copy in copies:
        pl.when(fits)(copy.start)
    for fits, copy in copies:
        pl.when(fits)(copy.wait)


def weight_kernel(scale, n_dp, n_seq, tok_ref, source_ref, *refs):
    low_ref, low_sem = refs[-2:]
    rows = tok_ref.shape[1] // n_seq
    core, me = lax.axis_index("head"), lax.axis_index("dp")
    copies = []
    for r in range(n_dp):
        for s in range(n_seq):
            index = s * n_dp + lax.rem(me - r + n_dp, n_dp)
            copies.append(
                pltpu.make_async_copy(
                    source_ref.at[index],
                    low_ref.at[r, :, pl.ds(s * rows, rows)],
                    low_sem.at[r * n_seq + s],
                )
            )
    for copy in copies:
        copy.start()
    for copy in copies:
        copy.wait()
    total = mm(low_ref[0], tok_ref[0], 1, 0)
    for r in range(1, n_dp):
        total = total + mm(low_ref[r], tok_ref[r], 1, 0)
    total = total * scale
    if len(refs) == 4:
        bc_ref, dt_ref = refs[:2]
        half = bc_ref.shape[1]
        bc_ref[...] = total[:half].T
        dt_ref[...] = total[half:]
        return
    own_bc, own_dt, bc_ref, dt_ref = refs[:4]
    half, heads = own_bc.shape[1], own_dt.shape[0]
    for k, (first, second) in enumerate(((own_bc[...], own_dt[...]), (total[:half].T, total[half:]))):
        side = lax.rem(core + k, 2)
        bc_ref[:, pl.ds(pl.multiple_of(side * half, 128), half)] = first
        dt_ref[pl.ds(pl.multiple_of(side * heads, 8), heads), :] = second


def relays(count):
    groups, _ = matchings(count)
    return [
        (kind, hop)
        for hop in range(1, count)
        for kind in (0, 1)
        if any(i - hop + 1 >= 0 or j + hop - 1 < count for i, j in groups[kind])
    ]


def relay(found, block, steps, *others):
    count = lax.axis_size("seq")
    _, pairs = matchings(count)
    for kind, hop in steps:
        source = block if hop == 1 else found[1 - kind, hop - 1]
        source = after(source, *others) if others else source
        found[kind, hop] = lax.ppermute(source, "seq", pairs[kind])
    return [found[step] for step in steps]


def chains(first, own, decay, inner, beside, riders, late):
    count = lax.axis_size("seq")
    place = lax.axis_index("seq")
    chunks = len(first)
    stores = [jnp.zeros((3,) + own.shape[2:], BF) for _ in range(chunks)]
    got = list(first)
    done, todo, extra = [], list(inner), []
    last = count + chunks - 2
    for slot in range(1, last + 1):
        steps = [(hop, slot - hop) for hop in range(1, count) if 0 <= slot - hop < chunks]
        sent = []
        for hop, k in steps:
            value = got[k]
            if hop == 1 and 0 < k < len(riders):
                value = jnp.where((place == 0) | (place == count - 1), value, riders[k])
            if hop > 1:
                value = jnp.where(place == hop - 1, own[0, k], own[1, k])
                value = (value + decay[k] * got[k].astype(F32)).astype(BF)
            sent.append(value)
        for (hop, k), value in zip(steps, sent):
            to = {i: i for i in range(count)}
            for i in (hop - 1, count - hop - 1):
                to[i], to[i + 1] = i + 1, i
            got[k] = lax.ppermute(value, "seq", sorted(to.items()))
            if hop == 1 and k < len(riders):
                riders[k] = got[k]
        for _ in range(-(-len(todo) // (last + 1 - slot))):
            done.append(todo.pop(0)(*sent))
        if slot == 1:
            extra = beside(*sent)
        if slot == last:
            k = steps[-1][1]
            got[k] = after(got[k], *late(*sent))
        if slot < last:
            held = [got[k] for _, k in steps] + [d[0] for d in done[-1:]]
            if slot == last - 1:
                held += extra
            new = slot < chunks
            if new:
                held.append(got[slot])
            kept = lax.optimization_barrier(tuple(held))
            for (_, k), a in zip(steps, kept):
                got[k] = a
            if new:
                got[slot] = kept[-1]
        for hop, k in steps:
            kind = jnp.where(place == hop, 0, jnp.where(place == count - hop - 1, 1, 2))
            zero = jnp.zeros_like(kind)
            stores[k] = lax.dynamic_update_slice(stores[k], got[k][None], (kind, zero, zero))
    done += [make() for make in todo]
    return stores, done


def body(tokens, ssd_input, grad_out, w_bc, w_dt, decay_rate, dt_bias):
    feats, x, g = tokens[0], ssd_input[0], grad_out[0]
    rows, width = feats.shape
    heads = decay_rate.shape[0]
    size = width // heads
    n_dp, n_seq = lax.axis_size("dp"), lax.axis_size("seq")
    part = width // n_dp
    state_n = w_bc.shape[1] // 2
    w_dt = w_dt.T
    rate, bias = decay_rate[None], dt_bias[None]

    pieces = call(split_kernel, [struct((rows, part), BF)] * n_dp, 1.9, feats)
    items = [pieces[0]] + [cyclic(pieces[r], "dp", r) for r in range(1, n_dp)]
    groups = items[:1]
    if n_dp > 1:
        groups.append(items[1] if n_dp == 2 else jnp.concatenate(items[1:], axis=0))
    found = [{} for _ in groups]
    slots = relays(n_seq)
    step = width // CHUNKS
    ride = n_seq == 4 and all(a.shape == (state_n, step) for a in groups)
    second = [(kind, hop) for kind, hop in slots if hop == 2 and not (ride and kind == 0)]
    near = relay(found[0], groups[0], slots[:2])
    partials, local = [project(items[0], w_bc, w_dt)], []
    for r in range(1, n_dp):
        item = after(items[r], partials[0])
        local.append(project(item, w_bc, w_dt))
        partials.append(cyclic(local[-1], "dp", -r))
    spare = relay(found[1], groups[1], slots[:2], *local) if n_dp > 1 else []
    partials[1:] = [after(a, *near) for a in partials[1:]]
    proj = partials + [cyclic(a, "head", 1) for a in partials]
    own, bc, hp, *outs = call(
        functools.partial(state_kernel, 2 * n_dp, size, int(ride)),
        (
            struct((2, CHUNKS, state_n, step), F32),
            struct((2 * rows, state_n), F32),
            struct((5 * heads, rows), F32),
        )
        + (struct((state_n, step), BF),) * CHUNKS
        + (struct((1, step), F32),) * CHUNKS,
        0.1,
        *proj,
        x,
        g,
        rate,
        bias,
        *([found[0][1, 1]] if ride else []),
    )
    first, decay = outs[:CHUNKS], outs[CHUNKS:]
    pairs = width // (2 * size) // PARTS
    span = width // PARTS
    shared = []

    def inner(q, *others):
        held = after(bc, *others) if others else bc
        square = struct((rows, rows), F32)
        block = pl.BlockSpec((rows, span), lambda _: (0, q))
        out = call(
            functools.partial(inner_kernel, q * pairs, pairs, size),
            ([square] if q == 0 else [])
            + [struct((rows, span), F32), square, struct((2, 2 * pairs, rows), F32)],
                2.6,
            held,
            hp,
            x,
            g,
            *shared,
            scratch=(pltpu.VMEM((rows, 2 * span), BF), pltpu.VMEM((rows, 2 * span), BF)),
            specs=[VMEM, VMEM, block, block] + [VMEM] * len(shared),
        )
        if q == 0:
            shared.append(out[0])
            out = out[1:]
        return out

    weights = [w_bc, w_dt]

    def beside(*others):
        for r in range(1, n_dp):
            weights.extend(cyclic(after(a, *others), "dp", r) for a in (w_bc, w_dt))
        return weights[2:] + relay(found[0], groups[0], second, *others)

    def late(*others):
        return relay(found[1], groups[1], second, *others) if n_dp > 1 else []

    first[0] = after(first[0], *spare)
    riders = [f[1, 1] for f in found] if ride else []
    calls = [functools.partial(inner, q) for q in range(PARTS)]
    stores, inners = chains(first, own, decay, calls, beside, riders, late)
    for f, a in zip(found, riders):
        f[0, 2] = a
    done = [relay(f, a, [t for t in slots if t not in f], stores[-1]) for f, a in zip(found, groups)]
    each = PARTS // CHUNKS
    grad_x, back = None, []
    for k in range(CHUNKS):
        last = k == CHUNKS - 1
        block = pl.BlockSpec((rows, step), lambda _, k=k: (0, k))
        made = (k + 1) * (heads // CHUNKS)
        sums = (struct((rows + heads, rows), F32), struct((rows, rows), F32))
        inputs = [stores[k], x, g, bc, hp, rate]
        for q in range(3):
            inputs += [a[q] for a in inners[k * each : (k + 1) * each]]
        specs = [VMEM, block, block] + [VMEM] * (len(inputs) - 3)
        if k > 0:
            inputs += [grad_x] + back
            specs += [HBM, VMEM]
        grad_x, *back = call(
            functools.partial(outer_kernel, k, CHUNKS, size, each),
            (struct((rows, width), BF),)
            + (sums if last else (struct((2 * rows + made, rows), F32),)),
            5.4 / CHUNKS,
            *inputs,
            scratch=(pltpu.VMEM((rows, 2 * step), BF), pltpu.VMEM((rows, 2 * step), BF)),
            specs=specs,
            out_specs=(block,) + (VMEM,) * (2 if last else 1),
            aliases={len(inputs) - 2: 0} if k > 0 else {},
        )
    keep, give = back
    toks = []
    for f, a in zip(found, groups):
        toks += [a] + [f[step] for step in slots]
    slots = [(0, 0)] + slots
    ordered = call(
        functools.partial(order_kernel, n_dp, n_seq, slots),
        struct((n_dp, n_seq * rows, part), BF),
        1.0,
        *toks,
        scratch=[pltpu.SemaphoreType.DMA((n_dp, len(slots)))],
    )
    taken = after(cyclic(give, "head", 1), ordered)
    count = n_dp * n_seq
    copies = call(low_kernel, struct((count, rows + heads, rows), BF), 1.2, keep, taken)
    mine = copies[0]
    lows = lax.all_to_all(copies, ("seq", "dp"), 0, 0, tiled=True)
    other = cyclic(mine, "head", 1)
    grads = call(
        functools.partial(token_kernel, n_dp),
        struct((rows, width), BF),
        2.9,
        mine,
        other,
        *weights,
    )
    lows = after(lows, grads)
    swapped = cyclic(lows, "head", 1)
    cols = 2 * (rows + heads)
    halves_made = []
    for k, source in enumerate((lows, swapped)):
        halves_made = call(
            functools.partial(weight_kernel, 1.0 / (rows * n_seq * n_dp), n_dp, n_seq),
            (struct((part, (k + 1) * state_n), F32), struct(((k + 1) * heads, part), F32)),
            2.0,
            ordered,
            source,
            *halves_made,
            limit=LIMIT + 2 * n_dp * n_seq * rows * cols,
            scratch=(
                pltpu.VMEM((n_dp, rows + heads, n_seq * rows), BF),
                pltpu.SemaphoreType.DMA((count,)),
            ),
        )
    grad_bc, grad_dt = halves_made
    return grad_x[None], grads[None], grad_bc, grad_dt.T


def solution(mesh):
    in_specs = (
        P(("grp", "dp"), "seq", "head"),
        P(("grp", "dp"), "seq", "head"),
        P(("grp", "dp"), "seq", "head"),
        P(("head", "dp"), None),
        P(("head", "dp"), None),
        P("head"),
        P("head"),
    )
    out_specs = (
        P(("grp", "dp"), "seq", "head"),
        P(("grp", "dp"), "seq", "head"),
        P(("grp", "head", "dp"), None),
        P(("grp", "head", "dp"), None),
    )
    return jax.shard_map(body, mesh=mesh, in_specs=in_specs, out_specs=out_specs, check_vma=False)
```

```python
import functools

import jax
import jax.numpy as jnp
from jax import lax
from jax.experimental import pallas as pl
from jax.experimental.pallas import tpu as pltpu
from jax.sharding import PartitionSpec as P

CHUNKS = 2
PARTS = 4
BF = jnp.bfloat16
F32 = jnp.float32
TOP = lax.Precision.HIGHEST
PER_US = 1.15e9
LIMIT = 16 * 1024 * 1024


def cyclic(a, axis, by):
    count = lax.axis_size(axis)
    return lax.ppermute(a, axis, [(i, (i + by) % count) for i in range(count)])


def mm(a, b, ca, cb, precision=None):
    return lax.dot_general(
        a, b, (((ca,), (cb,)), ((), ())), preferred_element_type=F32, precision=precision
    )


def halves(a):
    high = a.astype(BF)
    return high, (a - high.astype(F32)).astype(BF)


def head_lanes(heads, width, size, first=0):
    row = lax.broadcasted_iota(jnp.int32, (heads, width), 0)
    col = lax.broadcasted_iota(jnp.int32, (heads, width), 1) + first
    low = row * size
    return jnp.where((col >= low) & (col < low + size), 1.0, 0.0).astype(F32)


def spread(a, pick):
    high, low = halves(a)
    both = jnp.concatenate([pick, pick], axis=0)
    return mm(jnp.concatenate([high, low], axis=0), both, 0, 0)


VMEM = pl.BlockSpec(memory_space=pltpu.VMEM)
HBM = pl.BlockSpec(memory_space=pltpu.HBM)


def call(kernel, out_shape, span_us, *args, scratch=(), specs=None, out_specs=None, aliases={}, limit=LIMIT):
    size = sum(a.size * a.dtype.itemsize for a in args)
    return pl.pallas_call(
        kernel,
        out_shape=out_shape,
        grid=(1,),
        in_specs=specs or [VMEM] * len(args),
        out_specs=out_specs or jax.tree.map(lambda _: VMEM, out_shape),
        input_output_aliases=aliases,
        scratch_shapes=list(scratch),
        compiler_params=pltpu.CompilerParams(vmem_limit_bytes=limit),
        cost_estimate=pl.CostEstimate(
            flops=int(span_us * PER_US), bytes_accessed=size, transcendentals=0
        ),
    )(*args)


def struct(shape, dtype):
    return jax.ShapeDtypeStruct(shape, dtype)


def after(a, *others):
    return lax.optimization_barrier((a, others))[0]


def matchings(count):
    groups = [[(i, i + 1) for i in range(kind, count - 1, 2)] for kind in (0, 1)]
    pairs = []
    for group in groups:
        to = {i: i for i in range(count)}
        for i, j in group:
            to[i], to[j] = j, i
        pairs.append(sorted(to.items()))
    return groups, pairs


def split_kernel(a_ref, *outs):
    count = len(outs)
    me = lax.axis_index("dp")
    part = outs[0].shape[1]
    for r in range(count):
        at = pl.multiple_of(lax.rem(me + r, count) * part, 128)
        outs[r][...] = a_ref[:, pl.ds(at, part)]


def project_kernel(a_ref, bc_ref, dt_ref, out_ref):
    a = a_ref[...]
    state_n = bc_ref.shape[1] // 2
    rows = a.shape[0]
    bc = mm(a, bc_ref[...], 1, 0)
    out_ref[0:rows, :] = bc[:, :state_n]
    out_ref[rows : 2 * rows, :] = bc[:, state_n:]
    out_ref[2 * rows :, :] = mm(dt_ref[...], a, 1, 1)


def project(a, w_bc, w_dt):
    rows = a.shape[0]
    total = 2 * rows + w_dt.shape[0]
    return call(
        project_kernel,
        struct((total, w_bc.shape[1] // 2), F32),
        2.1,
        a,
        w_bc,
        w_dt,
    )


def state_kernel(count, size, ride, *refs):
    proj = refs[:count]
    x_ref, g_ref, rate_ref, bias_ref = refs[count : count + 4]
    riders = refs[count + 4 : count + 4 + ride]
    own_ref, bc_ref, hp_ref = refs[count + 4 + ride : count + 7 + ride]
    outs = refs[count + 7 + ride :]
    firsts, decays = outs[: len(outs) // 2], outs[len(outs) // 2 :]
    heads = rate_ref.shape[1]
    rows = x_ref.shape[0]
    rate, bias = rate_ref[...].T, bias_ref[...].T
    chunks, step = own_ref.shape[1], own_ref.shape[3]
    first = pl.multiple_of(2 * rows + lax.axis_index("head") * heads, 8)
    bc = proj[0][0 : 2 * rows, :]
    pre = proj[0][pl.ds(first, heads), :] + bias
    for ref in proj[1:]:
        bc = bc + ref[0 : 2 * rows, :]
        pre = pre + ref[pl.ds(first, heads), :]
    bc_ref[...] = bc
    dt = jnp.maximum(pre, 0.0) + jnp.log1p(jnp.exp(-jnp.abs(pre)))
    row = lax.broadcasted_iota(jnp.int32, (rows, rows), 0)
    col = lax.broadcasted_iota(jnp.int32, (rows, rows), 1)
    cum = mm(-dt * rate, jnp.where(row <= col, 1.0, 0.0), 1, 0, TOP)
    last = cum[:, rows - 1 : rows]
    grow = jnp.exp(cum)
    w = jnp.exp(last - cum) * dt
    decay = jnp.exp(last)
    for k, part in enumerate((pre, dt, cum, grow, w)):
        hp_ref[k * heads : (k + 1) * heads, :] = part
    place = lax.axis_index("seq")
    lowest = place == 0
    sides = []
    for vec in (bc[:rows], bc[rows:]):
        high, low = halves(vec.T)
        sides.append((jnp.concatenate([high, low], axis=1), high))
    for k in range(chunks):
        pick = head_lanes(heads, step, size, k * step)
        decays[k][...] = jnp.sum(pick * decay, axis=0, keepdims=True)
        pick = pick.astype(BF)
        both = []
        for kind, (scale, ref) in enumerate(((w, x_ref), (grow, g_ref))):
            wide, high = sides[kind]
            value = spread(scale, pick) * ref[:, k * step : (k + 1) * step].astype(F32)
            top, rest = halves(value)
            value = mm(wide, jnp.concatenate([top, top], axis=0), 1, 0) + mm(high, rest, 1, 0)
            own_ref[kind, k] = value
            both.append(value)
        firsts[k][...] = jnp.where(lowest, both[0], both[1]).astype(BF)
        if k < ride:
            rider = riders[k]

            @pl.when((place > 0) & (place < lax.axis_size("seq") - 1))
            def _():
                firsts[k][...] = rider[...]


def inner_kernel(first, pairs, size, bc_ref, hp_ref, x_ref, g_ref, *refs):
    gx_ref, ds_ref, sums_ref = refs[-5:-2]
    gy_ref, xg_ref = refs[-2:]
    rows = x_ref.shape[0]
    heads = hp_ref.shape[0] // 5
    lanes = 2 * size
    width = pairs * lanes
    if len(refs) == 6 and first > 0:
        scores = refs[0][...]
    else:
        scores = mm(bc_ref[rows : 2 * rows, :], bc_ref[0:rows, :], 1, 1, TOP)
        refs[0][...] = scores
    row = lax.broadcasted_iota(jnp.int32, (rows, rows), 0)
    col = lax.broadcasted_iota(jnp.int32, (rows, rows), 1)
    causal = row >= col
    dt = hp_ref[heads : 2 * heads, :]
    cum = hp_ref[2 * heads : 3 * heads, :]
    cum_t = cum.T
    lane = lax.broadcasted_iota(jnp.int32, (rows, lanes), 1)
    sides = [jnp.where(lane < size, 1.0, 0.0).astype(BF), jnp.where(lane < size, 0.0, 1.0).astype(BF)]
    ds = jnp.zeros((rows, rows), F32)
    for j in range(pairs):
        place = slice(j * lanes, (j + 1) * lanes)
        x, g = x_ref[:, place], g_ref[:, place]
        xs = jnp.concatenate([x * s for s in sides], axis=0)
        gs = jnp.concatenate([g * s for s in sides], axis=0)
        m = mm(gs, x, 1, 1)
        kern = []
        for i in range(2):
            h = 2 * (first + j) + i
            gap = cum_t[:, h : h + 1] - cum[h : h + 1, :]
            fall = jnp.exp(jnp.where(causal, gap, -jnp.inf)) * dt[h : h + 1, :]
            kern.append((fall * scores).astype(BF))
            ds = ds + fall * m[i * rows : (i + 1) * rows]
        y = mm(jnp.concatenate(kern, axis=1), xs, 1, 0)
        gx = mm(jnp.concatenate(kern, axis=0), gs, 0, 0)
        gx_ref[:, place] = gx
        late = slice(width + j * lanes, width + (j + 1) * lanes)
        gy_ref[:, place], gy_ref[:, late] = halves(g.astype(F32) * y)
        xg_ref[:, place], xg_ref[:, late] = halves(x.astype(F32) * gx)
    ds_ref[...] = ds
    pick = head_lanes(2 * pairs, width, size).astype(BF)
    pick = jnp.concatenate([pick, pick], axis=1)
    sums_ref[0] = mm(pick, gy_ref[...], 1, 1)
    sums_ref[1] = mm(pick, xg_ref[...], 1, 1)


def outer_kernel(k, chunks, size, parts, *refs):
    store_ref, x_ref, g_ref, bc_ref, hp_ref, rate_ref = refs[:6]
    gxs, dss, sums = (refs[6 + q * parts : 6 + (q + 1) * parts] for q in range(3))
    rest = refs[6 + 3 * parts :]
    wv_ref, eu_ref = rest[-2:]
    rows, step = x_ref.shape
    all_heads = rate_ref.shape[1]
    heads = all_heads // chunks
    mine = slice(k * heads, (k + 1) * heads)
    piece = step // parts
    b, c = bc_ref[0:rows, :], bc_ref[rows : 2 * rows, :]
    pre, dt, cum, grow, w = (
        hp_ref[q * all_heads + k * heads : q * all_heads + (k + 1) * heads, :] for q in range(5)
    )
    rate = rate_ref[...].T[mine]
    ds = dss[0][...]
    for ref in dss[1:]:
        ds = ds + ref[...]
    db = mm(c, ds, 0, 0, TOP)
    dc = mm(b, ds, 0, 1, TOP)
    b_wide = jnp.concatenate(halves(b), axis=1)
    c_wide = jnp.concatenate(halves(c), axis=1)
    pick = head_lanes(heads, step, size).astype(BF)
    incoming, outgoing = store_ref[0], store_ref[1]
    u = mm(c_wide, jnp.concatenate([incoming, incoming], axis=0), 1, 0)
    v = mm(b_wide, jnp.concatenate([outgoing, outgoing], axis=0), 1, 0)
    scale = spread(w, pick)
    wx = scale * x_ref[...].astype(F32)
    eg = spread(grow, pick) * g_ref[...].astype(F32)
    grad_ref = rest[-5] if k == chunks - 1 else rest[-4]
    for q in range(parts):
        place = slice(q * piece, (q + 1) * piece)
        grad_ref[:, place] = (gxs[q][...] + scale[:, place] * v[:, place]).astype(BF)
    wv_ref[:, :step], wv_ref[:, step:] = halves(wx * v)
    eu_ref[:, :step], eu_ref[:, step:] = halves(eg * u)
    db = db + mm(
        jnp.concatenate([outgoing, outgoing], axis=1), jnp.concatenate(halves(wx), axis=1), 1, 1
    )
    dc = dc + mm(
        jnp.concatenate([incoming, incoming], axis=1), jnp.concatenate(halves(eg), axis=1), 1, 1
    )
    both = jnp.sum(incoming.astype(F32) * outgoing.astype(F32), axis=0, keepdims=True)
    ddecay = jnp.sum(pick.astype(F32) * both, axis=1, keepdims=True)
    pick = jnp.concatenate([pick, pick], axis=1)
    wdw = mm(pick, wv_ref[...], 1, 1)
    egu = mm(pick, eu_ref[...], 1, 1)
    rowsum = jnp.concatenate([s[0] for s in sums], axis=0)
    colsum = jnp.concatenate([s[1] for s in sums], axis=0)
    dcum = rowsum - colsum + egu - wdw
    row = lax.broadcasted_iota(jnp.int32, (rows, rows), 0)
    col = lax.broadcasted_iota(jnp.int32, (rows, rows), 1)
    rev = mm(dcum, jnp.where(row >= col, 1.0, 0.0), 1, 0, TOP)
    decay = grow[:, rows - 1 : rows]
    rev = rev + jnp.sum(wdw, axis=1, keepdims=True) + decay * ddecay
    gate = 1.0 / (1.0 + jnp.exp(-pre))
    small = 1e-30
    ratio = jnp.where(dt > small, gate / jnp.maximum(dt, small), 1.0)
    graw = (colsum + wdw) * ratio - rate * rev * gate
    if k > 0:
        before_ref = rest[1]
        db = db + before_ref[0:rows, :]
        dc = dc + before_ref[rows : 2 * rows, :]
        graw = jnp.concatenate([before_ref[2 * rows :, :], graw], axis=0)
    if k == chunks - 1:
        keep_ref, give_ref = rest[-4], rest[-3]
        core = lax.axis_index("head")
        keep_ref[0:rows, :] = jnp.where(core == 0, db, dc)
        keep_ref[rows:, :] = graw
        give_ref[...] = jnp.where(core == 0, dc, db)
    else:
        back_ref = rest[-3]
        back_ref[0:rows, :] = db
        back_ref[rows : 2 * rows, :] = dc
        back_ref[2 * rows :, :] = graw


def low_kernel(keep_ref, taken_ref, out_ref):
    rows = taken_ref.shape[0]
    low = keep_ref[0:rows, :] + taken_ref[...]
    low = jnp.concatenate([low, keep_ref[rows:, :]], axis=0).astype(BF)
    for k in range(out_ref.shape[0]):
        out_ref[k] = low


def token_kernel(count, mine_ref, other_ref, *refs):
    out_ref = refs[2 * count]
    me, core = lax.axis_index("dp"), lax.axis_index("head")
    part, cols = refs[0].shape
    half = cols // 2
    heads = refs[1].shape[0] // 2
    for r in range(count):
        at = pl.multiple_of(lax.rem(me - r + count, count) * part, 128)
        total = None
        for k, ref in enumerate((mine_ref, other_ref)):
            at_col = pl.multiple_of(lax.rem(core + k, 2) * half, 128)
            at_row = pl.multiple_of(lax.rem(core + k, 2) * heads, 16)
            term = mm(ref[0:half, :], refs[2 * r][:, pl.ds(at_col, half)], 0, 1)
            term = term + mm(ref[half:, :], refs[2 * r + 1][pl.ds(at_row, heads), :], 0, 0)
            total = term if total is None else total + term
        out_ref[:, pl.ds(at, part)] = total.astype(BF)


def order_kernel(n_dp, n_seq, slots, *refs):
    out_ref, sem = refs[-2:]
    toks = refs[:-2]
    rows = toks[0].shape[0]
    place = lax.axis_index("seq")
    even = lax.rem(place, 2) == 0
    copies = []
    for r in range(n_dp):
        for k, (kind, hop) in enumerate(slots):
            above = even if kind == 0 else ~even
            block = jnp.where(above, place + hop, place - hop)
            fits = (block >= 0) & (block < n_seq)
            if hop > 0 and kind == 1:
                fits = fits & jnp.where(above, place < n_seq - 1, place > 0)
            at = pl.multiple_of(jnp.clip(block, 0, n_seq - 1) * rows, 128)
            source = toks[k] if r == 0 else toks[len(slots) + k].at[pl.ds((r - 1) * rows, rows)]
            copy = pltpu.make_async_copy(source, out_ref.at[r, pl.ds(at, rows)], sem.at[r, k])
            copies.append((fits, copy))
    for fits, copy in copies:
        pl.when(fits)(copy.start)
    for fits, copy in copies:
        pl.when(fits)(copy.wait)


def weight_kernel(scale, n_dp, n_seq, tok_ref, source_ref, *refs):
    low_ref, low_sem = refs[-2:]
    rows = tok_ref.shape[1] // n_seq
    core, me = lax.axis_index("head"), lax.axis_index("dp")
    copies = []
    for r in range(n_dp):
        for s in range(n_seq):
            index = s * n_dp + lax.rem(me - r + n_dp, n_dp)
            copies.append(
                pltpu.make_async_copy(
                    source_ref.at[index],
                    low_ref.at[r, :, pl.ds(s * rows, rows)],
                    low_sem.at[r * n_seq + s],
                )
            )
    for copy in copies:
        copy.start()
    for copy in copies:
        copy.wait()
    total = mm(low_ref[0], tok_ref[0], 1, 0)
    for r in range(1, n_dp):
        total = total + mm(low_ref[r], tok_ref[r], 1, 0)
    total = total * scale
    if len(refs) == 4:
        bc_ref, dt_ref = refs[:2]
        half = bc_ref.shape[1]
        bc_ref[...] = total[:half].T
        dt_ref[...] = total[half:]
        return
    own_bc, own_dt, bc_ref, dt_ref = refs[:4]
    half, heads = own_bc.shape[1], own_dt.shape[0]
    for k, (first, second) in enumerate(((own_bc[...], own_dt[...]), (total[:half].T, total[half:]))):
        side = lax.rem(core + k, 2)
        bc_ref[:, pl.ds(pl.multiple_of(side * half, 128), half)] = first
        dt_ref[pl.ds(pl.multiple_of(side * heads, 8), heads), :] = second


def relays(count):
    groups, _ = matchings(count)
    return [
        (kind, hop)
        for hop in range(1, count)
        for kind in (0, 1)
        if any(i - hop + 1 >= 0 or j + hop - 1 < count for i, j in groups[kind])
    ]


def relay(found, block, steps, *others):
    count = lax.axis_size("seq")
    _, pairs = matchings(count)
    for kind, hop in steps:
        source = block if hop == 1 else found[1 - kind, hop - 1]
        source = after(source, *others) if others else source
        found[kind, hop] = lax.ppermute(source, "seq", pairs[kind])
    return [found[step] for step in steps]


def chains(first, own, decay, inner, beside, riders, late):
    count = lax.axis_size("seq")
    place = lax.axis_index("seq")
    chunks = len(first)
    stores = [jnp.zeros((3,) + own.shape[2:], BF) for _ in range(chunks)]
    got = list(first)
    done, todo, extra = [], list(inner), []
    last = count + chunks - 2
    for slot in range(1, last + 1):
        steps = [(hop, slot - hop) for hop in range(1, count) if 0 <= slot - hop < chunks]
        sent = []
        for hop, k in steps:
            value = got[k]
            if hop == 1 and 0 < k < len(riders):
                value = jnp.where((place == 0) | (place == count - 1), value, riders[k])
            if hop > 1:
                value = jnp.where(place == hop - 1, own[0, k], own[1, k])
                value = (value + decay[k] * got[k].astype(F32)).astype(BF)
            sent.append(value)
        for (hop, k), value in zip(steps, sent):
            to = {i: i for i in range(count)}
            for i in (hop - 1, count - hop - 1):
                to[i], to[i + 1] = i + 1, i
            got[k] = lax.ppermute(value, "seq", sorted(to.items()))
            if hop == 1 and k < len(riders):
                riders[k] = got[k]
        for _ in range(-(-len(todo) // (last + 1 - slot))):
            done.append(todo.pop(0)(*sent))
        if slot == 1:
            extra = beside(*sent)
        if slot == last:
            k = steps[-1][1]
            got[k] = after(got[k], *late(*sent))
        if slot < last:
            held = [got[k] for _, k in steps] + [d[0] for d in done[-1:]]
            if slot == last - 1:
                held += extra
            new = slot < chunks
            if new:
                held.append(got[slot])
            kept = lax.optimization_barrier(tuple(held))
            for (_, k), a in zip(steps, kept):
                got[k] = a
            if new:
                got[slot] = kept[-1]
        for hop, k in steps:
            kind = jnp.where(place == hop, 0, jnp.where(place == count - hop - 1, 1, 2))
            zero = jnp.zeros_like(kind)
            stores[k] = lax.dynamic_update_slice(stores[k], got[k][None], (kind, zero, zero))
    done += [make() for make in todo]
    return stores, done


def body(tokens, ssd_input, grad_out, w_bc, w_dt, decay_rate, dt_bias):
    feats, x, g = tokens[0], ssd_input[0], grad_out[0]
    rows, width = feats.shape
    heads = decay_rate.shape[0]
    size = width // heads
    n_dp, n_seq = lax.axis_size("dp"), lax.axis_size("seq")
    part = width // n_dp
    state_n = w_bc.shape[1] // 2
    w_dt = w_dt.T
    rate, bias = decay_rate[None], dt_bias[None]

    pieces = call(split_kernel, [struct((rows, part), BF)] * n_dp, 1.9, feats)
    items = [pieces[0]] + [cyclic(pieces[r], "dp", r) for r in range(1, n_dp)]
    groups = items[:1]
    if n_dp > 1:
        groups.append(items[1] if n_dp == 2 else jnp.concatenate(items[1:], axis=0))
    found = [{} for _ in groups]
    slots = relays(n_seq)
    step = width // CHUNKS
    ride = n_seq == 4 and all(a.shape == (state_n, step) for a in groups)
    second = [(kind, hop) for kind, hop in slots if hop == 2 and not (ride and kind == 0)]
    near = relay(found[0], groups[0], slots[:2])
    partials, local = [project(items[0], w_bc, w_dt)], []
    for r in range(1, n_dp):
        item = after(items[r], partials[0])
        local.append(project(item, w_bc, w_dt))
        partials.append(cyclic(local[-1], "dp", -r))
    spare = relay(found[1], groups[1], slots[:2], *local) if n_dp > 1 else []
    partials[1:] = [after(a, *near) for a in partials[1:]]
    proj = partials + [cyclic(a, "head", 1) for a in partials]
    own, bc, hp, *outs = call(
        functools.partial(state_kernel, 2 * n_dp, size, int(ride)),
        (
            struct((2, CHUNKS, state_n, step), F32),
            struct((2 * rows, state_n), F32),
            struct((5 * heads, rows), F32),
        )
        + (struct((state_n, step), BF),) * CHUNKS
        + (struct((1, step), F32),) * CHUNKS,
        0.1,
        *proj,
        x,
        g,
        rate,
        bias,
        *([found[0][1, 1]] if ride else []),
    )
    first, decay = outs[:CHUNKS], outs[CHUNKS:]
    pairs = width // (2 * size) // PARTS
    span = width // PARTS
    shared = []

    def inner(q, *others):
        held = after(bc, *others, *(spare if q == 0 else [])) if others else bc
        square = struct((rows, rows), F32)
        block = pl.BlockSpec((rows, span), lambda _: (0, q))
        out = call(
            functools.partial(inner_kernel, q * pairs, pairs, size),
            ([square] if q == 0 else [])
            + [struct((rows, span), F32), square, struct((2, 2 * pairs, rows), F32)],
                2.6,
            held,
            hp,
            x,
            g,
            *shared,
            scratch=(pltpu.VMEM((rows, 2 * span), BF), pltpu.VMEM((rows, 2 * span), BF)),
            specs=[VMEM, VMEM, block, block] + [VMEM] * len(shared),
        )
        if q == 0:
            shared.append(out[0])
            out = out[1:]
        return out

    weights = [w_bc, w_dt]

    def beside(*others):
        for r in range(1, n_dp):
            weights.extend(cyclic(after(a, *others), "dp", r) for a in (w_bc, w_dt))
        return weights[2:] + relay(found[0], groups[0], second, *others)

    def late(*others):
        return relay(found[1], groups[1], second, *others) if n_dp > 1 else []

    first[0] = after(first[0], *spare[: 1 if ride else 2])
    riders = [f[1, 1] for f in found] if ride else []
    calls = [functools.partial(inner, q) for q in range(PARTS)]
    stores, inners = chains(first, own, decay, calls, beside, riders, late)
    for f, a in zip(found, riders):
        f[0, 2] = a
    done = [relay(f, a, [t for t in slots if t not in f], stores[-1]) for f, a in zip(found, groups)]
    each = PARTS // CHUNKS
    grad_x, back = None, []
    for k in range(CHUNKS):
        last = k == CHUNKS - 1
        block = pl.BlockSpec((rows, step), lambda _, k=k: (0, k))
        made = (k + 1) * (heads // CHUNKS)
        sums = (struct((rows + heads, rows), F32), struct((rows, rows), F32))
        inputs = [stores[k], x, g, bc, hp, rate]
        for q in range(3):
            inputs += [a[q] for a in inners[k * each : (k + 1) * each]]
        specs = [VMEM, block, block] + [VMEM] * (len(inputs) - 3)
        if k > 0:
            inputs += [grad_x] + back
            specs += [HBM, VMEM]
        grad_x, *back = call(
            functools.partial(outer_kernel, k, CHUNKS, size, each),
            (struct((rows, width), BF),)
            + (sums if last else (struct((2 * rows + made, rows), F32),)),
            5.4 / CHUNKS,
            *inputs,
            scratch=(pltpu.VMEM((rows, 2 * step), BF), pltpu.VMEM((rows, 2 * step), BF)),
            specs=specs,
            out_specs=(block,) + (VMEM,) * (2 if last else 1),
            aliases={len(inputs) - 2: 0} if k > 0 else {},
        )
    keep, give = back
    toks = []
    for f, a in zip(found, groups):
        toks += [a] + [f[step] for step in slots]
    slots = [(0, 0)] + slots
    ordered = call(
        functools.partial(order_kernel, n_dp, n_seq, slots),
        struct((n_dp, n_seq * rows, part), BF),
        1.0,
        *toks,
        scratch=[pltpu.SemaphoreType.DMA((n_dp, len(slots)))],
    )
    taken = after(cyclic(give, "head", 1), ordered)
    count = n_dp * n_seq
    copies = call(low_kernel, struct((count, rows + heads, rows), BF), 1.2, keep, taken)
    mine = copies[0]
    lows = lax.all_to_all(copies, ("seq", "dp"), 0, 0, tiled=True)
    other = cyclic(mine, "head", 1)
    grads = call(
        functools.partial(token_kernel, n_dp),
        struct((rows, width), BF),
        2.9,
        mine,
        other,
        *weights,
    )
    lows = after(lows, grads)
    swapped = cyclic(lows, "head", 1)
    cols = 2 * (rows + heads)
    halves_made = []
    for k, source in enumerate((lows, swapped)):
        halves_made = call(
            functools.partial(weight_kernel, 1.0 / (rows * n_seq * n_dp), n_dp, n_seq),
            (struct((part, (k + 1) * state_n), F32), struct(((k + 1) * heads, part), F32)),
            2.0,
            ordered,
            source,
            *halves_made,
            limit=LIMIT + 2 * n_dp * n_seq * rows * cols,
            scratch=(
                pltpu.VMEM((n_dp, rows + heads, n_seq * rows), BF),
                pltpu.SemaphoreType.DMA((count,)),
            ),
        )
    grad_bc, grad_dt = halves_made
    return grad_x[None], grads[None], grad_bc, grad_dt.T


def solution(mesh):
    in_specs = (
        P(("grp", "dp"), "seq", "head"),
        P(("grp", "dp"), "seq", "head"),
        P(("grp", "dp"), "seq", "head"),
        P(("head", "dp"), None),
        P(("head", "dp"), None),
        P("head"),
        P("head"),
    )
    out_specs = (
        P(("grp", "dp"), "seq", "head"),
        P(("grp", "dp"), "seq", "head"),
        P(("grp", "head", "dp"), None),
        P(("grp", "head", "dp"), None),
    )
    return jax.shard_map(body, mesh=mesh, in_specs=in_specs, out_specs=out_specs, check_vma=False)
```

```python
import functools

import jax
import jax.numpy as jnp
from jax import lax
from jax.experimental import pallas as pl
from jax.experimental.pallas import tpu as pltpu
from jax.sharding import PartitionSpec as P

CHUNKS = 2
PARTS = 4
BF = jnp.bfloat16
F32 = jnp.float32
TOP = lax.Precision.HIGHEST
PER_US = 1.15e9
LIMIT = 16 * 1024 * 1024


def cyclic(a, axis, by):
    count = lax.axis_size(axis)
    return lax.ppermute(a, axis, [(i, (i + by) % count) for i in range(count)])


def mm(a, b, ca, cb, precision=None):
    return lax.dot_general(
        a, b, (((ca,), (cb,)), ((), ())), preferred_element_type=F32, precision=precision
    )


def halves(a):
    high = a.astype(BF)
    return high, (a - high.astype(F32)).astype(BF)


def head_lanes(heads, width, size, first=0):
    row = lax.broadcasted_iota(jnp.int32, (heads, width), 0)
    col = lax.broadcasted_iota(jnp.int32, (heads, width), 1) + first
    low = row * size
    return jnp.where((col >= low) & (col < low + size), 1.0, 0.0).astype(F32)


def spread(a, pick):
    high, low = halves(a)
    both = jnp.concatenate([pick, pick], axis=0)
    return mm(jnp.concatenate([high, low], axis=0), both, 0, 0)


VMEM = pl.BlockSpec(memory_space=pltpu.VMEM)
HBM = pl.BlockSpec(memory_space=pltpu.HBM)


def call(kernel, out_shape, span_us, *args, scratch=(), specs=None, out_specs=None, aliases={}, limit=LIMIT):
    size = sum(a.size * a.dtype.itemsize for a in args)
    return pl.pallas_call(
        kernel,
        out_shape=out_shape,
        grid=(1,),
        in_specs=specs or [VMEM] * len(args),
        out_specs=out_specs or jax.tree.map(lambda _: VMEM, out_shape),
        input_output_aliases=aliases,
        scratch_shapes=list(scratch),
        compiler_params=pltpu.CompilerParams(vmem_limit_bytes=limit),
        cost_estimate=pl.CostEstimate(
            flops=int(span_us * PER_US), bytes_accessed=size, transcendentals=0
        ),
    )(*args)


def struct(shape, dtype):
    return jax.ShapeDtypeStruct(shape, dtype)


def after(a, *others):
    return lax.optimization_barrier((a, others))[0]


def matchings(count):
    groups = [[(i, i + 1) for i in range(kind, count - 1, 2)] for kind in (0, 1)]
    pairs = []
    for group in groups:
        to = {i: i for i in range(count)}
        for i, j in group:
            to[i], to[j] = j, i
        pairs.append(sorted(to.items()))
    return groups, pairs


def split_kernel(a_ref, *outs):
    count = len(outs)
    me = lax.axis_index("dp")
    part = outs[0].shape[1]
    for r in range(count):
        at = pl.multiple_of(lax.rem(me + r, count) * part, 128)
        outs[r][...] = a_ref[:, pl.ds(at, part)]


def project_kernel(a_ref, bc_ref, dt_ref, out_ref):
    a = a_ref[...]
    state_n = bc_ref.shape[1] // 2
    rows = a.shape[0]
    bc = mm(a, bc_ref[...], 1, 0)
    out_ref[0:rows, :] = bc[:, :state_n]
    out_ref[rows : 2 * rows, :] = bc[:, state_n:]
    out_ref[2 * rows :, :] = mm(dt_ref[...], a, 1, 1)


def project(a, w_bc, w_dt):
    rows = a.shape[0]
    total = 2 * rows + w_dt.shape[0]
    return call(
        project_kernel,
        struct((total, w_bc.shape[1] // 2), F32),
        2.1,
        a,
        w_bc,
        w_dt,
    )


def state_kernel(count, size, ride, *refs):
    proj = refs[:count]
    x_ref, g_ref, rate_ref, bias_ref = refs[count : count + 4]
    riders = refs[count + 4 : count + 4 + ride]
    own_ref, bc_ref, hp_ref = refs[count + 4 + ride : count + 7 + ride]
    outs = refs[count + 7 + ride :]
    firsts, decays = outs[: len(outs) // 2], outs[len(outs) // 2 :]
    heads = rate_ref.shape[1]
    rows = x_ref.shape[0]
    rate, bias = rate_ref[...].T, bias_ref[...].T
    chunks, step = own_ref.shape[1], own_ref.shape[3]
    first = pl.multiple_of(2 * rows + lax.axis_index("head") * heads, 8)
    bc = proj[0][0 : 2 * rows, :]
    pre = proj[0][pl.ds(first, heads), :] + bias
    for ref in proj[1:]:
        bc = bc + ref[0 : 2 * rows, :]
        pre = pre + ref[pl.ds(first, heads), :]
    bc_ref[...] = bc
    dt = jnp.maximum(pre, 0.0) + jnp.log1p(jnp.exp(-jnp.abs(pre)))
    row = lax.broadcasted_iota(jnp.int32, (rows, rows), 0)
    col = lax.broadcasted_iota(jnp.int32, (rows, rows), 1)
    cum = mm(-dt * rate, jnp.where(row <= col, 1.0, 0.0), 1, 0, TOP)
    last = cum[:, rows - 1 : rows]
    grow = jnp.exp(cum)
    w = jnp.exp(last - cum) * dt
    decay = jnp.exp(last)
    for k, part in enumerate((pre, dt, cum, grow, w)):
        hp_ref[k * heads : (k + 1) * heads, :] = part
    place = lax.axis_index("seq")
    lowest = place == 0
    sides = []
    for vec in (bc[:rows], bc[rows:]):
        high, low = halves(vec.T)
        sides.append((jnp.concatenate([high, low], axis=1), high))
    for k in range(chunks):
        pick = head_lanes(heads, step, size, k * step)
        decays[k][...] = jnp.sum(pick * decay, axis=0, keepdims=True)
        pick = pick.astype(BF)
        both = []
        for kind, (scale, ref) in enumerate(((w, x_ref), (grow, g_ref))):
            wide, high = sides[kind]
            value = spread(scale, pick) * ref[:, k * step : (k + 1) * step].astype(F32)
            top, rest = halves(value)
            value = mm(wide, jnp.concatenate([top, top], axis=0), 1, 0) + mm(high, rest, 1, 0)
            own_ref[kind, k] = value
            both.append(value)
        firsts[k][...] = jnp.where(lowest, both[0], both[1]).astype(BF)
        if k < ride:
            rider = riders[k]

            @pl.when((place > 0) & (place < lax.axis_size("seq") - 1))
            def _():
                firsts[k][...] = rider[...]


def inner_kernel(first, pairs, size, bc_ref, hp_ref, x_ref, g_ref, *refs):
    gx_ref, ds_ref, sums_ref = refs[-5:-2]
    gy_ref, xg_ref = refs[-2:]
    rows = x_ref.shape[0]
    heads = hp_ref.shape[0] // 5
    lanes = 2 * size
    width = pairs * lanes
    if len(refs) == 6 and first > 0:
        scores = refs[0][...]
    else:
        scores = mm(bc_ref[rows : 2 * rows, :], bc_ref[0:rows, :], 1, 1, TOP)
        refs[0][...] = scores
    row = lax.broadcasted_iota(jnp.int32, (rows, rows), 0)
    col = lax.broadcasted_iota(jnp.int32, (rows, rows), 1)
    causal = row >= col
    dt = hp_ref[heads : 2 * heads, :]
    cum = hp_ref[2 * heads : 3 * heads, :]
    cum_t = cum.T
    lane = lax.broadcasted_iota(jnp.int32, (rows, lanes), 1)
    sides = [jnp.where(lane < size, 1.0, 0.0).astype(BF), jnp.where(lane < size, 0.0, 1.0).astype(BF)]
    ds = jnp.zeros((rows, rows), F32)
    for j in range(pairs):
        place = slice(j * lanes, (j + 1) * lanes)
        x, g = x_ref[:, place], g_ref[:, place]
        xs = jnp.concatenate([x * s for s in sides], axis=0)
        gs = jnp.concatenate([g * s for s in sides], axis=0)
        m = mm(gs, x, 1, 1)
        kern = []
        for i in range(2):
            h = 2 * (first + j) + i
            gap = cum_t[:, h : h + 1] - cum[h : h + 1, :]
            fall = jnp.exp(jnp.where(causal, gap, -jnp.inf)) * dt[h : h + 1, :]
            kern.append((fall * scores).astype(BF))
            ds = ds + fall * m[i * rows : (i + 1) * rows]
        y = mm(jnp.concatenate(kern, axis=1), xs, 1, 0)
        gx = mm(jnp.concatenate(kern, axis=0), gs, 0, 0)
        gx_ref[:, place] = gx
        late = slice(width + j * lanes, width + (j + 1) * lanes)
        gy_ref[:, place], gy_ref[:, late] = halves(g.astype(F32) * y)
        xg_ref[:, place], xg_ref[:, late] = halves(x.astype(F32) * gx)
    ds_ref[...] = ds
    pick = head_lanes(2 * pairs, width, size).astype(BF)
    pick = jnp.concatenate([pick, pick], axis=1)
    sums_ref[0] = mm(pick, gy_ref[...], 1, 1)
    sums_ref[1] = mm(pick, xg_ref[...], 1, 1)


def outer_kernel(k, chunks, size, parts, *refs):
    store_ref, x_ref, g_ref, bc_ref, hp_ref, rate_ref = refs[:6]
    gxs, dss, sums = (refs[6 + q * parts : 6 + (q + 1) * parts] for q in range(3))
    rest = refs[6 + 3 * parts :]
    wv_ref, eu_ref = rest[-2:]
    rows, step = x_ref.shape
    all_heads = rate_ref.shape[1]
    heads = all_heads // chunks
    mine = slice(k * heads, (k + 1) * heads)
    piece = step // parts
    b, c = bc_ref[0:rows, :], bc_ref[rows : 2 * rows, :]
    pre, dt, cum, grow, w = (
        hp_ref[q * all_heads + k * heads : q * all_heads + (k + 1) * heads, :] for q in range(5)
    )
    rate = rate_ref[...].T[mine]
    ds = dss[0][...]
    for ref in dss[1:]:
        ds = ds + ref[...]
    db = mm(c, ds, 0, 0, TOP)
    dc = mm(b, ds, 0, 1, TOP)
    b_wide = jnp.concatenate(halves(b), axis=1)
    c_wide = jnp.concatenate(halves(c), axis=1)
    pick = head_lanes(heads, step, size).astype(BF)
    incoming, outgoing = store_ref[0], store_ref[1]
    u = mm(c_wide, jnp.concatenate([incoming, incoming], axis=0), 1, 0)
    v = mm(b_wide, jnp.concatenate([outgoing, outgoing], axis=0), 1, 0)
    scale = spread(w, pick)
    wx = scale * x_ref[...].astype(F32)
    eg = spread(grow, pick) * g_ref[...].astype(F32)
    grad_ref = rest[-5] if k == chunks - 1 else rest[-4]
    for q in range(parts):
        place = slice(q * piece, (q + 1) * piece)
        grad_ref[:, place] = (gxs[q][...] + scale[:, place] * v[:, place]).astype(BF)
    wv_ref[:, :step], wv_ref[:, step:] = halves(wx * v)
    eu_ref[:, :step], eu_ref[:, step:] = halves(eg * u)
    db = db + mm(
        jnp.concatenate([outgoing, outgoing], axis=1), jnp.concatenate(halves(wx), axis=1), 1, 1
    )
    dc = dc + mm(
        jnp.concatenate([incoming, incoming], axis=1), jnp.concatenate(halves(eg), axis=1), 1, 1
    )
    both = jnp.sum(incoming.astype(F32) * outgoing.astype(F32), axis=0, keepdims=True)
    ddecay = jnp.sum(pick.astype(F32) * both, axis=1, keepdims=True)
    pick = jnp.concatenate([pick, pick], axis=1)
    wdw = mm(pick, wv_ref[...], 1, 1)
    egu = mm(pick, eu_ref[...], 1, 1)
    rowsum = jnp.concatenate([s[0] for s in sums], axis=0)
    colsum = jnp.concatenate([s[1] for s in sums], axis=0)
    dcum = rowsum - colsum + egu - wdw
    row = lax.broadcasted_iota(jnp.int32, (rows, rows), 0)
    col = lax.broadcasted_iota(jnp.int32, (rows, rows), 1)
    rev = mm(dcum, jnp.where(row >= col, 1.0, 0.0), 1, 0, TOP)
    decay = grow[:, rows - 1 : rows]
    rev = rev + jnp.sum(wdw, axis=1, keepdims=True) + decay * ddecay
    gate = 1.0 / (1.0 + jnp.exp(-pre))
    small = 1e-30
    ratio = jnp.where(dt > small, gate / jnp.maximum(dt, small), 1.0)
    graw = (colsum + wdw) * ratio - rate * rev * gate
    if k > 0:
        before_ref = rest[1]
        db = db + before_ref[0:rows, :]
        dc = dc + before_ref[rows : 2 * rows, :]
        graw = jnp.concatenate([before_ref[2 * rows :, :], graw], axis=0)
    if k == chunks - 1:
        keep_ref, give_ref = rest[-4], rest[-3]
        core = lax.axis_index("head")
        keep_ref[0:rows, :] = jnp.where(core == 0, db, dc)
        keep_ref[rows:, :] = graw
        give_ref[...] = jnp.where(core == 0, dc, db)
    else:
        back_ref = rest[-3]
        back_ref[0:rows, :] = db
        back_ref[rows : 2 * rows, :] = dc
        back_ref[2 * rows :, :] = graw


def low_kernel(keep_ref, taken_ref, out_ref):
    rows = taken_ref.shape[0]
    low = keep_ref[0:rows, :] + taken_ref[...]
    low = jnp.concatenate([low, keep_ref[rows:, :]], axis=0).astype(BF)
    for k in range(out_ref.shape[0]):
        out_ref[k] = low


def token_kernel(count, mine_ref, other_ref, *refs):
    out_ref = refs[2 * count]
    me, core = lax.axis_index("dp"), lax.axis_index("head")
    part, cols = refs[0].shape
    half = cols // 2
    heads = refs[1].shape[0] // 2
    for r in range(count):
        at = pl.multiple_of(lax.rem(me - r + count, count) * part, 128)
        total = None
        for k, ref in enumerate((mine_ref, other_ref)):
            at_col = pl.multiple_of(lax.rem(core + k, 2) * half, 128)
            at_row = pl.multiple_of(lax.rem(core + k, 2) * heads, 16)
            term = mm(ref[0:half, :], refs[2 * r][:, pl.ds(at_col, half)], 0, 1)
            term = term + mm(ref[half:, :], refs[2 * r + 1][pl.ds(at_row, heads), :], 0, 0)
            total = term if total is None else total + term
        out_ref[:, pl.ds(at, part)] = total.astype(BF)


def order_kernel(n_dp, n_seq, slots, *refs):
    out_ref, sem = refs[-2:]
    toks = refs[:-2]
    rows = toks[0].shape[0]
    place = lax.axis_index("seq")
    even = lax.rem(place, 2) == 0
    copies = []
    for r in range(n_dp):
        for k, (kind, hop) in enumerate(slots):
            above = even if kind == 0 else ~even
            block = jnp.where(above, place + hop, place - hop)
            fits = (block >= 0) & (block < n_seq)
            if hop > 0 and kind == 1:
                fits = fits & jnp.where(above, place < n_seq - 1, place > 0)
            at = pl.multiple_of(jnp.clip(block, 0, n_seq - 1) * rows, 128)
            source = toks[k] if r == 0 else toks[len(slots) + k].at[pl.ds((r - 1) * rows, rows)]
            copy = pltpu.make_async_copy(source, out_ref.at[r, pl.ds(at, rows)], sem.at[r, k])
            copies.append((fits, copy))
    for fits, copy in copies:
        pl.when(fits)(copy.start)
    for fits, copy in copies:
        pl.when(fits)(copy.wait)


def weight_kernel(scale, n_dp, n_seq, tok_ref, source_ref, *refs):
    low_ref, low_sem = refs[-2:]
    rows = tok_ref.shape[1] // n_seq
    core, me = lax.axis_index("head"), lax.axis_index("dp")
    copies = []
    for r in range(n_dp):
        for s in range(n_seq):
            index = s * n_dp + lax.rem(me - r + n_dp, n_dp)
            copies.append(
                pltpu.make_async_copy(
                    source_ref.at[index],
                    low_ref.at[r, :, pl.ds(s * rows, rows)],
                    low_sem.at[r * n_seq + s],
                )
            )
    for copy in copies:
        copy.start()
    for copy in copies:
        copy.wait()
    total = mm(low_ref[0], tok_ref[0], 1, 0)
    for r in range(1, n_dp):
        total = total + mm(low_ref[r], tok_ref[r], 1, 0)
    total = total * scale
    if len(refs) == 4:
        bc_ref, dt_ref = refs[:2]
        half = bc_ref.shape[1]
        bc_ref[...] = total[:half].T
        dt_ref[...] = total[half:]
        return
    own_bc, own_dt, bc_ref, dt_ref = refs[:4]
    half, heads = own_bc.shape[1], own_dt.shape[0]
    for k, (first, second) in enumerate(((own_bc[...], own_dt[...]), (total[:half].T, total[half:]))):
        side = lax.rem(core + k, 2)
        bc_ref[:, pl.ds(pl.multiple_of(side * half, 128), half)] = first
        dt_ref[pl.ds(pl.multiple_of(side * heads, 8), heads), :] = second


def relays(count):
    groups, _ = matchings(count)
    return [
        (kind, hop)
        for hop in range(1, count)
        for kind in (0, 1)
        if any(i - hop + 1 >= 0 or j + hop - 1 < count for i, j in groups[kind])
    ]


def relay(found, block, steps, *others):
    count = lax.axis_size("seq")
    _, pairs = matchings(count)
    for kind, hop in steps:
        source = block if hop == 1 else found[1 - kind, hop - 1]
        source = after(source, *others) if others else source
        found[kind, hop] = lax.ppermute(source, "seq", pairs[kind])
    return [found[step] for step in steps]


def chains(first, own, decay, inner, beside, riders, late):
    count = lax.axis_size("seq")
    place = lax.axis_index("seq")
    chunks = len(first)
    stores = [jnp.zeros((3,) + own.shape[2:], BF) for _ in range(chunks)]
    got = list(first)
    done, todo, extra = [], list(inner), []
    last = count + chunks - 2
    for slot in range(1, last + 1):
        steps = [(hop, slot - hop) for hop in range(1, count) if 0 <= slot - hop < chunks]
        sent = []
        for hop, k in steps:
            value = got[k]
            if hop == 1 and 0 < k < len(riders):
                value = jnp.where((place == 0) | (place == count - 1), value, riders[k])
            if hop > 1:
                value = jnp.where(place == hop - 1, own[0, k], own[1, k])
                value = (value + decay[k] * got[k].astype(F32)).astype(BF)
            sent.append(value)
        for (hop, k), value in zip(steps, sent):
            to = {i: i for i in range(count)}
            for i in (hop - 1, count - hop - 1):
                to[i], to[i + 1] = i + 1, i
            got[k] = lax.ppermute(value, "seq", sorted(to.items()))
            if hop == 1 and k < len(riders):
                riders[k] = got[k]
        for _ in range(-(-len(todo) // (last + 1 - slot))):
            done.append(todo.pop(0)(*sent))
        if slot == 1:
            extra = beside(*sent)
        if slot == last:
            k = steps[-1][1]
            got[k] = after(got[k], *late(*sent))
        if slot < last:
            held = [got[k] for _, k in steps] + [d[0] for d in done[-1:]]
            if slot == last - 1:
                held += extra
            new = slot < chunks
            if new:
                held.append(got[slot])
            kept = lax.optimization_barrier(tuple(held))
            for (_, k), a in zip(steps, kept):
                got[k] = a
            if new:
                got[slot] = kept[-1]
        for hop, k in steps:
            kind = jnp.where(place == hop, 0, jnp.where(place == count - hop - 1, 1, 2))
            zero = jnp.zeros_like(kind)
            stores[k] = lax.dynamic_update_slice(stores[k], got[k][None], (kind, zero, zero))
    done += [make() for make in todo]
    return stores, done


def body(tokens, ssd_input, grad_out, w_bc, w_dt, decay_rate, dt_bias):
    feats, x, g = tokens[0], ssd_input[0], grad_out[0]
    rows, width = feats.shape
    heads = decay_rate.shape[0]
    size = width // heads
    n_dp, n_seq = lax.axis_size("dp"), lax.axis_size("seq")
    part = width // n_dp
    state_n = w_bc.shape[1] // 2
    w_dt = w_dt.T
    rate, bias = decay_rate[None], dt_bias[None]

    pieces = call(split_kernel, [struct((rows, part), BF)] * n_dp, 1.9, feats, limit=48 * 1024 * 1024)
    items = [pieces[0]] + [cyclic(pieces[r], "dp", r) for r in range(1, n_dp)]
    groups = items[:1]
    if n_dp > 1:
        groups.append(items[1] if n_dp == 2 else jnp.concatenate(items[1:], axis=0))
    found = [{} for _ in groups]
    slots = relays(n_seq)
    step = width // CHUNKS
    ride = n_seq == 4 and all(a.shape == (state_n, step) for a in groups)
    second = [(kind, hop) for kind, hop in slots if hop == 2 and not (ride and kind == 0)]
    near = relay(found[0], groups[0], slots[:2])
    partials, local = [project(items[0], w_bc, w_dt)], []
    for r in range(1, n_dp):
        item = after(items[r], partials[0])
        local.append(project(item, w_bc, w_dt))
        partials.append(cyclic(local[-1], "dp", -r))
    spare = relay(found[1], groups[1], slots[:2], *local) if n_dp > 1 else []
    partials[1:] = [after(a, *near) for a in partials[1:]]
    proj = partials + [cyclic(a, "head", 1) for a in partials]
    own, bc, hp, *outs = call(
        functools.partial(state_kernel, 2 * n_dp, size, int(ride)),
        (
            struct((2, CHUNKS, state_n, step), F32),
            struct((2 * rows, state_n), F32),
            struct((5 * heads, rows), F32),
        )
        + (struct((state_n, step), BF),) * CHUNKS
        + (struct((1, step), F32),) * CHUNKS,
        0.1,
        *proj,
        x,
        g,
        rate,
        bias,
        *([found[0][1, 1]] if ride else []),
    )
    first, decay = outs[:CHUNKS], outs[CHUNKS:]
    pairs = width // (2 * size) // PARTS
    span = width // PARTS
    shared = []

    def inner(q, *others):
        held = after(bc, *others) if others else bc
        square = struct((rows, rows), F32)
        block = pl.BlockSpec((rows, span), lambda _: (0, q))
        out = call(
            functools.partial(inner_kernel, q * pairs, pairs, size),
            ([square] if q == 0 else [])
            + [struct((rows, span), F32), square, struct((2, 2 * pairs, rows), F32)],
                2.6,
            held,
            hp,
            x,
            g,
            *shared,
            scratch=(pltpu.VMEM((rows, 2 * span), BF), pltpu.VMEM((rows, 2 * span), BF)),
            specs=[VMEM, VMEM, block, block] + [VMEM] * len(shared),
        )
        if q == 0:
            shared.append(out[0])
            out = out[1:]
        return out

    weights = [w_bc, w_dt]

    def beside(*others):
        for r in range(1, n_dp):
            weights.extend(cyclic(after(a, *others), "dp", r) for a in (w_bc, w_dt))
        return weights[2:] + relay(found[0], groups[0], second, *others)

    def late(*others):
        return relay(found[1], groups[1], second, *others) if n_dp > 1 else []

    first[0] = after(first[0], *spare)
    riders = [f[1, 1] for f in found] if ride else []
    calls = [functools.partial(inner, q) for q in range(PARTS)]
    stores, inners = chains(first, own, decay, calls, beside, riders, late)
    for f, a in zip(found, riders):
        f[0, 2] = a
    done = [relay(f, a, [t for t in slots if t not in f], stores[-1]) for f, a in zip(found, groups)]
    each = PARTS // CHUNKS
    grad_x, back = None, []
    for k in range(CHUNKS):
        last = k == CHUNKS - 1
        block = pl.BlockSpec((rows, step), lambda _, k=k: (0, k))
        made = (k + 1) * (heads // CHUNKS)
        sums = (struct((rows + heads, rows), F32), struct((rows, rows), F32))
        inputs = [stores[k], x, g, bc, hp, rate]
        for q in range(3):
            inputs += [a[q] for a in inners[k * each : (k + 1) * each]]
        specs = [VMEM, block, block] + [VMEM] * (len(inputs) - 3)
        if k > 0:
            inputs += [grad_x] + back
            specs += [HBM, VMEM]
        grad_x, *back = call(
            functools.partial(outer_kernel, k, CHUNKS, size, each),
            (struct((rows, width), BF),)
            + (sums if last else (struct((2 * rows + made, rows), F32),)),
            5.4 / CHUNKS,
            *inputs,
            scratch=(pltpu.VMEM((rows, 2 * step), BF), pltpu.VMEM((rows, 2 * step), BF)),
            specs=specs,
            out_specs=(block,) + (VMEM,) * (2 if last else 1),
            aliases={len(inputs) - 2: 0} if k > 0 else {},
        )
    keep, give = back
    toks = []
    for f, a in zip(found, groups):
        toks += [a] + [f[step] for step in slots]
    slots = [(0, 0)] + slots
    ordered = call(
        functools.partial(order_kernel, n_dp, n_seq, slots),
        struct((n_dp, n_seq * rows, part), BF),
        1.0,
        *toks,
        scratch=[pltpu.SemaphoreType.DMA((n_dp, len(slots)))],
    )
    taken = after(cyclic(give, "head", 1), ordered)
    count = n_dp * n_seq
    copies = call(low_kernel, struct((count, rows + heads, rows), BF), 1.2, keep, taken)
    mine = copies[0]
    lows = lax.all_to_all(copies, ("seq", "dp"), 0, 0, tiled=True)
    other = cyclic(mine, "head", 1)
    grads = call(
        functools.partial(token_kernel, n_dp),
        struct((rows, width), BF),
        2.9,
        mine,
        other,
        *weights,
    )
    lows = after(lows, grads)
    swapped = cyclic(lows, "head", 1)
    cols = 2 * (rows + heads)
    halves_made = []
    for k, source in enumerate((lows, swapped)):
        halves_made = call(
            functools.partial(weight_kernel, 1.0 / (rows * n_seq * n_dp), n_dp, n_seq),
            (struct((part, (k + 1) * state_n), F32), struct(((k + 1) * heads, part), F32)),
            2.0,
            ordered,
            source,
            *halves_made,
            limit=LIMIT + 2 * n_dp * n_seq * rows * cols,
            scratch=(
                pltpu.VMEM((n_dp, rows + heads, n_seq * rows), BF),
                pltpu.SemaphoreType.DMA((count,)),
            ),
        )
    grad_bc, grad_dt = halves_made
    return grad_x[None], grads[None], grad_bc, grad_dt.T


def solution(mesh):
    in_specs = (
        P(("grp", "dp"), "seq", "head"),
        P(("grp", "dp"), "seq", "head"),
        P(("grp", "dp"), "seq", "head"),
        P(("head", "dp"), None),
        P(("head", "dp"), None),
        P("head"),
        P("head"),
    )
    out_specs = (
        P(("grp", "dp"), "seq", "head"),
        P(("grp", "dp"), "seq", "head"),
        P(("grp", "head", "dp"), None),
        P(("grp", "head", "dp"), None),
    )
    return jax.shard_map(body, mesh=mesh, in_specs=in_specs, out_specs=out_specs, check_vma=False)
```
